128 devices in a mesh: seq: 16 (over z, y), exp: 8 (over x, core).
Axes of the slice: x: 4, y: 4, z: 4, core: 2. Of those that a mesh axis runs over, the one named last changes fastest.
Arguments:
- layer_input: bfloat16 [16384, 2048], P(('seq', 'exp')), may hold values from -24 to 24, as said below
- attn_gain: float32 [2048], replicated, may hold values from 0.1 to 1.9
- query_proj: bfloat16 [2048, 3072], P(None, 'exp'), may hold values from -0.1875 to 0.1875
- latent_proj: bfloat16 [2048, 576], replicated, may hold values from -0.125 to 0.125
- latent_gain: float32 [512], replicated, may hold values from 0.1 to 1.9
- kv_proj: bfloat16 [512, 4096], P(None, 'exp'), may hold values from -0.25 to 0.25
- output_proj: bfloat16 [2048, 2048], P('exp'), may hold values from -3 to 3
- ffn_gain: float32 [2048], replicated, may hold values from 0.1 to 1.9
- router_proj: float32 [2048, 8], replicated, may hold values from -0.0625 to 0.0625
- shared_gate_up: bfloat16 [2048, 2, 2816], P(None, None, 'exp'), may hold values from -0.125 to 0.125
- shared_down: bfloat16 [2816, 2048], P('exp'), may hold values from -0.15625 to 0.15625
- expert_gate_up: bfloat16 [8, 2048, 2816], P('exp'), may hold values from -0.125 to 0.125
- expert_down: bfloat16 [8, 1408, 2048], P('exp'), may hold values from -0.625 to 0.625
- segment_ids: int32 [16384], replicated, may hold values from 0 to 31, as said below
- expert_routes: int32 [16384, 6], P(('seq', 'exp')), may hold values from 0 to 7, all different within a row; in each aligned block of 128 rows (0 to 127, 128 to 255, ...) at most 128 rows name the same one
- out_grad: bfloat16 [16384, 2048], P(('seq', 'exp')), may hold values from -6 to 6
Outputs:
- layer_output: bfloat16 [16384, 2048], P(('seq', 'exp'))
- input_grad: bfloat16 [16384, 2048], P(('seq', 'exp'))
- attn_gain_grad: float32 [2048], replicated
- query_proj_grad: float32 [2048, 3072], P(None, 'exp')
- latent_proj_grad: float32 [2048, 576], replicated
- latent_gain_grad: float32 [512], replicated
- kv_proj_grad: float32 [512, 4096], P(None, 'exp')
- output_proj_grad: float32 [2048, 2048], P('exp')
- ffn_gain_grad: float32 [2048], replicated
- router_grad: float32 [2048, 8], replicated
- shared_gate_up_grad: float32 [2048, 2, 2816], P('seq', None, 'exp')
- shared_down_grad: float32 [2816, 2048], P('exp', 'seq')
- expert_gate_up_grad: float32 [8, 2048, 2816], P('exp', 'seq')
- expert_down_grad: float32 [8, 1408, 2048], P('exp', None, 'seq')
The draws below stay inside these ranges and needn't reach their ends.
Inputs may be any that keep to these rules, and one draw needn't show every extreme that they name: `layer_input`: the block's input. `segment_ids`: never falls along the tokens; every document lies within one packed sequence of 2048 tokens, and the documents of packed sequence s are numbered 4 s to 4 s + 3. `expert_routes`: each token names 6 different experts; the 128 rows of one device name one expert at most 128 times.
All inputs are finite; a program needn't handle non-finite values.
Results may differ from the reference program's by a relative error of at most 0.029.
Values may be sent and summed in bfloat16 or wider, within the bound.
A program may use at most 256 MiB of HBM per device.

```python
import math
import jax
import jax.numpy as jnp
import numpy as np
from jax import lax

D = 2048
HEADS = 16
NOPE = 128
ROPE = 64
VDIM = 128
LAT = 512
F = 1408
TOP = 6
EXPERTS = 8
FS = 2816
TM = 128
SEQ_LEN = 2048
TOKENS = 16384
CAP = 128


def draw_layer_input(key, part):
    key = jax.random.fold_in(key, 11)
    row_key, column_key, entry_key = jax.random.split(key, 3)
    column_scale = jnp.exp(jax.random.uniform(column_key, (1, D), jnp.float32, math.log(0.5), math.log(2.0)))
    entries = jnp.clip(jax.random.normal(entry_key, (TOKENS, D), jnp.float32), -4.0, 4.0)
    row_scale = jnp.exp(jax.random.uniform(row_key, (TOKENS, 1), jnp.float32, math.log(0.3), math.log(3.0)))
    return (entries * row_scale * column_scale).astype(jnp.bfloat16)


def draw_segment_ids(key, part):
    key = jax.random.fold_in(key, 23)
    first_key, second_key, third_key = jax.random.split(key, 3)
    seq_count = TOKENS // SEQ_LEN
    first_end = jax.random.randint(first_key, (seq_count, 1), 1, TM)
    long_end = jax.random.randint(second_key, (seq_count, 1), SEQ_LEN - TM + 1, SEQ_LEN)
    offset = jax.random.randint(third_key, (seq_count, 1), 0, TM)
    last_start = jnp.minimum(long_end + offset, SEQ_LEN - 1)
    local = jnp.arange(SEQ_LEN, dtype=jnp.int32)[None, :]
    number = jnp.arange(seq_count, dtype=jnp.int32)[:, None] * 4
    ids = number + (local >= first_end).astype(jnp.int32) + (local >= long_end).astype(jnp.int32) + (local >= last_start).astype(jnp.int32)
    return ids.reshape(TOKENS)


def block_levels(stream_key, extent, shards, low, top_value):
    def one(dim, parts):
        draws = jax.random.uniform(jax.random.fold_in(jax.random.fold_in(stream_key, 6), dim), (parts,), jnp.float32, low / len(shards), top_value / len(shards))
        return jnp.repeat(jnp.exp(draws), extent[dim] // parts).reshape((-1,) + (1,) * (len(extent) - dim - 1))

    factor_of = one(*shards[0])
    for cut in shards[1:]:
        factor_of = factor_of * one(*cut)
    return factor_of


def assign_block(stream_key, own, number, rows, amount, top, reach, lean):
    sequence = jax.random.permutation(stream_key, amount)
    heavy_load, common = shares(amount, rows * top, reach, lean, True), shares(amount, rows * top, reach, lean, False)
    places = jnp.arange(amount)

    def named(tallies, turn):
        used = int((tallies > 0).sum())
        fixed = max(1, used // 4)
        passed = fixed + (places - fixed + turn * (used - fixed)) % max(1, amount - fixed)
        return jnp.zeros((amount,), jnp.int32).at[sequence[jnp.where(places < fixed, places, passed)]].set(jnp.asarray(tallies, jnp.int32))

    tallies = jnp.where(number % 4 == 0, named(heavy_load, number // 4), named(common, number - number // 4 - 1))
    mixed = jax.random.permutation(jax.random.fold_in(own, 3), amount)
    giver, taker = mixed[0:amount // 2 * 2:2], mixed[1:amount // 2 * 2:2]
    slack = jnp.minimum(tallies[giver] - 1, reach - tallies[taker]) // 2
    slack = jnp.where((giver == sequence[0]) | (taker == sequence[0]) | (tallies[taker] == 0), 0, jnp.maximum(slack, 0))
    passed = jax.random.randint(jax.random.fold_in(own, 4), (amount // 2,), 0, 1 << 20) % (slack + 1)
    tallies = tallies.at[giver].add(-passed).at[taker].add(passed)
    items = jnp.searchsorted(jnp.cumsum(tallies), jnp.arange(rows * top), side="right").astype(jnp.int32)
    grid = items.reshape(top, rows).T
    grid = grid[jax.random.permutation(jax.random.fold_in(own, 1), rows)]
    turn = jax.random.randint(jax.random.fold_in(own, 2), (rows, 1), 0, top)
    return jnp.take_along_axis(grid, (jnp.arange(top)[None, :] + turn) % top, axis=1)


def shares(count, total, limit, slope, full):
    portions = [(1 << 20) // math.isqrt(standing ** slope) + 1 for standing in range(1, count + 1)]
    largest = limit if full else min(limit, max(-(-total // count), total * portions[0] // sum(portions)))
    least = 1 if total - largest >= count - 1 else 0
    counts, rest = [largest] + [least] * (count - 1), total - largest - least * (count - 1)
    while rest > 0:
        candidates = [i for i in range(1, count) if counts[i] < largest] or [i for i in range(1, count) if counts[i] < limit]
        mass, remaining = sum([portions[i] for i in candidates]), rest
        for i in candidates:
            more = min(limit - counts[i], max(1, remaining * portions[i] // mass), rest)
            counts[i] = counts[i] + more
            rest = rest - more
    return np.array(counts)


def noise(stream_key, extent, scale, reach, shards=(), kind=jnp.bfloat16):
    drawn = scale * jax.random.normal(stream_key, extent, jnp.float32)
    if shards:
        drawn = drawn * block_levels(stream_key, extent, shards, -0.22, 0.18)
    return jnp.clip(drawn, -reach, reach).astype(kind)


def setup_inputs(seed: int = 0) -> dict:
    keys = jax.random.split(jax.random.key(seed), 17)
    layer_input = draw_layer_input(jax.random.fold_in(keys[16], 71), 0)
    attn_gain = jnp.clip(1.0 + 0.18 * jax.random.normal(keys[1], (D,), jnp.float32), 0.1, 1.9)
    query_proj = noise(keys[2], (D, HEADS * (NOPE + ROPE)), (D // 2) ** -0.5, 0.1875, ((1, 8),))
    latent_proj = noise(keys[3], (D, LAT + ROPE), D ** -0.5, 0.125)
    latent_gain = jnp.clip(1.0 + 0.18 * jax.random.normal(keys[4], (LAT,), jnp.float32), 0.1, 1.9)
    kv_proj = noise(keys[5], (LAT, HEADS * (NOPE + VDIM)), LAT ** -0.5, 0.25, ((1, 8),))
    output_proj = noise(keys[6], (HEADS * VDIM, D), 4 ** -0.5, 3.0, ((0, 8),))
    ffn_gain = jnp.clip(1.0 + 0.18 * jax.random.normal(keys[7], (D,), jnp.float32), 0.1, 1.9)
    router_proj = noise(keys[8], (D, EXPERTS), (4 * D) ** -0.5, 0.0625, (), jnp.float32)
    shared_gate_up = noise(keys[9], (D, 2, FS), D ** -0.5, 0.125, ((2, 8),))
    shared_down = noise(keys[10], (FS, D), (FS // 2) ** -0.5, 0.15625, ((0, 8),))
    expert_gate_up = noise(keys[11], (EXPERTS, D, 2 * F), D ** -0.5, 0.125, ((0, 8),))
    expert_down = noise(keys[12], (EXPERTS, F, D), (F // 16) ** -0.5, 0.625, ((0, 8),))
    segment_ids = draw_segment_ids(jax.random.fold_in(keys[16], 71), 0)
    expert_routes_keys = jax.random.split(jax.random.fold_in(keys[14], 1), TOKENS // TM)
    expert_routes_turns = jax.random.permutation(jax.random.fold_in(keys[14], 3), TOKENS // TM)
    expert_routes = jax.vmap(lambda own, number: assign_block(jax.random.fold_in(keys[14], 2), own, number, TM, EXPERTS, TOP, CAP, 1))(expert_routes_keys, expert_routes_turns).reshape((TOKENS, TOP))
    out_grad = noise(keys[15], (TOKENS, D), 1.0, 6.0, ((0, 128),))
    return dict(layer_input=layer_input, attn_gain=attn_gain, query_proj=query_proj, latent_proj=latent_proj, latent_gain=latent_gain, kv_proj=kv_proj, output_proj=output_proj, ffn_gain=ffn_gain, router_proj=router_proj, shared_gate_up=shared_gate_up, shared_down=shared_down, expert_gate_up=expert_gate_up, expert_down=expert_down, segment_ids=segment_ids, expert_routes=expert_routes, out_grad=out_grad)


@jax.custom_vjp
def low(v):
    return lax.optimization_barrier(v.astype(jnp.bfloat16)).astype(jnp.float32)

@jax.custom_vjp
def low_back(v):
    return v

def low_keep(v):
    return (low(v), None)

def low_pass(kept, grad):
    return (grad,)

def back_keep(v):
    return (v, None)

def back_low(kept, grad):
    return (low(grad),)
low.defvjp(low_keep, low_pass)
low_back.defvjp(back_keep, back_low)
highest = lax.Precision.HIGHEST
EPSILON = 1e-06

def rms_scale(tensor, gain_vec):
    return tensor * lax.rsqrt(lax.optimization_barrier(jnp.mean(tensor * tensor, axis=-1, keepdims=True)) + EPSILON) * gain_vec

def silu(tensor):
    return tensor * jax.nn.sigmoid(tensor)

def rotate(tensor, position, direction):
    half_width = tensor.shape[-1] // 2
    frequency = jnp.exp(jnp.arange(half_width, dtype=jnp.float32) * (-math.log(10000.0) / half_width))
    angles = position.astype(jnp.float32)[:, None] * frequency[None, :]
    shape_out = (tensor.shape[0],) + (1,) * (tensor.ndim - 2) + (half_width,)
    cosine = jnp.cos(angles).reshape(shape_out)
    sine_term = direction * jnp.sin(angles).reshape(shape_out)
    first_half = tensor[..., :half_width]
    second_half = tensor[..., half_width:]
    return jnp.concatenate([first_half * cosine - second_half * sine_term, first_half * sine_term + second_half * cosine], axis=-1)

def layer_forward(params, segment_ids, expert_routes):
    layer_input, attn_gain, query_proj, latent_proj, latent_gain, kv_proj, output_proj, ffn_gain, router_proj, shared_gate_up, shared_down, expert_gate_up, expert_down = params
    position = jnp.arange(TOKENS, dtype=jnp.int32)
    rope_pos = position % SEQ_LEN
    normed_in = low(rms_scale(layer_input, attn_gain))
    query_raw = low_back(jnp.dot(normed_in, query_proj, precision=highest)).reshape(TOKENS, HEADS, NOPE + ROPE)
    queries = low(jnp.concatenate([query_raw[..., :NOPE], rotate(query_raw[..., NOPE:], rope_pos, 1.0)], axis=-1))
    latent_raw = low_back(jnp.dot(normed_in, latent_proj, precision=highest))
    latent_normed = low(rms_scale(latent_raw[:, :LAT], latent_gain))
    rope_key = low(rotate(latent_raw[:, LAT:], rope_pos, 1.0))
    packed = low(low_back(jnp.dot(latent_normed, kv_proj, precision=highest))).reshape(TOKENS, HEADS, NOPE + VDIM)
    key_nope = packed[..., :NOPE]
    values = packed[..., NOPE:]
    score_scale = (NOPE + ROPE) ** (-0.5)
    seq_count = TOKENS // SEQ_LEN
    block_rows = math.gcd(SEQ_LEN, 512)
    block_count = SEQ_LEN // block_rows
    local_pos = jnp.arange(SEQ_LEN, dtype=jnp.int32)

    def attend_sequence(pieces):
        seq_queries, seq_keys, seq_rope, seq_values, seq_seg = pieces

        def attend(block):
            query_block, block_pos, block_seg = block
            scores = (jnp.einsum('qhc,khc->hqk', query_block[..., :NOPE], seq_keys, precision=highest) + jnp.einsum('qhc,kc->hqk', query_block[..., NOPE:], seq_rope, precision=highest)) * score_scale
            scores = low_back(scores)
            allowed = (block_seg[:, None] == seq_seg[None, :]) & (local_pos[None, :] <= block_pos[:, None])
            scores = jnp.where(allowed[None], scores, -1e+30)
            top_score = lax.optimization_barrier(jnp.max(scores, axis=-1, keepdims=True))
            weights = jnp.exp(scores - top_score)
            soft_weights = weights / lax.optimization_barrier(jnp.sum(weights, axis=-1, keepdims=True))
            return jnp.einsum('hqk,khc->qhc', low(soft_weights), seq_values, precision=highest)
        return lax.map(jax.checkpoint(attend), (seq_queries.reshape(block_count, block_rows, HEADS, NOPE + ROPE), local_pos.reshape(block_count, block_rows), seq_seg.reshape(block_count, block_rows)))
    head_rows = lax.map(attend_sequence, (queries.reshape(seq_count, SEQ_LEN, HEADS, NOPE + ROPE), key_nope.reshape(seq_count, SEQ_LEN, HEADS, NOPE), rope_key.reshape(seq_count, SEQ_LEN, ROPE), values.reshape(seq_count, SEQ_LEN, HEADS, VDIM), segment_ids.reshape(seq_count, SEQ_LEN)))
    heads_out = low(low_back(head_rows.reshape(TOKENS, HEADS * VDIM)))
    attn_out = low_back(jnp.dot(heads_out, output_proj, precision=highest))
    residual = layer_input + attn_out
    normed_mid = low(rms_scale(residual, ffn_gain))
    logits = jnp.dot(normed_mid, router_proj, precision=highest)
    logit_top = lax.optimization_barrier(jnp.max(logits, axis=-1, keepdims=True))
    logit_exp = jnp.exp(logits - logit_top)
    gate_probs = logit_exp / lax.optimization_barrier(jnp.sum(logit_exp, axis=-1, keepdims=True))
    route_weights = jnp.take_along_axis(gate_probs, expert_routes, axis=1)
    shared_pre = low_back(jnp.einsum('td,dgf->tgf', normed_mid, shared_gate_up, precision=highest))
    shared_act = low(silu(shared_pre[:, 0]) * shared_pre[:, 1])
    shared_out = jnp.dot(shared_act, shared_down, precision=highest)
    routed = jnp.zeros_like(residual)
    for expert_id in range(EXPERTS):
        picked = lax.optimization_barrier(jnp.sum(jnp.where(expert_routes == expert_id, route_weights, 0.0), axis=1))
        sent_rows = low_back(normed_mid)
        expert_pre = low_back(jnp.dot(sent_rows, expert_gate_up[expert_id], precision=highest))
        active = low(silu(expert_pre[:, :F]) * expert_pre[:, F:])
        returned = low(low_back(jnp.dot(active, expert_down[expert_id], precision=highest)))
        routed = routed + picked[:, None] * returned
    return residual + (shared_out + routed)

def reference(layer_input, attn_gain, query_proj, latent_proj, latent_gain, kv_proj, output_proj, ffn_gain, router_proj, shared_gate_up, shared_down, expert_gate_up, expert_down, segment_ids, expert_routes, out_grad):
    params = tuple((member.astype(jnp.float32) for member in (layer_input, attn_gain, query_proj, latent_proj, latent_gain, kv_proj, output_proj, ffn_gain, router_proj, shared_gate_up, shared_down, expert_gate_up, expert_down)))

    def forward(*inputs):
        return layer_forward(inputs, segment_ids, expert_routes)
    output, pullback = jax.vjp(forward, *params)
    gradients = pullback(out_grad.astype(jnp.float32))
    return (output.astype(jnp.bfloat16), gradients[0].astype(jnp.bfloat16), gradients[1], gradients[2], gradients[3], gradients[4], gradients[5], gradients[6], gradients[7], gradients[8], gradients[9], gradients[10], gradients[11], gradients[12])
```

```python
import math

import jax
import jax.numpy as jnp
from jax import lax
from jax.sharding import PartitionSpec as P

NOPE = 128
ROPE = 64
VDIM = 128
LAT = 512
F = 1408
TOP = 6
EXPERTS = 8


highest = lax.Precision.HIGHEST
EPSILON = 1e-06


def shifted_pair(block, distance):
    pairs = range(0, lax.axis_size("seq"), 2)
    route = [(i, i + 1) if distance > 0 else (i + 1, i) for i in pairs]
    return lax.ppermute(block, "seq", route)


def rms_scale(tensor, gain_vec):
    return (
        tensor * lax.rsqrt(jnp.mean(tensor * tensor, axis=-1, keepdims=True) + EPSILON) * gain_vec
    )


def rms_back(tensor, gain_vec, upstream):
    inverse = lax.rsqrt(jnp.mean(tensor * tensor, axis=-1, keepdims=True) + EPSILON)
    gain_grad = jnp.sum(upstream * tensor * inverse, axis=0)
    scaled = upstream * gain_vec
    inner = jnp.mean(scaled * tensor, axis=-1, keepdims=True)
    return (inverse * scaled - tensor * inverse**3 * inner, gain_grad)


def silu(tensor):
    return tensor * jax.nn.sigmoid(tensor)


def silu_back(gate_pre, up_pre, upstream):
    logistic = jax.nn.sigmoid(gate_pre)
    return (
        upstream * up_pre * logistic * (1.0 + gate_pre * (1.0 - logistic)),
        upstream * gate_pre * logistic,
    )


def rotate(tensor, position, direction):
    half_width = tensor.shape[-1] // 2
    frequency = jnp.exp(
        jnp.arange(half_width, dtype=jnp.float32) * (-math.log(10000.0) / half_width)
    )
    angles = position.astype(jnp.float32)[:, None] * frequency[None, :]
    shape_out = (tensor.shape[0],) + (1,) * (tensor.ndim - 2) + (half_width,)
    cosine = jnp.cos(angles).reshape(shape_out)
    sine_term = direction * jnp.sin(angles).reshape(shape_out)
    first_half = tensor[..., :half_width]
    second_half = tensor[..., half_width:]
    return jnp.concatenate(
        [
            first_half * cosine - second_half * sine_term,
            first_half * sine_term + second_half * cosine,
        ],
        axis=-1,
    )


def gather_rows(tensor):
    return lax.all_gather(tensor, "exp", axis=0, tiled=True)


def sum_rows(tensor):
    return lax.psum_scatter(
        tensor.astype(jnp.bfloat16), "exp", scatter_dimension=0, tiled=True
    ).astype(jnp.float32)


def add_own(full_term, own_term, row_offset):
    current = lax.dynamic_slice_in_dim(full_term, row_offset, own_term.shape[0], 0)
    return lax.dynamic_update_slice_in_dim(full_term, current + own_term, row_offset, 0)


def expand_keys(latent_all, kv_proj, head_count):
    return (
        jnp.dot(latent_all, kv_proj, preferred_element_type=jnp.float32)
        .astype(jnp.bfloat16)
        .reshape(latent_all.shape[0], head_count, NOPE + VDIM)
    )


def score_block(queries, packed, rope_all, query_pos, query_seg, key_pos, key_seg):
    score_scale = (NOPE + ROPE) ** (-0.5)
    nope_part = jnp.einsum(
        "qhc,khc->hqk", queries[..., :NOPE], packed[..., :NOPE], preferred_element_type=jnp.float32
    )
    rope_part = jnp.einsum(
        "qhc,kc->hqk", queries[..., NOPE:], rope_all, preferred_element_type=jnp.float32
    )
    allowed = (query_seg[:, None] == key_seg[None, :]) & (key_pos[None, :] <= query_pos[:, None])
    return jnp.where(allowed[None], (nope_part + rope_part) * score_scale, -1e30)


def local(
    layer_input,
    attn_gain,
    query_proj,
    latent_proj,
    latent_gain,
    kv_proj,
    output_proj,
    ffn_gain,
    router_proj,
    shared_gate_up,
    shared_down,
    expert_gate_up,
    expert_down,
    segment_ids,
    expert_routes,
    out_grad,
):
    f32 = jnp.float32
    bf16 = jnp.bfloat16
    exp_count = lax.axis_size("exp")
    own_rows = layer_input.shape[0]
    model_width = layer_input.shape[1]
    block_rows = own_rows * exp_count
    key_rows = 2 * block_rows
    head_count = query_proj.shape[1] // (NOPE + ROPE)
    score_scale = (NOPE + ROPE) ** (-0.5)
    block_start = lax.axis_index("seq") * block_rows
    row_offset = lax.axis_index("exp") * own_rows
    query_pos = block_start + jnp.arange(block_rows, dtype=jnp.int32)
    own_pos = block_start + row_offset + jnp.arange(own_rows, dtype=jnp.int32)
    query_seg = lax.dynamic_slice_in_dim(segment_ids, block_start, block_rows)
    key_start = block_start - block_rows
    key_pos = key_start + jnp.arange(key_rows, dtype=jnp.int32)
    prev_seg = lax.dynamic_slice_in_dim(segment_ids, jnp.maximum(key_start, 0), block_rows)
    prev_seg = jnp.where(key_start >= 0, prev_seg, -1)
    key_seg = jnp.concatenate([prev_seg, query_seg], axis=0)
    input_f = layer_input.astype(f32)
    normed_low = rms_scale(input_f, attn_gain).astype(bf16)
    normed_all = gather_rows(normed_low)
    query_raw = jnp.dot(normed_all, query_proj, preferred_element_type=f32).reshape(
        block_rows, head_count, NOPE + ROPE
    )
    queries = jnp.concatenate(
        [query_raw[..., :NOPE], rotate(query_raw[..., NOPE:], query_pos % key_rows, 1.0)], axis=-1
    ).astype(bf16)
    latent_raw = jnp.dot(normed_low, latent_proj, preferred_element_type=f32)
    latent_normed = rms_scale(latent_raw[:, :LAT], latent_gain).astype(bf16)
    rope_key = rotate(latent_raw[:, LAT:], own_pos % key_rows, 1.0).astype(bf16)
    hot = jnp.sum(
        expert_routes[:, :, None] == jnp.arange(EXPERTS, dtype=jnp.int32)[None, None, :], axis=1
    ).astype(bf16)
    key_latent = jnp.concatenate([latent_normed, rope_key], axis=-1)
    prev_latent = shifted_pair(key_latent, 1)
    gathered = gather_rows(jnp.concatenate([key_latent, prev_latent, hot], axis=-1))
    width = LAT + ROPE
    keys_all = jnp.concatenate([gathered[:, width : 2 * width], gathered[:, :width]], axis=0)
    hot_all = gathered[:, 2 * width :].astype(f32)
    latent_all = keys_all[:, :LAT]
    rope_all = keys_all[:, LAT:]
    packed = expand_keys(latent_all, kv_proj, head_count)
    scores = score_block(queries, packed, rope_all, query_pos, query_seg, key_pos, key_seg)
    top_score = jnp.max(scores, axis=-1, keepdims=True)
    weights = jnp.exp(scores - top_score)
    weight_sum = jnp.sum(weights, axis=-1, keepdims=True)
    soft_weights = weights / weight_sum
    log_total = top_score + jnp.log(weight_sum)
    head_rows = jnp.einsum(
        "hqk,khc->qhc", soft_weights.astype(bf16), packed[..., NOPE:], preferred_element_type=f32
    )
    heads_low = head_rows.astype(bf16).reshape(block_rows, head_count * VDIM)
    attn_rows = sum_rows(jnp.dot(heads_low, output_proj, preferred_element_type=f32))
    residual = input_f + attn_rows
    mid_low = rms_scale(residual, ffn_gain).astype(bf16)
    mid_all = gather_rows(mid_low)
    grad_f = out_grad.astype(f32)
    grad_all = gather_rows(out_grad)
    router_high = lax.reduce_precision(router_proj, 8, 7)
    router_rest = router_proj - router_high
    router_mid = lax.reduce_precision(router_rest, 8, 7)
    router_low = router_rest - router_mid
    logits = jnp.dot(
        mid_all,
        jnp.concatenate([router_high, router_mid, router_low], axis=1).astype(bf16),
        preferred_element_type=f32,
    )
    logits = logits[:, :EXPERTS] + (logits[:, EXPERTS : 2 * EXPERTS] + logits[:, 2 * EXPERTS :])
    logit_top = jnp.max(logits, axis=-1, keepdims=True)
    logit_exp = jnp.exp(logits - logit_top)
    gate_probs = logit_exp / jnp.sum(logit_exp, axis=-1, keepdims=True)
    own_expert = (jnp.arange(EXPERTS) == lax.axis_index("exp")).astype(f32)[None, :]
    own_prob = jnp.sum(gate_probs * hot_all * own_expert, axis=1, keepdims=True)
    shared_gate = jnp.dot(mid_all, shared_gate_up[:, 0], preferred_element_type=f32)
    shared_up = jnp.dot(mid_all, shared_gate_up[:, 1], preferred_element_type=f32)
    shared_act = silu(shared_gate) * shared_up
    expert_pre = jnp.dot(mid_all, expert_gate_up[0], preferred_element_type=f32)
    expert_gate, expert_up = expert_pre[:, :F], expert_pre[:, F:]
    expert_act = silu(expert_gate) * expert_up
    act_all = jnp.concatenate([shared_act, expert_act * own_prob], axis=1).astype(bf16)
    down_all = jnp.concatenate([shared_down, expert_down[0]], axis=0)
    moe_part = jnp.dot(act_all, down_all, preferred_element_type=f32)
    dact_all = jnp.einsum("td,fd->tf", grad_all, down_all, preferred_element_type=f32)
    shared_width = shared_down.shape[0]
    shared_dgate, shared_dup = silu_back(shared_gate, shared_up, dact_all[:, :shared_width])
    expert_dact = dact_all[:, shared_width:]
    weight_grad = jnp.sum(expert_act * expert_dact, axis=1, keepdims=True)
    expert_dgate, expert_dup = silu_back(expert_gate, expert_up, expert_dact * own_prob)
    logit_term = (own_prob * weight_grad) * (own_expert - gate_probs)
    shared_dpre = jnp.concatenate([shared_dgate, shared_dup], axis=1).astype(bf16)
    expert_dpre = jnp.concatenate([expert_dgate, expert_dup], axis=1).astype(bf16)
    shared_both = jnp.concatenate([shared_gate_up[:, 0], shared_gate_up[:, 1]], axis=1)
    mid_grad_all = (
        jnp.einsum("tf,df->td", shared_dpre, shared_both, preferred_element_type=f32)
        + jnp.einsum("tf,df->td", expert_dpre, expert_gate_up[0], preferred_element_type=f32)
        + jnp.einsum("te,de->td", logit_term, router_proj, preferred_element_type=f32)
    )
    mid_grad = sum_rows(mid_grad_all)
    router_term = jnp.einsum("td,te->de", mid_all, logit_term.astype(bf16), preferred_element_type=f32)
    layer_output = (residual + sum_rows(moe_part)).astype(bf16)
    mid_input_grad, ffn_gain_term = rms_back(residual, ffn_gain, mid_grad)
    residual_grad = grad_f + mid_input_grad
    attn_grad_all = gather_rows(residual_grad.astype(bf16))
    output_term = jnp.einsum("tc,td->cd", heads_low, attn_grad_all, preferred_element_type=f32)
    heads_grad = (
        jnp.einsum("td,cd->tc", attn_grad_all, output_proj, preferred_element_type=f32)
        .astype(bf16)
        .reshape(block_rows, head_count, VDIM)
    )
    latent_back, rope_back = latent_all, rope_all
    packed_back = packed
    scores_back = score_block(
        queries, packed_back, rope_back, query_pos, query_seg, key_pos, key_seg
    )
    soft_back = jnp.exp(scores_back - log_total)
    prob_grad = jnp.einsum(
        "qhc,khc->hqk", heads_grad, packed_back[..., NOPE:], preferred_element_type=f32
    )
    score_grad = (
        soft_back * (prob_grad - jnp.sum(soft_back * prob_grad, axis=-1, keepdims=True))
    ).astype(bf16)
    query_nope_grad = score_scale * jnp.einsum(
        "hqk,khc->qhc", score_grad, packed_back[..., :NOPE], preferred_element_type=f32
    )
    query_rope_grad = score_scale * jnp.einsum(
        "hqk,kc->qhc", score_grad, rope_back, preferred_element_type=f32
    )
    query_raw_grad = (
        jnp.concatenate(
            [query_nope_grad, rotate(query_rope_grad, query_pos % key_rows, -1.0)], axis=-1
        )
        .astype(bf16)
        .reshape(block_rows, head_count * (NOPE + ROPE))
    )
    key_nope_grad = score_scale * jnp.einsum(
        "hqk,qhc->khc", score_grad, queries[..., :NOPE], preferred_element_type=f32
    )
    rope_key_grad = score_scale * jnp.einsum(
        "hqk,qhc->kc", score_grad, queries[..., NOPE:], preferred_element_type=f32
    )
    value_grad = jnp.einsum(
        "hqk,qhc->khc", soft_back.astype(bf16), heads_grad, preferred_element_type=f32
    )
    packed_grad = (
        jnp.concatenate([key_nope_grad, value_grad], axis=-1)
        .astype(bf16)
        .reshape(key_rows, head_count * (NOPE + VDIM))
    )
    kv_term = jnp.einsum("tl,tc->lc", latent_back, packed_grad, preferred_element_type=f32)
    latent_grad_all = jnp.einsum("tc,lc->tl", packed_grad, kv_proj, preferred_element_type=f32)
    key_grad = jnp.concatenate([latent_grad_all, rope_key_grad], axis=-1)
    both_grad = sum_rows(jnp.concatenate([key_grad[block_rows:], key_grad[:block_rows]], axis=1))
    own_key_grad = both_grad[:, :width] + shifted_pair(
        both_grad[:, width:].astype(bf16), -1
    ).astype(f32)
    latent_own = own_key_grad[:, :LAT]
    rope_own = own_key_grad[:, LAT:]
    query_term = jnp.einsum("td,tc->dc", normed_all, query_raw_grad, preferred_element_type=f32)
    in_grad_all = jnp.einsum("tc,dc->td", query_raw_grad, query_proj, preferred_element_type=f32)
    latent_pre_grad, latent_gain_term = rms_back(latent_raw[:, :LAT], latent_gain, latent_own)
    latent_raw_grad = jnp.concatenate(
        [latent_pre_grad, rotate(rope_own, own_pos % key_rows, -1.0)], axis=-1
    ).astype(bf16)
    latent_raw_all = gather_rows(latent_raw_grad)
    slice_width = model_width // exp_count
    normed_slice = lax.dynamic_slice_in_dim(
        normed_all, lax.axis_index("exp") * slice_width, slice_width, 1
    )
    latent_term = jnp.einsum("td,tc->dc", normed_slice, latent_raw_all, preferred_element_type=f32)
    in_grad_own = jnp.einsum("tc,dc->td", latent_raw_grad, latent_proj, preferred_element_type=f32)
    normed_grad = sum_rows(add_own(in_grad_all, in_grad_own, row_offset))
    input_part, attn_gain_term = rms_back(input_f, attn_gain, normed_grad)
    input_grad = (residual_grad + input_part).astype(bf16)
    down_term = jnp.einsum("td,tf->df", grad_all, act_all, preferred_element_type=f32)
    gate_term = jnp.einsum(
        "td,tf->df",
        mid_all,
        jnp.concatenate([expert_dpre, shared_dpre], axis=1),
        preferred_element_type=f32,
    )
    down_sum = lax.psum_scatter(
        down_term.astype(bf16), "seq", scatter_dimension=0, tiled=True
    ).astype(f32)
    gate_sum = lax.psum_scatter(
        gate_term.astype(bf16), "seq", scatter_dimension=0, tiled=True
    ).astype(f32)
    shared_down_sum = down_sum[:, :shared_width].T
    expert_down_sum = down_sum[:, shared_width:].T[None]
    expert_gate_sum = gate_sum[None, :, : 2 * F]
    shared_gate_sum = gate_sum[:, 2 * F :].reshape(own_rows, 2, shared_width)
    query_sum, kv_sum, output_sum, latent_sum = (
        term.astype(f32)
        for term in lax.psum(
            tuple(
                term.astype(bf16) for term in (query_term, kv_term, output_term, latent_term)
            ),
            "seq",
        )
    )
    latent_sum = gather_rows(latent_sum.astype(bf16)).astype(f32)
    attn_gain_sum, latent_gain_sum, ffn_gain_sum, router_sum = lax.psum(
        (attn_gain_term, latent_gain_term, ffn_gain_term, router_term), ("seq", "exp")
    )
    return (
        layer_output,
        input_grad,
        attn_gain_sum,
        query_sum,
        latent_sum,
        latent_gain_sum,
        kv_sum,
        output_sum,
        ffn_gain_sum,
        router_sum,
        shared_gate_sum,
        shared_down_sum,
        expert_gate_sum,
        expert_down_sum,
    )


def solution(mesh):
    in_specs = (
        P(("seq", "exp"), None),
        P(),
        P(None, "exp"),
        P(),
        P(),
        P(None, "exp"),
        P("exp", None),
        P(),
        P(),
        P(None, None, "exp"),
        P("exp", None),
        P("exp", None, None),
        P("exp", None, None),
        P(),
        P(("seq", "exp"), None),
        P(("seq", "exp"), None),
    )
    out_specs = (
        P(("seq", "exp"), None),
        P(("seq", "exp"), None),
        P(),
        P(None, "exp"),
        P(),
        P(),
        P(None, "exp"),
        P("exp", None),
        P(),
        P(),
        P("seq", None, "exp"),
        P("exp", "seq"),
        P("exp", "seq", None),
        P("exp", None, "seq"),
    )
    return jax.shard_map(local, mesh=mesh, in_specs=in_specs, out_specs=out_specs, check_vma=False)
```

```python
import functools
import math

import jax
import jax.numpy as jnp
from jax import lax
from jax.experimental import pallas as pl
from jax.experimental.pallas import tpu as pltpu
from jax.sharding import PartitionSpec as P

NOPE = 128
ROPE = 64
VDIM = 128
LAT = 512
F = 1408
TOP = 6
EXPERTS = 8


VM = pltpu.VMEM
f32 = jnp.float32
bf16 = jnp.bfloat16
EPSILON = 1e-06


def _send(src, dst, send, recv, peer):
    copy = pltpu.make_async_remote_copy(
        src_ref=src, dst_ref=dst, send_sem=send, recv_sem=recv,
        device_id=peer, device_id_type=pl.DeviceIdType.MESH)
    copy.start()
    return copy


def greet(peers):
    barrier = pltpu.get_barrier_semaphore()
    for peer in peers:
        pl.semaphore_signal(barrier, inc=1, device_id=peer, device_id_type=pl.DeviceIdType.MESH)
    pl.semaphore_wait(barrier, len(peers))


def small_sum_kernel(src, out, slots, send, recv):
    me, spot = lax.axis_index("exp"), lax.axis_index("seq")
    chip, core = me // 2, me % 2
    row, col = spot // 4, spot % 4
    axes = [
        (core, 2, lambda i: {"exp": chip * 2 + i}),
        (chip, 4, lambda i: {"exp": i * 2 + core}),
        (col, 4, lambda i: {"seq": row * 4 + i}),
        (row, 4, lambda i: {"seq": i * 4 + col}),
    ]
    greet([name(lax.rem(place + d, n)) for place, n, name in axes for d in range(1, n)])
    out[...] = src[...]
    count = 0
    sends = []
    for stage, (place, n, name) in enumerate(axes):
        slots[stage, place] = out[...]
        here = [
            _send(slots.at[stage, place], slots.at[stage, place], send.at[count + d - 1], recv.at[count + d - 1], name(lax.rem(place + d, n)))
            for d in range(1, n)
        ]
        count += n - 1
        for c in here:
            c.wait_recv()
        total = slots[stage, 0]
        for i in range(1, n):
            total = total + slots[stage, i]
        out[...] = total
        sends += here
    for c in sends:
        c.wait_send()


def small_sum(vec, ident, name):
    return pl.pallas_call(
        small_sum_kernel,
        out_shape=jax.ShapeDtypeStruct(vec.shape, f32),
        in_specs=[pl.BlockSpec(memory_space=VM)],
        out_specs=pl.BlockSpec(memory_space=VM),
        scratch_shapes=[pltpu.VMEM((4, 4) + vec.shape, f32), pltpu.SemaphoreType.DMA((10,)), pltpu.SemaphoreType.DMA((10,))],
        compiler_params=pltpu.CompilerParams(collective_id=ident, has_side_effects=True, vmem_limit_bytes=48 << 20),
        name=name,
    )(vec)


class Sems:
    def __init__(self, send, recv):
        self.send, self.recv, self.used, self.sent = send, recv, 0, []

    def start(self, src, dst, peer):
        c = _send(src, dst, self.send.at[self.used], self.recv.at[self.used], peer)
        self.used += 1
        self.sent.append(c)
        return c

    def finish(self):
        for c in self.sent:
            c.wait_send()


def ring_sum(sems, place, peer, block, hop, last):
    right, left = peer(lax.rem(place + 1, 4)), peer(lax.rem(place + 3, 4))
    to = [lax.rem(place + d, 4) for d in range(4)]

    def add(ref, other):
        ref[...] = (ref[...].astype(f32) + other[...].astype(f32)).astype(ref.dtype)

    far_a = sems.start(block(to[2], 0), hop.at[0], right)
    far_b = sems.start(block(to[2], 1), hop.at[1], left)
    dir_b = sems.start(block(to[1], 1), last.at[0], right)
    dir_a = sems.start(block(to[3], 0), last.at[1], left)
    yield
    far_a.wait_recv()
    add(block(to[1], 0), hop.at[0])
    acc_a = sems.start(block(to[1], 0), last.at[2], right)
    yield
    far_b.wait_recv()
    add(block(to[3], 1), hop.at[1])
    acc_b = sems.start(block(to[3], 1), last.at[3], left)
    yield
    dir_b.wait_recv()
    dir_a.wait_recv()
    add(block(to[0], 1), last.at[0])
    add(block(to[0], 0), last.at[1])
    yield
    acc_a.wait_recv()
    add(block(to[0], 0), last.at[2])
    yield
    acc_b.wait_recv()
    add(block(to[0], 1), last.at[3])


def ring_gather(sems, place, peer, block):
    right, left = peer(lax.rem(place + 1, 4)), peer(lax.rem(place + 3, 4))
    to = [lax.rem(place + d, 4) for d in range(4)]
    ra = sems.start(block(to[0], 0), block(to[0], 0), right)
    lb = sems.start(block(to[0], 1), block(to[0], 1), left)
    rb = sems.start(block(to[0], 1), block(to[0], 1), right)
    la = sems.start(block(to[0], 0), block(to[0], 0), left)
    yield
    ra.wait_recv()
    fa = sems.start(block(to[3], 0), block(to[3], 0), right)
    yield
    lb.wait_recv()
    fb = sems.start(block(to[1], 1), block(to[1], 1), left)
    yield
    rb.wait_recv()
    la.wait_recv()
    yield
    fa.wait_recv()
    yield
    fb.wait_recv()


def together(*streams):
    streams = list(streams)
    while streams:
        for s in list(streams):
            try:
                next(s)
            except StopIteration:
                streams.remove(s)


def seq_sum_kernel(cols, src, out, work, hop1, last1, hop2, last2, send, recv):
    spot = lax.axis_index("seq")
    z, y = spot // 4, spot % 4
    peers = [lambda i: {"seq": z * 4 + i}, lambda i: {"seq": i * 4 + y}]
    places = [y, z]
    greet([peers[0](lax.rem(y + 1, 4)), peers[0](lax.rem(y + 3, 4)), peers[1](lax.rem(z + 1, 4)), peers[1](lax.rem(z + 3, 4))])
    work[...] = src[...]
    sems = Sems(send, recv)
    half = cols // 2

    def stream(part):
        first, second = (0, 1) if part == 0 else (1, 0)
        def wide(ref):
            return lambda i, h: ref.at[part, pl.ds(i * 4 + 2 * h, 2)]

        def narrow(ref):
            return lambda i, h: ref.at[part, places[first] * 4 + i, :, pl.ds(h * half, half)]

        yield from ring_sum(sems, places[first], peers[first], wide(work), hop1.at[part], last1.at[part])
        yield from ring_sum(sems, places[second], peers[second], narrow(work), hop2.at[part], last2.at[part])
        own = places[first] * 4 + places[second]
        out[part, own] = work[part, own]
        yield from ring_gather(sems, places[second], peers[second], narrow(out))
        yield from ring_gather(sems, places[first], peers[first], wide(out))

    together(stream(0), stream(1))
    sems.finish()


def seq_sum(parts, ident, name):
    _, _, rows, cols = parts.shape
    bf16 = jnp.bfloat16
    return pl.pallas_call(
        functools.partial(seq_sum_kernel, cols),
        out_shape=jax.ShapeDtypeStruct(parts.shape, bf16),
        in_specs=[pl.BlockSpec(memory_space=VM)],
        out_specs=pl.BlockSpec(memory_space=VM),
        scratch_shapes=[
            pltpu.VMEM(parts.shape, bf16),
            pltpu.VMEM((2, 2, 2, rows, cols), bf16), pltpu.VMEM((2, 4, 2, rows, cols), bf16),
            pltpu.VMEM((2, 2, rows, cols // 2), bf16), pltpu.VMEM((2, 4, rows, cols // 2), bf16),
            pltpu.SemaphoreType.DMA((48,)), pltpu.SemaphoreType.DMA((48,))],
        compiler_params=pltpu.CompilerParams(collective_id=ident, has_side_effects=True, vmem_limit_bytes=56 << 20),
        name=name,
    )(parts)


def x_places():
    me = lax.axis_index("exp")
    chip, core = me // 2, me % 2
    right = lax.rem(chip + 1, 4) * 2 + core
    left = lax.rem(chip + 3, 4) * 2 + core
    far = lax.rem(chip + 2, 4) * 2 + core
    return me, chip, core, right, left, far


def gather_kernel(rows, src, out, send, recv, local):
    me, chip, core, right, left, far = x_places()
    sibling = chip * 2 + 1 - core
    greet([{"exp": right}, {"exp": left}, {"exp": sibling}])
    half = rows // 2

    def at(owner, part):
        return out.at[pl.ds(pl.multiple_of(owner * rows + part * half, half), half)]

    def both(owner):
        return out.at[pl.ds(pl.multiple_of(owner * rows, rows), rows)]

    A, B = 0, 1
    def own(part):
        return src.at[pl.ds(part * half, half)]
    copies = []
    ra = _send(own(A), at(me, A), send.at[0], recv.at[0], {"exp": right})
    lb = _send(own(B), at(me, B), send.at[1], recv.at[1], {"exp": left})
    rb = _send(own(B), at(me, B), send.at[2], recv.at[2], {"exp": right})
    la = _send(own(A), at(me, A), send.at[3], recv.at[3], {"exp": left})
    sib = _send(src, both(me), send.at[4], recv.at[4], {"exp": sibling})
    mine = pltpu.make_async_copy(src, both(me), local)
    mine.start()
    ra.wait_recv()
    far_a = _send(at(left, A), at(left, A), send.at[5], recv.at[5], {"exp": right})
    s_la = _send(at(left, A), at(left, A), send.at[6], recv.at[6], {"exp": sibling})
    lb.wait_recv()
    far_b = _send(at(right, B), at(right, B), send.at[7], recv.at[7], {"exp": left})
    s_rb = _send(at(right, B), at(right, B), send.at[8], recv.at[8], {"exp": sibling})
    rb.wait_recv()
    s_lb = _send(at(left, B), at(left, B), send.at[9], recv.at[9], {"exp": sibling})
    la.wait_recv()
    s_ra = _send(at(right, A), at(right, A), send.at[10], recv.at[10], {"exp": sibling})
    far_a.wait_recv()
    s_fa = _send(at(far, A), at(far, A), send.at[11], recv.at[11], {"exp": sibling})
    far_b.wait_recv()
    s_fb = _send(at(far, B), at(far, B), send.at[12], recv.at[12], {"exp": sibling})
    mine.wait()
    for c in (sib, s_la, s_rb, s_lb, s_ra, s_fa, s_fb):
        c.wait_recv()
    for c in (ra, lb, rb, la, sib, far_a, s_la, far_b, s_rb, s_lb, s_ra, s_fa, s_fb):
        c.wait_send()


def gather_x(block, ident, name):
    rows, cols = block.shape
    return pl.pallas_call(
        functools.partial(gather_kernel, rows),
        out_shape=jax.ShapeDtypeStruct((rows * 8, cols), block.dtype),
        in_specs=[pl.BlockSpec(memory_space=VM)],
        out_specs=pl.BlockSpec(memory_space=VM),
        scratch_shapes=[pltpu.SemaphoreType.DMA((13,)), pltpu.SemaphoreType.DMA((13,)), pltpu.SemaphoreType.DMA],
        compiler_params=pltpu.CompilerParams(collective_id=ident, has_side_effects=True, vmem_limit_bytes=48 << 20),
        name=name,
    )(block)


def scatter_kernel(rows, src, out, pair, hop, last, send, recv):
    me, chip, core, right, left, far = x_places()
    sibling = chip * 2 + 1 - core
    greet([{"exp": right}, {"exp": left}, {"exp": sibling}])
    half = rows // 2
    f32 = jnp.float32
    order = [2, 1, 3, 0]
    sib = []
    for i, dist in enumerate(order):
        owner = lax.rem(chip + dist, 4) * 2 + 1 - core
        sib.append(_send(src.at[pl.ds(pl.multiple_of(owner * rows, rows), rows)], pair.at[dist], send.at[i], recv.at[i], {"exp": sibling}))

    def fold(i, dist):
        sib[i].wait_recv()
        owner = lax.rem(chip + dist, 4) * 2 + core
        mine = src[pl.ds(pl.multiple_of(owner * rows, rows), rows)]
        pair[dist] = (pair[dist].astype(f32) + mine.astype(f32)).astype(pair.dtype)

    A = pl.ds(0, half)
    B = pl.ds(half, half)
    fold(0, 2)
    far_a = _send(pair.at[2, A], hop.at[0], send.at[4], recv.at[4], {"exp": right})
    far_b = _send(pair.at[2, B], hop.at[1], send.at[5], recv.at[5], {"exp": left})
    fold(1, 1)
    dir_b = _send(pair.at[1, B], last.at[0], send.at[6], recv.at[6], {"exp": right})
    fold(2, 3)
    dir_a = _send(pair.at[3, A], last.at[1], send.at[7], recv.at[7], {"exp": left})
    far_a.wait_recv()
    pair[1, A] = (pair[1, A].astype(f32) + hop[0].astype(f32)).astype(pair.dtype)
    acc_a = _send(pair.at[1, A], last.at[2], send.at[8], recv.at[8], {"exp": right})
    far_b.wait_recv()
    pair[3, B] = (pair[3, B].astype(f32) + hop[1].astype(f32)).astype(pair.dtype)
    acc_b = _send(pair.at[3, B], last.at[3], send.at[9], recv.at[9], {"exp": left})
    sib[3].wait_recv()
    mine = src[pl.ds(pl.multiple_of(me * rows, rows), rows)].astype(f32) + pair[0].astype(f32)
    dir_b.wait_recv()
    dir_a.wait_recv()
    acc_a.wait_recv()
    acc_b.wait_recv()
    out[A] = mine[:half] + last[1].astype(f32) + last[2].astype(f32)
    out[B] = mine[half:] + last[0].astype(f32) + last[3].astype(f32)
    for c in sib + [far_a, far_b, dir_b, dir_a, acc_a, acc_b]:
        c.wait_send()


def scatter_x(part, ident, name):
    rows, cols = part.shape[0] // 8, part.shape[1]
    bf16 = jnp.bfloat16
    return pl.pallas_call(
        functools.partial(scatter_kernel, rows),
        out_shape=jax.ShapeDtypeStruct((rows, cols), jnp.float32),
        in_specs=[pl.BlockSpec(memory_space=VM)],
        out_specs=pl.BlockSpec(memory_space=VM),
        scratch_shapes=[pltpu.VMEM((4, rows, cols), bf16), pltpu.VMEM((2, rows // 2, cols), bf16), pltpu.VMEM((4, rows // 2, cols), bf16),
                        pltpu.SemaphoreType.DMA((10,)), pltpu.SemaphoreType.DMA((10,))],
        compiler_params=pltpu.CompilerParams(collective_id=ident, has_side_effects=True, vmem_limit_bytes=48 << 20),
        name=name,
    )(part)


def shifted_pair(block, distance):
    pairs = range(0, lax.axis_size("seq"), 2)
    route = [(i, i + 1) if distance > 0 else (i + 1, i) for i in pairs]
    return lax.ppermute(block, "seq", route)


def rms_scale(tensor, gain_vec):
    return (
        tensor * lax.rsqrt(jnp.mean(tensor * tensor, axis=-1, keepdims=True) + EPSILON) * gain_vec
    )


def rms_back(tensor, gain_vec, upstream):
    inverse = lax.rsqrt(jnp.mean(tensor * tensor, axis=-1, keepdims=True) + EPSILON)
    gain_grad = jnp.sum(upstream * tensor * inverse, axis=0)
    scaled = upstream * gain_vec
    inner = jnp.mean(scaled * tensor, axis=-1, keepdims=True)
    return (inverse * scaled - tensor * inverse**3 * inner, gain_grad)


def silu(tensor):
    return tensor * jax.nn.sigmoid(tensor)


def silu_back(gate_pre, up_pre, upstream):
    logistic = jax.nn.sigmoid(gate_pre)
    return (
        upstream * up_pre * logistic * (1.0 + gate_pre * (1.0 - logistic)),
        upstream * gate_pre * logistic,
    )


def rotate(tensor, position, direction):
    half_width = tensor.shape[-1] // 2
    frequency = jnp.exp(
        jnp.arange(half_width, dtype=jnp.float32) * (-math.log(10000.0) / half_width)
    )
    angles = position.astype(jnp.float32)[:, None] * frequency[None, :]
    shape_out = (tensor.shape[0],) + (1,) * (tensor.ndim - 2) + (half_width,)
    cosine = jnp.cos(angles).reshape(shape_out)
    sine_term = direction * jnp.sin(angles).reshape(shape_out)
    first_half = tensor[..., :half_width]
    second_half = tensor[..., half_width:]
    return jnp.concatenate(
        [
            first_half * cosine - second_half * sine_term,
            first_half * sine_term + second_half * cosine,
        ],
        axis=-1,
    )


def add_own(full_term, own_term, row_offset):
    current = lax.dynamic_slice_in_dim(full_term, row_offset, own_term.shape[0], 0)
    return lax.dynamic_update_slice_in_dim(full_term, current + own_term, row_offset, 0)


def expand_keys(latent_all, kv_proj, head_count):
    return (
        jnp.dot(latent_all, kv_proj, preferred_element_type=jnp.float32)
        .astype(jnp.bfloat16)
        .reshape(latent_all.shape[0], head_count, NOPE + VDIM)
    )


def score_block(queries, packed, rope_all, query_pos, query_seg, key_pos, key_seg):
    score_scale = (NOPE + ROPE) ** (-0.5)
    nope_part = jnp.einsum(
        "qhc,khc->hqk", queries[..., :NOPE], packed[..., :NOPE], preferred_element_type=jnp.float32
    )
    rope_part = jnp.einsum(
        "qhc,kc->hqk", queries[..., NOPE:], rope_all, preferred_element_type=jnp.float32
    )
    allowed = (query_seg[:, None] == key_seg[None, :]) & (key_pos[None, :] <= query_pos[:, None])
    return jnp.where(allowed[None], (nope_part + rope_part) * score_scale, -1e30)


def local(
    layer_input,
    attn_gain,
    query_proj,
    latent_proj,
    latent_gain,
    kv_proj,
    output_proj,
    ffn_gain,
    router_proj,
    shared_gate_up,
    shared_down,
    expert_gate_up,
    expert_down,
    segment_ids,
    expert_routes,
    out_grad,
):
    exp_count = lax.axis_size("exp")
    own_rows = layer_input.shape[0]
    model_width = layer_input.shape[1]
    block_rows = own_rows * exp_count
    key_rows = 2 * block_rows
    head_count = query_proj.shape[1] // (NOPE + ROPE)
    score_scale = (NOPE + ROPE) ** (-0.5)
    block_start = lax.axis_index("seq") * block_rows
    row_offset = lax.axis_index("exp") * own_rows
    query_pos = block_start + jnp.arange(block_rows, dtype=jnp.int32)
    own_pos = block_start + row_offset + jnp.arange(own_rows, dtype=jnp.int32)
    query_seg = lax.dynamic_slice_in_dim(segment_ids, block_start, block_rows)
    key_start = block_start - block_rows
    key_pos = key_start + jnp.arange(key_rows, dtype=jnp.int32)
    prev_seg = lax.dynamic_slice_in_dim(segment_ids, jnp.maximum(key_start, 0), block_rows)
    prev_seg = jnp.where(key_start >= 0, prev_seg, -1)
    key_seg = jnp.concatenate([prev_seg, query_seg], axis=0)
    input_f = layer_input.astype(f32)
    normed_low = rms_scale(input_f, attn_gain).astype(bf16)
    normed_all = gather_x(normed_low, 0, "gather_0")
    query_raw = jnp.dot(normed_all, query_proj, preferred_element_type=f32).reshape(
        block_rows, head_count, NOPE + ROPE
    )
    queries = jnp.concatenate(
        [query_raw[..., :NOPE], rotate(query_raw[..., NOPE:], query_pos % key_rows, 1.0)], axis=-1
    ).astype(bf16)
    latent_raw = jnp.dot(normed_low, latent_proj, preferred_element_type=f32)
    latent_normed = rms_scale(latent_raw[:, :LAT], latent_gain).astype(bf16)
    rope_key = rotate(latent_raw[:, LAT:], own_pos % key_rows, 1.0).astype(bf16)
    hot = jnp.sum(
        expert_routes[:, :, None] == jnp.arange(EXPERTS, dtype=jnp.int32)[None, None, :], axis=1
    ).astype(bf16)
    key_latent = jnp.concatenate([latent_normed, rope_key], axis=-1)
    prev_latent = shifted_pair(key_latent, 1)
    gathered = gather_x(jnp.concatenate([key_latent, prev_latent, hot], axis=-1), 1, "gather_1")
    width = LAT + ROPE
    keys_all = jnp.concatenate([gathered[:, width : 2 * width], gathered[:, :width]], axis=0)
    hot_all = gathered[:, 2 * width :].astype(f32)
    latent_all = keys_all[:, :LAT]
    rope_all = keys_all[:, LAT:]
    packed = expand_keys(latent_all, kv_proj, head_count)
    scores = score_block(queries, packed, rope_all, query_pos, query_seg, key_pos, key_seg)
    top_score = jnp.max(scores, axis=-1, keepdims=True)
    weights = jnp.exp(scores - top_score)
    weight_sum = jnp.sum(weights, axis=-1, keepdims=True)
    soft_weights = weights / weight_sum
    log_total = top_score + jnp.log(weight_sum)
    head_rows = jnp.einsum(
        "hqk,khc->qhc", soft_weights.astype(bf16), packed[..., NOPE:], preferred_element_type=f32
    )
    heads_low = head_rows.astype(bf16).reshape(block_rows, head_count * VDIM)
    attn_rows = scatter_x((jnp.dot(heads_low, output_proj, preferred_element_type=f32)).astype(bf16), 10, "scatter_0")
    residual = input_f + attn_rows
    mid_low = rms_scale(residual, ffn_gain).astype(bf16)
    mid_all = gather_x(mid_low, 2, "gather_2")
    grad_f = out_grad.astype(f32)
    grad_all = gather_x(out_grad, 3, "gather_3")
    router_high = lax.reduce_precision(router_proj, 8, 7)
    router_rest = router_proj - router_high
    router_mid = lax.reduce_precision(router_rest, 8, 7)
    router_low = router_rest - router_mid
    logits = jnp.dot(
        mid_all,
        jnp.concatenate([router_high, router_mid, router_low], axis=1).astype(bf16),
        preferred_element_type=f32,
    )
    logits = logits[:, :EXPERTS] + (logits[:, EXPERTS : 2 * EXPERTS] + logits[:, 2 * EXPERTS :])
    logit_top = jnp.max(logits, axis=-1, keepdims=True)
    logit_exp = jnp.exp(logits - logit_top)
    gate_probs = logit_exp / jnp.sum(logit_exp, axis=-1, keepdims=True)
    own_expert = (jnp.arange(EXPERTS) == lax.axis_index("exp")).astype(f32)[None, :]
    own_prob = jnp.sum(gate_probs * hot_all * own_expert, axis=1, keepdims=True)
    shared_gate = jnp.dot(mid_all, shared_gate_up[:, 0], preferred_element_type=f32)
    shared_up = jnp.dot(mid_all, shared_gate_up[:, 1], preferred_element_type=f32)
    shared_act = silu(shared_gate) * shared_up
    expert_pre = jnp.dot(mid_all, expert_gate_up[0], preferred_element_type=f32)
    expert_gate, expert_up = expert_pre[:, :F], expert_pre[:, F:]
    expert_act = silu(expert_gate) * expert_up
    act_all = jnp.concatenate([shared_act, expert_act * own_prob], axis=1).astype(bf16)
    down_all = jnp.concatenate([shared_down, expert_down[0]], axis=0)
    moe_part = jnp.dot(act_all, down_all, preferred_element_type=f32)
    dact_all = jnp.einsum("td,fd->tf", grad_all, down_all, preferred_element_type=f32)
    shared_width = shared_down.shape[0]
    shared_dgate, shared_dup = silu_back(shared_gate, shared_up, dact_all[:, :shared_width])
    expert_dact = dact_all[:, shared_width:]
    weight_grad = jnp.sum(expert_act * expert_dact, axis=1, keepdims=True)
    expert_dgate, expert_dup = silu_back(expert_gate, expert_up, expert_dact * own_prob)
    logit_term = (own_prob * weight_grad) * (own_expert - gate_probs)
    shared_dpre = jnp.concatenate([shared_dgate, shared_dup], axis=1).astype(bf16)
    expert_dpre = jnp.concatenate([expert_dgate, expert_dup], axis=1).astype(bf16)
    shared_both = jnp.concatenate([shared_gate_up[:, 0], shared_gate_up[:, 1]], axis=1)
    down_term = jnp.einsum("td,tf->df", grad_all, act_all, preferred_element_type=f32)
    gate_term = jnp.einsum(
        "td,tf->df",
        mid_all,
        jnp.concatenate([expert_dpre, shared_dpre], axis=1),
        preferred_element_type=f32,
    )
    weight_terms = jnp.concatenate([gate_term.astype(bf16), down_term.astype(bf16)], axis=1)
    weight_terms, shared_dpre, expert_dpre = lax.optimization_barrier(
        (weight_terms, shared_dpre, expert_dpre)
    )
    weight_sum = lax.psum_scatter(weight_terms, "seq", scatter_dimension=0, tiled=True)
    gate_sum = weight_sum[:, : 2 * F + 2 * shared_width].astype(f32)
    down_sum = weight_sum[:, 2 * F + 2 * shared_width :].astype(f32)
    shared_down_sum = down_sum[:, :shared_width].T
    expert_down_sum = down_sum[:, shared_width:].T[None]
    expert_gate_sum = gate_sum[None, :, : 2 * F]
    shared_gate_sum = gate_sum[:, 2 * F :].reshape(own_rows, 2, shared_width)
    mid_grad_all = (
        jnp.einsum("tf,df->td", shared_dpre, shared_both, preferred_element_type=f32)
        + jnp.einsum("tf,df->td", expert_dpre, expert_gate_up[0], preferred_element_type=f32)
        + jnp.einsum("te,de->td", logit_term, router_proj, preferred_element_type=f32)
    )
    mid_grad = scatter_x((mid_grad_all).astype(bf16), 11, "scatter_1")
    router_term = jnp.einsum("td,te->de", mid_all, logit_term.astype(bf16), preferred_element_type=f32)
    layer_output = (residual + scatter_x((moe_part).astype(bf16), 12, "scatter_2")).astype(bf16)
    mid_input_grad, ffn_gain_term = rms_back(residual, ffn_gain, mid_grad)
    residual_grad = grad_f + mid_input_grad
    attn_grad_all = gather_x(residual_grad.astype(bf16), 4, "gather_4")
    output_term = jnp.einsum("tc,td->cd", heads_low, attn_grad_all, preferred_element_type=f32)
    heads_grad = (
        jnp.einsum("td,cd->tc", attn_grad_all, output_proj, preferred_element_type=f32)
        .astype(bf16)
        .reshape(block_rows, head_count, VDIM)
    )
    latent_back, rope_back = latent_all, rope_all
    packed_back = packed
    scores_back = score_block(
        queries, packed_back, rope_back, query_pos, query_seg, key_pos, key_seg
    )
    soft_back = jnp.exp(scores_back - log_total)
    prob_grad = jnp.einsum(
        "qhc,khc->hqk", heads_grad, packed_back[..., NOPE:], preferred_element_type=f32
    )
    score_grad = (
        soft_back * (prob_grad - jnp.sum(soft_back * prob_grad, axis=-1, keepdims=True))
    ).astype(bf16)
    query_nope_grad = score_scale * jnp.einsum(
        "hqk,khc->qhc", score_grad, packed_back[..., :NOPE], preferred_element_type=f32
    )
    query_rope_grad = score_scale * jnp.einsum(
        "hqk,kc->qhc", score_grad, rope_back, preferred_element_type=f32
    )
    query_raw_grad = (
        jnp.concatenate(
            [query_nope_grad, rotate(query_rope_grad, query_pos % key_rows, -1.0)], axis=-1
        )
        .astype(bf16)
        .reshape(block_rows, head_count * (NOPE + ROPE))
    )
    key_nope_grad = score_scale * jnp.einsum(
        "hqk,qhc->khc", score_grad, queries[..., :NOPE], preferred_element_type=f32
    )
    rope_key_grad = score_scale * jnp.einsum(
        "hqk,qhc->kc", score_grad, queries[..., NOPE:], preferred_element_type=f32
    )
    value_grad = jnp.einsum(
        "hqk,qhc->khc", soft_back.astype(bf16), heads_grad, preferred_element_type=f32
    )
    packed_grad = (
        jnp.concatenate([key_nope_grad, value_grad], axis=-1)
        .astype(bf16)
        .reshape(key_rows, head_count * (NOPE + VDIM))
    )
    kv_term = jnp.einsum("tl,tc->lc", latent_back, packed_grad, preferred_element_type=f32)
    latent_grad_all = jnp.einsum("tc,lc->tl", packed_grad, kv_proj, preferred_element_type=f32)
    key_grad = jnp.concatenate([latent_grad_all, rope_key_grad], axis=-1)
    both_grad = scatter_x((jnp.concatenate([key_grad[block_rows:], key_grad[:block_rows]], axis=1)).astype(bf16), 13, "scatter_3")
    own_key_grad = both_grad[:, :width] + shifted_pair(
        both_grad[:, width:].astype(bf16), -1
    ).astype(f32)
    latent_own = own_key_grad[:, :LAT]
    rope_own = own_key_grad[:, LAT:]
    query_term = jnp.einsum("td,tc->dc", normed_all, query_raw_grad, preferred_element_type=f32)
    in_grad_all = jnp.einsum("tc,dc->td", query_raw_grad, query_proj, preferred_element_type=f32)
    latent_pre_grad, latent_gain_term = rms_back(latent_raw[:, :LAT], latent_gain, latent_own)
    latent_raw_grad = jnp.concatenate(
        [latent_pre_grad, rotate(rope_own, own_pos % key_rows, -1.0)], axis=-1
    ).astype(bf16)
    latent_raw_all = gather_x(latent_raw_grad, 5, "gather_5")
    slice_width = model_width // exp_count
    normed_slice = lax.dynamic_slice_in_dim(
        normed_all, lax.axis_index("exp") * slice_width, slice_width, 1
    )
    latent_term = jnp.einsum("td,tc->dc", normed_slice, latent_raw_all, preferred_element_type=f32)
    in_grad_own = jnp.einsum("tc,dc->td", latent_raw_grad, latent_proj, preferred_element_type=f32)
    normed_grad = scatter_x((add_own(in_grad_all, in_grad_own, row_offset)).astype(bf16), 14, "scatter_4")
    input_part, attn_gain_term = rms_back(input_f, attn_gain, normed_grad)
    input_grad = (residual_grad + input_part).astype(bf16)
    spots = lax.axis_size("seq")
    wide = LAT
    query_rows = query_term.shape[0] // 2
    query_flat = jnp.concatenate(
        [
            jnp.concatenate([query_term[:query_rows, :256], query_term[query_rows:, :256]], axis=1),
            query_term[:, 256:].reshape(4, query_rows // 2, 128).transpose(1, 0, 2).reshape(-1, wide),
        ],
        axis=0,
    ).reshape(spots, -1, wide)
    output_flat = jnp.stack(
        [output_term[:, i * wide : (i + 1) * wide].reshape(spots, -1, wide) for i in range(4)], axis=1
    ).reshape(spots, -1, wide)
    kv_flat = kv_term.reshape(spots, -1, wide)
    latent_turned = latent_term.T
    latent_rows = latent_turned.shape[0] // 2
    latent_flat = jnp.concatenate([latent_turned[:latent_rows], latent_turned[latent_rows:]], axis=1)
    latent_one = latent_flat[: spots * 16].reshape(spots, 16, wide)
    latent_two = latent_flat[spots * 16 :].reshape(spots, -1, wide)
    pad = 16 - latent_two.shape[1]
    flat = jnp.stack(
        [
            jnp.concatenate([query_flat, latent_one], axis=1),
            jnp.pad(
                jnp.concatenate([kv_flat, output_flat, latent_two], axis=1), ((0, 0), (0, pad), (0, 0))
            ),
        ]
    ).astype(bf16)
    total = seq_sum(flat, 20, "seq_sum").astype(f32)
    query_count, kv_count = query_flat.shape[1], kv_flat.shape[1]
    output_count = output_flat.shape[1]
    query_back = total[0, :, :query_count].reshape(-1, wide)
    query_sum = jnp.concatenate(
        [
            jnp.concatenate([query_back[:query_rows, :256], query_back[:query_rows, 256:]], axis=0),
            query_back[query_rows:].reshape(-1, 4, 128).transpose(1, 0, 2).reshape(-1, 128),
        ],
        axis=1,
    )
    kv_sum = total[1, :, :kv_count].reshape(kv_term.shape)
    output_back = total[1, :, kv_count : kv_count + output_count].reshape(spots, 4, -1, wide)
    output_sum = jnp.concatenate([output_back[:, i].reshape(-1, wide) for i in range(4)], axis=1)
    latent_back = jnp.concatenate(
        [
            total[0, :, query_count:].reshape(-1, wide),
            total[1, :, kv_count + output_count : -pad].reshape(-1, wide),
        ],
        axis=0,
    )
    half_wide = wide // 2
    latent_sum = jnp.concatenate([latent_back[:, :half_wide], latent_back[:, half_wide:]], axis=0).T
    latent_sum = gather_x(latent_sum.astype(bf16), 6, "gather_6").astype(f32)
    small = jnp.concatenate(
        [
            router_term.reshape(-1),
            attn_gain_term,
            ffn_gain_term,
            latent_gain_term,
            jnp.zeros((512,), f32),
        ]
    ).reshape(-1, 128)
    small = small_sum(small, 21, "small_sum").reshape(-1)
    router_sum = small[: model_width * EXPERTS].reshape(model_width, EXPERTS)
    gains = small[model_width * EXPERTS :]
    attn_gain_sum = gains[:model_width]
    ffn_gain_sum = gains[model_width : 2 * model_width]
    latent_gain_sum = gains[2 * model_width : 2 * model_width + LAT]
    return (
        layer_output,
        input_grad,
        attn_gain_sum,
        query_sum,
        latent_sum,
        latent_gain_sum,
        kv_sum,
        output_sum,
        ffn_gain_sum,
        router_sum,
        shared_gate_sum,
        shared_down_sum,
        expert_gate_sum,
        expert_down_sum,
    )


def solution(mesh):
    in_specs = (
        P(("seq", "exp"), None),
        P(),
        P(None, "exp"),
        P(),
        P(),
        P(None, "exp"),
        P("exp", None),
        P(),
        P(),
        P(None, None, "exp"),
        P("exp", None),
        P("exp", None, None),
        P("exp", None, None),
        P(),
        P(("seq", "exp"), None),
        P(("seq", "exp"), None),
    )
    out_specs = (
        P(("seq", "exp"), None),
        P(("seq", "exp"), None),
        P(),
        P(None, "exp"),
        P(),
        P(),
        P(None, "exp"),
        P("exp", None),
        P(),
        P(),
        P("seq", None, "exp"),
        P("exp", "seq"),
        P("exp", "seq", None),
        P("exp", None, "seq"),
    )
    return jax.shard_map(local, mesh=mesh, in_specs=in_specs, out_specs=out_specs, check_vma=False)
```

```python
import functools
import math

import jax
import jax.numpy as jnp
from jax import lax
from jax.experimental import pallas as pl
from jax.experimental.pallas import tpu as pltpu
from jax.sharding import PartitionSpec as P

NOPE = 128
ROPE = 64
VDIM = 128
LAT = 512
F = 1408
EXPERTS = 8
EPSILON = 1e-06

VM = pltpu.VMEM
f32 = jnp.float32
bf16 = jnp.bfloat16


class Sems:
    def __init__(self, send, recv):
        self.send, self.recv, self.used, self.sent = send, recv, 0, []

    def start(self, src, dst, peer):
        copy = pltpu.make_async_remote_copy(
            src_ref=src,
            dst_ref=dst,
            send_sem=self.send.at[self.used],
            recv_sem=self.recv.at[self.used],
            device_id=peer,
            device_id_type=pl.DeviceIdType.MESH,
        )
        copy.start()
        self.used += 1
        self.sent.append(copy)
        return copy

    def finish(self):
        for copy in self.sent:
            copy.wait_send()


class Place:
    def __init__(self):
        me, spot = lax.axis_index("exp"), lax.axis_index("seq")
        self.me = me
        self.chip, self.core = me // 2, me % 2
        self.z, self.y = spot // 4, spot % 4
        self.sibling = {"exp": self.chip * 2 + 1 - self.core}
        self.across = [lambda i: {"exp": i * 2 + self.core}, lambda i: {"seq": self.z * 4 + i}, lambda i: {"seq": i * 4 + self.y}]
        self.along = [self.chip, self.y, self.z]

    def hop(self, axis, distance):
        return self.across[axis](lax.rem(self.along[axis] + distance, 4))


def greet(peers):
    barrier = pltpu.get_barrier_semaphore()
    for peer in peers:
        pl.semaphore_signal(barrier, inc=1, device_id=peer, device_id_type=pl.DeviceIdType.MESH)
    pl.semaphore_wait(barrier, len(peers))


def together(*streams):
    streams = list(streams)
    while streams:
        for stream in list(streams):
            try:
                next(stream)
            except StopIteration:
                streams.remove(stream)


def gather_stream(sems, at, src, out, rows, local):
    half = rows // 2
    right, left = at.hop(0, 1), at.hop(0, 3)
    me = at.me
    near_right = lax.rem(at.chip + 1, 4) * 2 + at.core
    near_left = lax.rem(at.chip + 3, 4) * 2 + at.core
    far = lax.rem(at.chip + 2, 4) * 2 + at.core

    def part(owner, h):
        return out.at[pl.ds(pl.multiple_of(owner * rows + h * half, half), half)]

    def own(h):
        return src.at[pl.ds(h * half, half)]

    ra = sems.start(own(0), part(me, 0), right)
    lb = sems.start(own(1), part(me, 1), left)
    rb = sems.start(own(1), part(me, 1), right)
    la = sems.start(own(0), part(me, 0), left)
    sib = [sems.start(src, out.at[pl.ds(pl.multiple_of(me * rows, rows), rows)], at.sibling)]
    mine = pltpu.make_async_copy(src, out.at[pl.ds(pl.multiple_of(me * rows, rows), rows)], local)
    mine.start()
    yield
    ra.wait_recv()
    far_a = sems.start(part(near_left, 0), part(near_left, 0), right)
    sib.append(sems.start(part(near_left, 0), part(near_left, 0), at.sibling))
    lb.wait_recv()
    far_b = sems.start(part(near_right, 1), part(near_right, 1), left)
    sib.append(sems.start(part(near_right, 1), part(near_right, 1), at.sibling))
    yield
    rb.wait_recv()
    sib.append(sems.start(part(near_left, 1), part(near_left, 1), at.sibling))
    la.wait_recv()
    sib.append(sems.start(part(near_right, 0), part(near_right, 0), at.sibling))
    yield
    far_a.wait_recv()
    sib.append(sems.start(part(far, 0), part(far, 0), at.sibling))
    far_b.wait_recv()
    sib.append(sems.start(part(far, 1), part(far, 1), at.sibling))
    yield
    mine.wait()
    for copy in sib:
        copy.wait_recv()


def scatter_stream(sems, at, src, pair, hop, last, rows, done):
    half = rows // 2
    right, left = at.hop(0, 1), at.hop(0, 3)
    order = (2, 1, 3, 0)
    sib = []
    for dist in order:
        owner = lax.rem(at.chip + dist, 4) * 2 + 1 - at.core
        sib.append(sems.start(src.at[pl.ds(pl.multiple_of(owner * rows, rows), rows)], pair.at[dist], at.sibling))

    def fold(i):
        sib[i].wait_recv()
        owner = lax.rem(at.chip + order[i], 4) * 2 + at.core
        mine = src[pl.ds(pl.multiple_of(owner * rows, rows), rows)]
        pair[order[i]] = (pair[order[i]].astype(f32) + mine.astype(f32)).astype(bf16)

    def add(ref, other):
        ref[...] = (ref[...].astype(f32) + other[...].astype(f32)).astype(bf16)

    first, second = pl.ds(0, half), pl.ds(half, half)
    yield
    fold(0)
    far_a = sems.start(pair.at[2, first], hop.at[0], right)
    far_b = sems.start(pair.at[2, second], hop.at[1], left)
    yield
    fold(1)
    dir_b = sems.start(pair.at[1, second], last.at[0], right)
    fold(2)
    dir_a = sems.start(pair.at[3, first], last.at[1], left)
    yield
    far_a.wait_recv()
    add(pair.at[1, first], hop.at[0])
    acc_a = sems.start(pair.at[1, first], last.at[2], right)
    far_b.wait_recv()
    add(pair.at[3, second], hop.at[1])
    acc_b = sems.start(pair.at[3, second], last.at[3], left)
    yield
    sib[3].wait_recv()
    dir_b.wait_recv()
    dir_a.wait_recv()
    acc_a.wait_recv()
    acc_b.wait_recv()
    for h, ends in ((0, (1, 2)), (1, (0, 3))):
        mine = src[pl.ds(pl.multiple_of(at.me * rows + h * half, half), half)].astype(f32)
        total = mine + pair[0, pl.ds(h * half, half)].astype(f32)
        done(h, total + last[ends[0]].astype(f32) + last[ends[1]].astype(f32))


def scatter_scratch(rows, cols):
    return [
        pltpu.VMEM((4, rows, cols), bf16),
        pltpu.VMEM((2, rows // 2, cols), bf16),
        pltpu.VMEM((4, rows // 2, cols), bf16),
    ]


def ring_sum(sems, at, axis, block, hop, last):
    right, left = at.hop(axis, 1), at.hop(axis, 3)
    to = [lax.rem(at.along[axis] + d, 4) for d in range(4)]

    def add(ref, other):
        ref[...] = (ref[...].astype(f32) + other[...].astype(f32)).astype(bf16)

    far_a = sems.start(block(to[2], 0), hop.at[0], right)
    far_b = sems.start(block(to[2], 1), hop.at[1], left)
    dir_b = sems.start(block(to[1], 1), last.at[0], right)
    dir_a = sems.start(block(to[3], 0), last.at[1], left)
    yield
    far_a.wait_recv()
    add(block(to[1], 0), hop.at[0])
    acc_a = sems.start(block(to[1], 0), last.at[2], right)
    far_b.wait_recv()
    add(block(to[3], 1), hop.at[1])
    acc_b = sems.start(block(to[3], 1), last.at[3], left)
    yield
    dir_b.wait_recv()
    dir_a.wait_recv()
    add(block(to[0], 1), last.at[0])
    add(block(to[0], 0), last.at[1])
    yield
    acc_a.wait_recv()
    add(block(to[0], 0), last.at[2])
    acc_b.wait_recv()
    add(block(to[0], 1), last.at[3])


def ring_gather(sems, at, axis, block):
    right, left = at.hop(axis, 1), at.hop(axis, 3)
    to = [lax.rem(at.along[axis] + d, 4) for d in range(4)]
    ra = sems.start(block(to[0], 0), block(to[0], 0), right)
    lb = sems.start(block(to[0], 1), block(to[0], 1), left)
    rb = sems.start(block(to[0], 1), block(to[0], 1), right)
    la = sems.start(block(to[0], 0), block(to[0], 0), left)
    yield
    ra.wait_recv()
    fa = sems.start(block(to[3], 0), block(to[3], 0), right)
    lb.wait_recv()
    fb = sems.start(block(to[1], 1), block(to[1], 1), left)
    yield
    rb.wait_recv()
    la.wait_recv()
    yield
    fa.wait_recv()
    fb.wait_recv()


def seq_stream(sems, at, work, out, scratch, axes):
    half = work.shape[1] // 2
    hop1, last1, hop2, last2 = scratch

    def wide(ref):
        return lambda i, h: ref.at[pl.ds(i * 4 + 2 * h, 2)]

    def narrow(ref):
        return lambda i, h: ref.at[at.along[axes[0]] * 4 + i, pl.ds(h * half, half)]

    yield from ring_sum(sems, at, axes[0], wide(work), hop1, last1)
    yield from ring_sum(sems, at, axes[1], narrow(work), hop2, last2)
    own = at.along[axes[0]] * 4 + at.along[axes[1]]
    out[own] = work[own]
    yield from ring_gather(sems, at, axes[1], narrow(out))
    yield from ring_gather(sems, at, axes[0], wide(out))


def seq_scratch(rows, cols):
    return [
        pltpu.VMEM((2, 2, rows, cols), bf16),
        pltpu.VMEM((4, 2, rows, cols), bf16),
        pltpu.VMEM((2, rows // 2, cols), bf16),
        pltpu.VMEM((4, rows // 2, cols), bf16),
    ]


def seq_direct(sems, at, work, out, wide_in, narrow_in):
    y, z = at.y, at.z
    copies = [sems.start(work.at[pl.ds(lax.rem(y + d, 4) * 4, 4)], wide_in.at[d - 1], at.hop(1, d)) for d in (1, 2, 3)]
    yield
    for copy in copies:
        copy.wait_recv()
    mine = pl.ds(y * 4, 4)
    work[mine] = (
        work[mine].astype(f32) + wide_in[0].astype(f32) + (wide_in[1].astype(f32) + wide_in[2].astype(f32))
    ).astype(bf16)
    copies = [sems.start(work.at[y * 4 + lax.rem(z + d, 4)], narrow_in.at[d - 1], at.hop(2, d)) for d in (1, 2, 3)]
    yield
    for copy in copies:
        copy.wait_recv()
    own = y * 4 + z
    out[own] = (
        work[own].astype(f32) + narrow_in[0].astype(f32) + (narrow_in[1].astype(f32) + narrow_in[2].astype(f32))
    ).astype(bf16)
    copies = [sems.start(out.at[own], out.at[own], at.hop(2, d)) for d in (1, 2, 3)]
    yield
    for copy in copies:
        copy.wait_recv()
    copies = [sems.start(out.at[mine], out.at[mine], at.hop(1, d)) for d in (1, 2, 3)]
    yield
    for copy in copies:
        copy.wait_recv()


def small_stream(sems, at, slots, out):
    stages = [(at.core, 2, lambda d: at.sibling)] + [
        (at.along[axis], 4, functools.partial(at.hop, axis)) for axis in range(3)
    ]
    for stage, (place, count, name) in enumerate(stages):
        if stage:
            slots[stage, place] = out[...]
        copies = [sems.start(slots.at[stage, place], slots.at[stage, place], name(d)) for d in range(1, count)]
        yield
        for copy in copies:
            copy.wait_recv()
        total = slots[stage, 0]
        for i in range(1, count):
            total = total + slots[stage, i]
        out[...] = total


def swapped(tensor):
    lane = lax.broadcasted_iota(jnp.int32, tensor.shape, 1)
    return jnp.where(lane % 64 < 32, pltpu.roll(tensor, 96, 1), pltpu.roll(tensor, 32, 1))


SHARED_TILE = 384
MLP_TILES = (("s", 0, 384), ("e", 0, 512), ("e", 512, 512), ("e", 1024, 384))
ROW_STEP = 256


def dot_nn(a, b):
    return lax.dot_general(a, b, (((1,), (0,)), ((), ())), preferred_element_type=f32)


def dot_nt(a, b):
    return lax.dot_general(a, b, (((1,), (1,)), ((), ())), preferred_element_type=f32)


def dot_tn(a, b):
    return lax.dot_general(a, b, (((0,), (0,)), ((), ())), preferred_element_type=f32)


def mlp_kernel(
    mid_h, grad_h, pair_s_h, pair_e_h, down_s_h, down_e_h, router, router_turned, hot,
    mid_part, moe_part, router_out, terms_h,
    mid, grad, pair_s, pair_e, down_s, down_e, act, dpre, logit, stage, load, store,
):
    rows, width = mid_h.shape
    expert = lax.axis_index("exp")
    sources = [(mid_h, mid), (grad_h, grad), (pair_s_h, pair_s), (down_s_h, down_s), (pair_e_h, pair_e), (down_e_h, down_e)]
    loads = [pltpu.make_async_copy(src, dst, load.at[i]) for i, (src, dst) in enumerate(sources)]
    for c in loads:
        c.start()
    for c in loads[:4]:
        c.wait()
    lane = lax.broadcasted_iota(jnp.int32, (ROW_STEP, 128), 1)
    own_lane = lane == expert

    def block(index):
        return pl.ds(pl.multiple_of(index * ROW_STEP, ROW_STEP), ROW_STEP)

    def gates(r):
        raw = dot_nn(mid[r], router[...])
        raw = raw + (pltpu.roll(raw, 128 - EXPERTS, 1) + pltpu.roll(raw, 128 - 2 * EXPERTS, 1))
        raw = jnp.where(lane < EXPERTS, raw, -1e30)
        raw = jnp.exp(raw - jnp.max(raw, axis=1, keepdims=True))
        probs = raw / jnp.sum(raw, axis=1, keepdims=True)
        own = jnp.sum(jnp.where(own_lane, probs * hot[r].astype(f32), 0.0), axis=1, keepdims=True)
        return own, probs

    def piece(r, kind, start, size, own):
        pair, down = (pair_s, down_s) if kind == "s" else (pair_e, down_e)
        span = SHARED_TILE if kind == "s" else F
        act_at = F if kind == "s" else 0
        dpre_at = 2 * F if kind == "s" else 0
        gate = dot_nn(mid[r], pair[:, start : start + size])
        up = dot_nn(mid[r], pair[:, span + start : span + start + size])
        dact = dot_nt(grad[r], down[start : start + size])
        logistic = 1.0 / (1.0 + jnp.exp(-gate))
        passed = gate * logistic
        out = passed * up
        total = None
        if kind == "e":
            total = jnp.sum(out * dact, axis=1, keepdims=True)
            out = out * own
            dact = dact * own
        act[r, act_at + start : act_at + start + size] = out.astype(bf16)
        slope = logistic + passed * (1.0 - logistic)
        dpre[r, dpre_at + start : dpre_at + start + size] = (dact * up * slope).astype(bf16)
        dpre[r, dpre_at + span + start : dpre_at + span + start + size] = (dact * passed).astype(bf16)
        return total

    @pl.loop(0, rows // ROW_STEP)
    def _(index):
        piece(block(index), *MLP_TILES[0], None)

    loads[4].wait()
    loads[5].wait()

    @pl.loop(0, rows // ROW_STEP)
    def _(index):
        r = block(index)
        own, probs = gates(r)
        total = piece(r, *MLP_TILES[1], own)
        for tile in MLP_TILES[2:]:
            total = total + piece(r, *tile, own)
        logit[r] = ((own * total) * (jnp.where(own_lane, 1.0, 0.0) - probs)).astype(bf16)

    half = width // 2
    count = 0

    def flush(slot, at):
        return pltpu.make_async_copy(stage.at[slot], terms_h.at[pl.ds(at[0], half), pl.ds(at[1], 512)], store.at[slot])

    def tiles_of(left, right, columns, offset):
        @pl.loop(0, columns // 512)
        def _(index):
            spot = pl.multiple_of(index * 512, 512)
            for part in range(2):
                @pl.when(index > 0)
                def _():
                    flush(part, (part * half, pl.multiple_of(spot + offset - 512, 512))).wait()
                stage[part] = dot_tn(left[:, part * half : (part + 1) * half], right[:, pl.ds(spot, 512)]).astype(bf16)
                flush(part, (part * half, pl.multiple_of(spot + offset, 512))).start()
        for part in range(2):
            flush(part, (part * half, columns - 512 + offset)).wait()

    tiles_of(mid, dpre, dpre.shape[1], 0)
    tiles_of(grad, act, act.shape[1] // 512 * 512, dpre.shape[1])
    tail = act.shape[1] // 512 * 512
    rest = act.shape[1] - tail
    for part in range(2):
        stage[part, :, :rest] = dot_tn(grad[:, part * half : (part + 1) * half], act[:, tail:]).astype(bf16)
        last = pltpu.make_async_copy(
            stage.at[part, :, pl.ds(0, rest)],
            terms_h.at[pl.ds(part * half, half), pl.ds(dpre.shape[1] + tail, rest)], store.at[part])
        last.start()
    router_out[...] = dot_tn(logit[...], mid[...])[:EXPERTS]
    for part in range(2):
        pltpu.make_async_copy(
            stage.at[part, :, pl.ds(0, rest)],
            terms_h.at[pl.ds(part * half, half), pl.ds(dpre.shape[1] + tail, rest)], store.at[part]).wait()

    @pl.loop(0, rows // ROW_STEP)
    def _(index):
        r = block(index)
        total = dot_nt(dpre[r, : 2 * F], pair_e[...]) + dot_nt(dpre[r, 2 * F :], pair_s[...])
        mid_part[r] = (total + dot_nn(logit[r], router_turned[...])).astype(bf16)
        moe_part[r] = (dot_nn(act[r, :F], down_e[...]) + dot_nn(act[r, F:], down_s[...])).astype(bf16)


def mlp(mid_all, grad_all, pair_s, pair_e, down_s, down_e, router, router_turned, hot):
    rows, width = mid_all.shape
    hidden = F + SHARED_TILE
    whole = pl.BlockSpec(memory_space=VM)
    held = pl.BlockSpec(memory_space=pl.ANY)
    return pl.pallas_call(
        mlp_kernel,
        out_shape=[
            jax.ShapeDtypeStruct((rows, width), bf16),
            jax.ShapeDtypeStruct((rows, width), bf16),
            jax.ShapeDtypeStruct((EXPERTS, width), f32),
            jax.ShapeDtypeStruct((width, 3 * hidden), bf16),
        ],
        in_specs=[held] * 6 + [whole] * 3,
        out_specs=[whole, whole, whole, held],
        scratch_shapes=[
            pltpu.VMEM(mid_all.shape, bf16), pltpu.VMEM(grad_all.shape, bf16),
            pltpu.VMEM(pair_s.shape, bf16), pltpu.VMEM(pair_e.shape, bf16),
            pltpu.VMEM(down_s.shape, bf16), pltpu.VMEM(down_e.shape, bf16),
            pltpu.VMEM((rows, hidden), bf16), pltpu.VMEM((rows, 2 * hidden), bf16),
            pltpu.VMEM((rows, 128), bf16), pltpu.VMEM((2, width // 2, 512), bf16),
            pltpu.SemaphoreType.DMA((6,)), pltpu.SemaphoreType.DMA((2,)),
        ],
        compiler_params=pltpu.CompilerParams(vmem_limit_bytes=63 << 20),
        cost_estimate=pl.CostEstimate(flops=18 * rows * width * hidden, bytes_accessed=60 << 20, transcendentals=rows * hidden),
        name="mlp",
    )(mid_all, grad_all, pair_s, pair_e, down_s, down_e, router, router_turned, hot)


ATT = 256
SCALE = (NOPE + ROPE) ** (-0.5)
LOG2E = 1.4426950408889634


def score_pieces(q, packed, ropes, qseg, kseg, head, i):
    rows = pl.ds(ATT * i, ATT)
    prev = packed.shape[0] - q.shape[0]
    lane = lax.broadcasted_iota(jnp.int32, (ATT, 2 * ROPE), 1)
    rope = jnp.where(lane // ROPE == head, q[rows, 2 * NOPE :], jnp.zeros((), bf16))
    query = jnp.concatenate([q[rows, head * NOPE : (head + 1) * NOPE], rope], axis=1)
    edge = prev + ATT * i
    pieces = []
    for start, end in ((0, edge), (edge, edge + ATT)):
        keys = jnp.concatenate(
            [packed[start:end, head * 2 * NOPE : head * 2 * NOPE + NOPE], ropes[start:end]], axis=1
        )
        scores = dot_nt(query, keys)
        allowed = qseg[rows] == kseg[:, start:end]
        if start:
            allowed = allowed & (
                lax.broadcasted_iota(jnp.int32, scores.shape, 1)
                <= lax.broadcasted_iota(jnp.int32, scores.shape, 0)
            )
        pieces.append((start, end, jnp.where(allowed, scores, -1e30), keys))
    return query, pieces


def attend_kernel(q, packed, ropes, qseg, kseg, heads, lse):
    for head in range(2):
        for i in range(q.shape[0] // ATT):
            rows = pl.ds(ATT * i, ATT)
            _, pieces = score_pieces(q, packed, ropes, qseg, kseg, head, i)
            top = jnp.maximum(*[jnp.max(scores, axis=1, keepdims=True) for _, _, scores, _ in pieces])
            total, out = 0.0, 0.0
            for start, end, scores, _ in pieces:
                weights = jnp.exp2((scores - top) * (SCALE * LOG2E))
                total = total + jnp.sum(weights, axis=1, keepdims=True)
                values = packed[start:end, head * 2 * NOPE + NOPE : (head + 1) * 2 * NOPE]
                out = out + dot_nn(weights.astype(bf16), values)
            heads[rows, head * VDIM : (head + 1) * VDIM] = (out / total).astype(bf16)
            lse[head, rows] = top * (SCALE * LOG2E) + jnp.log2(total)


def attend(q, packed, ropes, qseg, kseg):
    whole = pl.BlockSpec(memory_space=VM)
    rows = q.shape[0]
    return pl.pallas_call(
        attend_kernel,
        out_shape=[jax.ShapeDtypeStruct((rows, 2 * VDIM), bf16), jax.ShapeDtypeStruct((2, rows, 1), f32)],
        in_specs=[whole] * 5,
        out_specs=[whole] * 2,
        compiler_params=pltpu.CompilerParams(vmem_limit_bytes=56 << 20),
        name="attend",
    )(q, packed, ropes, qseg, kseg)


def attend_back_kernel(
    grad, wo, heads, q, packed, ropes, qseg, kseg, lse, cosine, sine, kv_proj, latents,
    dq, key_grad, kvo, head_grad, dkey, dvalue, drope, dpacked,
):
    rows = q.shape[0]
    prev = packed.shape[0] - rows
    step = 256
    for i in range(rows // step):
        r = pl.ds(i * step, step)
        head_grad[r] = dot_nt(grad[r], wo[...]).astype(bf16)
    for head in range(2):
        dkey[...] = jnp.zeros_like(dkey)
        dvalue[...] = jnp.zeros_like(dvalue)
        for i in range(rows // ATT):
            r = pl.ds(ATT * i, ATT)
            query, pieces = score_pieces(q, packed, ropes, qseg, kseg, head, i)
            upstream = head_grad[r, head * VDIM : (head + 1) * VDIM]
            probs, dprobs = [], []
            inner = 0.0
            for start, end, scores, _ in pieces:
                p = jnp.exp2(scores * (SCALE * LOG2E) - lse[head, r])
                d = dot_nt(upstream, packed[start:end, head * 2 * NOPE + NOPE : (head + 1) * 2 * NOPE])
                inner = inner + jnp.sum(p * d, axis=1, keepdims=True)
                probs.append(p)
                dprobs.append(d)
            dquery = 0.0
            for (start, end, _, keys), p, d in zip(pieces, probs, dprobs):
                ds = (p * (d - inner)).astype(bf16)
                dquery = dquery + dot_nn(ds, keys)
                dkey[start:end] += dot_tn(ds, query)
                dvalue[start:end] += dot_tn(p.astype(bf16), upstream)
            dquery = dquery * SCALE
            dq[r, head * NOPE : (head + 1) * NOPE] = dquery[:, :NOPE].astype(bf16)
            rope = dquery[:, NOPE:]
            rope = rope * cosine[r] - swapped(rope) * sine[r]
            lane = lax.broadcasted_iota(jnp.int32, rope.shape, 1)
            if head == 0:
                dq[r, 2 * NOPE :] = rope.astype(bf16)
            else:
                dq[r, 2 * NOPE :] = jnp.where(lane < ROPE, dq[r, 2 * NOPE :], rope.astype(bf16))
        dpacked[:, head * 2 * NOPE : head * 2 * NOPE + NOPE] = (dkey[:, :NOPE] * SCALE).astype(bf16)
        dpacked[:, head * 2 * NOPE + NOPE : (head + 1) * 2 * NOPE] = dvalue[...].astype(bf16)
        if head == 0:
            drope[...] = dkey[:, NOPE:]
        else:
            drope[...] += dkey[:, NOPE:]
    span = LAT + 2 * ROPE
    for i in range(packed.shape[0] // 512):
        r = pl.ds(512 * i, 512)
        at = span if i * 512 < prev else 0
        to = pl.ds(512 * i - (0 if i * 512 < prev else prev), 512)
        key_grad[to, at : at + LAT] = dot_nt(dpacked[r], kv_proj[...]).astype(bf16)
        rope = drope[r]
        key_grad[to, at + LAT : at + span] = ((rope + pltpu.roll(rope, ROPE, 1)) * SCALE).astype(bf16)
    spots, wide = kvo.shape[0], kvo.shape[2]
    kv = dot_tn(latents[...], dpacked[...]).astype(bf16)
    kv_rows = kv.shape[0] // spots
    kvo[:, :kv_rows] = kv.reshape(spots, kv_rows, wide)
    out_rows = wo.shape[0] // spots
    for j in range(grad.shape[1] // wide):
        term = dot_tn(heads[...], grad[:, j * wide : (j + 1) * wide]).astype(bf16)
        kvo[:, kv_rows + j * out_rows : kv_rows + (j + 1) * out_rows] = term.reshape(spots, out_rows, wide)


def attend_back(grad, wo, heads, q, packed, ropes, qseg, kseg, lse, cosine, sine, kv_proj, latents):
    whole = pl.BlockSpec(memory_space=VM)
    rows, keys = q.shape[0], packed.shape[0]
    spots = lax.axis_size("seq")
    kvo_rows = (kv_proj.shape[0] * kv_proj.shape[1] + wo.shape[0] * wo.shape[1]) // spots // LAT
    return pl.pallas_call(
        attend_back_kernel,
        out_shape=[
            jax.ShapeDtypeStruct(q.shape, bf16),
            jax.ShapeDtypeStruct((rows, 2 * (LAT + 2 * ROPE)), bf16),
            jax.ShapeDtypeStruct((spots, kvo_rows, LAT), bf16),
        ],
        in_specs=[whole] * 13,
        out_specs=[whole] * 3,
        scratch_shapes=[
            pltpu.VMEM((rows, 2 * VDIM), bf16),
            pltpu.VMEM((keys, 2 * NOPE), f32),
            pltpu.VMEM((keys, VDIM), f32),
            pltpu.VMEM((keys, 2 * ROPE), f32),
            pltpu.VMEM(packed.shape, bf16),
        ],
        compiler_params=pltpu.CompilerParams(vmem_limit_bytes=56 << 20),
        name="attend_back",
    )(grad, wo, heads, q, packed, ropes, qseg, kseg, lse, cosine, sine, kv_proj, latents)


SPAN = LAT + 2 * ROPE


def tail_kernel(
    dq, key_grad, kvo, normed, wq, wl, raw, latent_gain, cosine, sine, gain, upstream, rows_in, small_in,
    query_out, kvo_out, latent_out, grad_out, small_out,
    work0, work1, key_sum, in_part, in_sum, in_own, lat_rows, lat_all, lat_work, lat_sum, prev_out, prev_in, small,
    r0, r1, r2, r3, s0, s1, s2, s3, k0, k1, k2, n0, n1, n2, lw, ln, send, recv, local,
):
    at = Place()
    sems = Sems(send, recv)
    greet([at.sibling] + [at.hop(axis, d) for axis in range(3) for d in (1, 2, 3)])
    rows = raw.shape[0]
    half = rows // 2
    own = pl.ds(pl.multiple_of(at.me * rows, rows), rows)

    def keep_key(h, total):
        key_sum[h * half : (h + 1) * half] = total

    def keep_in(h, total):
        in_sum[h * half : (h + 1) * half] = total

    keys = scatter_stream(sems, at, key_grad, k0, k1, k2, rows, keep_key)
    next(keys)
    work0[...] = dot_tn(normed[...], dq[...]).astype(bf16).reshape(work0.shape)
    work1[...] = kvo[...]
    first = seq_stream(sems, at, work0, query_out, (r0, r1, r2, r3), (1, 2))
    second = seq_stream(sems, at, work1, kvo_out, (s0, s1, s2, s3), (2, 1))
    next(first)
    next(second)
    next(keys)
    gain_part = jnp.zeros((1, normed.shape[1]), f32)
    step = 256
    for i in range(dq.shape[0] // step):
        r = pl.ds(i * step, step)
        part = dot_nt(dq[r], wq[...])
        gain_part = gain_part + jnp.sum(part * normed[r].astype(f32), axis=0, keepdims=True)
        in_part[r] = part.astype(bf16)
        if i == 1:
            next(keys)
    in_rows = scatter_stream(sems, at, in_part, n0, n1, n2, rows, keep_in)
    running = []

    def latents():
        yield from keys
        prev_out[...] = key_sum[:, SPAN:].astype(bf16)
        partner = at.across[1](at.y + 1 - 2 * lax.rem(at.y, 2))
        swap = sems.start(prev_out, prev_in, partner)
        yield
        swap.wait_recv()
        own_grad = key_sum[:, :SPAN] + jnp.where(lax.rem(at.y, 2) == 0, prev_in[...].astype(f32), 0.0)
        x = raw[...]
        inverse = lax.rsqrt(jnp.mean(x * x, axis=1, keepdims=True) + EPSILON)
        u = own_grad[:, :LAT]
        lat_gain_part = jnp.sum(u * x * inverse, axis=0, keepdims=True)
        s = u * latent_gain[...]
        inner = jnp.mean(s * x, axis=1, keepdims=True)
        lat_rows[:, :LAT] = (inverse * s - x * (inverse * inverse * inverse) * inner).astype(bf16)
        rope = own_grad[:, LAT:]
        rope = rope * cosine[...] - swapped(rope) * sine[...]
        lane = lax.broadcasted_iota(jnp.int32, rope.shape, 1)
        lat_rows[:, LAT:] = jnp.where(lane < ROPE, rope, 0.0).astype(bf16)
        gathered = gather_stream(sems, at, lat_rows, lat_all, rows, local.at[0])
        next(gathered)
        in_own[...] = dot_nt(lat_rows[...], wl[...])
        attn_gain = gain_part + jnp.sum(in_own[...] * normed[own].astype(f32), axis=0, keepdims=True)
        small[0, at.core] = small_in[...]
        small[0, at.core, EXPERTS : EXPERTS + 1] = attn_gain / gain[...]
        small[0, at.core, EXPERTS + 2 : EXPERTS + 3, :LAT] = lat_gain_part
        running.append(small_stream(sems, at, small, small_out))
        yield from gathered
        width = lat_work.shape[0] * lat_work.shape[1]
        mine = normed[:, pl.ds(pl.multiple_of(at.me * width, width), width)]
        lat_work[...] = dot_tn(mine, lat_all[...]).astype(bf16).reshape(lat_work.shape)
        yield from seq_direct(sems, at, lat_work, lat_sum, lw, ln)
        yield from gather_stream(sems, at, lat_sum, latent_out, lat_sum.shape[0], local.at[1])

    running += [latents(), in_rows, first, second]
    while running:
        for stream in list(running):
            try:
                next(stream)
            except StopIteration:
                running.remove(stream)
    u = in_sum[...] + in_own[...]
    x = rows_in[...].astype(f32)
    inverse = lax.rsqrt(jnp.mean(x * x, axis=1, keepdims=True) + EPSILON)
    s = u * gain[...]
    inner = jnp.mean(s * x, axis=1, keepdims=True)
    grad_out[...] = (upstream[...] + (inverse * s - x * (inverse * inverse * inverse) * inner)).astype(bf16)
    sems.finish()


def tail(dq, key_grad, kvo, normed, wq, wl, raw, latent_gain, cosine, sine, gain, upstream, rows_in, small_in):
    whole = pl.BlockSpec(memory_space=VM)
    rows, width = rows_in.shape
    spots = kvo.shape[0]
    query_shape = (spots, width // spots, dq.shape[1])
    slice_rows = width // lax.axis_size("exp") // spots
    lat_shape = (spots, slice_rows, SPAN)
    return pl.pallas_call(
        tail_kernel,
        out_shape=[
            jax.ShapeDtypeStruct(query_shape, bf16),
            jax.ShapeDtypeStruct(kvo.shape, bf16),
            jax.ShapeDtypeStruct((8 * spots, slice_rows, SPAN), bf16),
            jax.ShapeDtypeStruct((rows, width), bf16),
            jax.ShapeDtypeStruct(small_in.shape, f32),
        ],
        in_specs=[whole] * 14,
        out_specs=[whole] * 5,
        scratch_shapes=[
            pltpu.VMEM(query_shape, bf16),
            pltpu.VMEM(kvo.shape, bf16),
            pltpu.VMEM((rows, 2 * SPAN), f32),
            pltpu.VMEM((8 * rows, width), bf16),
            pltpu.VMEM((rows, width), f32),
            pltpu.VMEM((rows, width), f32),
            pltpu.VMEM((rows, SPAN), bf16),
            pltpu.VMEM((8 * rows, SPAN), bf16),
            pltpu.VMEM(lat_shape, bf16),
            pltpu.VMEM(lat_shape, bf16),
            pltpu.VMEM((rows, SPAN), bf16),
            pltpu.VMEM((rows, SPAN), bf16),
            pltpu.VMEM((4, 4) + small_in.shape, f32),
            *seq_scratch(*query_shape[1:]),
            *seq_scratch(*kvo.shape[1:]),
            *scatter_scratch(rows, 2 * SPAN),
            *scatter_scratch(rows, width),
            pltpu.VMEM((3, 4, slice_rows, SPAN), bf16),
            pltpu.VMEM((3, slice_rows, SPAN), bf16),
            pltpu.SemaphoreType.DMA((120,)),
            pltpu.SemaphoreType.DMA((120,)),
            pltpu.SemaphoreType.DMA((2,)),
        ],
        compiler_params=pltpu.CompilerParams(collective_id=3, has_side_effects=True, vmem_limit_bytes=60 << 20),
        name="tail",
    )(dq, key_grad, kvo, normed, wq, wl, raw, latent_gain, cosine, sine, gain, upstream, rows_in, small_in)


def start_kernel(
    rows_in, gain, wl, latent_gain, wq, kv_proj, cosine, sine, own_cosine, own_sine, hot,
    normed, q, packed, keys, hot_all, raw,
    own_normed, ext, ext_all, prev_out, send, recv, local,
):
    at = Place()
    sems = Sems(send, recv)
    partner = at.across[1](at.y + 1 - 2 * lax.rem(at.y, 2))
    greet([at.hop(0, 1), at.hop(0, 3), at.sibling, partner])
    rows = rows_in.shape[0]
    x = rows_in[...].astype(f32)
    own_normed[...] = (x * lax.rsqrt(jnp.mean(x * x, axis=1, keepdims=True) + EPSILON) * gain[...]).astype(bf16)
    big = gather_stream(sems, at, own_normed, normed, rows, local.at[0])
    next(big)
    lat = dot_nn(own_normed[...], wl[...])
    raw[...] = lat[:, :LAT]
    x = lat[:, :LAT]
    x = x * lax.rsqrt(jnp.mean(x * x, axis=1, keepdims=True) + EPSILON) * latent_gain[...]
    rope = lat[:, LAT:]
    rope = rope * own_cosine[...] + swapped(rope) * own_sine[...]
    rope = rope + pltpu.roll(rope, ROPE, 1)
    prev_out[:, :LAT] = x.astype(bf16)
    prev_out[:, LAT:] = rope.astype(bf16)
    swap = sems.start(prev_out, ext.at[:, pl.ds(SPAN, SPAN)], partner)
    ext[:, :SPAN] = prev_out[...]
    ext[:, 2 * SPAN :] = hot[...]
    next(big)
    swap.wait_recv()
    little = gather_stream(sems, at, ext, ext_all, rows, local.at[1])
    next(little)
    together(big, little)
    block = normed.shape[0]
    step = 256
    for i in range(block // step):
        r = pl.ds(i * step, step)
        query = dot_nn(normed[r], wq[...])
        q[r, : 2 * NOPE] = query[:, : 2 * NOPE].astype(bf16)
        rope = query[:, 2 * NOPE :]
        q[r, 2 * NOPE :] = (rope * cosine[r] + swapped(rope) * sine[r]).astype(bf16)
    for part in range(2):
        r = slice((1 - part) * block, (2 - part) * block)
        keys[r] = ext_all[:, part * SPAN : (part + 1) * SPAN]
        packed[r] = dot_nn(ext_all[:, part * SPAN : part * SPAN + LAT], kv_proj[...]).astype(bf16)
    hot_all[...] = ext_all[:, 2 * SPAN :]
    sems.finish()


def start(rows_in, gain, wl, latent_gain, wq, kv_proj, cosine, sine, own_cosine, own_sine, hot):
    whole = pl.BlockSpec(memory_space=VM)
    rows, width = rows_in.shape
    block = 8 * rows
    ext_width = 2 * SPAN + hot.shape[1]
    return pl.pallas_call(
        start_kernel,
        out_shape=[
            jax.ShapeDtypeStruct((block, width), bf16),
            jax.ShapeDtypeStruct((block, wq.shape[1]), bf16),
            jax.ShapeDtypeStruct((2 * block, kv_proj.shape[1]), bf16),
            jax.ShapeDtypeStruct((2 * block, SPAN), bf16),
            jax.ShapeDtypeStruct((block, hot.shape[1]), bf16),
            jax.ShapeDtypeStruct((rows, LAT), f32),
        ],
        in_specs=[whole] * 11,
        out_specs=[whole] * 6,
        scratch_shapes=[
            pltpu.VMEM((rows, width), bf16),
            pltpu.VMEM((rows, ext_width), bf16),
            pltpu.VMEM((block, ext_width), bf16),
            pltpu.VMEM((rows, SPAN), bf16),
            pltpu.SemaphoreType.DMA((27,)),
            pltpu.SemaphoreType.DMA((27,)),
            pltpu.SemaphoreType.DMA((2,)),
        ],
        compiler_params=pltpu.CompilerParams(collective_id=0, has_side_effects=True, vmem_limit_bytes=56 << 20),
        name="start",
    )(rows_in, gain, wl, latent_gain, wq, kv_proj, cosine, sine, own_cosine, own_sine, hot)


def middle_kernel(
    heads, wo, rows_in, gain, residual, mid_all, part, own_mid, p0, p1, p2, send, recv, local
):
    at = Place()
    sems = Sems(send, recv)
    rows = rows_in.shape[0]
    half = rows // 2
    step = 256
    for i in range(heads.shape[0] // step):
        r = pl.ds(i * step, step)
        part[r] = dot_nn(heads[r], wo[...]).astype(bf16)
    greet([at.hop(0, 1), at.hop(0, 3), at.sibling])

    def done(h, total):
        r = slice(h * half, (h + 1) * half)
        x = rows_in[r].astype(f32) + total
        residual[r] = x
        own_mid[r] = (x * lax.rsqrt(jnp.mean(x * x, axis=1, keepdims=True) + EPSILON) * gain[...]).astype(bf16)

    together(scatter_stream(sems, at, part, p0, p1, p2, rows, done))
    together(gather_stream(sems, at, own_mid, mid_all, rows, local))
    sems.finish()


def middle(heads, wo, rows_in, gain):
    whole = pl.BlockSpec(memory_space=VM)
    rows, width = rows_in.shape
    return pl.pallas_call(
        middle_kernel,
        out_shape=[jax.ShapeDtypeStruct((rows, width), f32), jax.ShapeDtypeStruct((8 * rows, width), bf16)],
        in_specs=[whole] * 4,
        out_specs=[whole] * 2,
        scratch_shapes=[
            pltpu.VMEM((8 * rows, width), bf16),
            pltpu.VMEM((rows, width), bf16),
            *scatter_scratch(rows, width),
            pltpu.SemaphoreType.DMA((23,)),
            pltpu.SemaphoreType.DMA((23,)),
            pltpu.SemaphoreType.DMA,
        ],
        compiler_params=pltpu.CompilerParams(collective_id=1, has_side_effects=True, vmem_limit_bytes=56 << 20),
        name="middle",
    )(heads, wo, rows_in, gain)


def turn_kernel(
    part, residual, gain, upstream, residual_grad, gain_term, grad_all, own_grad, p0, p1, p2, send, recv, local
):
    at = Place()
    sems = Sems(send, recv)
    rows = residual.shape[0]
    half = rows // 2
    greet([at.hop(0, 1), at.hop(0, 3), at.sibling])
    gain_term[...] = jnp.zeros_like(gain_term)

    def done(h, total):
        r = slice(h * half, (h + 1) * half)
        x = residual[r]
        inverse = lax.rsqrt(jnp.mean(x * x, axis=1, keepdims=True) + EPSILON)
        gain_term[...] += jnp.sum(total * x * inverse, axis=0, keepdims=True)
        s = total * gain[...]
        inner = jnp.mean(s * x, axis=1, keepdims=True)
        grad = upstream[r].astype(f32) + (inverse * s - x * (inverse * inverse * inverse) * inner)
        residual_grad[r] = grad
        own_grad[r] = grad.astype(bf16)

    together(scatter_stream(sems, at, part, p0, p1, p2, rows, done))
    together(gather_stream(sems, at, own_grad, grad_all, rows, local))
    sems.finish()


def turn(part, residual, gain, upstream):
    whole = pl.BlockSpec(memory_space=VM)
    rows, width = residual.shape
    return pl.pallas_call(
        turn_kernel,
        out_shape=[
            jax.ShapeDtypeStruct((rows, width), f32),
            jax.ShapeDtypeStruct((1, width), f32),
            jax.ShapeDtypeStruct((8 * rows, width), bf16),
        ],
        in_specs=[whole] * 4,
        out_specs=[whole] * 3,
        scratch_shapes=[
            pltpu.VMEM((rows, width), bf16),
            *scatter_scratch(rows, width),
            pltpu.SemaphoreType.DMA((23,)),
            pltpu.SemaphoreType.DMA((23,)),
            pltpu.SemaphoreType.DMA,
        ],
        compiler_params=pltpu.CompilerParams(collective_id=2, has_side_effects=True, vmem_limit_bytes=56 << 20),
        name="turn",
    )(part, residual, gain, upstream)


def tables(position):
    lane = jnp.arange(2 * ROPE, dtype=jnp.int32)
    half = ROPE // 2
    frequency = jnp.exp((lane % half).astype(f32) * (-math.log(10000.0) / half))
    angles = position.astype(f32)[:, None] * frequency[None, :]
    sign = jnp.where(lane % ROPE < half, -1.0, 1.0)
    return jnp.cos(angles), jnp.sin(angles) * sign[None, :]


def local(
    layer_input, attn_gain, query_proj, latent_proj, latent_gain, kv_proj, output_proj, ffn_gain, router_proj,
    shared_gate_up, shared_down, expert_gate_up, expert_down, segment_ids, expert_routes, out_grad,
):
    own_rows, model_width = layer_input.shape
    block_rows = own_rows * lax.axis_size("exp")
    seq_rows = 2 * block_rows
    block_start = lax.axis_index("seq") * block_rows
    row_offset = lax.axis_index("exp") * own_rows
    query_pos = block_start + jnp.arange(block_rows, dtype=jnp.int32)
    query_seg = lax.dynamic_slice_in_dim(segment_ids, block_start, block_rows)
    key_start = block_start - block_rows
    prev_seg = lax.dynamic_slice_in_dim(segment_ids, jnp.maximum(key_start, 0), block_rows)
    prev_seg = jnp.where(key_start >= 0, prev_seg, -1)
    key_seg = jnp.concatenate([prev_seg, query_seg], axis=0)
    cosine, sine = tables(query_pos % seq_rows)
    own_cosine = lax.dynamic_slice_in_dim(cosine, row_offset, own_rows)
    own_sine = lax.dynamic_slice_in_dim(sine, row_offset, own_rows)
    head = NOPE + ROPE
    wq = jnp.concatenate(
        [
            query_proj[:, :NOPE],
            query_proj[:, head : head + NOPE],
            query_proj[:, NOPE:head],
            query_proj[:, head + NOPE :],
        ],
        axis=1,
    )
    wl = jnp.pad(latent_proj, ((0, 0), (0, SPAN - latent_proj.shape[1])))
    hot = jnp.sum(
        expert_routes[:, :, None] == jnp.arange(128, dtype=jnp.int32)[None, None, :], axis=1
    ).astype(bf16)
    attn_row, latent_row, ffn_row = attn_gain[None], latent_gain[None], ffn_gain[None]
    normed_all, q, packed, keys, hot_all, latent_raw = start(
        layer_input, attn_row, wl, latent_row, wq, kv_proj, cosine, sine, own_cosine, own_sine, hot
    )
    ropes, latents = keys[:, LAT:], keys[:, :LAT]
    late_grad, q = lax.optimization_barrier((out_grad, q))
    grad_all = lax.all_gather(late_grad, "exp", axis=0, tiled=True)
    qseg, kseg = query_seg[:, None], key_seg[None, :]
    heads, lse = attend(q, packed, ropes, qseg, kseg)
    residual, mid_all = middle(heads, output_proj, layer_input, ffn_row)

    router_high = lax.reduce_precision(router_proj, 8, 7)
    router_rest = router_proj - router_high
    router_mid = lax.reduce_precision(router_rest, 8, 7)
    router_low = router_rest - router_mid
    router_pieces = jnp.concatenate([router_high, router_mid, router_low], axis=1).astype(bf16)
    router_pieces = jnp.pad(router_pieces, ((0, 0), (0, 128 - 3 * EXPERTS)))
    router_turned = jnp.pad(router_proj.T.astype(bf16), ((0, 128 - EXPERTS), (0, 0)))
    shared_width = shared_down.shape[0]
    fill = SHARED_TILE - shared_width
    pair_s = jnp.pad(shared_gate_up, ((0, 0), (0, 0), (0, fill))).reshape(model_width, 2 * SHARED_TILE)
    down_s = jnp.pad(shared_down, ((0, fill), (0, 0)))
    mid_part, moe_part, router_term, weight_terms = mlp(
        mid_all, grad_all, pair_s, expert_gate_up[0], down_s, expert_down[0], router_pieces, router_turned, hot_all
    )
    weight_sum = lax.psum_scatter(weight_terms, "seq", scatter_dimension=0, tiled=True)
    residual_grad, ffn_term, attn_grad_all = turn(mid_part, residual, ffn_row, out_grad)
    dq, key_grad, kvo = attend_back(
        attn_grad_all, output_proj, heads, q, packed, ropes, qseg, kseg, lse, cosine, sine, kv_proj, latents
    )
    weight_sum, moe_part, dq = lax.optimization_barrier((weight_sum, moe_part, dq))
    moe_rows = lax.psum_scatter(moe_part, "exp", scatter_dimension=0, tiled=True)
    small = jnp.concatenate([router_term, jnp.zeros_like(ffn_term), ffn_term, jnp.zeros((6, model_width), f32)], axis=0)
    query_sum, kvo_sum, latent_sum, input_grad, small = tail(
        dq, key_grad, kvo, normed_all, wq, wl, latent_raw, latent_row, own_cosine, own_sine, attn_row,
        residual_grad, layer_input, small,
    )
    layer_output = (residual + moe_rows.astype(f32)).astype(bf16)
    query_sum = query_sum.reshape(model_width, -1)
    query_sum = jnp.concatenate(
        [
            query_sum[:, :NOPE],
            query_sum[:, 2 * NOPE : 2 * NOPE + ROPE],
            query_sum[:, NOPE : 2 * NOPE],
            query_sum[:, 2 * NOPE + ROPE :],
        ],
        axis=1,
    ).astype(f32)
    spots = kvo_sum.shape[0]
    kv_rows = kv_proj.shape[0] // spots
    kv_sum = kvo_sum[:, :kv_rows].reshape(kv_proj.shape).astype(f32)
    out_rows = output_proj.shape[0] // spots
    output_sum = (
        kvo_sum[:, kv_rows:]
        .reshape(spots, -1, out_rows, LAT)
        .transpose(0, 2, 1, 3)
        .reshape(output_proj.shape)
        .astype(f32)
    )
    latent_sum = latent_sum.reshape(model_width, SPAN)[:, : LAT + ROPE].astype(f32)
    pair_width = 2 * (F + SHARED_TILE)
    expert_gate_sum = weight_sum[None, :, : 2 * F].astype(f32)
    shared_gate_sum = (
        weight_sum[:, 2 * F : pair_width].reshape(own_rows, 2, SHARED_TILE)[..., :shared_width].astype(f32)
    )
    expert_down_sum = weight_sum[:, pair_width : pair_width + F].astype(f32).T[None]
    shared_down_sum = weight_sum[:, pair_width + F : pair_width + F + shared_width].astype(f32).T
    return (
        layer_output,
        input_grad,
        small[EXPERTS],
        query_sum,
        latent_sum,
        small[EXPERTS + 2, :LAT],
        kv_sum,
        output_sum,
        small[EXPERTS + 1],
        small[:EXPERTS].T,
        shared_gate_sum,
        shared_down_sum,
        expert_gate_sum,
        expert_down_sum,
    )


def solution(mesh):
    in_specs = (
        P(("seq", "exp"), None),
        P(),
        P(None, "exp"),
        P(),
        P(),
        P(None, "exp"),
        P("exp", None),
        P(),
        P(),
        P(None, None, "exp"),
        P("exp", None),
        P("exp", None, None),
        P("exp", None, None),
        P(),
        P(("seq", "exp"), None),
        P(("seq", "exp"), None),
    )
    out_specs = (
        P(("seq", "exp"), None),
        P(("seq", "exp"), None),
        P(),
        P(None, "exp"),
        P(),
        P(),
        P(None, "exp"),
        P("exp", None),
        P(),
        P(),
        P("seq", None, "exp"),
        P("exp", "seq"),
        P("exp", "seq", None),
        P("exp", None, "seq"),
    )
    return jax.shard_map(local, mesh=mesh, in_specs=in_specs, out_specs=out_specs, check_vma=False)
```

```python
import functools
import math

import jax
import jax.numpy as jnp
import numpy as np
from jax import lax
from jax.experimental import pallas as pl
from jax.experimental.pallas import tpu as pltpu
from jax.sharding import PartitionSpec as P

NOPE = 128
ROPE = 64
VDIM = 128
LAT = 512
F = 1408
EXPERTS = 8
EPSILON = 1e-06

VM = pltpu.VMEM
f32 = jnp.float32
bf16 = jnp.bfloat16


class Sems:
    def __init__(self, send, recv):
        self.send, self.recv, self.used, self.sent = send, recv, 0, []

    def start(self, src, dst, peer):
        copy = pltpu.make_async_remote_copy(
            src_ref=src,
            dst_ref=dst,
            send_sem=self.send.at[self.used],
            recv_sem=self.recv.at[self.used],
            device_id=peer,
            device_id_type=pl.DeviceIdType.MESH,
        )
        copy.start()
        self.used += 1
        self.sent.append(copy)
        return copy

    def finish(self):
        for copy in self.sent:
            copy.wait_send()


class Place:
    def __init__(self):
        me, spot = lax.axis_index("exp"), lax.axis_index("seq")
        self.me = me
        self.chip, self.core = me // 2, me % 2
        self.z, self.y = spot // 4, spot % 4
        self.sibling = {"exp": self.chip * 2 + 1 - self.core}
        self.across = [lambda i: {"exp": i * 2 + self.core}, lambda i: {"seq": self.z * 4 + i}, lambda i: {"seq": i * 4 + self.y}]
        self.along = [self.chip, self.y, self.z]

    def hop(self, axis, distance):
        return self.across[axis](lax.rem(self.along[axis] + distance, 4))


def greet(peers):
    barrier = pltpu.get_barrier_semaphore()
    for peer in peers:
        pl.semaphore_signal(barrier, inc=1, device_id=peer, device_id_type=pl.DeviceIdType.MESH)
    pl.semaphore_wait(barrier, len(peers))


def together(*streams):
    streams = list(streams)
    while streams:
        for stream in list(streams):
            try:
                next(stream)
            except StopIteration:
                streams.remove(stream)


def gather_stream(sems, at, src, out, rows, local):
    half = rows // 2
    right, left = at.hop(0, 1), at.hop(0, 3)
    me = at.me
    near_right = lax.rem(at.chip + 1, 4) * 2 + at.core
    near_left = lax.rem(at.chip + 3, 4) * 2 + at.core
    far = lax.rem(at.chip + 2, 4) * 2 + at.core

    def part(owner, h):
        return out.at[pl.ds(pl.multiple_of(owner * rows + h * half, half), half)]

    def own(h):
        return src.at[pl.ds(h * half, half)]

    ra = sems.start(own(0), part(me, 0), right)
    lb = sems.start(own(1), part(me, 1), left)
    rb = sems.start(own(1), part(me, 1), right)
    la = sems.start(own(0), part(me, 0), left)
    sib = [sems.start(src, out.at[pl.ds(pl.multiple_of(me * rows, rows), rows)], at.sibling)]
    mine = pltpu.make_async_copy(src, out.at[pl.ds(pl.multiple_of(me * rows, rows), rows)], local)
    mine.start()
    yield
    ra.wait_recv()
    far_a = sems.start(part(near_left, 0), part(near_left, 0), right)
    sib.append(sems.start(part(near_left, 0), part(near_left, 0), at.sibling))
    lb.wait_recv()
    far_b = sems.start(part(near_right, 1), part(near_right, 1), left)
    sib.append(sems.start(part(near_right, 1), part(near_right, 1), at.sibling))
    yield
    rb.wait_recv()
    sib.append(sems.start(part(near_left, 1), part(near_left, 1), at.sibling))
    la.wait_recv()
    sib.append(sems.start(part(near_right, 0), part(near_right, 0), at.sibling))
    yield
    far_a.wait_recv()
    sib.append(sems.start(part(far, 0), part(far, 0), at.sibling))
    far_b.wait_recv()
    sib.append(sems.start(part(far, 1), part(far, 1), at.sibling))
    yield
    mine.wait()
    for copy in sib:
        copy.wait_recv()


def scatter_stream(sems, at, src, pair, hop, last, rows, done, ready=None):
    half = rows // 2
    right, left = at.hop(0, 1), at.hop(0, 3)
    order = (2, 1, 3, 0)
    sib = []

    def offer(dist):
        if ready is not None:
            ready(dist)
        owner = lax.rem(at.chip + dist, 4) * 2 + 1 - at.core
        sib.append(sems.start(src.at[pl.ds(pl.multiple_of(owner * rows, rows), rows)], pair.at[dist], at.sibling))

    def fold(i):
        sib[i].wait_recv()
        owner = lax.rem(at.chip + order[i], 4) * 2 + at.core
        mine = src[pl.ds(pl.multiple_of(owner * rows, rows), rows)]
        pair[order[i]] = (pair[order[i]].astype(f32) + mine.astype(f32)).astype(bf16)

    def add(ref, other):
        ref[...] = (ref[...].astype(f32) + other[...].astype(f32)).astype(bf16)

    first, second = pl.ds(0, half), pl.ds(half, half)
    offer(2)
    offer(1)
    if ready is None:
        offer(3)
        offer(0)
        yield
    fold(0)
    far_a = sems.start(pair.at[2, first], hop.at[0], right)
    far_b = sems.start(pair.at[2, second], hop.at[1], left)
    if ready is None:
        yield
    else:
        offer(3)
    fold(1)
    dir_b = sems.start(pair.at[1, second], last.at[0], right)
    if ready is not None:
        offer(0)
    fold(2)
    dir_a = sems.start(pair.at[3, first], last.at[1], left)
    yield
    far_a.wait_recv()
    add(pair.at[1, first], hop.at[0])
    acc_a = sems.start(pair.at[1, first], last.at[2], right)
    far_b.wait_recv()
    add(pair.at[3, second], hop.at[1])
    acc_b = sems.start(pair.at[3, second], last.at[3], left)
    yield
    sib[3].wait_recv()
    dir_b.wait_recv()
    dir_a.wait_recv()
    acc_a.wait_recv()
    acc_b.wait_recv()
    for h, ends in ((0, (1, 2)), (1, (0, 3))):
        mine = src[pl.ds(pl.multiple_of(at.me * rows + h * half, half), half)].astype(f32)
        total = mine + pair[0, pl.ds(h * half, half)].astype(f32)
        done(h, total + last[ends[0]].astype(f32) + last[ends[1]].astype(f32))


def scatter_scratch(rows, cols):
    return [
        pltpu.VMEM((4, rows, cols), bf16),
        pltpu.VMEM((2, rows // 2, cols), bf16),
        pltpu.VMEM((4, rows // 2, cols), bf16),
    ]


def ring_sum(sems, at, axis, block, hop, last):
    right, left = at.hop(axis, 1), at.hop(axis, 3)
    to = [lax.rem(at.along[axis] + d, 4) for d in range(4)]

    def add(ref, other):
        ref[...] = (ref[...].astype(f32) + other[...].astype(f32)).astype(bf16)

    far_a = sems.start(block(to[2], 0), hop.at[0], right)
    far_b = sems.start(block(to[2], 1), hop.at[1], left)
    dir_b = sems.start(block(to[1], 1), last.at[0], right)
    dir_a = sems.start(block(to[3], 0), last.at[1], left)
    yield
    far_a.wait_recv()
    add(block(to[1], 0), hop.at[0])
    acc_a = sems.start(block(to[1], 0), last.at[2], right)
    far_b.wait_recv()
    add(block(to[3], 1), hop.at[1])
    acc_b = sems.start(block(to[3], 1), last.at[3], left)
    yield
    dir_b.wait_recv()
    dir_a.wait_recv()
    add(block(to[0], 1), last.at[0])
    add(block(to[0], 0), last.at[1])
    yield
    acc_a.wait_recv()
    add(block(to[0], 0), last.at[2])
    acc_b.wait_recv()
    add(block(to[0], 1), last.at[3])


def ring_gather(sems, at, axis, block):
    right, left = at.hop(axis, 1), at.hop(axis, 3)
    to = [lax.rem(at.along[axis] + d, 4) for d in range(4)]
    ra = sems.start(block(to[0], 0), block(to[0], 0), right)
    lb = sems.start(block(to[0], 1), block(to[0], 1), left)
    rb = sems.start(block(to[0], 1), block(to[0], 1), right)
    la = sems.start(block(to[0], 0), block(to[0], 0), left)
    yield
    ra.wait_recv()
    fa = sems.start(block(to[3], 0), block(to[3], 0), right)
    lb.wait_recv()
    fb = sems.start(block(to[1], 1), block(to[1], 1), left)
    yield
    rb.wait_recv()
    la.wait_recv()
    yield
    fa.wait_recv()
    fb.wait_recv()


def seq_stream(sems, at, work, out, scratch, axes):
    half = work.shape[1] // 2
    hop1, last1, hop2, last2 = scratch

    def wide(ref):
        return lambda i, h: ref.at[pl.ds(i * 4 + 2 * h, 2)]

    def narrow(ref):
        return lambda i, h: ref.at[at.along[axes[0]] * 4 + i, pl.ds(h * half, half)]

    yield from ring_sum(sems, at, axes[0], wide(work), hop1, last1)
    yield from ring_sum(sems, at, axes[1], narrow(work), hop2, last2)
    own = at.along[axes[0]] * 4 + at.along[axes[1]]
    out[own] = work[own]
    yield from ring_gather(sems, at, axes[1], narrow(out))
    yield from ring_gather(sems, at, axes[0], wide(out))


def seq_scratch(rows, cols):
    return [
        pltpu.VMEM((2, 2, rows, cols), bf16),
        pltpu.VMEM((4, 2, rows, cols), bf16),
        pltpu.VMEM((2, rows // 2, cols), bf16),
        pltpu.VMEM((4, rows // 2, cols), bf16),
    ]


def seq_direct(sems, at, work, out, wide_in, narrow_in):
    y, z = at.y, at.z
    copies = [sems.start(work.at[pl.ds(lax.rem(y + d, 4) * 4, 4)], wide_in.at[d - 1], at.hop(1, d)) for d in (1, 2, 3)]
    yield
    for copy in copies:
        copy.wait_recv()
    mine = pl.ds(y * 4, 4)
    work[mine] = (
        work[mine].astype(f32) + wide_in[0].astype(f32) + (wide_in[1].astype(f32) + wide_in[2].astype(f32))
    ).astype(bf16)
    copies = [sems.start(work.at[y * 4 + lax.rem(z + d, 4)], narrow_in.at[d - 1], at.hop(2, d)) for d in (1, 2, 3)]
    yield
    for copy in copies:
        copy.wait_recv()
    own = y * 4 + z
    out[own] = (
        work[own].astype(f32) + narrow_in[0].astype(f32) + (narrow_in[1].astype(f32) + narrow_in[2].astype(f32))
    ).astype(bf16)
    copies = [sems.start(out.at[own], out.at[own], at.hop(2, d)) for d in (1, 2, 3)]
    yield
    for copy in copies:
        copy.wait_recv()
    copies = [sems.start(out.at[mine], out.at[mine], at.hop(1, d)) for d in (1, 2, 3)]
    yield
    for copy in copies:
        copy.wait_recv()


def small_stream(sems, at, slots, out):
    stages = [(at.core, 2, lambda d: at.sibling)] + [
        (at.along[axis], 4, functools.partial(at.hop, axis)) for axis in range(3)
    ]
    for stage, (place, count, name) in enumerate(stages):
        if stage:
            slots[stage, place] = out[...]
        copies = [sems.start(slots.at[stage, place], slots.at[stage, place], name(d)) for d in range(1, count)]
        yield
        for copy in copies:
            copy.wait_recv()
        total = slots[stage, 0]
        for i in range(1, count):
            total = total + slots[stage, i]
        out[...] = total


def swapped(tensor):
    lane = lax.broadcasted_iota(jnp.int32, tensor.shape, 1)
    return jnp.where(lane % 64 < 32, pltpu.roll(tensor, 96, 1), pltpu.roll(tensor, 32, 1))


PAD = 384
ROW_STEP = 256


def dot_nn(a, b):
    return lax.dot_general(a, b, (((1,), (0,)), ((), ())), preferred_element_type=f32)


def dot_nt(a, b):
    return lax.dot_general(a, b, (((1,), (1,)), ((), ())), preferred_element_type=f32)


def dot_tn(a, b):
    return lax.dot_general(a, b, (((0,), (0,)), ((), ())), preferred_element_type=f32)


def row_block(index):
    return pl.ds(pl.multiple_of(index * ROW_STEP, ROW_STEP), ROW_STEP)


def router_pieces(router):
    high = router.astype(bf16).astype(f32)
    middle_part = (router - high).astype(bf16).astype(f32)
    low = router - high - middle_part
    fill = jnp.zeros((128 - 3 * EXPERTS, router.shape[1]), f32)
    return jnp.concatenate([high, middle_part, low, fill], axis=0).astype(bf16)


def mlp_kernel(
    mid_h, grad_h, pair_s_h, pair_e_h, down_s_h, down_e_h, router, hot,
    terms_h, act_h, dpre_h, logit, router_out,
    mid, grad, pair_s, pair_e, down_s, down_e, act, dpre, pieces, stage, load, store, keep,
):
    rows, width = mid_h.shape
    shared = down_s.shape[0]
    expert = lax.axis_index("exp")
    sources = [(mid_h, mid), (grad_h, grad), (pair_s_h, pair_s), (down_s_h, down_s), (pair_e_h, pair_e), (down_e_h, down_e)]
    loads = [pltpu.make_async_copy(src, dst, load.at[i]) for i, (src, dst) in enumerate(sources)]
    for c in loads:
        c.start()
    pieces[...] = router_pieces(router[...])
    for c in loads[:4]:
        c.wait()
    lane = lax.broadcasted_iota(jnp.int32, (ROW_STEP, 128), 1)
    own_lane = lane == expert

    def gates(r):
        raw = dot_nt(mid[r], pieces[...])
        raw = raw + (pltpu.roll(raw, 128 - EXPERTS, 1) + pltpu.roll(raw, 128 - 2 * EXPERTS, 1))
        raw = jnp.where(lane < EXPERTS, raw, -1e30)
        raw = jnp.exp(raw - jnp.max(raw, axis=1, keepdims=True))
        probs = raw / jnp.sum(raw, axis=1, keepdims=True)
        own = jnp.sum(jnp.where(own_lane, probs * hot[r].astype(f32), 0.0), axis=1, keepdims=True)
        return own, probs

    def piece(r, gate, up, dact, act_at, gate_at, up_at, own):
        size = gate.shape[1]
        logistic = 1.0 / (1.0 + jnp.exp(-gate))
        passed = gate * logistic
        out = passed * up
        total = None
        if own is not None:
            total = jnp.sum(out * dact, axis=1, keepdims=True)
            out = out * own
            dact = dact * own
        act[r, act_at : act_at + size] = out.astype(bf16)
        slope = logistic + passed * (1.0 - logistic)
        dpre[r, gate_at : gate_at + size] = (dact * up * slope).astype(bf16)
        dpre[r, up_at : up_at + size] = (dact * passed).astype(bf16)
        return total

    @pl.loop(0, rows // ROW_STEP)
    def _(index):
        r = row_block(index)
        gate, up = dot_nt(mid[r], pair_s[:shared]), dot_nt(mid[r], pair_s[shared:])
        piece(r, gate, up, dot_nt(grad[r], down_s[...]), F, 2 * F, 2 * F + PAD, None)

    loads[4].wait()
    loads[5].wait()

    @pl.loop(0, rows // ROW_STEP)
    def _(index):
        r = row_block(index)
        own, probs = gates(r)
        total = 0.0
        for start, end in ((0, 512), (512, 1024), (1024, F)):
            gate, up = dot_nn(mid[r], pair_e[:, start:end]), dot_nn(mid[r], pair_e[:, F + start : F + end])
            total = total + piece(r, gate, up, dot_nt(grad[r], down_e[start:end]), start, start, F + start, own)
        logit[r] = ((own * total) * (jnp.where(own_lane, 1.0, 0.0) - probs)).astype(bf16)

    keeps = [pltpu.make_async_copy(act, act_h, keep.at[0]), pltpu.make_async_copy(dpre, dpre_h, keep.at[1])]
    for c in keeps:
        c.start()

    half = width // 2
    slots = half // 128
    jobs = []
    for start in range(0, 2 * F, 512):
        size = min(512, 2 * F - start)
        jobs.append((mid, dpre, start, size, start, True))
    for start in range(0, F, 512):
        size = min(512, F - start)
        jobs.append((grad, act, start, size, 2 * F + start, False))
    for index, (left, right, start) in enumerate(((mid, dpre, 2 * F), (mid, dpre, 2 * F + PAD), (grad, act, F))):
        jobs.append((left, right, start, shared, 3 * F + index * shared, False))

    def flush(part, at, size):
        return pltpu.make_async_copy(
            stage.at[part, :, pl.ds(0, size)], terms_h.at[pl.ds(part * slots, slots), pl.ds(at, size)], store.at[part]
        )

    before = None
    for left, right, start, size, at, by_column in jobs:
        for part in range(2):
            if before is not None:
                flush(part, *before).wait()
            wide = left[:, part * half : (part + 1) * half]
            if by_column:
                value = dot_tn(wide, right[:, start : start + size]).astype(bf16)
                for s in range(slots):
                    for c in range(size // 128):
                        stage[part, s, c * 128 : (c + 1) * 128] = value[s * 128 : (s + 1) * 128, c * 128 : (c + 1) * 128]
            else:
                value = dot_tn(right[:, start : start + size], wide).astype(bf16)
                for s in range(slots):
                    stage[part, s, :size] = value[:, s * 128 : (s + 1) * 128]
            flush(part, at, size).start()
        before = (at, size)
    router_out[...] = dot_tn(logit[...], mid[...])[:EXPERTS]
    for part in range(2):
        flush(part, *before).wait()
    for c in keeps:
        c.wait()


def mlp(mid_all, grad_all, pair_s, pair_e, down_s, down_e, router, hot):
    rows, width = mid_all.shape
    shared = down_s.shape[0]
    whole = pl.BlockSpec(memory_space=VM)
    held = pl.BlockSpec(memory_space=pl.ANY)
    act_shape, dpre_shape = (rows, F + PAD), (rows, 2 * (F + PAD))
    return pl.pallas_call(
        mlp_kernel,
        out_shape=[
            jax.ShapeDtypeStruct((width // 128, 3 * (F + shared), 128), bf16),
            jax.ShapeDtypeStruct(act_shape, bf16),
            jax.ShapeDtypeStruct(dpre_shape, bf16),
            jax.ShapeDtypeStruct((rows, 128), bf16),
            jax.ShapeDtypeStruct((EXPERTS, width), f32),
        ],
        in_specs=[held] * 6 + [whole] * 2,
        out_specs=[held, held, held, whole, whole],
        scratch_shapes=[
            pltpu.VMEM(mid_all.shape, bf16), pltpu.VMEM(grad_all.shape, bf16),
            pltpu.VMEM(pair_s.shape, bf16), pltpu.VMEM(pair_e.shape, bf16),
            pltpu.VMEM(down_s.shape, bf16), pltpu.VMEM(down_e.shape, bf16),
            pltpu.VMEM(act_shape, bf16), pltpu.VMEM(dpre_shape, bf16),
            pltpu.VMEM((128, width), bf16), pltpu.VMEM((2, width // 256, 512, 128), bf16),
            pltpu.SemaphoreType.DMA((6,)), pltpu.SemaphoreType.DMA((2,)), pltpu.SemaphoreType.DMA((2,)),
        ],
        compiler_params=pltpu.CompilerParams(vmem_limit_bytes=62 << 20),
        cost_estimate=pl.CostEstimate(flops=12 * rows * width * (F + shared), bytes_accessed=60 << 20, transcendentals=rows * F),
        name="mlp",
    )(mid_all, grad_all, pair_s, pair_e, down_s, down_e, router, hot)


def turn_kernel(
    dpre_h, act_h, pair_s_h, pair_e_h, down_s_h, down_e_h, logit, router, residual, gain, upstream,
    residual_grad, gain_term, grad_all, moe_part,
    dpre, act, pair_s, pair_e, down_s, down_e, part, pieces, own_grad, p0, p1, p2, load, send, recv, local,
):
    at = Place()
    sems = Sems(send, recv)
    rows = residual.shape[0]
    half = rows // 2
    shared = down_s.shape[0]
    sources = [
        (dpre_h, dpre), (pair_e_h.at[:, pl.ds(0, F)], pair_e.at[:, pl.ds(0, F)]),
        (pair_e_h.at[:, pl.ds(F, F)], pair_e.at[:, pl.ds(F, F)]), (pair_s_h, pair_s),
        (act_h, act), (down_e_h, down_e), (down_s_h, down_s),
    ]
    loads = [pltpu.make_async_copy(src, dst, load.at[i]) for i, (src, dst) in enumerate(sources)]
    for c in loads:
        c.start()
    greet([at.hop(0, 1), at.hop(0, 3), at.sibling])
    gain_term[...] = jnp.zeros_like(gain_term)
    pieces[...] = router_pieces(router[...])
    loads[0].wait()

    def ready(dist):
        r = row_block(lax.rem(at.chip + dist, 4))
        if dist == 2:
            loads[1].wait()
        total = dot_nt(dpre[r, :F], pair_e[:, :F])
        if dist == 2:
            loads[2].wait()
        total = total + dot_nt(dpre[r, F : 2 * F], pair_e[:, F:])
        if dist == 2:
            loads[3].wait()
        total = total + dot_nn(dpre[r, 2 * F : 2 * F + shared], pair_s[:shared])
        total = total + dot_nn(dpre[r, 2 * F + PAD : 2 * F + PAD + shared], pair_s[shared:])
        part[r] = (total + dot_nn(logit[r], pieces[...])).astype(bf16)

    def done(h, total):
        r = slice(h * half, (h + 1) * half)
        x = residual[r]
        inverse = lax.rsqrt(jnp.mean(x * x, axis=1, keepdims=True) + EPSILON)
        gain_term[...] += jnp.sum(total * x * inverse, axis=0, keepdims=True)
        s = total * gain[...]
        inner = jnp.mean(s * x, axis=1, keepdims=True)
        grad = upstream[r].astype(f32) + (inverse * s - x * (inverse * inverse * inverse) * inner)
        residual_grad[r] = grad
        own_grad[r] = grad.astype(bf16)

    def moe(index):
        r = pl.ds(index * ROW_STEP, ROW_STEP)
        moe_part[r] = (dot_nn(act[r, :F], down_e[...]) + dot_nn(act[r, F : F + shared], down_s[...])).astype(bf16)

    together(scatter_stream(sems, at, part, p0, p1, p2, rows, done, ready))
    for c in loads[4:]:
        c.wait()
    gathered = gather_stream(sems, at, own_grad, grad_all, rows, local)
    next(gathered)
    for index in range(4):
        moe(index)
        next(gathered, None)
    together(gathered)
    sems.finish()


def turn(dpre, act, pair_s, pair_e, down_s, down_e, logit, router, residual, gain, upstream):
    whole = pl.BlockSpec(memory_space=VM)
    held = pl.BlockSpec(memory_space=pl.ANY)
    rows, width = residual.shape
    return pl.pallas_call(
        turn_kernel,
        out_shape=[
            jax.ShapeDtypeStruct((rows, width), f32),
            jax.ShapeDtypeStruct((1, width), f32),
            jax.ShapeDtypeStruct((8 * rows, width), bf16),
            jax.ShapeDtypeStruct((8 * rows, width), bf16),
        ],
        in_specs=[held] * 6 + [whole] * 5,
        out_specs=[whole] * 4,
        scratch_shapes=[
            pltpu.VMEM(dpre.shape, bf16), pltpu.VMEM(act.shape, bf16),
            pltpu.VMEM(pair_s.shape, bf16), pltpu.VMEM(pair_e.shape, bf16),
            pltpu.VMEM(down_s.shape, bf16), pltpu.VMEM(down_e.shape, bf16),
            pltpu.VMEM((8 * rows, width), bf16),
            pltpu.VMEM((128, width), bf16),
            pltpu.VMEM((rows, width), bf16),
            *scatter_scratch(rows, width),
            pltpu.SemaphoreType.DMA((7,)),
            pltpu.SemaphoreType.DMA((23,)),
            pltpu.SemaphoreType.DMA((23,)),
            pltpu.SemaphoreType.DMA,
        ],
        compiler_params=pltpu.CompilerParams(collective_id=2, has_side_effects=True, vmem_limit_bytes=62 << 20),
        name="turn",
    )(dpre, act, pair_s, pair_e, down_s, down_e, logit, router, residual, gain, upstream)


SPAN = LAT + 2 * ROPE
ATT = 256
SCALE = (NOPE + ROPE) ** (-0.5)
LOG2E = 1.4426950408889634


def segments(segs, count):
    spot = lax.axis_index("seq")
    own = segs[:, pl.ds(pl.multiple_of(spot * count, count), count)].astype(f32)
    before = segs[:, pl.ds(pl.multiple_of(jnp.maximum(spot - 1, 0) * count, count), count)].astype(f32)
    before = jnp.where(lax.rem(spot, 2) == 1, before, -1.0)
    column = jnp.transpose(jnp.broadcast_to(own, (128, count)))[:, :1]
    return column, jnp.concatenate([before, own], axis=1)


def score_pieces(q, packed, keys_all, qseg, kseg, head, i):
    rows = slice(ATT * i, ATT * (i + 1))
    prev = packed.shape[0] - q.shape[0]
    lane = lax.broadcasted_iota(jnp.int32, (ATT, 2 * ROPE), 1)
    rope = jnp.where(lane // ROPE == head, q[rows, 2 * NOPE :], jnp.zeros((), bf16))
    query = jnp.concatenate([q[rows, head * NOPE : (head + 1) * NOPE], rope], axis=1)
    edge = prev + ATT * i
    pieces = []
    for start, end in ((0, edge), (edge, edge + ATT)):
        keys = jnp.concatenate(
            [packed[start:end, head * 2 * NOPE : head * 2 * NOPE + NOPE], keys_all[start:end, LAT:]], axis=1
        )
        scores = dot_nt(query, keys)
        allowed = qseg[rows] == kseg[:, start:end]
        if start:
            allowed = allowed & (
                lax.broadcasted_iota(jnp.int32, scores.shape, 1)
                <= lax.broadcasted_iota(jnp.int32, scores.shape, 0)
            )
        pieces.append((start, end, jnp.where(allowed, scores, -1e30), keys))
    return query, pieces


def attend_kernel(q, packed, keys_all, segs, heads, lse):
    qseg, kseg = segments(segs, q.shape[0])
    for head in range(2):
        for i in range(q.shape[0] // ATT):
            rows = pl.ds(ATT * i, ATT)
            _, pieces = score_pieces(q, packed, keys_all, qseg, kseg, head, i)
            top = jnp.maximum(*[jnp.max(scores, axis=1, keepdims=True) for _, _, scores, _ in pieces])
            total, out = 0.0, 0.0
            for start, end, scores, _ in pieces:
                weights = jnp.exp2((scores - top) * (SCALE * LOG2E))
                total = total + jnp.sum(weights, axis=1, keepdims=True)
                values = packed[start:end, head * 2 * NOPE + NOPE : (head + 1) * 2 * NOPE]
                out = out + dot_nn(weights.astype(bf16), values)
            heads[rows, head * VDIM : (head + 1) * VDIM] = (out / total).astype(bf16)
            lse[head, rows] = top * (SCALE * LOG2E) + jnp.log2(total)


def attend(q, packed, keys_all, segs):
    whole = pl.BlockSpec(memory_space=VM)
    rows = q.shape[0]
    return pl.pallas_call(
        attend_kernel,
        out_shape=[jax.ShapeDtypeStruct((rows, 2 * VDIM), bf16), jax.ShapeDtypeStruct((2, rows, 1), f32)],
        in_specs=[whole] * 4,
        out_specs=[whole] * 2,
        compiler_params=pltpu.CompilerParams(vmem_limit_bytes=56 << 20),
        name="attend",
    )(q, packed, keys_all, segs)


def attend_back_kernel(
    grad, wo, heads, q, packed, keys_all, segs, lse, kv_proj, moe_part, residual, cosine_h, sine_h,
    dq, key_grad, kvo, layer_out,
    head_grad, dkey, dvalue, drope, dpacked, nope, rope_sum, cosine, sine, p0, p1, p2, send, recv, local,
):
    at = Place()
    sems = Sems(send, recv)
    block = pl.ds(pl.multiple_of(lax.rem(at.y, 2) * q.shape[0], q.shape[0]), q.shape[0])
    loads = [
        pltpu.make_async_copy(cosine_h.at[block], cosine, local.at[0]),
        pltpu.make_async_copy(sine_h.at[block], sine, local.at[1]),
    ]
    for c in loads:
        c.start()
    greet([at.hop(0, 1), at.hop(0, 3), at.sibling])
    own_rows = residual.shape[0]

    def done(h, total):
        r = slice(h * (own_rows // 2), (h + 1) * (own_rows // 2))
        layer_out[r] = (residual[r] + total).astype(bf16)

    moe = scatter_stream(sems, at, moe_part, p0, p1, p2, own_rows, done)
    next(moe)
    qseg, kseg = segments(segs, q.shape[0])
    rows = q.shape[0]
    prev = packed.shape[0] - rows
    step = 256
    for i in range(rows // step):
        r = pl.ds(i * step, step)
        head_grad[r] = dot_nt(grad[r], wo[...]).astype(bf16)
    for head in range(2):
        dkey[...] = jnp.zeros_like(dkey)
        dvalue[...] = jnp.zeros_like(dvalue)
        for i in range(rows // ATT):
            r = pl.ds(ATT * i, ATT)
            query, pieces = score_pieces(q, packed, keys_all, qseg, kseg, head, i)
            upstream = head_grad[r, head * VDIM : (head + 1) * VDIM]
            probs, dprobs = [], []
            inner = 0.0
            for start, end, scores, _ in pieces:
                p = jnp.exp2(scores * (SCALE * LOG2E) - lse[head, r])
                d = dot_nt(upstream, packed[start:end, head * 2 * NOPE + NOPE : (head + 1) * 2 * NOPE])
                inner = inner + jnp.sum(p * d, axis=1, keepdims=True)
                probs.append(p)
                dprobs.append(d)
            dquery = 0.0
            for (start, end, _, keys), p, d in zip(pieces, probs, dprobs):
                ds = (p * (d - inner)).astype(bf16)
                dquery = dquery + dot_nn(ds, keys)
                dkey[start:end] += dot_tn(ds, query)
                dvalue[start:end] += dot_tn(p.astype(bf16), upstream)
            dquery = dquery * SCALE
            nope[head, r] = dquery[:, :NOPE]
            rope = dquery[:, NOPE:]
            lane = lax.broadcasted_iota(jnp.int32, rope.shape, 1)
            if head == 0:
                rope_sum[r] = rope
            else:
                rope = jnp.where(lane < ROPE, rope_sum[r], rope)
                if i == 0:
                    for c in loads:
                        c.wait()
                rope = rope * cosine[r] - swapped(rope) * sine[r]
                turned = pltpu.roll(nope[1, r], ROPE, 1)
                dq[r, :NOPE] = nope[0, r].astype(bf16)
                dq[r, NOPE : 2 * NOPE] = jnp.where(lane < ROPE, rope, turned).astype(bf16)
                dq[r, 2 * NOPE :] = jnp.where(lane < ROPE, turned, rope).astype(bf16)
            next(moe, None)
        dpacked[:, head * 2 * NOPE : head * 2 * NOPE + NOPE] = (dkey[:, :NOPE] * SCALE).astype(bf16)
        dpacked[:, head * 2 * NOPE + NOPE : (head + 1) * 2 * NOPE] = dvalue[...].astype(bf16)
        if head == 0:
            drope[...] = dkey[:, NOPE:]
        else:
            drope[...] += dkey[:, NOPE:]
    span = SPAN
    for i in range(packed.shape[0] // 512):
        r = pl.ds(512 * i, 512)
        at = span if i * 512 < prev else 0
        to = pl.ds(512 * i - (0 if i * 512 < prev else prev), 512)
        key_grad[to, at : at + LAT] = dot_nt(dpacked[r], kv_proj[...]).astype(bf16)
        rope = drope[r]
        key_grad[to, at + LAT : at + span] = ((rope + pltpu.roll(rope, ROPE, 1)) * SCALE).astype(bf16)
    spots, wide = kvo.shape[0], kvo.shape[2]
    kv = dot_tn(keys_all[:, :LAT], dpacked[...]).astype(bf16)
    kv_rows = kv.shape[0] // spots
    kvo[:, :kv_rows] = kv.reshape(spots, kv_rows, wide)
    out_rows = wo.shape[0] // spots
    for j in range(grad.shape[1] // wide):
        term = dot_tn(heads[...], grad[:, j * wide : (j + 1) * wide]).astype(bf16)
        kvo[:, kv_rows + j * out_rows : kv_rows + (j + 1) * out_rows] = term.reshape(spots, out_rows, wide)
    together(moe)
    sems.finish()


def attend_back(grad, wo, heads, q, packed, keys_all, segs, lse, kv_proj, moe_part, residual, cosine, sine):
    whole = pl.BlockSpec(memory_space=VM)
    held = pl.BlockSpec(memory_space=pl.ANY)
    rows, keys = q.shape[0], packed.shape[0]
    own_rows, width = residual.shape
    spots = lax.axis_size("seq")
    kvo_rows = (kv_proj.shape[0] * kv_proj.shape[1] + wo.shape[0] * wo.shape[1]) // spots // LAT
    return pl.pallas_call(
        attend_back_kernel,
        out_shape=[
            jax.ShapeDtypeStruct(q.shape, bf16),
            jax.ShapeDtypeStruct((rows, 2 * SPAN), bf16),
            jax.ShapeDtypeStruct((spots, kvo_rows, LAT), bf16),
            jax.ShapeDtypeStruct((own_rows, width), bf16),
        ],
        in_specs=[whole] * 11 + [held] * 2,
        out_specs=[whole] * 4,
        scratch_shapes=[
            pltpu.VMEM((rows, 2 * VDIM), bf16),
            pltpu.VMEM((keys, 2 * NOPE), f32),
            pltpu.VMEM((keys, VDIM), f32),
            pltpu.VMEM((keys, 2 * ROPE), f32),
            pltpu.VMEM(packed.shape, bf16),
            pltpu.VMEM((2, rows, NOPE), f32),
            pltpu.VMEM((rows, 2 * ROPE), f32),
            pltpu.VMEM((rows, 2 * ROPE), f32),
            pltpu.VMEM((rows, 2 * ROPE), f32),
            *scatter_scratch(own_rows, width),
            pltpu.SemaphoreType.DMA((10,)),
            pltpu.SemaphoreType.DMA((10,)),
            pltpu.SemaphoreType.DMA((2,)),
        ],
        compiler_params=pltpu.CompilerParams(collective_id=4, has_side_effects=True, vmem_limit_bytes=60 << 20),
        name="attend_back",
    )(grad, wo, heads, q, packed, keys_all, segs, lse, kv_proj, moe_part, residual, cosine, sine)


def tail_kernel(
    dq, key_grad, kvo, normed, wq, wl, raw, latent_gain, gain, upstream, rows_in, router_in, ffn_in, cosine_h, sine_h,
    query_out, kvo_out, latent_out, grad_out, small_out,
    work0, work1, key_sum, in_part, in_sum, in_own, lat_rows, lat_all, lat_work, lat_sum, prev_out, prev_in, small,
    r0, r1, r2, r3, s0, s1, s2, s3, k0, k1, k2, n0, n1, n2, lw, ln, cosine, sine, send, recv, local,
):
    at = Place()
    sems = Sems(send, recv)
    greet([at.sibling] + [at.hop(axis, d) for axis in range(3) for d in (1, 2, 3)])
    rows = raw.shape[0]
    half = rows // 2
    own = pl.ds(pl.multiple_of(at.me * rows, rows), rows)

    def keep_key(h, total):
        key_sum[h * half : (h + 1) * half] = total

    def keep_in(h, total):
        in_sum[h * half : (h + 1) * half] = total

    spot = pl.multiple_of(lax.rem(at.y, 2) * 8 * rows + at.me * rows, rows)
    loads = [
        pltpu.make_async_copy(cosine_h.at[pl.ds(spot, rows)], cosine, local.at[2]),
        pltpu.make_async_copy(sine_h.at[pl.ds(spot, rows)], sine, local.at[3]),
    ]
    for c in loads:
        c.start()
    keys = scatter_stream(sems, at, key_grad, k0, k1, k2, rows, keep_key)
    next(keys)
    work0[...] = dot_tn(normed[...], dq[...]).astype(bf16).reshape(work0.shape)
    work1[...] = kvo[...]
    first = seq_stream(sems, at, work0, query_out, (r0, r1, r2, r3), (1, 2))
    second = seq_stream(sems, at, work1, kvo_out, (s0, s1, s2, s3), (2, 1))
    next(first)
    next(second)
    next(keys)
    gain_part = jnp.zeros((1, normed.shape[1]), f32)
    step = 256
    for i in range(dq.shape[0] // step):
        r = pl.ds(i * step, step)
        part = dot_nt(dq[r], wq[...])
        gain_part = gain_part + jnp.sum(part * normed[r].astype(f32), axis=0, keepdims=True)
        in_part[r] = part.astype(bf16)
        if i == 1:
            next(keys)
    in_rows = scatter_stream(sems, at, in_part, n0, n1, n2, rows, keep_in)
    running = []

    def latents():
        yield from keys
        prev_out[...] = key_sum[:, SPAN:].astype(bf16)
        partner = at.across[1](at.y + 1 - 2 * lax.rem(at.y, 2))
        swap = sems.start(prev_out, prev_in, partner)
        yield
        swap.wait_recv()
        own_grad = key_sum[:, :SPAN] + jnp.where(lax.rem(at.y, 2) == 0, prev_in[...].astype(f32), 0.0)
        x = raw[...]
        inverse = lax.rsqrt(jnp.mean(x * x, axis=1, keepdims=True) + EPSILON)
        u = own_grad[:, :LAT]
        lat_gain_part = jnp.sum(u * x * inverse, axis=0, keepdims=True)
        s = u * latent_gain[...]
        inner = jnp.mean(s * x, axis=1, keepdims=True)
        lat_rows[:, :LAT] = (inverse * s - x * (inverse * inverse * inverse) * inner).astype(bf16)
        rope = own_grad[:, LAT:]
        for c in loads:
            c.wait()
        rope = rope * cosine[...] - swapped(rope) * sine[...]
        lane = lax.broadcasted_iota(jnp.int32, rope.shape, 1)
        lat_rows[:, LAT:] = jnp.where(lane < ROPE, rope, 0.0).astype(bf16)
        gathered = gather_stream(sems, at, lat_rows, lat_all, rows, local.at[0])
        next(gathered)
        in_own[...] = dot_nn(lat_rows[:, : LAT + ROPE], wl[...])
        attn_gain = gain_part + jnp.sum(in_own[...] * normed[own].astype(f32), axis=0, keepdims=True)
        small[0, at.core, :EXPERTS] = router_in[...]
        small[0, at.core, EXPERTS:] = jnp.zeros_like(router_in)
        small[0, at.core, EXPERTS : EXPERTS + 1] = attn_gain / gain[...]
        small[0, at.core, EXPERTS + 1 : EXPERTS + 2] = ffn_in[...]
        small[0, at.core, EXPERTS + 2 : EXPERTS + 3, :LAT] = lat_gain_part
        running.append(small_stream(sems, at, small, small_out))
        yield from gathered
        width = lat_work.shape[0] * lat_work.shape[1]
        mine = normed[:, pl.ds(pl.multiple_of(at.me * width, width), width)]
        lat_work[...] = dot_tn(mine, lat_all[...]).astype(bf16).reshape(lat_work.shape)
        yield from seq_direct(sems, at, lat_work, lat_sum, lw, ln)
        yield from gather_stream(sems, at, lat_sum, latent_out, lat_sum.shape[0], local.at[1])

    running += [latents(), in_rows, first, second]
    while running:
        for stream in list(running):
            try:
                next(stream)
            except StopIteration:
                running.remove(stream)
    u = in_sum[...] + in_own[...]
    x = rows_in[...].astype(f32)
    inverse = lax.rsqrt(jnp.mean(x * x, axis=1, keepdims=True) + EPSILON)
    s = u * gain[...]
    inner = jnp.mean(s * x, axis=1, keepdims=True)
    grad_out[...] = (upstream[...] + (inverse * s - x * (inverse * inverse * inverse) * inner)).astype(bf16)
    sems.finish()


def tail(dq, key_grad, kvo, normed, wq, wl, raw, latent_gain, gain, upstream, rows_in, router_in, ffn_in, cosine, sine):
    whole = pl.BlockSpec(memory_space=VM)
    rows, width = rows_in.shape
    spots = kvo.shape[0]
    query_shape = (spots, width // spots, dq.shape[1])
    slice_rows = width // lax.axis_size("exp") // spots
    lat_shape = (spots, slice_rows, SPAN)
    return pl.pallas_call(
        tail_kernel,
        out_shape=[
            jax.ShapeDtypeStruct(query_shape, bf16),
            jax.ShapeDtypeStruct(kvo.shape, bf16),
            jax.ShapeDtypeStruct((8 * spots, slice_rows, SPAN), bf16),
            jax.ShapeDtypeStruct((rows, width), bf16),
            jax.ShapeDtypeStruct((2 * EXPERTS, width), f32),
        ],
        in_specs=[whole] * 13 + [pl.BlockSpec(memory_space=pl.ANY)] * 2,
        out_specs=[whole] * 5,
        scratch_shapes=[
            pltpu.VMEM(query_shape, bf16),
            pltpu.VMEM(kvo.shape, bf16),
            pltpu.VMEM((rows, 2 * SPAN), f32),
            pltpu.VMEM((8 * rows, width), bf16),
            pltpu.VMEM((rows, width), f32),
            pltpu.VMEM((rows, width), f32),
            pltpu.VMEM((rows, SPAN), bf16),
            pltpu.VMEM((8 * rows, SPAN), bf16),
            pltpu.VMEM(lat_shape, bf16),
            pltpu.VMEM(lat_shape, bf16),
            pltpu.VMEM((rows, SPAN), bf16),
            pltpu.VMEM((rows, SPAN), bf16),
            pltpu.VMEM((4, 4, 2 * EXPERTS, width), f32),
            *seq_scratch(*query_shape[1:]),
            *seq_scratch(*kvo.shape[1:]),
            *scatter_scratch(rows, 2 * SPAN),
            *scatter_scratch(rows, width),
            pltpu.VMEM((3, 4, slice_rows, SPAN), bf16),
            pltpu.VMEM((3, slice_rows, SPAN), bf16),
            pltpu.VMEM((rows, 2 * ROPE), f32),
            pltpu.VMEM((rows, 2 * ROPE), f32),
            pltpu.SemaphoreType.DMA((120,)),
            pltpu.SemaphoreType.DMA((120,)),
            pltpu.SemaphoreType.DMA((4,)),
        ],
        compiler_params=pltpu.CompilerParams(collective_id=3, has_side_effects=True, vmem_limit_bytes=60 << 20),
        name="tail",
    )(dq, key_grad, kvo, normed, wq, wl, raw, latent_gain, gain, upstream, rows_in, router_in, ffn_in, cosine, sine)


def start_kernel(
    rows_in, gain, wl, latent_gain, wq, kv_proj, routes, cosine_h, sine_h,
    normed, q, packed, keys, hot_all, raw,
    own_normed, ext, ext_all, prev_out, cosine, sine, send, recv, local,
):
    at = Place()
    sems = Sems(send, recv)
    rows = rows_in.shape[0]
    block = 8 * rows
    half_seq = pl.ds(pl.multiple_of(lax.rem(at.y, 2) * block, block), block)
    loads = [
        pltpu.make_async_copy(cosine_h.at[half_seq], cosine, local.at[2]),
        pltpu.make_async_copy(sine_h.at[half_seq], sine, local.at[3]),
    ]
    for c in loads:
        c.start()
    x = rows_in[...].astype(f32)
    own_normed[...] = (x * lax.rsqrt(jnp.mean(x * x, axis=1, keepdims=True) + EPSILON) * gain[...]).astype(bf16)
    partner = at.across[1](at.y + 1 - 2 * lax.rem(at.y, 2))
    greet([at.hop(0, 1), at.hop(0, 3), at.sibling, partner])
    big = gather_stream(sems, at, own_normed, normed, rows, local.at[0])
    next(big)
    lat = dot_nt(own_normed[...], wl[...])
    raw[...] = lat[:, :LAT]
    x = lat[:, :LAT]
    x = x * lax.rsqrt(jnp.mean(x * x, axis=1, keepdims=True) + EPSILON) * latent_gain[...]
    rope = jnp.concatenate([lat[:, LAT:], lat[:, LAT:]], axis=1)
    for c in loads:
        c.wait()
    own = pl.ds(pl.multiple_of(at.me * rows, rows), rows)
    rope = rope * cosine[own] + swapped(rope) * sine[own]
    number = lax.broadcasted_iota(jnp.int32, (128, rows), 0)
    hot = jnp.zeros((128, rows), f32)
    for k in range(routes.shape[0]):
        hot = hot + jnp.where(number == routes[k : k + 1], 1.0, 0.0)
    hot = pltpu.roll(jnp.transpose(hot), ROPE, 1)
    lane = lax.broadcasted_iota(jnp.int32, rope.shape, 1)
    prev_out[:, :LAT] = x.astype(bf16)
    prev_out[:, LAT:] = jnp.where(lane < ROPE, rope, hot).astype(bf16)
    swap = sems.start(prev_out, ext.at[:, pl.ds(SPAN, SPAN)], partner)
    ext[:, :SPAN] = prev_out[...]
    next(big)
    swap.wait_recv()
    little = gather_stream(sems, at, ext, ext_all, rows, local.at[1])
    next(little)
    together(big, little)
    step = 256
    lane = lax.broadcasted_iota(jnp.int32, (step, 2 * ROPE), 1)
    for i in range(block // step):
        r = pl.ds(i * step, step)
        query = dot_nn(normed[r], wq[...])
        q[r, :NOPE] = query[:, :NOPE].astype(bf16)
        one, two = query[:, NOPE : 2 * NOPE], query[:, 2 * NOPE :]
        q[r, NOPE : 2 * NOPE] = jnp.where(lane < ROPE, pltpu.roll(one, ROPE, 1), pltpu.roll(two, ROPE, 1)).astype(bf16)
        rope = jnp.where(lane < ROPE, one, two)
        q[r, 2 * NOPE :] = (rope * cosine[r] + swapped(rope) * sine[r]).astype(bf16)
    for part in range(2):
        r = slice((1 - part) * block, (2 - part) * block)
        keys[r, :LAT] = ext_all[:, part * SPAN : part * SPAN + LAT]
        rope = ext_all[:, part * SPAN + LAT : (part + 1) * SPAN].astype(f32)
        turned = pltpu.roll(rope, ROPE, 1)
        if part == 0:
            hot_all[...] = turned.astype(bf16)
        wide_lane = lax.broadcasted_iota(jnp.int32, rope.shape, 1)
        keys[r, LAT:] = jnp.where(wide_lane < ROPE, rope, turned).astype(bf16)
        packed[r] = dot_nn(ext_all[:, part * SPAN : part * SPAN + LAT], kv_proj[...]).astype(bf16)
    sems.finish()


def start(rows_in, gain, wl, latent_gain, wq, kv_proj, routes, cosine, sine):
    whole = pl.BlockSpec(memory_space=VM)
    rows, width = rows_in.shape
    block = 8 * rows
    return pl.pallas_call(
        start_kernel,
        out_shape=[
            jax.ShapeDtypeStruct((block, width), bf16),
            jax.ShapeDtypeStruct((block, wq.shape[1]), bf16),
            jax.ShapeDtypeStruct((2 * block, kv_proj.shape[1]), bf16),
            jax.ShapeDtypeStruct((2 * block, SPAN), bf16),
            jax.ShapeDtypeStruct((block, 2 * ROPE), bf16),
            jax.ShapeDtypeStruct((rows, LAT), f32),
        ],
        in_specs=[whole] * 7 + [pl.BlockSpec(memory_space=pl.ANY)] * 2,
        out_specs=[whole] * 6,
        scratch_shapes=[
            pltpu.VMEM((rows, width), bf16),
            pltpu.VMEM((rows, 2 * SPAN), bf16),
            pltpu.VMEM((block, 2 * SPAN), bf16),
            pltpu.VMEM((rows, SPAN), bf16),
            pltpu.VMEM((block, 2 * ROPE), f32),
            pltpu.VMEM((block, 2 * ROPE), f32),
            pltpu.SemaphoreType.DMA((27,)),
            pltpu.SemaphoreType.DMA((27,)),
            pltpu.SemaphoreType.DMA((4,)),
        ],
        compiler_params=pltpu.CompilerParams(collective_id=0, has_side_effects=True, vmem_limit_bytes=56 << 20),
        name="start",
    )(rows_in, gain, wl, latent_gain, wq, kv_proj, routes, cosine, sine)


def middle_kernel(
    heads, wo, rows_in, gain, residual, mid_all, part, own_mid, p0, p1, p2, send, recv, local
):
    at = Place()
    sems = Sems(send, recv)
    rows = rows_in.shape[0]
    half = rows // 2
    step = 256
    for i in range(heads.shape[0] // step):
        r = pl.ds(i * step, step)
        part[r] = dot_nn(heads[r], wo[...]).astype(bf16)
    greet([at.hop(0, 1), at.hop(0, 3), at.sibling])

    def done(h, total):
        r = slice(h * half, (h + 1) * half)
        x = rows_in[r].astype(f32) + total
        residual[r] = x
        own_mid[r] = (x * lax.rsqrt(jnp.mean(x * x, axis=1, keepdims=True) + EPSILON) * gain[...]).astype(bf16)

    together(scatter_stream(sems, at, part, p0, p1, p2, rows, done))
    together(gather_stream(sems, at, own_mid, mid_all, rows, local))
    sems.finish()


def middle(heads, wo, rows_in, gain):
    whole = pl.BlockSpec(memory_space=VM)
    rows, width = rows_in.shape
    return pl.pallas_call(
        middle_kernel,
        out_shape=[jax.ShapeDtypeStruct((rows, width), f32), jax.ShapeDtypeStruct((8 * rows, width), bf16)],
        in_specs=[whole] * 4,
        out_specs=[whole] * 2,
        scratch_shapes=[
            pltpu.VMEM((8 * rows, width), bf16),
            pltpu.VMEM((rows, width), bf16),
            *scatter_scratch(rows, width),
            pltpu.SemaphoreType.DMA((23,)),
            pltpu.SemaphoreType.DMA((23,)),
            pltpu.SemaphoreType.DMA,
        ],
        compiler_params=pltpu.CompilerParams(collective_id=1, has_side_effects=True, vmem_limit_bytes=56 << 20),
        name="middle",
    )(heads, wo, rows_in, gain)


def finish_kernel(weights, query, kvo, latent, expert_gate, expert_down, shared_gate, shared_down, query_out, kv_out, out_out, latent_out):
    for c in range(expert_gate.shape[1] // 128):
        expert_gate[:, c * 128 : (c + 1) * 128] = weights[c * 128 : (c + 1) * 128].astype(f32)
    spot = expert_gate.shape[1]
    for ref in (expert_down, shared_gate, shared_down):
        ref[...] = weights[spot : spot + ref.shape[0]].astype(f32)
        spot += ref.shape[0]
    query_out[...] = query[...].reshape(query_out.shape).astype(f32)
    spots, _, wide = kvo.shape
    kv_rows = kv_out.shape[0] // spots
    kv_out[...] = kvo[:, :kv_rows].reshape(kv_out.shape).astype(f32)
    out_rows = out_out.shape[0] // spots
    for j in range(out_out.shape[1] // wide):
        piece = kvo[:, kv_rows + j * out_rows : kv_rows + (j + 1) * out_rows]
        out_out[:, j * wide : (j + 1) * wide] = piece.reshape(out_out.shape[0], wide).astype(f32)
    step = 512
    for i in range(latent_out.shape[1] // step):
        spot = step // latent.shape[1]
        rows = latent[i * spot : (i + 1) * spot].reshape(step, latent.shape[2]).astype(f32)
        latent_out[:, i * step : (i + 1) * step] = jnp.transpose(rows)[: latent_out.shape[0]]


def finish(weights, query, kvo, latent, shared, model_width, kv_shape, out_shape):
    whole = pl.BlockSpec(memory_space=VM)
    shapes = [
        (128, 2 * F), (F, 128), (2 * shared, 128), (shared, 128),
        (model_width, query.shape[2]), kv_shape, out_shape, (LAT + ROPE, model_width),
    ]
    return pl.pallas_call(
        finish_kernel,
        out_shape=[jax.ShapeDtypeStruct(shape, f32) for shape in shapes],
        in_specs=[whole] * 4,
        out_specs=[whole] * 8,
        compiler_params=pltpu.CompilerParams(vmem_limit_bytes=56 << 20),
        name="finish",
    )(weights, query, kvo, latent)


def tables(seq_rows):
    lane = np.arange(2 * ROPE)
    half = ROPE // 2
    frequency = np.exp((lane % half) * (-math.log(10000.0) / half))
    angles = np.arange(seq_rows)[:, None] * frequency[None, :]
    sign = np.where(lane % ROPE < half, -1.0, 1.0)
    return np.cos(angles).astype(np.float32), (np.sin(angles) * sign[None, :]).astype(np.float32)


def local(
    layer_input, attn_gain, query_proj, latent_proj, latent_gain, kv_proj, output_proj, ffn_gain, router_proj,
    shared_gate_up, shared_down, expert_gate_up, expert_down, segment_ids, expert_routes, out_grad,
):
    own_rows, model_width = layer_input.shape
    cosine, sine = tables(2 * own_rows * lax.axis_size("exp"))
    wl = latent_proj.T
    router = router_proj.T
    shared = shared_down.shape[0]
    pair_s = shared_gate_up.transpose(1, 2, 0).reshape(2 * shared, model_width)
    pair_e, down_e = expert_gate_up[0], expert_down[0]
    segs = segment_ids[None]
    attn_row, latent_row, ffn_row = attn_gain[None], latent_gain[None], ffn_gain[None]
    normed_all, q, packed, keys, hot, latent_raw = start(
        layer_input, attn_row, wl, latent_row, query_proj, kv_proj, expert_routes.T, cosine, sine
    )
    late_grad, q = lax.optimization_barrier((out_grad, q))
    grad_all = lax.all_gather(late_grad, "exp", axis=0, tiled=True)
    heads, lse = attend(q, packed, keys, segs)
    residual, mid_all = middle(heads, output_proj, layer_input, ffn_row)
    terms, act, dpre, logit, router_term = mlp(
        mid_all, grad_all, pair_s, pair_e, shared_down, down_e, router, hot
    )
    weight_sum = lax.psum_scatter(terms.reshape(-1, 128), "seq", scatter_dimension=0, tiled=True)
    residual_grad, ffn_term, attn_grad_all, moe_part = turn(
        dpre, act, pair_s, pair_e, shared_down, down_e, logit, router, residual, ffn_row, out_grad
    )
    dq, key_grad, kvo, layer_output = attend_back(
        attn_grad_all, output_proj, heads, q, packed, keys, segs, lse, kv_proj, moe_part, residual, cosine, sine
    )
    query_sum, kvo_sum, latent_sum, input_grad, small = tail(
        dq, key_grad, kvo, normed_all, query_proj, wl, latent_raw, latent_row, attn_row,
        residual_grad, layer_input, router_term, ffn_term, cosine, sine,
    )
    expert_gate, expert_down_sum, shared_gate, shared_down_sum, query_sum, kv_sum, output_sum, latent_sum = finish(
        weight_sum, query_sum, kvo_sum, latent_sum, shared, model_width, kv_proj.shape, output_proj.shape
    )
    return (
        layer_output,
        input_grad,
        small[EXPERTS],
        query_sum,
        latent_sum.T,
        small[EXPERTS + 2, :LAT],
        kv_sum,
        output_sum,
        small[EXPERTS + 1],
        small[:EXPERTS].T,
        shared_gate.reshape(2, shared, 128).transpose(2, 0, 1),
        shared_down_sum,
        expert_gate[None],
        expert_down_sum[None],
    )


def solution(mesh):
    in_specs = (
        P(("seq", "exp"), None),
        P(),
        P(None, "exp"),
        P(),
        P(),
        P(None, "exp"),
        P("exp", None),
        P(),
        P(),
        P(None, None, "exp"),
        P("exp", None),
        P("exp", None, None),
        P("exp", None, None),
        P(),
        P(("seq", "exp"), None),
        P(("seq", "exp"), None),
    )
    out_specs = (
        P(("seq", "exp"), None),
        P(("seq", "exp"), None),
        P(),
        P(None, "exp"),
        P(),
        P(),
        P(None, "exp"),
        P("exp", None),
        P(),
        P(),
        P("seq", None, "exp"),
        P("exp", "seq"),
        P("exp", "seq", None),
        P("exp", None, "seq"),
    )
    return jax.shard_map(local, mesh=mesh, in_specs=in_specs, out_specs=out_specs, check_vma=False)
```

```python
import functools
import math

import jax
import jax.numpy as jnp
import numpy as np
from jax import lax
from jax.experimental import pallas as pl
from jax.experimental.pallas import tpu as pltpu
from jax.sharding import PartitionSpec as P

NOPE = 128
ROPE = 64
VDIM = 128
LAT = 512
F = 1408
EXPERTS = 8
EPSILON = 1e-06

VM = pltpu.VMEM
f32 = jnp.float32
bf16 = jnp.bfloat16


class Sems:
    def __init__(self, send, recv):
        self.send, self.recv, self.used, self.sent = send, recv, 0, []

    def start(self, src, dst, peer):
        copy = pltpu.make_async_remote_copy(
            src_ref=src,
            dst_ref=dst,
            send_sem=self.send.at[self.used],
            recv_sem=self.recv.at[self.used],
            device_id=peer,
            device_id_type=pl.DeviceIdType.MESH,
        )
        copy.start()
        self.used += 1
        self.sent.append(copy)
        return copy

    def finish(self):
        for copy in self.sent:
            copy.wait_send()


class Place:
    def __init__(self):
        me, spot = lax.axis_index("exp"), lax.axis_index("seq")
        self.me = me
        self.chip, self.core = me // 2, me % 2
        self.z, self.y = spot // 4, spot % 4
        self.sibling = {"exp": self.chip * 2 + 1 - self.core}
        self.across = [lambda i: {"exp": i * 2 + self.core}, lambda i: {"seq": self.z * 4 + i}, lambda i: {"seq": i * 4 + self.y}]
        self.along = [self.chip, self.y, self.z]

    def hop(self, axis, distance):
        return self.across[axis](lax.rem(self.along[axis] + distance, 4))


def announce(peers):
    barrier = pltpu.get_barrier_semaphore()
    for peer in peers:
        pl.semaphore_signal(barrier, inc=1, device_id=peer, device_id_type=pl.DeviceIdType.MESH)
    return len(peers)


def meet(count):
    pl.semaphore_wait(pltpu.get_barrier_semaphore(), count)


def greet(peers):
    meet(announce(peers))


def together(*streams):
    streams = list(streams)
    while streams:
        for stream in list(streams):
            try:
                next(stream)
            except StopIteration:
                streams.remove(stream)


def gather_stream(sems, at, src, out, rows, local, arrived=None):
    half = rows // 2
    right, left = at.hop(0, 1), at.hop(0, 3)
    me = at.me
    near_right = lax.rem(at.chip + 1, 4) * 2 + at.core
    near_left = lax.rem(at.chip + 3, 4) * 2 + at.core
    far = lax.rem(at.chip + 2, 4) * 2 + at.core

    def part(owner, h):
        return out.at[pl.ds(pl.multiple_of(owner * rows + h * half, half), half)]

    def own(h):
        return src.at[pl.ds(h * half, half)]

    ra = sems.start(own(0), part(me, 0), right)
    lb = sems.start(own(1), part(me, 1), left)
    rb = sems.start(own(1), part(me, 1), right)
    la = sems.start(own(0), part(me, 0), left)
    sib = [sems.start(src, out.at[pl.ds(pl.multiple_of(me * rows, rows), rows)], at.sibling)]
    mine = pltpu.make_async_copy(src, out.at[pl.ds(pl.multiple_of(me * rows, rows), rows)], local)
    mine.start()
    if arrived is None:
        yield
    else:
        mine.wait()
        sib[0].wait_recv()
        arrived(0)
    ra.wait_recv()
    far_a = sems.start(part(near_left, 0), part(near_left, 0), right)
    sib.append(sems.start(part(near_left, 0), part(near_left, 0), at.sibling))
    lb.wait_recv()
    far_b = sems.start(part(near_right, 1), part(near_right, 1), left)
    sib.append(sems.start(part(near_right, 1), part(near_right, 1), at.sibling))
    if arrived is None:
        yield
    rb.wait_recv()
    sib.append(sems.start(part(near_left, 1), part(near_left, 1), at.sibling))
    la.wait_recv()
    sib.append(sems.start(part(near_right, 0), part(near_right, 0), at.sibling))
    yield
    if arrived is not None:
        sib[1].wait_recv()
        sib[3].wait_recv()
        arrived(3)
    far_a.wait_recv()
    sib.append(sems.start(part(far, 0), part(far, 0), at.sibling))
    far_b.wait_recv()
    sib.append(sems.start(part(far, 1), part(far, 1), at.sibling))
    yield
    if arrived is None:
        mine.wait()
        for copy in sib:
            copy.wait_recv()
    else:
        sib[2].wait_recv()
        sib[4].wait_recv()
        arrived(1)
        yield
        sib[5].wait_recv()
        sib[6].wait_recv()
        arrived(2)


def scatter_stream(sems, at, src, pair, hop, last, rows, done, ready=None):
    half = rows // 2
    right, left = at.hop(0, 1), at.hop(0, 3)
    order = (2, 1, 3, 0)
    sib = []

    def offer(dist):
        if ready is not None:
            ready(dist)
        owner = lax.rem(at.chip + dist, 4) * 2 + 1 - at.core
        sib.append(sems.start(src.at[pl.ds(pl.multiple_of(owner * rows, rows), rows)], pair.at[dist], at.sibling))

    def fold(i):
        sib[i].wait_recv()
        owner = lax.rem(at.chip + order[i], 4) * 2 + at.core
        mine = src[pl.ds(pl.multiple_of(owner * rows, rows), rows)]
        pair[order[i]] = (pair[order[i]].astype(f32) + mine.astype(f32)).astype(bf16)

    def add(ref, other):
        ref[...] = (ref[...].astype(f32) + other[...].astype(f32)).astype(bf16)

    first, second = pl.ds(0, half), pl.ds(half, half)
    offer(2)
    offer(1)
    if ready is None:
        offer(3)
        offer(0)
        yield
    fold(0)
    far_a = sems.start(pair.at[2, first], hop.at[0], right)
    far_b = sems.start(pair.at[2, second], hop.at[1], left)
    if ready is None:
        yield
    else:
        offer(3)
    fold(1)
    dir_b = sems.start(pair.at[1, second], last.at[0], right)
    fold(2)
    dir_a = sems.start(pair.at[3, first], last.at[1], left)
    yield
    far_a.wait_recv()
    add(pair.at[1, first], hop.at[0])
    acc_a = sems.start(pair.at[1, first], last.at[2], right)
    far_b.wait_recv()
    add(pair.at[3, second], hop.at[1])
    acc_b = sems.start(pair.at[3, second], last.at[3], left)
    if ready is not None:
        offer(0)
    yield
    sib[3].wait_recv()
    dir_b.wait_recv()
    dir_a.wait_recv()
    acc_a.wait_recv()
    acc_b.wait_recv()
    for h, ends in ((0, (1, 2)), (1, (0, 3))):
        mine = src[pl.ds(pl.multiple_of(at.me * rows + h * half, half), half)].astype(f32)
        total = mine + pair[0, pl.ds(h * half, half)].astype(f32)
        done(h, total + last[ends[0]].astype(f32) + last[ends[1]].astype(f32))


def scatter_scratch(rows, cols):
    return [
        pltpu.VMEM((4, rows, cols), bf16),
        pltpu.VMEM((2, rows // 2, cols), bf16),
        pltpu.VMEM((4, rows // 2, cols), bf16),
    ]


def ring_sum(sems, at, axis, block, hop, last):
    right, left = at.hop(axis, 1), at.hop(axis, 3)
    to = [lax.rem(at.along[axis] + d, 4) for d in range(4)]

    def add(ref, other):
        ref[...] = (ref[...].astype(f32) + other[...].astype(f32)).astype(bf16)

    far_a = sems.start(block(to[2], 0), hop.at[0], right)
    far_b = sems.start(block(to[2], 1), hop.at[1], left)
    dir_b = sems.start(block(to[1], 1), last.at[0], right)
    dir_a = sems.start(block(to[3], 0), last.at[1], left)
    yield
    far_a.wait_recv()
    add(block(to[1], 0), hop.at[0])
    acc_a = sems.start(block(to[1], 0), last.at[2], right)
    far_b.wait_recv()
    add(block(to[3], 1), hop.at[1])
    acc_b = sems.start(block(to[3], 1), last.at[3], left)
    yield
    dir_b.wait_recv()
    dir_a.wait_recv()
    acc_a.wait_recv()
    acc_b.wait_recv()
    for part, (one, two) in ((0, (1, 2)), (1, (0, 3))):
        ref = block(to[0], part)
        ref[...] = (ref[...].astype(f32) + last[one].astype(f32) + last[two].astype(f32)).astype(bf16)


def ring_gather(sems, at, axis, block):
    right, left = at.hop(axis, 1), at.hop(axis, 3)
    to = [lax.rem(at.along[axis] + d, 4) for d in range(4)]
    ra = sems.start(block(to[0], 0), block(to[0], 0), right)
    lb = sems.start(block(to[0], 1), block(to[0], 1), left)
    rb = sems.start(block(to[0], 1), block(to[0], 1), right)
    la = sems.start(block(to[0], 0), block(to[0], 0), left)
    yield
    ra.wait_recv()
    fa = sems.start(block(to[3], 0), block(to[3], 0), right)
    lb.wait_recv()
    fb = sems.start(block(to[1], 1), block(to[1], 1), left)
    yield
    for copy in (rb, la, fa, fb):
        copy.wait_recv()


def seq_stream(sems, at, work, out, scratch, axes):
    hop, last, narrow_in = scratch
    one, two = at.along[axes[0]], at.along[axes[1]]
    own = one * 4 + two

    def wide(ref):
        return lambda i, h: ref.at[pl.ds(i * 4 + 2 * h, 2)]

    yield from ring_sum(sems, at, axes[0], wide(work), hop, last)
    copies = [sems.start(work.at[one * 4 + lax.rem(two + d, 4)], narrow_in.at[d - 1], at.hop(axes[1], d)) for d in (1, 2, 3)]
    yield
    for copy in copies:
        copy.wait_recv()
    total = work[own].astype(f32) + narrow_in[0].astype(f32)
    out[own] = (total + (narrow_in[1].astype(f32) + narrow_in[2].astype(f32))).astype(bf16)
    copies = [sems.start(out.at[own], out.at[own], at.hop(axes[1], d)) for d in (1, 2, 3)]
    yield
    for copy in copies:
        copy.wait_recv()
    yield from ring_gather(sems, at, axes[0], wide(out))


def seq_scratch(rows, cols):
    return [
        pltpu.VMEM((2, 2, rows, cols), bf16),
        pltpu.VMEM((4, 2, rows, cols), bf16),
        pltpu.VMEM((3, rows, cols), bf16),
    ]


def seq_direct(sems, at, work, out, wide_in, narrow_in):
    y, z = at.y, at.z
    copies = [sems.start(work.at[pl.ds(lax.rem(y + d, 4) * 4, 4)], wide_in.at[d - 1], at.hop(1, d)) for d in (1, 2, 3)]
    yield
    for copy in copies:
        copy.wait_recv()
    mine = pl.ds(y * 4, 4)
    work[mine] = (
        work[mine].astype(f32) + wide_in[0].astype(f32) + (wide_in[1].astype(f32) + wide_in[2].astype(f32))
    ).astype(bf16)
    copies = [sems.start(work.at[y * 4 + lax.rem(z + d, 4)], narrow_in.at[d - 1], at.hop(2, d)) for d in (1, 2, 3)]
    yield
    for copy in copies:
        copy.wait_recv()
    own = y * 4 + z
    out[own] = (
        work[own].astype(f32) + narrow_in[0].astype(f32) + (narrow_in[1].astype(f32) + narrow_in[2].astype(f32))
    ).astype(bf16)
    copies = [sems.start(out.at[own], out.at[own], at.hop(2, d)) for d in (1, 2, 3)]
    yield
    for copy in copies:
        copy.wait_recv()
    copies = [sems.start(out.at[mine], out.at[mine], at.hop(1, d)) for d in (1, 2, 3)]
    yield
    for copy in copies:
        copy.wait_recv()


def small_stream(sems, at, slots, out):
    stages = [(at.core, 2, lambda d: at.sibling)] + [
        (at.along[axis], 4, functools.partial(at.hop, axis)) for axis in range(3)
    ]
    for stage, (place, count, name) in enumerate(stages):
        if stage:
            slots[stage, place] = out[...]
        copies = [sems.start(slots.at[stage, place], slots.at[stage, place], name(d)) for d in range(1, count)]
        yield
        for copy in copies:
            copy.wait_recv()
        total = slots[stage, 0]
        for i in range(1, count):
            total = total + slots[stage, i]
        out[...] = total


def swapped(tensor):
    lane = lax.broadcasted_iota(jnp.int32, tensor.shape, 1)
    return jnp.where(lane % 64 < 32, pltpu.roll(tensor, 96, 1), pltpu.roll(tensor, 32, 1))


PAD = 384
ROW_STEP = 256


def dot_nn(a, b):
    return lax.dot_general(a, b, (((1,), (0,)), ((), ())), preferred_element_type=f32)


def dot_nt(a, b):
    return lax.dot_general(a, b, (((1,), (1,)), ((), ())), preferred_element_type=f32)


def dot_tn(a, b):
    return lax.dot_general(a, b, (((0,), (0,)), ((), ())), preferred_element_type=f32)


def row_block(index):
    return pl.ds(pl.multiple_of(index * ROW_STEP, ROW_STEP), ROW_STEP)


def router_pieces(router):
    high = router.astype(bf16).astype(f32)
    middle_part = (router - high).astype(bf16).astype(f32)
    low = router - high - middle_part
    fill = jnp.zeros((128 - 3 * EXPERTS, router.shape[1]), f32)
    return jnp.concatenate([high, middle_part, low, fill], axis=0).astype(bf16)


def mlp_kernel(
    own_mid, own_grad, pair_s_h, pair_e_h, down_s_h, down_e_h, router, hot,
    terms_h, act_h, dpre_h, logit, router_out,
    mid, grad, pair_s, pair_e, down_s, down_e, act, dpre, pieces, stage, load, store, keep, send, recv, local,
):
    at = Place()
    sems = Sems(send, recv)
    rows, width = mid.shape
    shared = down_s.shape[0]
    expert = lax.axis_index("exp")
    sources = [(pair_e_h, pair_e), (pair_s_h, pair_s), (down_s_h, down_s), (down_e_h, down_e)]
    loads = [pltpu.make_async_copy(src, dst, load.at[i]) for i, (src, dst) in enumerate(sources)]
    for c in loads:
        c.start()
    count = announce([at.hop(0, 1), at.hop(0, 3), at.sibling])
    pieces[...] = router_pieces(router[...])
    meet(count)
    lane = lax.broadcasted_iota(jnp.int32, (ROW_STEP, 128), 1)
    own_lane = lane == expert

    def gates(r):
        raw = dot_nt(mid[r], pieces[...])
        raw = raw + (pltpu.roll(raw, 128 - EXPERTS, 1) + pltpu.roll(raw, 128 - 2 * EXPERTS, 1))
        raw = jnp.where(lane < EXPERTS, raw, -1e30)
        raw = jnp.exp(raw - jnp.max(raw, axis=1, keepdims=True))
        probs = raw / jnp.sum(raw, axis=1, keepdims=True)
        own = jnp.sum(jnp.where(own_lane, probs * hot[r].astype(f32), 0.0), axis=1, keepdims=True)
        return own, probs

    tiles = [(pair_e, start, min(512, F - start)) for start in range(0, F, 512)]

    def before_activation(dist):
        r = row_block(lax.rem(at.chip + dist, 4))
        if dist == 0:
            loads[0].wait()
        for _, start, size in tiles:
            dpre[r, start : start + size] = dot_nn(mid[r], pair_e[:, start : start + size]).astype(bf16)
            up = dot_nn(mid[r], pair_e[:, F + start : F + start + size])
            dpre[r, F + start : F + start + size] = up.astype(bf16)
        if dist == 0:
            loads[1].wait()
        dpre[r, 2 * F : 2 * F + shared] = dot_nt(mid[r], pair_s[:shared]).astype(bf16)
        dpre[r, 2 * F + PAD : 2 * F + PAD + shared] = dot_nt(mid[r], pair_s[shared:]).astype(bf16)

    def piece(r, dact, act_at, gate_at, up_at, own):
        size = dact.shape[1]
        gate, up = dpre[r, gate_at : gate_at + size].astype(f32), dpre[r, up_at : up_at + size].astype(f32)
        logistic = 1.0 / (1.0 + jnp.exp(-gate))
        passed = gate * logistic
        out = passed * up
        total = None
        if own is not None:
            total = jnp.sum(out * dact, axis=1, keepdims=True)
            out = out * own
            dact = dact * own
        act[r, act_at : act_at + size] = out.astype(bf16)
        slope = logistic + passed * (1.0 - logistic)
        dpre[r, gate_at : gate_at + size] = (dact * up * slope).astype(bf16)
        dpre[r, up_at : up_at + size] = (dact * passed).astype(bf16)
        return total

    mids = gather_stream(sems, at, own_mid, mid, own_mid.shape[0], local.at[0], before_activation)
    grads = gather_stream(sems, at, own_grad, grad, own_grad.shape[0], local.at[1])
    next(mids)
    next(grads)
    next(mids)
    next(mids)
    next(grads)
    together(mids)
    together(grads)
    loads[2].wait()
    loads[3].wait()

    @pl.loop(0, rows // ROW_STEP)
    def _(index):
        r = row_block(index)
        piece(r, dot_nt(grad[r], down_s[...]), F, 2 * F, 2 * F + PAD, None)
        own, probs = gates(r)
        total = 0.0
        for _, start, size in tiles:
            total = total + piece(r, dot_nt(grad[r], down_e[start : start + size]), start, start, F + start, own)
        logit[r] = ((own * total) * (jnp.where(own_lane, 1.0, 0.0) - probs)).astype(bf16)

    keeps = [pltpu.make_async_copy(act, act_h, keep.at[0]), pltpu.make_async_copy(dpre, dpre_h, keep.at[1])]
    for c in keeps:
        c.start()

    half = width // 2
    slots = half // 128
    jobs = []
    for start in range(0, 2 * F, 512):
        size = min(512, 2 * F - start)
        jobs.append((mid, dpre, start, size, start, True))
    for start in range(0, F, 512):
        size = min(512, F - start)
        jobs.append((grad, act, start, size, 2 * F + start, False))
    for index, (left, right, start) in enumerate(((mid, dpre, 2 * F), (mid, dpre, 2 * F + PAD), (grad, act, F))):
        jobs.append((left, right, start, shared, 3 * F + index * shared, False))

    def flush(part, at, size):
        return pltpu.make_async_copy(
            stage.at[part, :, pl.ds(0, size)], terms_h.at[pl.ds(part * slots, slots), pl.ds(at, size)], store.at[part]
        )

    before = None
    for left, right, start, size, at, by_column in jobs:
        for part in range(2):
            if before is not None:
                flush(part, *before).wait()
            wide = left[:, part * half : (part + 1) * half]
            if by_column:
                value = dot_tn(wide, right[:, start : start + size]).astype(bf16)
                for s in range(slots):
                    for c in range(size // 128):
                        stage[part, s, c * 128 : (c + 1) * 128] = value[s * 128 : (s + 1) * 128, c * 128 : (c + 1) * 128]
            else:
                value = dot_tn(right[:, start : start + size], wide).astype(bf16)
                for s in range(slots):
                    stage[part, s, :size] = value[:, s * 128 : (s + 1) * 128]
            flush(part, at, size).start()
        before = (at, size)
    router_out[...] = dot_tn(logit[...], mid[...])[:EXPERTS]
    for part in range(2):
        flush(part, *before).wait()
    for c in keeps:
        c.wait()
    sems.finish()


def mlp(own_mid, own_grad, pair_s, pair_e, down_s, down_e, router, hot):
    rows, width = 8 * own_mid.shape[0], own_mid.shape[1]
    shared = down_s.shape[0]
    whole = pl.BlockSpec(memory_space=VM)
    held = pl.BlockSpec(memory_space=pl.ANY)
    act_shape, dpre_shape = (rows, F + PAD), (rows, 2 * (F + PAD))
    return pl.pallas_call(
        mlp_kernel,
        out_shape=[
            jax.ShapeDtypeStruct((width // 128, 3 * (F + shared), 128), bf16),
            jax.ShapeDtypeStruct(act_shape, bf16),
            jax.ShapeDtypeStruct(dpre_shape, bf16),
            jax.ShapeDtypeStruct((rows, 128), bf16),
            jax.ShapeDtypeStruct((EXPERTS, width), f32),
        ],
        in_specs=[whole] * 2 + [held] * 4 + [whole] * 2,
        out_specs=[held, held, held, whole, whole],
        scratch_shapes=[
            pltpu.VMEM((rows, width), bf16), pltpu.VMEM((rows, width), bf16),
            pltpu.VMEM(pair_s.shape, bf16), pltpu.VMEM(pair_e.shape, bf16),
            pltpu.VMEM(down_s.shape, bf16), pltpu.VMEM(down_e.shape, bf16),
            pltpu.VMEM(act_shape, bf16), pltpu.VMEM(dpre_shape, bf16),
            pltpu.VMEM((128, width), bf16), pltpu.VMEM((2, width // 256, 512, 128), bf16),
            pltpu.SemaphoreType.DMA((4,)), pltpu.SemaphoreType.DMA((2,)), pltpu.SemaphoreType.DMA((2,)),
            pltpu.SemaphoreType.DMA((26,)), pltpu.SemaphoreType.DMA((26,)), pltpu.SemaphoreType.DMA((2,)),
        ],
        compiler_params=pltpu.CompilerParams(collective_id=5, has_side_effects=True, vmem_limit_bytes=62 << 20),
        cost_estimate=pl.CostEstimate(flops=12 * rows * width * (F + shared), bytes_accessed=60 << 20, transcendentals=rows * F),
        name="mlp",
    )(own_mid, own_grad, pair_s, pair_e, down_s, down_e, router, hot)


def turn_kernel(
    dpre_h, act_h, pair_s_h, pair_e_h, down_s_h, down_e_h, logit, router, residual, gain, upstream,
    residual_grad, gain_term, grad_all, moe_part,
    dpre, act, pair_s, pair_e, down_s, down_e, part, pieces, own_grad, p0, p1, p2, load, send, recv, local,
):
    at = Place()
    sems = Sems(send, recv)
    rows = residual.shape[0]
    half = rows // 2
    shared = down_s.shape[0]
    sources = [
        (dpre_h, dpre), (pair_e_h.at[:, pl.ds(0, F)], pair_e.at[:, pl.ds(0, F)]),
        (pair_e_h.at[:, pl.ds(F, F)], pair_e.at[:, pl.ds(F, F)]), (pair_s_h, pair_s),
        (act_h, act), (down_e_h, down_e), (down_s_h, down_s),
    ]
    loads = [pltpu.make_async_copy(src, dst, load.at[i]) for i, (src, dst) in enumerate(sources)]
    for c in loads:
        c.start()
    count = announce([at.hop(0, 1), at.hop(0, 3), at.sibling])
    gain_term[...] = jnp.zeros_like(gain_term)
    pieces[...] = router_pieces(router[...])
    loads[0].wait()

    def ready(dist):
        r = row_block(lax.rem(at.chip + dist, 4))
        if dist == 2:
            loads[1].wait()
        total = dot_nt(dpre[r, :F], pair_e[:, :F])
        if dist == 2:
            loads[2].wait()
        total = total + dot_nt(dpre[r, F : 2 * F], pair_e[:, F:])
        if dist == 2:
            loads[3].wait()
        total = total + dot_nn(dpre[r, 2 * F : 2 * F + shared], pair_s[:shared])
        total = total + dot_nn(dpre[r, 2 * F + PAD : 2 * F + PAD + shared], pair_s[shared:])
        part[r] = (total + dot_nn(logit[r], pieces[...])).astype(bf16)
        if dist == 2:
            meet(count)

    def done(h, total):
        r = slice(h * half, (h + 1) * half)
        x = residual[r]
        inverse = lax.rsqrt(jnp.mean(x * x, axis=1, keepdims=True) + EPSILON)
        gain_term[...] += jnp.sum(total * x * inverse, axis=0, keepdims=True)
        s = total * gain[...]
        inner = jnp.mean(s * x, axis=1, keepdims=True)
        grad = upstream[r].astype(f32) + (inverse * s - x * (inverse * inverse * inverse) * inner)
        residual_grad[r] = grad
        own_grad[r] = grad.astype(bf16)

    def moe(index):
        r = pl.ds(index * ROW_STEP, ROW_STEP)
        moe_part[r] = (dot_nn(act[r, :F], down_e[...]) + dot_nn(act[r, F : F + shared], down_s[...])).astype(bf16)

    together(scatter_stream(sems, at, part, p0, p1, p2, rows, done, ready))
    for c in loads[4:]:
        c.wait()
    gathered = gather_stream(sems, at, own_grad, grad_all, rows, local)
    next(gathered)
    for index in range(4):
        moe(index)
        next(gathered, None)
    together(gathered)
    sems.finish()


def turn(dpre, act, pair_s, pair_e, down_s, down_e, logit, router, residual, gain, upstream):
    whole = pl.BlockSpec(memory_space=VM)
    held = pl.BlockSpec(memory_space=pl.ANY)
    rows, width = residual.shape
    return pl.pallas_call(
        turn_kernel,
        out_shape=[
            jax.ShapeDtypeStruct((rows, width), f32),
            jax.ShapeDtypeStruct((1, width), f32),
            jax.ShapeDtypeStruct((8 * rows, width), bf16),
            jax.ShapeDtypeStruct((8 * rows, width), bf16),
        ],
        in_specs=[held] * 6 + [whole] * 5,
        out_specs=[whole] * 4,
        scratch_shapes=[
            pltpu.VMEM(dpre.shape, bf16), pltpu.VMEM(act.shape, bf16),
            pltpu.VMEM(pair_s.shape, bf16), pltpu.VMEM(pair_e.shape, bf16),
            pltpu.VMEM(down_s.shape, bf16), pltpu.VMEM(down_e.shape, bf16),
            pltpu.VMEM((8 * rows, width), bf16),
            pltpu.VMEM((128, width), bf16),
            pltpu.VMEM((rows, width), bf16),
            *scatter_scratch(rows, width),
            pltpu.SemaphoreType.DMA((7,)),
            pltpu.SemaphoreType.DMA((23,)),
            pltpu.SemaphoreType.DMA((23,)),
            pltpu.SemaphoreType.DMA,
        ],
        compiler_params=pltpu.CompilerParams(collective_id=2, has_side_effects=True, vmem_limit_bytes=62 << 20),
        name="turn",
    )(dpre, act, pair_s, pair_e, down_s, down_e, logit, router, residual, gain, upstream)


SPAN = LAT + 2 * ROPE
ATT = 256
SCALE = (NOPE + ROPE) ** (-0.5)
LOG2E = 1.4426950408889634


def segments(segs, count):
    spot = lax.axis_index("seq")
    own = segs[:, pl.ds(pl.multiple_of(spot * count, count), count)].astype(f32)
    before = segs[:, pl.ds(pl.multiple_of(jnp.maximum(spot - 1, 0) * count, count), count)].astype(f32)
    before = jnp.where(lax.rem(spot, 2) == 1, before, -1.0)
    column = jnp.transpose(jnp.broadcast_to(own, (128, count)))[:, :1]
    return column, jnp.concatenate([before, own], axis=1)


def score_pieces(q, packed, keys_all, qseg, kseg, head, i):
    rows = slice(ATT * i, ATT * (i + 1))
    prev = packed.shape[0] - q.shape[0]
    lane = lax.broadcasted_iota(jnp.int32, (ATT, 2 * ROPE), 1)
    rope = jnp.where(lane // ROPE == head, q[rows, 2 * NOPE :], jnp.zeros((), bf16))
    query = jnp.concatenate([q[rows, head * NOPE : (head + 1) * NOPE], rope], axis=1)
    edge = prev + ATT * i
    pieces = []
    for start, end in ((0, edge), (edge, edge + ATT)):
        keys = jnp.concatenate(
            [packed[start:end, head * 2 * NOPE : head * 2 * NOPE + NOPE], keys_all[start:end, LAT:]], axis=1
        )
        scores = dot_nt(query, keys)
        allowed = qseg[rows] == kseg[:, start:end]
        if start:
            allowed = allowed & (
                lax.broadcasted_iota(jnp.int32, scores.shape, 1)
                <= lax.broadcasted_iota(jnp.int32, scores.shape, 0)
            )
        pieces.append((start, end, jnp.where(allowed, scores, -1e30), keys))
    return query, pieces


def attend_kernel(
    q, packed, keys_all, segs, wo, rows_in, gain, heads, lse, residual, own_mid, part, column, p0, p1, p2, send, recv
):
    at = Place()
    sems = Sems(send, recv)
    count = announce([at.hop(0, 1), at.hop(0, 3), at.sibling])
    prev = packed.shape[0] - q.shape[0]
    rows = rows_in.shape[0]
    half = rows // 2
    qseg, kseg = segments(segs, q.shape[0])
    column[...] = qseg
    lane = lax.broadcasted_iota(jnp.int32, (ATT, 2 * ROPE), 1)
    shape = (ATT, packed.shape[0])
    ahead = lax.broadcasted_iota(jnp.int32, shape, 1) - lax.broadcasted_iota(jnp.int32, shape, 0)

    def ready(dist):
        index = lax.rem(at.chip + dist, 4)
        r = row_block(index)
        allowed = (column[r] == kseg) & (ahead <= index * ATT + prev)
        for head in range(2):
            rope = jnp.where(lane // ROPE == head, q[r, 2 * NOPE :], jnp.zeros((), bf16))
            query = jnp.concatenate([q[r, head * NOPE : (head + 1) * NOPE], rope], axis=1)
            keys = jnp.concatenate([packed[:, head * 2 * NOPE : head * 2 * NOPE + NOPE], keys_all[:, LAT:]], axis=1)
            scores = jnp.where(allowed, dot_nt(query, keys), -1e30)
            top = jnp.max(scores, axis=1, keepdims=True)
            weights = jnp.exp2((scores - top) * (SCALE * LOG2E))
            total = jnp.sum(weights, axis=1, keepdims=True)
            out = dot_nn(weights.astype(bf16), packed[:, head * 2 * NOPE + NOPE : (head + 1) * 2 * NOPE])
            heads[r, head * VDIM : (head + 1) * VDIM] = (out / total).astype(bf16)
            lse[head, r] = top * (SCALE * LOG2E) + jnp.log2(total)
        part[r] = dot_nn(heads[r], wo[...]).astype(bf16)
        if dist == 2:
            meet(count)

    def done(h, total):
        r = slice(h * half, (h + 1) * half)
        x = rows_in[r].astype(f32) + total
        residual[r] = x
        own_mid[r] = (x * lax.rsqrt(jnp.mean(x * x, axis=1, keepdims=True) + EPSILON) * gain[...]).astype(bf16)

    together(scatter_stream(sems, at, part, p0, p1, p2, rows, done, ready))
    sems.finish()


def attend(q, packed, keys_all, segs, wo, rows_in, gain):
    whole = pl.BlockSpec(memory_space=VM)
    block = q.shape[0]
    rows, width = rows_in.shape
    return pl.pallas_call(
        attend_kernel,
        out_shape=[
            jax.ShapeDtypeStruct((block, 2 * VDIM), bf16),
            jax.ShapeDtypeStruct((2, block, 1), f32),
            jax.ShapeDtypeStruct((rows, width), f32),
            jax.ShapeDtypeStruct((rows, width), bf16),
        ],
        in_specs=[whole] * 7,
        out_specs=[whole] * 4,
        scratch_shapes=[
            pltpu.VMEM((block, width), bf16),
            pltpu.VMEM((block, 1), f32),
            *scatter_scratch(rows, width),
            pltpu.SemaphoreType.DMA((10,)),
            pltpu.SemaphoreType.DMA((10,)),
        ],
        compiler_params=pltpu.CompilerParams(collective_id=1, has_side_effects=True, vmem_limit_bytes=56 << 20),
        name="attend",
    )(q, packed, keys_all, segs, wo, rows_in, gain)


def attend_back_kernel(
    grad, wo, heads, q, packed, keys_all, segs, lse, kv_proj, moe_part, residual, cosine_h, sine_h,
    dq, key_own, key_prev, kvo, layer_out,
    head_grad, dkey, dvalue, drope, dpacked, nope, rope_sum, cosine, sine, p0, p1, p2, send, recv, local,
):
    at = Place()
    sems = Sems(send, recv)
    block = pl.ds(pl.multiple_of(lax.rem(at.y, 2) * q.shape[0], q.shape[0]), q.shape[0])
    loads = [
        pltpu.make_async_copy(cosine_h.at[block], cosine, local.at[0]),
        pltpu.make_async_copy(sine_h.at[block], sine, local.at[1]),
    ]
    for c in loads:
        c.start()
    count = announce([at.hop(0, 1), at.hop(0, 3), at.sibling])
    own_rows = residual.shape[0]

    def done(h, total):
        r = slice(h * (own_rows // 2), (h + 1) * (own_rows // 2))
        layer_out[r] = (residual[r] + total).astype(bf16)

    rows = q.shape[0]
    prev = packed.shape[0] - rows
    step = 256
    for i in range(rows // step):
        r = pl.ds(i * step, step)
        head_grad[r] = dot_nt(grad[r], wo[...]).astype(bf16)
    meet(count)
    moe = scatter_stream(sems, at, moe_part, p0, p1, p2, own_rows, done)
    next(moe)
    qseg, kseg = segments(segs, q.shape[0])
    for head in range(2):
        dkey[...] = jnp.zeros_like(dkey)
        dvalue[...] = jnp.zeros_like(dvalue)
        for i in range(rows // ATT):
            r = pl.ds(ATT * i, ATT)
            query, pieces = score_pieces(q, packed, keys_all, qseg, kseg, head, i)
            upstream = head_grad[r, head * VDIM : (head + 1) * VDIM]
            probs, dprobs = [], []
            inner = 0.0
            for start, end, scores, _ in pieces:
                p = jnp.exp2(scores * (SCALE * LOG2E) - lse[head, r])
                d = dot_nt(upstream, packed[start:end, head * 2 * NOPE + NOPE : (head + 1) * 2 * NOPE])
                inner = inner + jnp.sum(p * d, axis=1, keepdims=True)
                probs.append(p)
                dprobs.append(d)
            dquery = 0.0
            for (start, end, _, keys), p, d in zip(pieces, probs, dprobs):
                ds = (p * (d - inner)).astype(bf16)
                dquery = dquery + dot_nn(ds, keys)
                dkey[start:end] += dot_tn(ds, query)
                dvalue[start:end] += dot_tn(p.astype(bf16), upstream)
            dquery = dquery * SCALE
            nope[head, r] = dquery[:, :NOPE]
            rope = dquery[:, NOPE:]
            lane = lax.broadcasted_iota(jnp.int32, rope.shape, 1)
            if head == 0:
                rope_sum[r] = rope
            else:
                rope = jnp.where(lane < ROPE, rope_sum[r], rope)
                if i == 0:
                    for c in loads:
                        c.wait()
                rope = rope * cosine[r] - swapped(rope) * sine[r]
                turned = pltpu.roll(nope[1, r], ROPE, 1)
                dq[r, :NOPE] = nope[0, r].astype(bf16)
                dq[r, NOPE : 2 * NOPE] = jnp.where(lane < ROPE, rope, turned).astype(bf16)
                dq[r, 2 * NOPE :] = jnp.where(lane < ROPE, turned, rope).astype(bf16)
            if (head, i) in ((0, 1), (0, 3), (1, 1)):
                next(moe, None)
        dpacked[:, head * 2 * NOPE : head * 2 * NOPE + NOPE] = (dkey[:, :NOPE] * SCALE).astype(bf16)
        dpacked[:, head * 2 * NOPE + NOPE : (head + 1) * 2 * NOPE] = dvalue[...].astype(bf16)
        if head == 0:
            drope[...] = dkey[:, NOPE:]
        else:
            drope[...] += dkey[:, NOPE:]
    for i in range(packed.shape[0] // 512):
        r = pl.ds(512 * i, 512)
        key_grad, to = (key_prev, r) if i * 512 < prev else (key_own, pl.ds(512 * i - prev, 512))
        key_grad[to, :LAT] = dot_nt(dpacked[r], kv_proj[...]).astype(bf16)
        rope = drope[r]
        key_grad[to, LAT:] = ((rope + pltpu.roll(rope, ROPE, 1)) * SCALE).astype(bf16)
    spots, wide = kvo.shape[0], kvo.shape[2]
    kv = dot_tn(keys_all[:, :LAT], dpacked[...]).astype(bf16)
    kv_rows = kv.shape[0] // spots
    kvo[:, :kv_rows] = kv.reshape(spots, kv_rows, wide)
    out_rows = wo.shape[0] // spots
    for j in range(grad.shape[1] // wide):
        term = dot_tn(heads[...], grad[:, j * wide : (j + 1) * wide]).astype(bf16)
        kvo[:, kv_rows + j * out_rows : kv_rows + (j + 1) * out_rows] = term.reshape(spots, out_rows, wide)
    together(moe)
    sems.finish()


def attend_back(grad, wo, heads, q, packed, keys_all, segs, lse, kv_proj, moe_part, residual, cosine, sine):
    whole = pl.BlockSpec(memory_space=VM)
    held = pl.BlockSpec(memory_space=pl.ANY)
    rows, keys = q.shape[0], packed.shape[0]
    own_rows, width = residual.shape
    spots = lax.axis_size("seq")
    kvo_rows = (kv_proj.shape[0] * kv_proj.shape[1] + wo.shape[0] * wo.shape[1]) // spots // LAT
    return pl.pallas_call(
        attend_back_kernel,
        out_shape=[
            jax.ShapeDtypeStruct(q.shape, bf16),
            jax.ShapeDtypeStruct((rows, SPAN), bf16),
            jax.ShapeDtypeStruct((rows, SPAN), bf16),
            jax.ShapeDtypeStruct((spots, kvo_rows, LAT), bf16),
            jax.ShapeDtypeStruct((own_rows, width), bf16),
        ],
        in_specs=[whole] * 11 + [held] * 2,
        out_specs=[whole] * 5,
        scratch_shapes=[
            pltpu.VMEM((rows, 2 * VDIM), bf16),
            pltpu.VMEM((keys, 2 * NOPE), f32),
            pltpu.VMEM((keys, VDIM), f32),
            pltpu.VMEM((keys, 2 * ROPE), f32),
            pltpu.VMEM(packed.shape, bf16),
            pltpu.VMEM((2, rows, NOPE), f32),
            pltpu.VMEM((rows, 2 * ROPE), f32),
            pltpu.VMEM((rows, 2 * ROPE), f32),
            pltpu.VMEM((rows, 2 * ROPE), f32),
            *scatter_scratch(own_rows, width),
            pltpu.SemaphoreType.DMA((10,)),
            pltpu.SemaphoreType.DMA((10,)),
            pltpu.SemaphoreType.DMA((2,)),
        ],
        compiler_params=pltpu.CompilerParams(collective_id=4, has_side_effects=True, vmem_limit_bytes=60 << 20),
        name="attend_back",
    )(grad, wo, heads, q, packed, keys_all, segs, lse, kv_proj, moe_part, residual, cosine, sine)


SEQ_TURNS = (1, 2, 3, 4, 5, 6)


def tail_kernel(
    dq, key_own, key_prev, kvo, raw, latent_gain, gain, router_in, ffn_in,
    normed_h, wq_h, wl_h, upstream_h, rows_h, cosine_h, sine_h,
    query_out, kvo_out, latent_out, grad_out, small_out,
    work0, work1, own_sum, prev_out, in_part, in_sum, in_own, lat_rows, lat_all, lat_work, lat_sum, prev_in, small,
    r0, r1, r2, s0, s1, s2, k0, k1, k2, j0, j1, j2, n0, n1, n2, lw, ln,
    normed, wq, wl, upstream, rows_in, cosine, sine, send, recv, local,
):
    at = Place()
    sems = Sems(send, recv)
    rows = raw.shape[0]
    half = rows // 2
    own = pl.ds(pl.multiple_of(at.me * rows, rows), rows)
    spot = pl.ds(pl.multiple_of(lax.rem(at.y, 2) * 8 * rows + at.me * rows, rows), rows)
    sources = (
        (normed_h, normed), (wq_h, wq), (wl_h, wl), (cosine_h.at[spot], cosine), (sine_h.at[spot], sine),
        (upstream_h, upstream), (rows_h, rows_in),
    )
    loads = [pltpu.make_async_copy(src, dst, local.at[2 + i]) for i, (src, dst) in enumerate(sources)]
    for c in loads:
        c.start()
    greet([at.sibling] + [at.hop(axis, d) for axis in range(3) for d in (1, 2, 3)])

    def keep_own(h, total):
        own_sum[h * half : (h + 1) * half] = total

    def keep_prev(h, total):
        prev_out[h * half : (h + 1) * half] = total.astype(bf16)

    def keep_in(h, total):
        in_sum[h * half : (h + 1) * half] = total

    prevs = scatter_stream(sems, at, key_prev, j0, j1, j2, rows, keep_prev)
    owns = scatter_stream(sems, at, key_own, k0, k1, k2, rows, keep_own)
    next(prevs)
    next(owns)
    work1[...] = kvo[...]
    second = seq_stream(sems, at, work1, kvo_out, (s0, s1, s2), (2, 1))
    next(second)
    next(prevs)
    next(owns)
    next(prevs)
    next(owns)
    loads[0].wait()
    work0[...] = dot_tn(normed[...], dq[...]).astype(bf16).reshape(work0.shape)
    first = seq_stream(sems, at, work0, query_out, (r0, r1, r2), (1, 2))
    next(first)
    next(prevs)
    next(owns)
    loads[1].wait()
    gain_part = jnp.zeros((1, normed.shape[1]), f32)
    step = 256
    for i in range(dq.shape[0] // step):
        r = pl.ds(i * step, step)
        part = dot_nt(dq[r], wq[...])
        gain_part = gain_part + jnp.sum(part * normed[r].astype(f32), axis=0, keepdims=True)
        in_part[r] = part.astype(bf16)
    in_rows = scatter_stream(sems, at, in_part, n0, n1, n2, rows, keep_in)
    running = []

    def latents():
        together(prevs)
        partner = at.across[1](at.y + 1 - 2 * lax.rem(at.y, 2))
        swap = sems.start(prev_out, prev_in, partner)
        together(owns)
        swap.wait_recv()
        own_grad = own_sum[...] + jnp.where(lax.rem(at.y, 2) == 0, prev_in[...].astype(f32), 0.0)
        x = raw[...]
        inverse = lax.rsqrt(jnp.mean(x * x, axis=1, keepdims=True) + EPSILON)
        u = own_grad[:, :LAT]
        lat_gain_part = jnp.sum(u * x * inverse, axis=0, keepdims=True)
        s = u * latent_gain[...]
        inner = jnp.mean(s * x, axis=1, keepdims=True)
        lat_rows[:, :LAT] = (inverse * s - x * (inverse * inverse * inverse) * inner).astype(bf16)
        rope = own_grad[:, LAT:]
        loads[3].wait()
        loads[4].wait()
        rope = rope * cosine[...] - swapped(rope) * sine[...]
        lane = lax.broadcasted_iota(jnp.int32, rope.shape, 1)
        lat_rows[:, LAT:] = jnp.where(lane < ROPE, rope, 0.0).astype(bf16)
        gathered = gather_stream(sems, at, lat_rows, lat_all, rows, local.at[0])
        next(gathered)
        running.append(in_rows)
        loads[2].wait()
        in_own[...] = dot_nn(lat_rows[:, : LAT + ROPE], wl[...])
        attn_gain = gain_part + jnp.sum(in_own[...] * normed[own].astype(f32), axis=0, keepdims=True)
        small[0, at.core, :EXPERTS] = router_in[...]
        small[0, at.core, EXPERTS:] = jnp.zeros_like(router_in)
        small[0, at.core, EXPERTS : EXPERTS + 1] = attn_gain / gain[...]
        small[0, at.core, EXPERTS + 1 : EXPERTS + 2] = ffn_in[...]
        small[0, at.core, EXPERTS + 2 : EXPERTS + 3, :LAT] = lat_gain_part
        running.append(small_stream(sems, at, small, small_out))
        yield from gathered
        width = lat_work.shape[0] * lat_work.shape[1]
        mine = normed[:, pl.ds(pl.multiple_of(at.me * width, width), width)]
        lat_work[...] = dot_tn(mine, lat_all[...]).astype(bf16).reshape(lat_work.shape)
        yield from seq_direct(sems, at, lat_work, lat_sum, lw, ln)
        yield from gather_stream(sems, at, lat_sum, latent_out, lat_sum.shape[0], local.at[1])

    chain = latents()
    running.append(chain)
    count = 0
    while running:
        for stream in list(running):
            try:
                next(stream)
            except StopIteration:
                running.remove(stream)
        count += 1
        if count in SEQ_TURNS:
            next(first, None)
            next(second, None)
    together(first, second)
    loads[5].wait()
    loads[6].wait()
    u = in_sum[...] + in_own[...]
    x = rows_in[...].astype(f32)
    inverse = lax.rsqrt(jnp.mean(x * x, axis=1, keepdims=True) + EPSILON)
    s = u * gain[...]
    inner = jnp.mean(s * x, axis=1, keepdims=True)
    grad_out[...] = (upstream[...] + (inverse * s - x * (inverse * inverse * inverse) * inner)).astype(bf16)
    sems.finish()


def tail(dq, key_own, key_prev, kvo, normed, wq, wl, raw, latent_gain, gain, upstream, rows_in, router_in, ffn_in, cosine, sine):
    whole = pl.BlockSpec(memory_space=VM)
    rows, width = rows_in.shape
    spots = kvo.shape[0]
    query_shape = (spots, width // spots, dq.shape[1])
    slice_rows = width // lax.axis_size("exp") // spots
    lat_shape = (spots, slice_rows, SPAN)
    return pl.pallas_call(
        tail_kernel,
        out_shape=[
            jax.ShapeDtypeStruct(query_shape, bf16),
            jax.ShapeDtypeStruct(kvo.shape, bf16),
            jax.ShapeDtypeStruct((8 * spots, slice_rows, SPAN), bf16),
            jax.ShapeDtypeStruct((rows, width), bf16),
            jax.ShapeDtypeStruct((2 * EXPERTS, width), f32),
        ],
        in_specs=[whole] * 9 + [pl.BlockSpec(memory_space=pl.ANY)] * 7,
        out_specs=[whole] * 5,
        scratch_shapes=[
            pltpu.VMEM(query_shape, bf16),
            pltpu.VMEM(kvo.shape, bf16),
            pltpu.VMEM((rows, SPAN), f32),
            pltpu.VMEM((rows, SPAN), bf16),
            pltpu.VMEM((8 * rows, width), bf16),
            pltpu.VMEM((rows, width), f32),
            pltpu.VMEM((rows, width), f32),
            pltpu.VMEM((rows, SPAN), bf16),
            pltpu.VMEM((8 * rows, SPAN), bf16),
            pltpu.VMEM(lat_shape, bf16),
            pltpu.VMEM(lat_shape, bf16),
            pltpu.VMEM((rows, SPAN), bf16),
            pltpu.VMEM((4, 4, 2 * EXPERTS, width), f32),
            *seq_scratch(*query_shape[1:]),
            *seq_scratch(*kvo.shape[1:]),
            *scatter_scratch(rows, SPAN),
            *scatter_scratch(rows, SPAN),
            *scatter_scratch(rows, width),
            pltpu.VMEM((3, 4, slice_rows, SPAN), bf16),
            pltpu.VMEM((3, slice_rows, SPAN), bf16),
            pltpu.VMEM(normed.shape, bf16),
            pltpu.VMEM(wq.shape, bf16),
            pltpu.VMEM(wl.shape, bf16),
            pltpu.VMEM(upstream.shape, f32),
            pltpu.VMEM(rows_in.shape, bf16),
            pltpu.VMEM((rows, 2 * ROPE), f32),
            pltpu.VMEM((rows, 2 * ROPE), f32),
            pltpu.SemaphoreType.DMA((130,)),
            pltpu.SemaphoreType.DMA((130,)),
            pltpu.SemaphoreType.DMA((9,)),
        ],
        compiler_params=pltpu.CompilerParams(collective_id=3, has_side_effects=True, vmem_limit_bytes=60 << 20),
        name="tail",
    )(dq, key_own, key_prev, kvo, raw, latent_gain, gain, router_in, ffn_in, normed, wq, wl, upstream, rows_in, cosine, sine)


def start_kernel(
    rows_in, gain, latent_gain, routes, wl_h, wq_h, kv_proj_h, cosine_h, sine_h,
    normed_h, q_h, packed_h, keys_h, hot_all, raw,
    normed, q, packed, keys, wl, wq, kv_proj,
    own_normed, ext, ext_all, prev_out, cosine, sine, send, recv, local, load, store,
):
    at = Place()
    sems = Sems(send, recv)
    rows = rows_in.shape[0]
    block = 8 * rows
    half_seq = pl.ds(pl.multiple_of(lax.rem(at.y, 2) * block, block), block)
    sources = (
        (wl_h, wl), (cosine_h.at[half_seq], cosine), (sine_h.at[half_seq], sine), (wq_h, wq), (kv_proj_h, kv_proj),
    )
    loads = [pltpu.make_async_copy(src, dst, load.at[i]) for i, (src, dst) in enumerate(sources)]
    for c in loads:
        c.start()
    partner = at.across[1](at.y + 1 - 2 * lax.rem(at.y, 2))
    count = announce([at.hop(0, 1), at.hop(0, 3), at.sibling, partner])
    x = rows_in[...].astype(f32)
    own_normed[...] = (x * lax.rsqrt(jnp.mean(x * x, axis=1, keepdims=True) + EPSILON) * gain[...]).astype(bf16)
    meet(count)
    big = gather_stream(sems, at, own_normed, normed, rows, local.at[0])
    next(big)
    loads[0].wait()
    lat = dot_nt(own_normed[...], wl[...])
    raw[...] = lat[:, :LAT]
    x = lat[:, :LAT]
    x = x * lax.rsqrt(jnp.mean(x * x, axis=1, keepdims=True) + EPSILON) * latent_gain[...]
    rope = jnp.concatenate([lat[:, LAT:], lat[:, LAT:]], axis=1)
    loads[1].wait()
    loads[2].wait()
    own = pl.ds(pl.multiple_of(at.me * rows, rows), rows)
    rope = rope * cosine[own] + swapped(rope) * sine[own]
    number = lax.broadcasted_iota(jnp.int32, (128, rows), 0)
    hot = jnp.zeros((128, rows), f32)
    for k in range(routes.shape[0]):
        hot = hot + jnp.where(number == routes[k : k + 1], 1.0, 0.0)
    hot = pltpu.roll(jnp.transpose(hot), ROPE, 1)
    lane = lax.broadcasted_iota(jnp.int32, rope.shape, 1)
    prev_out[:, :LAT] = x.astype(bf16)
    prev_out[:, LAT:] = jnp.where(lane < ROPE, rope, hot).astype(bf16)
    swap = sems.start(prev_out, ext.at[:, pl.ds(SPAN, SPAN)], partner)
    ext[:, :SPAN] = prev_out[...]
    next(big)
    swap.wait_recv()
    little = gather_stream(sems, at, ext, ext_all, rows, local.at[1])
    next(little)
    together(big)
    stores = [pltpu.make_async_copy(normed, normed_h, store.at[0])]
    stores[0].start()
    loads[3].wait()
    loads[4].wait()
    step = 256
    lane = lax.broadcasted_iota(jnp.int32, (step, 2 * ROPE), 1)
    for i in range(block // step):
        r = pl.ds(i * step, step)
        query = dot_nn(normed[r], wq[...])
        q[r, :NOPE] = query[:, :NOPE].astype(bf16)
        one, two = query[:, NOPE : 2 * NOPE], query[:, 2 * NOPE :]
        q[r, NOPE : 2 * NOPE] = jnp.where(lane < ROPE, pltpu.roll(one, ROPE, 1), pltpu.roll(two, ROPE, 1)).astype(bf16)
        rope = jnp.where(lane < ROPE, one, two)
        q[r, 2 * NOPE :] = (rope * cosine[r] + swapped(rope) * sine[r]).astype(bf16)
        if i % 2:
            next(little, None)
    stores.append(pltpu.make_async_copy(q, q_h, store.at[1]))
    stores[1].start()
    together(little)
    for part in range(2):
        r = pl.ds((1 - part) * block, block)
        keys[r, :LAT] = ext_all[:, part * SPAN : part * SPAN + LAT]
        rope = ext_all[:, part * SPAN + LAT : (part + 1) * SPAN].astype(f32)
        turned = pltpu.roll(rope, ROPE, 1)
        if part == 0:
            hot_all[...] = turned.astype(bf16)
        wide_lane = lax.broadcasted_iota(jnp.int32, rope.shape, 1)
        keys[r, LAT:] = jnp.where(wide_lane < ROPE, rope, turned).astype(bf16)
        packed[r] = dot_nn(ext_all[:, part * SPAN : part * SPAN + LAT], kv_proj[...]).astype(bf16)
        for ref, dst in ((keys, keys_h), (packed, packed_h)):
            stores.append(pltpu.make_async_copy(ref.at[r], dst.at[r], store.at[len(stores)]))
            stores[-1].start()
    for c in stores:
        c.wait()
    sems.finish()


def start(rows_in, gain, wl, latent_gain, wq, kv_proj, routes, cosine, sine):
    whole = pl.BlockSpec(memory_space=VM)
    held = pl.BlockSpec(memory_space=pl.ANY)
    rows, width = rows_in.shape
    block = 8 * rows
    shapes = [(block, width), (block, wq.shape[1]), (2 * block, kv_proj.shape[1]), (2 * block, SPAN)]
    return pl.pallas_call(
        start_kernel,
        out_shape=[jax.ShapeDtypeStruct(shape, bf16) for shape in shapes]
        + [jax.ShapeDtypeStruct((block, 2 * ROPE), bf16), jax.ShapeDtypeStruct((rows, LAT), f32)],
        in_specs=[whole] * 4 + [held] * 5,
        out_specs=[held] * 4 + [whole] * 2,
        scratch_shapes=[pltpu.VMEM(shape, bf16) for shape in shapes]
        + [pltpu.VMEM(x.shape, bf16) for x in (wl, wq, kv_proj)]
        + [
            pltpu.VMEM((rows, width), bf16),
            pltpu.VMEM((rows, 2 * SPAN), bf16),
            pltpu.VMEM((block, 2 * SPAN), bf16),
            pltpu.VMEM((rows, SPAN), bf16),
            pltpu.VMEM((block, 2 * ROPE), f32),
            pltpu.VMEM((block, 2 * ROPE), f32),
            pltpu.SemaphoreType.DMA((27,)),
            pltpu.SemaphoreType.DMA((27,)),
            pltpu.SemaphoreType.DMA((2,)),
            pltpu.SemaphoreType.DMA((5,)),
            pltpu.SemaphoreType.DMA((6,)),
        ],
        compiler_params=pltpu.CompilerParams(collective_id=0, has_side_effects=True, vmem_limit_bytes=56 << 20),
        name="start",
    )(rows_in, gain, latent_gain, routes, wl, wq, kv_proj, cosine, sine)


def finish_kernel(
    weights_h, query_h, kvo_h, latent_h, small,
    expert_gate_h, expert_down_h, shared_gate_h, shared_down_h, query_out_h, kv_out_h, out_out_h, latent_out_h,
    router_out, attn_out, ffn_out, lat_gain_out,
    weights, query, kvo, latent, expert_gate, expert_down, shared_gate, shared_down, query_out, kv_out, out_out, latent_out,
    load, store,
):
    pairs = ((latent_h, latent), (query_h, query), (kvo_h, kvo), (weights_h, weights))
    loads = [pltpu.make_async_copy(src, dst, load.at[i]) for i, (src, dst) in enumerate(pairs)]
    for c in loads:
        c.start()
    stores = []

    def put(src, dst):
        c = pltpu.make_async_copy(src, dst, store.at[len(stores)])
        c.start()
        stores.append(c)

    router_out[...] = small[:EXPERTS]
    attn_out[...] = small[EXPERTS : EXPERTS + 1]
    ffn_out[...] = small[EXPERTS + 1 : EXPERTS + 2]
    lat_gain_out[...] = small[EXPERTS + 2 : EXPERTS + 3, :LAT]
    loads[0].wait()
    step = 512
    for i in range(latent_out.shape[1] // step):
        spot = step // latent.shape[1]
        rows = latent[i * spot : (i + 1) * spot].reshape(step, latent.shape[2]).astype(f32)
        latent_out[:, i * step : (i + 1) * step] = jnp.transpose(rows)[: latent_out.shape[0]]
    put(latent_out, latent_out_h)
    loads[1].wait()
    query_out[...] = query[...].reshape(query_out.shape).astype(f32)
    put(query_out, query_out_h)
    loads[2].wait()
    spots, _, wide = kvo.shape
    kv_rows = kv_out.shape[0] // spots
    kv_out[...] = kvo[:, :kv_rows].reshape(kv_out.shape).astype(f32)
    put(kv_out, kv_out_h)
    out_rows = out_out.shape[0] // spots
    for j in range(out_out.shape[1] // wide):
        piece = kvo[:, kv_rows + j * out_rows : kv_rows + (j + 1) * out_rows]
        out_out[:, j * wide : (j + 1) * wide] = piece.reshape(out_out.shape[0], wide).astype(f32)
    put(out_out, out_out_h)
    loads[3].wait()
    for c in range(expert_gate.shape[1] // 128):
        expert_gate[:, c * 128 : (c + 1) * 128] = weights[c * 128 : (c + 1) * 128].astype(f32)
    put(expert_gate, expert_gate_h)
    spot = expert_gate.shape[1]
    for ref, dst in ((expert_down, expert_down_h), (shared_gate, shared_gate_h), (shared_down, shared_down_h)):
        ref[...] = weights[spot : spot + ref.shape[0]].astype(f32)
        put(ref, dst)
        spot += ref.shape[0]
    for c in stores:
        c.wait()


def finish(weights, query, kvo, latent, small, shared, model_width, kv_shape, out_shape):
    whole = pl.BlockSpec(memory_space=VM)
    held = pl.BlockSpec(memory_space=pl.ANY)
    shapes = [
        (128, 2 * F), (F, 128), (2 * shared, 128), (shared, 128),
        (model_width, query.shape[2]), kv_shape, out_shape, (LAT + ROPE, model_width),
    ]
    little = [(EXPERTS, model_width), (1, model_width), (1, model_width), (1, LAT)]
    return pl.pallas_call(
        finish_kernel,
        out_shape=[jax.ShapeDtypeStruct(shape, f32) for shape in shapes + little],
        in_specs=[held] * 4 + [whole],
        out_specs=[held] * 8 + [whole] * 4,
        scratch_shapes=[pltpu.VMEM(x.shape, bf16) for x in (weights, query, kvo, latent)]
        + [pltpu.VMEM(shape, f32) for shape in shapes]
        + [pltpu.SemaphoreType.DMA((4,)), pltpu.SemaphoreType.DMA((8,))],
        compiler_params=pltpu.CompilerParams(vmem_limit_bytes=56 << 20),
        name="finish",
    )(weights, query, kvo, latent, small)


def tables(seq_rows):
    lane = np.arange(2 * ROPE)
    half = ROPE // 2
    frequency = np.exp((lane % half) * (-math.log(10000.0) / half))
    angles = np.arange(seq_rows)[:, None] * frequency[None, :]
    sign = np.where(lane % ROPE < half, -1.0, 1.0)
    return np.cos(angles).astype(np.float32), (np.sin(angles) * sign[None, :]).astype(np.float32)


def local(
    layer_input, attn_gain, query_proj, latent_proj, latent_gain, kv_proj, output_proj, ffn_gain, router_proj,
    shared_gate_up, shared_down, expert_gate_up, expert_down, segment_ids, expert_routes, out_grad,
):
    own_rows, model_width = layer_input.shape
    cosine, sine = tables(2 * own_rows * lax.axis_size("exp"))
    wl = latent_proj.T
    router = router_proj.T
    shared = shared_down.shape[0]
    pair_s = shared_gate_up.transpose(1, 2, 0).reshape(2 * shared, model_width)
    pair_e, down_e = expert_gate_up[0], expert_down[0]
    segs = segment_ids[None]
    attn_row, latent_row, ffn_row = attn_gain[None], latent_gain[None], ffn_gain[None]
    normed_all, q, packed, keys, hot, latent_raw = start(
        layer_input, attn_row, wl, latent_row, query_proj, kv_proj, expert_routes.T, cosine, sine
    )
    heads, lse, residual, own_mid = attend(q, packed, keys, segs, output_proj, layer_input, ffn_row)
    terms, act, dpre, logit, router_term = mlp(
        own_mid, out_grad, pair_s, pair_e, shared_down, down_e, router, hot
    )
    weight_sum = lax.psum_scatter(terms.reshape(-1, 128), "seq", scatter_dimension=0, tiled=True)
    residual_grad, ffn_term, attn_grad_all, moe_part = turn(
        dpre, act, pair_s, pair_e, shared_down, down_e, logit, router, residual, ffn_row, out_grad
    )
    dq, key_own, key_prev, kvo, layer_output = attend_back(
        attn_grad_all, output_proj, heads, q, packed, keys, segs, lse, kv_proj, moe_part, residual, cosine, sine
    )
    query_sum, kvo_sum, latent_sum, input_grad, small = tail(
        dq, key_own, key_prev, kvo, normed_all, query_proj, wl, latent_raw, latent_row, attn_row,
        residual_grad, layer_input, router_term, ffn_term, cosine, sine,
    )
    (
        expert_gate, expert_down_sum, shared_gate, shared_down_sum, query_sum, kv_sum, output_sum, latent_sum,
        router_sum, attn_gain_sum, ffn_gain_sum, latent_gain_sum,
    ) = finish(
        weight_sum, query_sum, kvo_sum, latent_sum, small, shared, model_width, kv_proj.shape, output_proj.shape
    )
    return (
        layer_output,
        input_grad,
        attn_gain_sum[0],
        query_sum,
        latent_sum.T,
        latent_gain_sum[0],
        kv_sum,
        output_sum,
        ffn_gain_sum[0],
        router_sum.T,
        shared_gate.reshape(2, shared, 128).transpose(2, 0, 1),
        shared_down_sum,
        expert_gate[None],
        expert_down_sum[None],
    )


def solution(mesh):
    in_specs = (
        P(("seq", "exp"), None),
        P(),
        P(None, "exp"),
        P(),
        P(),
        P(None, "exp"),
        P("exp", None),
        P(),
        P(),
        P(None, None, "exp"),
        P("exp", None),
        P("exp", None, None),
        P("exp", None, None),
        P(),
        P(("seq", "exp"), None),
        P(("seq", "exp"), None),
    )
    out_specs = (
        P(("seq", "exp"), None),
        P(("seq", "exp"), None),
        P(),
        P(None, "exp"),
        P(),
        P(),
        P(None, "exp"),
        P("exp", None),
        P(),
        P(),
        P("seq", None, "exp"),
        P("exp", "seq"),
        P("exp", "seq", None),
        P("exp", None, "seq"),
    )
    return jax.shard_map(local, mesh=mesh, in_specs=in_specs, out_specs=out_specs, check_vma=False)
```

```python
import functools
import math

import jax
import jax.numpy as jnp
import numpy as np
from jax import lax
from jax.experimental import pallas as pl
from jax.experimental.pallas import tpu as pltpu
from jax.sharding import PartitionSpec as P

NOPE = 128
ROPE = 64
VDIM = 128
LAT = 512
F = 1408
EXPERTS = 8
EPSILON = 1e-06

VM = pltpu.VMEM
f32 = jnp.float32
bf16 = jnp.bfloat16


class Sems:
    def __init__(self, send, recv):
        self.send, self.recv, self.used, self.sent = send, recv, 0, []

    def start(self, src, dst, peer):
        copy = pltpu.make_async_remote_copy(
            src_ref=src,
            dst_ref=dst,
            send_sem=self.send.at[self.used],
            recv_sem=self.recv.at[self.used],
            device_id=peer,
            device_id_type=pl.DeviceIdType.MESH,
        )
        copy.start()
        self.used += 1
        self.sent.append(copy)
        return copy

    def finish(self):
        for copy in self.sent:
            copy.wait_send()


class Place:
    def __init__(self):
        me, spot = lax.axis_index("exp"), lax.axis_index("seq")
        self.me = me
        self.chip, self.core = me // 2, me % 2
        self.z, self.y = spot // 4, spot % 4
        self.sibling = {"exp": self.chip * 2 + 1 - self.core}
        self.across = [lambda i: {"exp": i * 2 + self.core}, lambda i: {"seq": self.z * 4 + i}, lambda i: {"seq": i * 4 + self.y}]
        self.along = [self.chip, self.y, self.z]

    def hop(self, axis, distance):
        return self.across[axis](lax.rem(self.along[axis] + distance, 4))


def announce(peers):
    barrier = pltpu.get_barrier_semaphore()
    for peer in peers:
        pl.semaphore_signal(barrier, inc=1, device_id=peer, device_id_type=pl.DeviceIdType.MESH)
    return len(peers)


def meet(count):
    pl.semaphore_wait(pltpu.get_barrier_semaphore(), count)


def greet(peers):
    meet(announce(peers))


def together(*streams):
    streams = list(streams)
    while streams:
        for stream in list(streams):
            try:
                next(stream)
            except StopIteration:
                streams.remove(stream)


def gather_stream(sems, at, src, out, rows, local, arrived=None, stride=None, offset=0):
    half = rows // 2
    stride = stride or rows
    right, left = at.hop(0, 1), at.hop(0, 3)
    me = at.me
    near_right = lax.rem(at.chip + 1, 4) * 2 + at.core
    near_left = lax.rem(at.chip + 3, 4) * 2 + at.core
    far = lax.rem(at.chip + 2, 4) * 2 + at.core

    def part(owner, h):
        return out.at[pl.ds(pl.multiple_of(owner * stride + offset + h * half, half), half)]

    def own(h):
        return src.at[pl.ds(h * half, half)]

    ra = sems.start(own(0), part(me, 0), right)
    lb = sems.start(own(1), part(me, 1), left)
    rb = sems.start(own(1), part(me, 1), right)
    la = sems.start(own(0), part(me, 0), left)
    sib = [sems.start(src, out.at[pl.ds(pl.multiple_of(me * stride + offset, rows), rows)], at.sibling)]
    mine = pltpu.make_async_copy(src, out.at[pl.ds(pl.multiple_of(me * stride + offset, rows), rows)], local)
    mine.start()
    if arrived is None:
        yield
    else:
        mine.wait()
        sib[0].wait_recv()
        arrived(0)
    ra.wait_recv()
    far_a = sems.start(part(near_left, 0), part(near_left, 0), right)
    sib.append(sems.start(part(near_left, 0), part(near_left, 0), at.sibling))
    lb.wait_recv()
    far_b = sems.start(part(near_right, 1), part(near_right, 1), left)
    sib.append(sems.start(part(near_right, 1), part(near_right, 1), at.sibling))
    if arrived is None:
        yield
    rb.wait_recv()
    sib.append(sems.start(part(near_left, 1), part(near_left, 1), at.sibling))
    la.wait_recv()
    sib.append(sems.start(part(near_right, 0), part(near_right, 0), at.sibling))
    yield
    if arrived is not None:
        sib[1].wait_recv()
        sib[3].wait_recv()
        arrived(3)
    far_a.wait_recv()
    sib.append(sems.start(part(far, 0), part(far, 0), at.sibling))
    far_b.wait_recv()
    sib.append(sems.start(part(far, 1), part(far, 1), at.sibling))
    yield
    if arrived is None:
        mine.wait()
        for copy in sib:
            copy.wait_recv()
    else:
        sib[2].wait_recv()
        sib[4].wait_recv()
        arrived(1)
        yield
        sib[5].wait_recv()
        sib[6].wait_recv()
        arrived(2)


def scatter_stream(sems, at, src, pair, hop, last, rows, done, ready=None, stride=None, offset=0):
    half = rows // 2
    stride = stride or rows
    right, left = at.hop(0, 1), at.hop(0, 3)
    order = (2, 1, 3, 0)
    sib = []

    def offer(dist):
        if ready is not None:
            ready(dist)
        owner = lax.rem(at.chip + dist, 4) * 2 + 1 - at.core
        sib.append(sems.start(src.at[pl.ds(pl.multiple_of(owner * stride + offset, rows), rows)], pair.at[dist], at.sibling))

    def fold(i):
        sib[i].wait_recv()
        owner = lax.rem(at.chip + order[i], 4) * 2 + at.core
        mine = src[pl.ds(pl.multiple_of(owner * stride + offset, rows), rows)]
        pair[order[i]] = (pair[order[i]].astype(f32) + mine.astype(f32)).astype(bf16)

    def add(ref, other):
        ref[...] = (ref[...].astype(f32) + other[...].astype(f32)).astype(bf16)

    first, second = pl.ds(0, half), pl.ds(half, half)
    offer(2)
    if ready is not None:
        yield
    offer(1)
    if ready is None:
        offer(3)
        offer(0)
        yield
    fold(0)
    far_a = sems.start(pair.at[2, first], hop.at[0], right)
    far_b = sems.start(pair.at[2, second], hop.at[1], left)
    yield
    if ready is not None:
        offer(3)
    fold(1)
    dir_b = sems.start(pair.at[1, second], last.at[0], right)
    fold(2)
    dir_a = sems.start(pair.at[3, first], last.at[1], left)
    yield
    far_a.wait_recv()
    add(pair.at[1, first], hop.at[0])
    acc_a = sems.start(pair.at[1, first], last.at[2], right)
    far_b.wait_recv()
    add(pair.at[3, second], hop.at[1])
    acc_b = sems.start(pair.at[3, second], last.at[3], left)
    if ready is not None:
        offer(0)
    yield
    sib[3].wait_recv()
    dir_b.wait_recv()
    dir_a.wait_recv()
    acc_a.wait_recv()
    acc_b.wait_recv()
    for h, ends in ((0, (1, 2)), (1, (0, 3))):
        mine = src[pl.ds(pl.multiple_of(at.me * stride + offset + h * half, half), half)].astype(f32)
        total = mine + pair[0, pl.ds(h * half, half)].astype(f32)
        done(h, total + last[ends[0]].astype(f32) + last[ends[1]].astype(f32))


def scatter_scratch(rows, cols):
    return [
        pltpu.VMEM((4, rows, cols), bf16),
        pltpu.VMEM((2, rows // 2, cols), bf16),
        pltpu.VMEM((4, rows // 2, cols), bf16),
    ]


def ring_sum(sems, at, axis, block, hop, last):
    right, left = at.hop(axis, 1), at.hop(axis, 3)
    to = [lax.rem(at.along[axis] + d, 4) for d in range(4)]

    def add(ref, other):
        ref[...] = (ref[...].astype(f32) + other[...].astype(f32)).astype(bf16)

    far_a = sems.start(block(to[2], 0), hop.at[0], right)
    far_b = sems.start(block(to[2], 1), hop.at[1], left)
    dir_b = sems.start(block(to[1], 1), last.at[0], right)
    dir_a = sems.start(block(to[3], 0), last.at[1], left)
    yield
    far_a.wait_recv()
    add(block(to[1], 0), hop.at[0])
    acc_a = sems.start(block(to[1], 0), last.at[2], right)
    far_b.wait_recv()
    add(block(to[3], 1), hop.at[1])
    acc_b = sems.start(block(to[3], 1), last.at[3], left)
    yield
    dir_b.wait_recv()
    dir_a.wait_recv()
    acc_a.wait_recv()
    acc_b.wait_recv()
    for part, (one, two) in ((0, (1, 2)), (1, (0, 3))):
        ref = block(to[0], part)
        ref[...] = (ref[...].astype(f32) + last[one].astype(f32) + last[two].astype(f32)).astype(bf16)


def ring_gather(sems, at, axis, block):
    right, left = at.hop(axis, 1), at.hop(axis, 3)
    to = [lax.rem(at.along[axis] + d, 4) for d in range(4)]
    ra = sems.start(block(to[0], 0), block(to[0], 0), right)
    lb = sems.start(block(to[0], 1), block(to[0], 1), left)
    rb = sems.start(block(to[0], 1), block(to[0], 1), right)
    la = sems.start(block(to[0], 0), block(to[0], 0), left)
    yield
    ra.wait_recv()
    fa = sems.start(block(to[3], 0), block(to[3], 0), right)
    lb.wait_recv()
    fb = sems.start(block(to[1], 1), block(to[1], 1), left)
    yield
    for copy in (rb, la, fa, fb):
        copy.wait_recv()


def seq_stream(sems, at, work, out, scratch, axes):
    hop, last, narrow_in = scratch
    one, two = at.along[axes[0]], at.along[axes[1]]
    own = one * 4 + two

    def wide(ref):
        return lambda i, h: ref.at[pl.ds(i * 4 + 2 * h, 2)]

    yield from ring_sum(sems, at, axes[0], wide(work), hop, last)
    copies = [sems.start(work.at[one * 4 + lax.rem(two + d, 4)], narrow_in.at[d - 1], at.hop(axes[1], d)) for d in (1, 2, 3)]
    yield
    for copy in copies:
        copy.wait_recv()
    total = work[own].astype(f32) + narrow_in[0].astype(f32)
    out[own] = (total + (narrow_in[1].astype(f32) + narrow_in[2].astype(f32))).astype(bf16)
    copies = [sems.start(out.at[own], out.at[own], at.hop(axes[1], d)) for d in (1, 2, 3)]
    yield
    for copy in copies:
        copy.wait_recv()
    yield from ring_gather(sems, at, axes[0], wide(out))


def seq_scatter(sems, at, work, out, scratch, axes):
    hop, last, narrow_in = scratch
    one, two = at.along[axes[0]], at.along[axes[1]]
    yield from ring_sum(sems, at, axes[0], lambda i, h: work.at[pl.ds(i * 4 + 2 * h, 2)], hop, last)
    copies = [sems.start(work.at[one * 4 + lax.rem(two + d, 4)], narrow_in.at[d - 1], at.hop(axes[1], d)) for d in (1, 2, 3)]
    yield
    for copy in copies:
        copy.wait_recv()
    total = work[one * 4 + two].astype(f32) + narrow_in[0].astype(f32)
    out[...] = (total + (narrow_in[1].astype(f32) + narrow_in[2].astype(f32))).astype(bf16)


def seq_scratch(rows, cols):
    return [
        pltpu.VMEM((2, 2, rows, cols), bf16),
        pltpu.VMEM((4, 2, rows, cols), bf16),
        pltpu.VMEM((3, rows, cols), bf16),
    ]


def seq_direct(sems, at, work, out, wide_in, narrow_in):
    y, z = at.y, at.z
    copies = [sems.start(work.at[pl.ds(lax.rem(y + d, 4) * 4, 4)], wide_in.at[d - 1], at.hop(1, d)) for d in (1, 2, 3)]
    yield
    for copy in copies:
        copy.wait_recv()
    mine = pl.ds(y * 4, 4)
    work[mine] = (
        work[mine].astype(f32) + wide_in[0].astype(f32) + (wide_in[1].astype(f32) + wide_in[2].astype(f32))
    ).astype(bf16)
    copies = [sems.start(work.at[y * 4 + lax.rem(z + d, 4)], narrow_in.at[d - 1], at.hop(2, d)) for d in (1, 2, 3)]
    yield
    for copy in copies:
        copy.wait_recv()
    own = y * 4 + z
    out[own] = (
        work[own].astype(f32) + narrow_in[0].astype(f32) + (narrow_in[1].astype(f32) + narrow_in[2].astype(f32))
    ).astype(bf16)
    copies = [sems.start(out.at[own], out.at[own], at.hop(2, d)) for d in (1, 2, 3)]
    yield
    for copy in copies:
        copy.wait_recv()
    copies = [sems.start(out.at[mine], out.at[mine], at.hop(1, d)) for d in (1, 2, 3)]
    yield
    for copy in copies:
        copy.wait_recv()


def small_stream(sems, at, slots, out):
    stages = [(at.core, 2, lambda d: at.sibling)] + [
        (at.along[axis], 4, functools.partial(at.hop, axis)) for axis in range(3)
    ]
    for stage, (place, count, name) in enumerate(stages):
        slots[stage, place] = out[...].astype(bf16)
        copies = [sems.start(slots.at[stage, place], slots.at[stage, place], name(d)) for d in range(1, count)]
        yield
        for copy in copies:
            copy.wait_recv()
        total = slots[stage, 0].astype(f32)
        for i in range(1, count):
            total = total + slots[stage, i].astype(f32)
        out[...] = total


def swapped(tensor):
    lane = lax.broadcasted_iota(jnp.int32, tensor.shape, 1)
    return jnp.where(lane % 64 < 32, pltpu.roll(tensor, 96, 1), pltpu.roll(tensor, 32, 1))


PAD = 384
EARLY = 768
ROW_STEP = 256


def dot_nn(a, b):
    return lax.dot_general(a, b, (((1,), (0,)), ((), ())), preferred_element_type=f32)


def dot_nt(a, b):
    return lax.dot_general(a, b, (((1,), (1,)), ((), ())), preferred_element_type=f32)


def dot_tn(a, b):
    return lax.dot_general(a, b, (((0,), (0,)), ((), ())), preferred_element_type=f32)


def row_block(index):
    return pl.ds(pl.multiple_of(index * ROW_STEP, ROW_STEP), ROW_STEP)


def router_pieces(router):
    high = router.astype(bf16).astype(f32)
    middle_part = (router - high).astype(bf16).astype(f32)
    low = router - high - middle_part
    fill = jnp.zeros((128 - 3 * EXPERTS, router.shape[1]), f32)
    return jnp.concatenate([high, middle_part, low, fill], axis=0).astype(bf16)


def mlp_kernel(
    own_mid, own_grad, pair_s_h, pair_e_h, down_s_h, down_e_h, router, hot,
    terms_h, act_h, dpre_h, logit, router_out, early,
    mid, grad, pair_s, pair_e, down_s, down_e, act, dpre, pieces, stage, work0, work1, r0, r1, r2, s0, s1, s2, load, store, keep, send, recv, local,
):
    at = Place()
    sems = Sems(send, recv)
    rows, width = mid.shape
    shared = down_s.shape[0]
    expert = lax.axis_index("exp")
    sources = [(pair_e_h, pair_e), (pair_s_h, pair_s), (down_s_h, down_s), (down_e_h, down_e)]
    loads = [pltpu.make_async_copy(src, dst, load.at[i]) for i, (src, dst) in enumerate(sources)]
    for c in loads:
        c.start()
    count = announce(
        [at.hop(0, 1), at.hop(0, 3), at.sibling] + [at.hop(axis, d) for axis in (1, 2) for d in (1, 2, 3)]
    )
    pieces[...] = router_pieces(router[...])
    meet(count)
    lane = lax.broadcasted_iota(jnp.int32, (ROW_STEP, 128), 1)
    own_lane = lane == expert

    def gates(r):
        raw = dot_nt(mid[r], pieces[...])
        raw = raw + (pltpu.roll(raw, 128 - EXPERTS, 1) + pltpu.roll(raw, 128 - 2 * EXPERTS, 1))
        raw = jnp.where(lane < EXPERTS, raw, -1e30)
        raw = jnp.exp(raw - jnp.max(raw, axis=1, keepdims=True))
        probs = raw / jnp.sum(raw, axis=1, keepdims=True)
        own = jnp.sum(jnp.where(own_lane, probs * hot[r].astype(f32), 0.0), axis=1, keepdims=True)
        return own, probs

    tiles = [(pair_e, start, min(512, F - start)) for start in range(0, F, 512)]

    def before_activation(dist):
        r = row_block(lax.rem(at.chip + dist, 4))
        if dist == 0:
            loads[0].wait()
        for _, start, size in tiles:
            dpre[r, start : start + size] = dot_nn(mid[r], pair_e[:, start : start + size]).astype(bf16)
            up = dot_nn(mid[r], pair_e[:, F + start : F + start + size])
            dpre[r, F + start : F + start + size] = up.astype(bf16)
        if dist == 0:
            loads[1].wait()
        dpre[r, 2 * F : 2 * F + shared] = dot_nt(mid[r], pair_s[:shared]).astype(bf16)
        dpre[r, 2 * F + PAD : 2 * F + PAD + shared] = dot_nt(mid[r], pair_s[shared:]).astype(bf16)

    def piece(r, dact, act_at, gate_at, up_at, own):
        size = dact.shape[1]
        gate, up = dpre[r, gate_at : gate_at + size].astype(f32), dpre[r, up_at : up_at + size].astype(f32)
        logistic = 1.0 / (1.0 + jnp.exp(-gate))
        passed = gate * logistic
        out = passed * up
        total = None
        if own is not None:
            total = jnp.sum(out * dact, axis=1, keepdims=True)
            out = out * own
            dact = dact * own
        act[r, act_at : act_at + size] = out.astype(bf16)
        slope = logistic + passed * (1.0 - logistic)
        dpre[r, gate_at : gate_at + size] = (dact * up * slope).astype(bf16)
        dpre[r, up_at : up_at + size] = (dact * passed).astype(bf16)
        return total

    mids = gather_stream(sems, at, own_mid, mid, own_mid.shape[0], local.at[0], before_activation)
    grads = gather_stream(sems, at, own_grad, grad, own_grad.shape[0], local.at[1])
    next(mids)
    next(grads)
    next(mids)
    next(mids)
    next(grads)
    together(mids)
    together(grads)
    loads[2].wait()
    loads[3].wait()

    @pl.loop(0, rows // ROW_STEP)
    def _(index):
        r = row_block(index)
        piece(r, dot_nt(grad[r], down_s[...]), F, 2 * F, 2 * F + PAD, None)
        own, probs = gates(r)
        total = 0.0
        for _, start, size in tiles:
            total = total + piece(r, dot_nt(grad[r], down_e[start : start + size]), start, start, F + start, own)
        logit[r] = ((own * total) * (jnp.where(own_lane, 1.0, 0.0) - probs)).astype(bf16)

    keeps = [pltpu.make_async_copy(act, act_h, keep.at[0]), pltpu.make_async_copy(dpre, dpre_h, keep.at[1])]
    for c in keeps:
        c.start()

    half = width // 2
    slots = half // 128
    early_rows = EARLY // 2
    for work, start, axis in ((work0, 0, 1), (work1, early_rows, 2)):
        for part in range(2):
            value = dot_tn(act[:, start : start + early_rows], grad[:, part * half : (part + 1) * half]).astype(bf16)
            for s in range(slots):
                z, y = divmod(part * slots + s, 4)
                work[y * 4 + z if axis == 1 else z * 4 + y] = value[:, s * 128 : (s + 1) * 128]
    sums = [
        seq_scatter(sems, at, work0, early.at[pl.ds(0, early_rows)], (r0, r1, r2), (1, 2)),
        seq_scatter(sems, at, work1, early.at[pl.ds(early_rows, early_rows)], (s0, s1, s2), (2, 1)),
    ]
    for stream in sums:
        next(stream)
    jobs = []
    for start in range(0, 2 * F, 512):
        size = min(512, 2 * F - start)
        jobs.append((mid, dpre, start, size, start, True))
    for start in range(EARLY, F, 512):
        size = min(512, F - start)
        jobs.append((grad, act, start, size, 2 * F + start - EARLY, False))
    for index, (left, right, start) in enumerate(((mid, dpre, 2 * F), (mid, dpre, 2 * F + PAD), (grad, act, F))):
        jobs.append((left, right, start, shared, 3 * F - EARLY + index * shared, False))

    def flush(part, spot, size):
        return pltpu.make_async_copy(
            stage.at[part, :, pl.ds(0, size)], terms_h.at[pl.ds(part * slots, slots), pl.ds(spot, size)], store.at[part]
        )

    before = None
    for number, (left, right, start, size, spot, by_column) in enumerate(jobs):
        for part in range(2):
            if before is not None:
                flush(part, *before).wait()
            wide = left[:, part * half : (part + 1) * half]
            if by_column:
                value = dot_tn(wide, right[:, start : start + size]).astype(bf16)
                for s in range(slots):
                    for c in range(size // 128):
                        stage[part, s, c * 128 : (c + 1) * 128] = value[s * 128 : (s + 1) * 128, c * 128 : (c + 1) * 128]
            else:
                value = dot_tn(right[:, start : start + size], wide).astype(bf16)
                for s in range(slots):
                    stage[part, s, :size] = value[:, s * 128 : (s + 1) * 128]
            flush(part, spot, size).start()
        before = (spot, size)
        if number in (3, 7):
            for stream in sums:
                next(stream)
    router_out[...] = dot_tn(logit[...], mid[...])[:EXPERTS]
    for part in range(2):
        flush(part, *before).wait()
    for c in keeps:
        c.wait()
    together(*sums)
    sems.finish()


def mlp(own_mid, own_grad, pair_s, pair_e, down_s, down_e, router, hot):
    rows, width = 8 * own_mid.shape[0], own_mid.shape[1]
    shared = down_s.shape[0]
    whole = pl.BlockSpec(memory_space=VM)
    held = pl.BlockSpec(memory_space=pl.ANY)
    act_shape, dpre_shape = (rows, F + PAD), (rows, 2 * (F + PAD))
    return pl.pallas_call(
        mlp_kernel,
        out_shape=[
            jax.ShapeDtypeStruct((width // 128, 3 * (F + shared) - EARLY, 128), bf16),
            jax.ShapeDtypeStruct(act_shape, bf16),
            jax.ShapeDtypeStruct(dpre_shape, bf16),
            jax.ShapeDtypeStruct((rows, 128), bf16),
            jax.ShapeDtypeStruct((EXPERTS, width), f32),
            jax.ShapeDtypeStruct((EARLY, 128), bf16),
        ],
        in_specs=[whole] * 2 + [held] * 4 + [whole] * 2,
        out_specs=[held, held, held, whole, whole, whole],
        scratch_shapes=[
            pltpu.VMEM((rows, width), bf16), pltpu.VMEM((rows, width), bf16),
            pltpu.VMEM(pair_s.shape, bf16), pltpu.VMEM(pair_e.shape, bf16),
            pltpu.VMEM(down_s.shape, bf16), pltpu.VMEM(down_e.shape, bf16),
            pltpu.VMEM(act_shape, bf16), pltpu.VMEM(dpre_shape, bf16),
            pltpu.VMEM((128, width), bf16), pltpu.VMEM((2, width // 256, 512, 128), bf16),
            pltpu.VMEM((width // 128, EARLY // 2, 128), bf16), pltpu.VMEM((width // 128, EARLY // 2, 128), bf16),
            *seq_scratch(EARLY // 2, 128), *seq_scratch(EARLY // 2, 128),
            pltpu.SemaphoreType.DMA((4,)), pltpu.SemaphoreType.DMA((2,)), pltpu.SemaphoreType.DMA((2,)),
            pltpu.SemaphoreType.DMA((44,)), pltpu.SemaphoreType.DMA((44,)), pltpu.SemaphoreType.DMA((2,)),
        ],
        compiler_params=pltpu.CompilerParams(collective_id=5, has_side_effects=True, vmem_limit_bytes=62 << 20),
        cost_estimate=pl.CostEstimate(flops=12 * rows * width * (F + shared), bytes_accessed=60 << 20, transcendentals=rows * F),
        name="mlp",
    )(own_mid, own_grad, pair_s, pair_e, down_s, down_e, router, hot)


def turn_kernel(
    dpre_h, act_h, pair_s_h, pair_e_h, down_s_h, down_e_h, logit, router, residual, gain, upstream,
    residual_grad, gain_term, grad_all, moe_part,
    dpre, act, pair_s, pair_e, down_s, down_e, part, pieces, own_grad, p0, p1, p2, o0, o1, o2, load, send, recv, local,
):
    at = Place()
    sems = Sems(send, recv)
    rows = residual.shape[0]
    half = rows // 2
    shared = down_s.shape[0]
    sources = [
        (dpre_h, dpre), (pair_e_h.at[:, pl.ds(0, F)], pair_e.at[:, pl.ds(0, F)]),
        (pair_e_h.at[:, pl.ds(F, F)], pair_e.at[:, pl.ds(F, F)]), (pair_s_h, pair_s),
        (act_h, act), (down_e_h, down_e), (down_s_h, down_s),
    ]
    loads = [pltpu.make_async_copy(src, dst, load.at[i]) for i, (src, dst) in enumerate(sources)]
    for c in loads:
        c.start()
    count = announce([at.hop(0, 1), at.hop(0, 3), at.sibling])
    gain_term[...] = jnp.zeros_like(gain_term)
    pieces[...] = router_pieces(router[...])
    loads[0].wait()

    def ready(dist):
        r = row_block(lax.rem(at.chip + dist, 4))
        if dist == 2:
            loads[1].wait()
        total = dot_nt(dpre[r, :F], pair_e[:, :F])
        if dist == 2:
            loads[2].wait()
        total = total + dot_nt(dpre[r, F : 2 * F], pair_e[:, F:])
        if dist == 2:
            loads[3].wait()
        total = total + dot_nn(dpre[r, 2 * F : 2 * F + shared], pair_s[:shared])
        total = total + dot_nn(dpre[r, 2 * F + PAD : 2 * F + PAD + shared], pair_s[shared:])
        part[r] = (total + dot_nn(logit[r], pieces[...])).astype(bf16)
        if dist == 2:
            meet(count)

    def done_from(first):
        def done(h, total):
            r = slice(first + h * (half // 2), first + (h + 1) * (half // 2))
            x = residual[r]
            inverse = lax.rsqrt(jnp.mean(x * x, axis=1, keepdims=True) + EPSILON)
            gain_term[...] += jnp.sum(total * x * inverse, axis=0, keepdims=True)
            s = total * gain[...]
            inner = jnp.mean(s * x, axis=1, keepdims=True)
            grad = upstream[r].astype(f32) + (inverse * s - x * (inverse * inverse * inverse) * inner)
            residual_grad[r] = grad
            own_grad[r] = grad.astype(bf16)

        return done

    def moe(index):
        r = pl.ds(index * ROW_STEP, ROW_STEP)
        moe_part[r] = (dot_nn(act[r, :F], down_e[...]) + dot_nn(act[r, F : F + shared], down_s[...])).astype(bf16)

    ones = scatter_stream(sems, at, part, p0, p1, p2, half, done_from(0), ready, rows, 0)
    twos = scatter_stream(sems, at, part, o0, o1, o2, half, done_from(half), lambda dist: None, rows, half)
    for _ in range(4):
        next(ones)
        next(twos)
    together(ones)
    first = gather_stream(sems, at, own_grad.at[pl.ds(0, half)], grad_all, half, local.at[0], None, rows, 0)
    next(first)
    together(twos)
    second = gather_stream(sems, at, own_grad.at[pl.ds(half, half)], grad_all, half, local.at[1], None, rows, half)
    next(second)
    for c in loads[4:]:
        c.wait()
    for index in range(4):
        moe(index)
        next(first, None)
        next(second, None)
    together(first, second)
    sems.finish()


def turn(dpre, act, pair_s, pair_e, down_s, down_e, logit, router, residual, gain, upstream):
    whole = pl.BlockSpec(memory_space=VM)
    held = pl.BlockSpec(memory_space=pl.ANY)
    rows, width = residual.shape
    return pl.pallas_call(
        turn_kernel,
        out_shape=[
            jax.ShapeDtypeStruct((rows, width), f32),
            jax.ShapeDtypeStruct((1, width), f32),
            jax.ShapeDtypeStruct((8 * rows, width), bf16),
            jax.ShapeDtypeStruct((8 * rows, width), bf16),
        ],
        in_specs=[held] * 6 + [whole] * 5,
        out_specs=[whole] * 4,
        scratch_shapes=[
            pltpu.VMEM(dpre.shape, bf16), pltpu.VMEM(act.shape, bf16),
            pltpu.VMEM(pair_s.shape, bf16), pltpu.VMEM(pair_e.shape, bf16),
            pltpu.VMEM(down_s.shape, bf16), pltpu.VMEM(down_e.shape, bf16),
            pltpu.VMEM((8 * rows, width), bf16),
            pltpu.VMEM((128, width), bf16),
            pltpu.VMEM((rows, width), bf16),
            *scatter_scratch(rows // 2, width),
            *scatter_scratch(rows // 2, width),
            pltpu.SemaphoreType.DMA((7,)),
            pltpu.SemaphoreType.DMA((46,)),
            pltpu.SemaphoreType.DMA((46,)),
            pltpu.SemaphoreType.DMA((2,)),
        ],
        compiler_params=pltpu.CompilerParams(collective_id=2, has_side_effects=True, vmem_limit_bytes=62 << 20),
        name="turn",
    )(dpre, act, pair_s, pair_e, down_s, down_e, logit, router, residual, gain, upstream)


SPAN = LAT + 2 * ROPE
ATT = 256
SCALE = (NOPE + ROPE) ** (-0.5)
LOG2E = 1.4426950408889634


def segments(segs, count):
    spot = lax.axis_index("seq")
    own = segs[:, pl.ds(pl.multiple_of(spot * count, count), count)].astype(f32)
    before = segs[:, pl.ds(pl.multiple_of(jnp.maximum(spot - 1, 0) * count, count), count)].astype(f32)
    before = jnp.where(lax.rem(spot, 2) == 1, before, -1.0)
    column = jnp.transpose(jnp.broadcast_to(own, (128, count)))[:, :1]
    return column, jnp.concatenate([before, own], axis=1)


def attend_kernel(
    q, packed, keys_all, segs, wo, rows_in, gain, heads, lse, residual, own_mid, part, column, p0, p1, p2, send, recv
):
    at = Place()
    sems = Sems(send, recv)
    count = announce([at.hop(0, 1), at.hop(0, 3), at.sibling])
    prev = packed.shape[0] - q.shape[0]
    rows = rows_in.shape[0]
    half = rows // 2
    qseg, kseg = segments(segs, q.shape[0])
    column[...] = qseg
    lane = lax.broadcasted_iota(jnp.int32, (ATT, 2 * ROPE), 1)
    shape = (ATT, packed.shape[0])
    ahead = lax.broadcasted_iota(jnp.int32, shape, 1) - lax.broadcasted_iota(jnp.int32, shape, 0)

    def ready(dist):
        index = lax.rem(at.chip + dist, 4)
        r = row_block(index)
        allowed = (column[r] == kseg) & (ahead <= index * ATT + prev)
        for head in range(2):
            rope = jnp.where(lane // ROPE == head, q[r, 2 * NOPE :], jnp.zeros((), bf16))
            query = jnp.concatenate([q[r, head * NOPE : (head + 1) * NOPE], rope], axis=1)
            keys = jnp.concatenate([packed[:, head * 2 * NOPE : head * 2 * NOPE + NOPE], keys_all[:, LAT:]], axis=1)
            scores = jnp.where(allowed, dot_nt(query, keys), -1e30)
            top = jnp.max(scores, axis=1, keepdims=True)
            weights = jnp.exp2((scores - top) * (SCALE * LOG2E))
            total = jnp.sum(weights, axis=1, keepdims=True)
            out = dot_nn(weights.astype(bf16), packed[:, head * 2 * NOPE + NOPE : (head + 1) * 2 * NOPE])
            heads[r, head * VDIM : (head + 1) * VDIM] = (out / total).astype(bf16)
            lse[head, r] = top * (SCALE * LOG2E) + jnp.log2(total)
        part[r] = dot_nn(heads[r], wo[...]).astype(bf16)
        if dist == 2:
            meet(count)

    def done(h, total):
        r = slice(h * half, (h + 1) * half)
        x = rows_in[r].astype(f32) + total
        residual[r] = x
        own_mid[r] = (x * lax.rsqrt(jnp.mean(x * x, axis=1, keepdims=True) + EPSILON) * gain[...]).astype(bf16)

    together(scatter_stream(sems, at, part, p0, p1, p2, rows, done, ready))
    sems.finish()


def attend(q, packed, keys_all, segs, wo, rows_in, gain):
    whole = pl.BlockSpec(memory_space=VM)
    block = q.shape[0]
    rows, width = rows_in.shape
    return pl.pallas_call(
        attend_kernel,
        out_shape=[
            jax.ShapeDtypeStruct((block, 2 * VDIM), bf16),
            jax.ShapeDtypeStruct((2, block, 1), f32),
            jax.ShapeDtypeStruct((rows, width), f32),
            jax.ShapeDtypeStruct((rows, width), bf16),
        ],
        in_specs=[whole] * 7,
        out_specs=[whole] * 4,
        scratch_shapes=[
            pltpu.VMEM((block, width), bf16),
            pltpu.VMEM((block, 1), f32),
            *scatter_scratch(rows, width),
            pltpu.SemaphoreType.DMA((10,)),
            pltpu.SemaphoreType.DMA((10,)),
        ],
        compiler_params=pltpu.CompilerParams(collective_id=1, has_side_effects=True, vmem_limit_bytes=56 << 20),
        name="attend",
    )(q, packed, keys_all, segs, wo, rows_in, gain)


def attend_back_kernel(
    grad, wo, heads, q, packed, keys_all, segs, lse, kv_proj, moe_part, residual, cosine_h, sine_h,
    dq, key_own, prev_out, kvo, layer_out,
    key_prev, head_grad, dkey, dvalue, drope, dpacked, dquery, cosine, sine,
    p0, p1, p2, k0, k1, k2, send, recv, local,
):
    at = Place()
    sems = Sems(send, recv)
    rows = q.shape[0]
    prev = packed.shape[0] - rows
    block = pl.ds(pl.multiple_of(lax.rem(at.y, 2) * rows, rows), rows)
    loads = [
        pltpu.make_async_copy(cosine_h.at[block], cosine, local.at[0]),
        pltpu.make_async_copy(sine_h.at[block], sine, local.at[1]),
    ]
    for c in loads:
        c.start()
    count = announce([at.hop(0, 1), at.hop(0, 3), at.sibling])
    own_rows = residual.shape[0]

    def done(h, total):
        r = slice(h * (own_rows // 2), (h + 1) * (own_rows // 2))
        layer_out[r] = (residual[r] + total).astype(bf16)

    def keep_prev(h, total):
        prev_out[h * (own_rows // 2) : (h + 1) * (own_rows // 2)] = total.astype(bf16)

    step = 256
    for i in range(rows // step):
        r = pl.ds(i * step, step)
        head_grad[r] = dot_nt(grad[r], wo[...]).astype(bf16)
    meet(count)
    moe = scatter_stream(sems, at, moe_part, p0, p1, p2, own_rows, done)
    next(moe)
    qseg, kseg = segments(segs, rows)

    def block_back(head, start, size, lo, hi, diagonal):
        r = slice(start, start + size)
        lane = lax.broadcasted_iota(jnp.int32, (size, 2 * ROPE), 1)
        rope = jnp.where(lane // ROPE == head, q[r, 2 * NOPE :], jnp.zeros((), bf16))
        query = jnp.concatenate([q[r, head * NOPE : (head + 1) * NOPE], rope], axis=1)
        keys = jnp.concatenate([packed[lo:hi, head * 2 * NOPE : head * 2 * NOPE + NOPE], keys_all[lo:hi, LAT:]], axis=1)
        scores = dot_nt(query, keys)
        allowed = qseg[r] == kseg[:, lo:hi]
        if diagonal:
            ahead = lax.broadcasted_iota(jnp.int32, scores.shape, 1) - lax.broadcasted_iota(jnp.int32, scores.shape, 0)
            allowed = allowed & (ahead <= start)
        p = jnp.exp2(jnp.where(allowed, scores * (SCALE * LOG2E) - lse[head, r], -1e30))
        upstream = head_grad[r, head * VDIM : (head + 1) * VDIM]
        out = heads[r, head * VDIM : (head + 1) * VDIM]
        inner = jnp.sum(upstream.astype(f32) * out.astype(f32), axis=1, keepdims=True)
        d = dot_nt(upstream, packed[lo:hi, head * 2 * NOPE + NOPE : (head + 1) * 2 * NOPE])
        ds = (p * (d - inner)).astype(bf16)
        dkey[lo:hi] += dot_tn(ds, query)
        dvalue[lo:hi] += dot_tn(p.astype(bf16), upstream)
        return dot_nn(ds, keys)

    def keys_back(head, lo, hi):
        dpacked[lo:hi, head * 2 * NOPE : head * 2 * NOPE + NOPE] = (dkey[lo:hi, :NOPE] * SCALE).astype(bf16)
        dpacked[lo:hi, head * 2 * NOPE + NOPE : (head + 1) * 2 * NOPE] = dvalue[lo:hi].astype(bf16)
        if head == 0:
            drope[lo:hi] = dkey[lo:hi, NOPE:]
        else:
            drope[lo:hi] += dkey[lo:hi, NOPE:]

    def latent_back(ref, lo):
        for start in range(0, rows, 512):
            r, to = slice(lo + start, lo + start + 512), slice(start, start + 512)
            ref[to, :LAT] = dot_nt(dpacked[r], kv_proj[...]).astype(bf16)
            rope = drope[r]
            ref[to, LAT:] = ((rope + pltpu.roll(rope, ROPE, 1)) * SCALE).astype(bf16)

    wide_step = 512
    for head in range(2):
        dkey[...] = jnp.zeros_like(dkey)
        dvalue[...] = jnp.zeros_like(dvalue)
        for start in range(0, rows, wide_step):
            dquery[head, start : start + wide_step] = block_back(head, start, wide_step, 0, prev, False)
            if (head, start) != (1, wide_step):
                next(moe, None)
        keys_back(head, 0, prev)
    latent_back(key_prev, 0)
    prevs = scatter_stream(sems, at, key_prev, k0, k1, k2, own_rows, keep_prev)
    next(prevs)
    for c in loads:
        c.wait()
    for head in range(2):
        dkey[prev:] = jnp.zeros_like(dkey[prev:])
        dvalue[prev:] = jnp.zeros_like(dvalue[prev:])
        for i in range(rows // ATT):
            r = slice(ATT * i, ATT * (i + 1))
            total = dquery[head, r] + block_back(head, ATT * i, ATT, prev, prev + ATT * (i + 1), True)
            dquery[head, r] = total * SCALE
            if head == 1:
                lane = lax.broadcasted_iota(jnp.int32, (ATT, 2 * ROPE), 1)
                rope = jnp.where(lane < ROPE, dquery[0, r, NOPE:], dquery[1, r, NOPE:])
                rope = rope * cosine[r] - swapped(rope) * sine[r]
                turned = pltpu.roll(dquery[1, r, :NOPE], ROPE, 1)
                dq[r, :NOPE] = dquery[0, r, :NOPE].astype(bf16)
                dq[r, NOPE : 2 * NOPE] = jnp.where(lane < ROPE, rope, turned).astype(bf16)
                dq[r, 2 * NOPE :] = jnp.where(lane < ROPE, turned, rope).astype(bf16)
            if (head, i) in ((0, 2), (1, 0), (1, 2)):
                next(prevs, None)
            if (head, i) == (1, 1):
                together(moe)
        keys_back(head, prev, prev + rows)
    latent_back(key_own, prev)
    spots, wide = kvo.shape[0], kvo.shape[2]
    kv = dot_tn(keys_all[:, :LAT], dpacked[...]).astype(bf16)
    kv_rows = kv.shape[0] // spots
    kvo[:, :kv_rows] = kv.reshape(spots, kv_rows, wide)
    out_rows = wo.shape[0] // spots
    for j in range(grad.shape[1] // wide):
        term = dot_tn(heads[...], grad[:, j * wide : (j + 1) * wide]).astype(bf16)
        kvo[:, kv_rows + j * out_rows : kv_rows + (j + 1) * out_rows] = term.reshape(spots, out_rows, wide)
    together(prevs)
    sems.finish()


def attend_back(grad, wo, heads, q, packed, keys_all, segs, lse, kv_proj, moe_part, residual, cosine, sine):
    whole = pl.BlockSpec(memory_space=VM)
    held = pl.BlockSpec(memory_space=pl.ANY)
    rows, keys = q.shape[0], packed.shape[0]
    own_rows, width = residual.shape
    spots = lax.axis_size("seq")
    kvo_rows = (kv_proj.shape[0] * kv_proj.shape[1] + wo.shape[0] * wo.shape[1]) // spots // LAT
    return pl.pallas_call(
        attend_back_kernel,
        out_shape=[
            jax.ShapeDtypeStruct(q.shape, bf16),
            jax.ShapeDtypeStruct((rows, SPAN), bf16),
            jax.ShapeDtypeStruct((own_rows, SPAN), bf16),
            jax.ShapeDtypeStruct((spots, kvo_rows, LAT), bf16),
            jax.ShapeDtypeStruct((own_rows, width), bf16),
        ],
        in_specs=[whole] * 11 + [held] * 2,
        out_specs=[whole] * 5,
        scratch_shapes=[
            pltpu.VMEM((rows, SPAN), bf16),
            pltpu.VMEM((rows, 2 * VDIM), bf16),
            pltpu.VMEM((keys, 2 * NOPE), f32),
            pltpu.VMEM((keys, VDIM), f32),
            pltpu.VMEM((keys, 2 * ROPE), f32),
            pltpu.VMEM(packed.shape, bf16),
            pltpu.VMEM((2, rows, 2 * NOPE), f32),
            pltpu.VMEM((rows, 2 * ROPE), f32),
            pltpu.VMEM((rows, 2 * ROPE), f32),
            *scatter_scratch(own_rows, width),
            *scatter_scratch(own_rows, SPAN),
            pltpu.SemaphoreType.DMA((20,)),
            pltpu.SemaphoreType.DMA((20,)),
            pltpu.SemaphoreType.DMA((2,)),
        ],
        compiler_params=pltpu.CompilerParams(collective_id=4, has_side_effects=True, vmem_limit_bytes=60 << 20),
        name="attend_back",
    )(grad, wo, heads, q, packed, keys_all, segs, lse, kv_proj, moe_part, residual, cosine, sine)


SEQ_TURNS = (1, 2, 3, 4, 5, 6)


def tail_kernel(
    dq, key_own, prev_out, kvo, raw, latent_gain, gain, router_in, ffn_in,
    normed_h, wq_h, wl_h, upstream_h, rows_h, cosine_h, sine_h,
    query_out, kvo_out, latent_out, grad_out, small_out,
    work0, work1, own_sum, in_part, in_sum, in_own, lat_rows, lat_all, lat_work, lat_sum, prev_in, small,
    r0, r1, r2, s0, s1, s2, k0, k1, k2, n0, n1, n2, lw, ln,
    normed, wq, wl, upstream, rows_in, cosine, sine, send, recv, local,
):
    at = Place()
    sems = Sems(send, recv)
    rows = raw.shape[0]
    half = rows // 2
    own = pl.ds(pl.multiple_of(at.me * rows, rows), rows)
    spot = pl.ds(pl.multiple_of(lax.rem(at.y, 2) * 8 * rows + at.me * rows, rows), rows)
    sources = (
        (normed_h, normed), (wq_h, wq), (wl_h, wl), (cosine_h.at[spot], cosine), (sine_h.at[spot], sine),
        (upstream_h, upstream), (rows_h, rows_in),
    )
    loads = [pltpu.make_async_copy(src, dst, local.at[2 + i]) for i, (src, dst) in enumerate(sources)]
    for c in loads:
        c.start()
    greet([at.sibling] + [at.hop(axis, d) for axis in range(3) for d in (1, 2, 3)])

    def keep_own(h, total):
        own_sum[h * half : (h + 1) * half] = total

    def keep_in(h, total):
        in_sum[h * half : (h + 1) * half] = total

    swap = sems.start(prev_out, prev_in, at.across[1](at.y + 1 - 2 * lax.rem(at.y, 2)))
    owns = scatter_stream(sems, at, key_own, k0, k1, k2, rows, keep_own)
    next(owns)
    work1[...] = kvo[...]
    second = seq_stream(sems, at, work1, kvo_out, (s0, s1, s2), (2, 1))
    next(second)
    next(owns)
    next(owns)
    loads[0].wait()
    work0[...] = dot_tn(normed[...], dq[...]).astype(bf16).reshape(work0.shape)
    first = seq_stream(sems, at, work0, query_out, (r0, r1, r2), (1, 2))
    next(first)
    next(owns)
    loads[1].wait()
    gain_part = jnp.zeros((1, normed.shape[1]), f32)
    step = 256
    for i in range(dq.shape[0] // step):
        r = pl.ds(i * step, step)
        part = dot_nt(dq[r], wq[...])
        gain_part = gain_part + jnp.sum(part * normed[r].astype(f32), axis=0, keepdims=True)
        in_part[r] = part.astype(bf16)
    in_rows = scatter_stream(sems, at, in_part, n0, n1, n2, rows, keep_in)
    running = []

    def latents():
        together(owns)
        swap.wait_recv()
        own_grad = own_sum[...] + jnp.where(lax.rem(at.y, 2) == 0, prev_in[...].astype(f32), 0.0)
        x = raw[...]
        inverse = lax.rsqrt(jnp.mean(x * x, axis=1, keepdims=True) + EPSILON)
        u = own_grad[:, :LAT]
        lat_gain_part = jnp.sum(u * x * inverse, axis=0, keepdims=True)
        s = u * latent_gain[...]
        inner = jnp.mean(s * x, axis=1, keepdims=True)
        lat_rows[:, :LAT] = (inverse * s - x * (inverse * inverse * inverse) * inner).astype(bf16)
        rope = own_grad[:, LAT:]
        loads[3].wait()
        loads[4].wait()
        rope = rope * cosine[...] - swapped(rope) * sine[...]
        lane = lax.broadcasted_iota(jnp.int32, rope.shape, 1)
        lat_rows[:, LAT:] = jnp.where(lane < ROPE, rope, 0.0).astype(bf16)
        gathered = gather_stream(sems, at, lat_rows, lat_all, rows, local.at[0])
        next(gathered)
        running.append(in_rows)
        loads[2].wait()
        in_own[...] = dot_nn(lat_rows[:, : LAT + ROPE], wl[...])
        attn_gain = gain_part + jnp.sum(in_own[...] * normed[own].astype(f32), axis=0, keepdims=True)
        small_out[:EXPERTS] = router_in[...]
        small_out[EXPERTS:] = jnp.zeros_like(router_in)
        small_out[EXPERTS : EXPERTS + 1] = attn_gain / gain[...]
        small_out[EXPERTS + 1 : EXPERTS + 2] = ffn_in[...]
        small_out[EXPERTS + 2 : EXPERTS + 3, :LAT] = lat_gain_part
        running.append(small_stream(sems, at, small, small_out))
        yield from gathered
        width = lat_work.shape[0] * lat_work.shape[1]
        mine = normed[:, pl.ds(pl.multiple_of(at.me * width, width), width)]
        lat_work[...] = dot_tn(mine, lat_all[...]).astype(bf16).reshape(lat_work.shape)
        yield from seq_direct(sems, at, lat_work, lat_sum, lw, ln)
        yield from gather_stream(sems, at, lat_sum, latent_out, lat_sum.shape[0], local.at[1])

    chain = latents()
    running.append(chain)
    count = 0
    while running:
        for stream in list(running):
            try:
                next(stream)
            except StopIteration:
                running.remove(stream)
        count += 1
        if count in SEQ_TURNS:
            next(first, None)
            next(second, None)
    together(first, second)
    loads[5].wait()
    loads[6].wait()
    u = in_sum[...] + in_own[...]
    x = rows_in[...].astype(f32)
    inverse = lax.rsqrt(jnp.mean(x * x, axis=1, keepdims=True) + EPSILON)
    s = u * gain[...]
    inner = jnp.mean(s * x, axis=1, keepdims=True)
    grad_out[...] = (upstream[...] + (inverse * s - x * (inverse * inverse * inverse) * inner)).astype(bf16)
    sems.finish()


def tail(dq, key_own, prev_out, kvo, normed, wq, wl, raw, latent_gain, gain, upstream, rows_in, router_in, ffn_in, cosine, sine):
    whole = pl.BlockSpec(memory_space=VM)
    rows, width = rows_in.shape
    spots = kvo.shape[0]
    query_shape = (spots, width // spots, dq.shape[1])
    slice_rows = width // lax.axis_size("exp") // spots
    lat_shape = (spots, slice_rows, SPAN)
    return pl.pallas_call(
        tail_kernel,
        out_shape=[
            jax.ShapeDtypeStruct(query_shape, bf16),
            jax.ShapeDtypeStruct(kvo.shape, bf16),
            jax.ShapeDtypeStruct((8 * spots, slice_rows, SPAN), bf16),
            jax.ShapeDtypeStruct((rows, width), bf16),
            jax.ShapeDtypeStruct((2 * EXPERTS, width), f32),
        ],
        in_specs=[whole] * 9 + [pl.BlockSpec(memory_space=pl.ANY)] * 7,
        out_specs=[whole] * 5,
        scratch_shapes=[
            pltpu.VMEM(query_shape, bf16),
            pltpu.VMEM(kvo.shape, bf16),
            pltpu.VMEM((rows, SPAN), f32),
            pltpu.VMEM((8 * rows, width), bf16),
            pltpu.VMEM((rows, width), f32),
            pltpu.VMEM((rows, width), f32),
            pltpu.VMEM((rows, SPAN), bf16),
            pltpu.VMEM((8 * rows, SPAN), bf16),
            pltpu.VMEM(lat_shape, bf16),
            pltpu.VMEM(lat_shape, bf16),
            pltpu.VMEM((rows, SPAN), bf16),
            pltpu.VMEM((4, 4, 2 * EXPERTS, width), bf16),
            *seq_scratch(*query_shape[1:]),
            *seq_scratch(*kvo.shape[1:]),
            *scatter_scratch(rows, SPAN),
            *scatter_scratch(rows, width),
            pltpu.VMEM((3, 4, slice_rows, SPAN), bf16),
            pltpu.VMEM((3, slice_rows, SPAN), bf16),
            pltpu.VMEM(normed.shape, bf16),
            pltpu.VMEM(wq.shape, bf16),
            pltpu.VMEM(wl.shape, bf16),
            pltpu.VMEM(upstream.shape, f32),
            pltpu.VMEM(rows_in.shape, bf16),
            pltpu.VMEM((rows, 2 * ROPE), f32),
            pltpu.VMEM((rows, 2 * ROPE), f32),
            pltpu.SemaphoreType.DMA((130,)),
            pltpu.SemaphoreType.DMA((130,)),
            pltpu.SemaphoreType.DMA((9,)),
        ],
        compiler_params=pltpu.CompilerParams(collective_id=3, has_side_effects=True, vmem_limit_bytes=60 << 20),
        name="tail",
    )(dq, key_own, prev_out, kvo, raw, latent_gain, gain, router_in, ffn_in, normed, wq, wl, upstream, rows_in, cosine, sine)


def start_kernel(
    rows_in, gain, latent_gain, routes, wl_h, wq_h, kv_proj_h, cosine_h, sine_h,
    normed_h, q_h, packed_h, keys_h, hot_all, raw,
    normed, q, packed, keys, wl, wq, kv_proj,
    own_normed, ext, ext_all, prev_out, cosine, sine, send, recv, local, load, store,
):
    at = Place()
    sems = Sems(send, recv)
    rows = rows_in.shape[0]
    block = 8 * rows
    half_seq = pl.ds(pl.multiple_of(lax.rem(at.y, 2) * block, block), block)
    sources = (
        (wl_h, wl), (cosine_h.at[half_seq], cosine), (sine_h.at[half_seq], sine), (wq_h, wq), (kv_proj_h, kv_proj),
    )
    loads = [pltpu.make_async_copy(src, dst, load.at[i]) for i, (src, dst) in enumerate(sources)]
    for c in loads:
        c.start()
    partner = at.across[1](at.y + 1 - 2 * lax.rem(at.y, 2))
    count = announce([at.hop(0, 1), at.hop(0, 3), at.sibling, partner])
    x = rows_in[...].astype(f32)
    own_normed[...] = (x * lax.rsqrt(jnp.mean(x * x, axis=1, keepdims=True) + EPSILON) * gain[...]).astype(bf16)
    meet(count)
    big = gather_stream(sems, at, own_normed, normed, rows, local.at[0])
    next(big)
    loads[0].wait()
    lat = dot_nt(own_normed[...], wl[...])
    raw[...] = lat[:, :LAT]
    x = lat[:, :LAT]
    x = x * lax.rsqrt(jnp.mean(x * x, axis=1, keepdims=True) + EPSILON) * latent_gain[...]
    rope = jnp.concatenate([lat[:, LAT:], lat[:, LAT:]], axis=1)
    loads[1].wait()
    loads[2].wait()
    own = pl.ds(pl.multiple_of(at.me * rows, rows), rows)
    rope = rope * cosine[own] + swapped(rope) * sine[own]
    number = lax.broadcasted_iota(jnp.int32, (128, rows), 0)
    hot = jnp.zeros((128, rows), f32)
    for k in range(routes.shape[0]):
        hot = hot + jnp.where(number == routes[k : k + 1], 1.0, 0.0)
    hot = pltpu.roll(jnp.transpose(hot), ROPE, 1)
    lane = lax.broadcasted_iota(jnp.int32, rope.shape, 1)
    prev_out[:, :LAT] = x.astype(bf16)
    prev_out[:, LAT:] = jnp.where(lane < ROPE, rope, hot).astype(bf16)
    swap = sems.start(prev_out, ext.at[:, pl.ds(SPAN, SPAN)], partner)
    ext[:, :SPAN] = prev_out[...]
    next(big)
    swap.wait_recv()
    little = gather_stream(sems, at, ext, ext_all, rows, local.at[1])
    next(little)
    together(big)
    stores = [pltpu.make_async_copy(normed, normed_h, store.at[0])]
    stores[0].start()
    loads[3].wait()
    loads[4].wait()
    step = 256
    lane = lax.broadcasted_iota(jnp.int32, (step, 2 * ROPE), 1)
    for i in range(block // step):
        r = pl.ds(i * step, step)
        query = dot_nn(normed[r], wq[...])
        q[r, :NOPE] = query[:, :NOPE].astype(bf16)
        one, two = query[:, NOPE : 2 * NOPE], query[:, 2 * NOPE :]
        q[r, NOPE : 2 * NOPE] = jnp.where(lane < ROPE, pltpu.roll(one, ROPE, 1), pltpu.roll(two, ROPE, 1)).astype(bf16)
        rope = jnp.where(lane < ROPE, one, two)
        q[r, 2 * NOPE :] = (rope * cosine[r] + swapped(rope) * sine[r]).astype(bf16)
        if i % 2:
            next(little, None)
    stores.append(pltpu.make_async_copy(q, q_h, store.at[1]))
    stores[1].start()
    together(little)
    for part in range(2):
        r = pl.ds((1 - part) * block, block)
        keys[r, :LAT] = ext_all[:, part * SPAN : part * SPAN + LAT]
        rope = ext_all[:, part * SPAN + LAT : (part + 1) * SPAN].astype(f32)
        turned = pltpu.roll(rope, ROPE, 1)
        if part == 0:
            hot_all[...] = turned.astype(bf16)
        wide_lane = lax.broadcasted_iota(jnp.int32, rope.shape, 1)
        keys[r, LAT:] = jnp.where(wide_lane < ROPE, rope, turned).astype(bf16)
        packed[r] = dot_nn(ext_all[:, part * SPAN : part * SPAN + LAT], kv_proj[...]).astype(bf16)
        for ref, dst in ((keys, keys_h), (packed, packed_h)):
            stores.append(pltpu.make_async_copy(ref.at[r], dst.at[r], store.at[len(stores)]))
            stores[-1].start()
    for c in stores:
        c.wait()
    sems.finish()


def start(rows_in, gain, wl, latent_gain, wq, kv_proj, routes, cosine, sine):
    whole = pl.BlockSpec(memory_space=VM)
    held = pl.BlockSpec(memory_space=pl.ANY)
    rows, width = rows_in.shape
    block = 8 * rows
    shapes = [(block, width), (block, wq.shape[1]), (2 * block, kv_proj.shape[1]), (2 * block, SPAN)]
    return pl.pallas_call(
        start_kernel,
        out_shape=[jax.ShapeDtypeStruct(shape, bf16) for shape in shapes]
        + [jax.ShapeDtypeStruct((block, 2 * ROPE), bf16), jax.ShapeDtypeStruct((rows, LAT), f32)],
        in_specs=[whole] * 4 + [held] * 5,
        out_specs=[held] * 4 + [whole] * 2,
        scratch_shapes=[pltpu.VMEM(shape, bf16) for shape in shapes]
        + [pltpu.VMEM(x.shape, bf16) for x in (wl, wq, kv_proj)]
        + [
            pltpu.VMEM((rows, width), bf16),
            pltpu.VMEM((rows, 2 * SPAN), bf16),
            pltpu.VMEM((block, 2 * SPAN), bf16),
            pltpu.VMEM((rows, SPAN), bf16),
            pltpu.VMEM((block, 2 * ROPE), f32),
            pltpu.VMEM((block, 2 * ROPE), f32),
            pltpu.SemaphoreType.DMA((27,)),
            pltpu.SemaphoreType.DMA((27,)),
            pltpu.SemaphoreType.DMA((2,)),
            pltpu.SemaphoreType.DMA((5,)),
            pltpu.SemaphoreType.DMA((6,)),
        ],
        compiler_params=pltpu.CompilerParams(collective_id=0, has_side_effects=True, vmem_limit_bytes=56 << 20),
        name="start",
    )(rows_in, gain, latent_gain, routes, wl, wq, kv_proj, cosine, sine)


def finish_kernel(
    weights_h, query_h, kvo_h, latent_h, small, early,
    expert_gate_h, expert_down_h, shared_gate_h, shared_down_h, query_out_h, kv_out_h, out_out_h, latent_out_h,
    router_out, attn_out, ffn_out, lat_gain_out,
    weights, query, kvo, latent, expert_gate, expert_down, shared_gate, shared_down, query_out, kv_out, out_out, latent_out,
    load, store,
):
    pairs = ((latent_h, latent), (query_h, query), (kvo_h, kvo), (weights_h, weights))
    loads = [pltpu.make_async_copy(src, dst, load.at[i]) for i, (src, dst) in enumerate(pairs)]
    for c in loads:
        c.start()
    stores = []

    def put(src, dst):
        c = pltpu.make_async_copy(src, dst, store.at[len(stores)])
        c.start()
        stores.append(c)

    router_out[...] = small[:EXPERTS]
    attn_out[...] = small[EXPERTS : EXPERTS + 1]
    ffn_out[...] = small[EXPERTS + 1 : EXPERTS + 2]
    lat_gain_out[...] = small[EXPERTS + 2 : EXPERTS + 3, :LAT]
    loads[0].wait()
    step = 512
    for i in range(latent_out.shape[1] // step):
        spot = step // latent.shape[1]
        rows = latent[i * spot : (i + 1) * spot].reshape(step, latent.shape[2]).astype(f32)
        latent_out[:, i * step : (i + 1) * step] = jnp.transpose(rows)[: latent_out.shape[0]]
    put(latent_out, latent_out_h)
    loads[1].wait()
    query_out[...] = query[...].reshape(query_out.shape).astype(f32)
    put(query_out, query_out_h)
    loads[2].wait()
    spots, _, wide = kvo.shape
    kv_rows = kv_out.shape[0] // spots
    kv_out[...] = kvo[:, :kv_rows].reshape(kv_out.shape).astype(f32)
    put(kv_out, kv_out_h)
    out_rows = out_out.shape[0] // spots
    for j in range(out_out.shape[1] // wide):
        piece = kvo[:, kv_rows + j * out_rows : kv_rows + (j + 1) * out_rows]
        out_out[:, j * wide : (j + 1) * wide] = piece.reshape(out_out.shape[0], wide).astype(f32)
    put(out_out, out_out_h)
    loads[3].wait()
    for c in range(expert_gate.shape[1] // 128):
        expert_gate[:, c * 128 : (c + 1) * 128] = weights[c * 128 : (c + 1) * 128].astype(f32)
    put(expert_gate, expert_gate_h)
    spot = expert_gate.shape[1]
    for ref, dst in ((expert_down, expert_down_h), (shared_gate, shared_gate_h), (shared_down, shared_down_h)):
        skip = 0
        if ref is expert_down:
            skip = early.shape[0]
            ref[:skip] = early[...].astype(f32)
        ref[skip:] = weights[spot : spot + ref.shape[0] - skip].astype(f32)
        put(ref, dst)
        spot += ref.shape[0] - skip
    for c in stores:
        c.wait()


def finish(weights, query, kvo, latent, small, early, shared, model_width, kv_shape, out_shape):
    whole = pl.BlockSpec(memory_space=VM)
    held = pl.BlockSpec(memory_space=pl.ANY)
    shapes = [
        (128, 2 * F), (F, 128), (2 * shared, 128), (shared, 128),
        (model_width, query.shape[2]), kv_shape, out_shape, (LAT + ROPE, model_width),
    ]
    little = [(EXPERTS, model_width), (1, model_width), (1, model_width), (1, LAT)]
    return pl.pallas_call(
        finish_kernel,
        out_shape=[jax.ShapeDtypeStruct(shape, f32) for shape in shapes + little],
        in_specs=[held] * 4 + [whole] * 2,
        out_specs=[held] * 8 + [whole] * 4,
        scratch_shapes=[pltpu.VMEM(x.shape, bf16) for x in (weights, query, kvo, latent)]
        + [pltpu.VMEM(shape, f32) for shape in shapes]
        + [pltpu.SemaphoreType.DMA((4,)), pltpu.SemaphoreType.DMA((8,))],
        compiler_params=pltpu.CompilerParams(vmem_limit_bytes=56 << 20),
        name="finish",
    )(weights, query, kvo, latent, small, early)


def tables(seq_rows):
    lane = np.arange(2 * ROPE)
    half = ROPE // 2
    frequency = np.exp((lane % half) * (-math.log(10000.0) / half))
    angles = np.arange(seq_rows)[:, None] * frequency[None, :]
    sign = np.where(lane % ROPE < half, -1.0, 1.0)
    return np.cos(angles).astype(np.float32), (np.sin(angles) * sign[None, :]).astype(np.float32)


def local(
    layer_input, attn_gain, query_proj, latent_proj, latent_gain, kv_proj, output_proj, ffn_gain, router_proj,
    shared_gate_up, shared_down, expert_gate_up, expert_down, segment_ids, expert_routes, out_grad,
):
    own_rows, model_width = layer_input.shape
    cosine, sine = tables(2 * own_rows * lax.axis_size("exp"))
    wl = latent_proj.T
    router = router_proj.T
    shared = shared_down.shape[0]
    pair_s = shared_gate_up.transpose(1, 2, 0).reshape(2 * shared, model_width)
    pair_e, down_e = expert_gate_up[0], expert_down[0]
    segs = segment_ids[None]
    attn_row, latent_row, ffn_row = attn_gain[None], latent_gain[None], ffn_gain[None]
    normed_all, q, packed, keys, hot, latent_raw = start(
        layer_input, attn_row, wl, latent_row, query_proj, kv_proj, expert_routes.T, cosine, sine
    )
    heads, lse, residual, own_mid = attend(q, packed, keys, segs, output_proj, layer_input, ffn_row)
    terms, act, dpre, logit, router_term, early = mlp(
        own_mid, out_grad, pair_s, pair_e, shared_down, down_e, router, hot
    )
    weight_sum = lax.psum_scatter(terms.reshape(-1, 128), "seq", scatter_dimension=0, tiled=True)
    residual_grad, ffn_term, attn_grad_all, moe_part = turn(
        dpre, act, pair_s, pair_e, shared_down, down_e, logit, router, residual, ffn_row, out_grad
    )
    dq, key_own, prev_sum, kvo, layer_output = attend_back(
        attn_grad_all, output_proj, heads, q, packed, keys, segs, lse, kv_proj, moe_part, residual, cosine, sine
    )
    query_sum, kvo_sum, latent_sum, input_grad, small = tail(
        dq, key_own, prev_sum, kvo, normed_all, query_proj, wl, latent_raw, latent_row, attn_row,
        residual_grad, layer_input, router_term, ffn_term, cosine, sine,
    )
    (
        expert_gate, expert_down_sum, shared_gate, shared_down_sum, query_sum, kv_sum, output_sum, latent_sum,
        router_sum, attn_gain_sum, ffn_gain_sum, latent_gain_sum,
    ) = finish(
        weight_sum, query_sum, kvo_sum, latent_sum, small, early, shared, model_width, kv_proj.shape, output_proj.shape
    )
    return (
        layer_output,
        input_grad,
        attn_gain_sum[0],
        query_sum,
        latent_sum.T,
        latent_gain_sum[0],
        kv_sum,
        output_sum,
        ffn_gain_sum[0],
        router_sum.T,
        shared_gate.reshape(2, shared, 128).transpose(2, 0, 1),
        shared_down_sum,
        expert_gate[None],
        expert_down_sum[None],
    )


def solution(mesh):
    in_specs = (
        P(("seq", "exp"), None),
        P(),
        P(None, "exp"),
        P(),
        P(),
        P(None, "exp"),
        P("exp", None),
        P(),
        P(),
        P(None, None, "exp"),
        P("exp", None),
        P("exp", None, None),
        P("exp", None, None),
        P(),
        P(("seq", "exp"), None),
        P(("seq", "exp"), None),
    )
    out_specs = (
        P(("seq", "exp"), None),
        P(("seq", "exp"), None),
        P(),
        P(None, "exp"),
        P(),
        P(),
        P(None, "exp"),
        P("exp", None),
        P(),
        P(),
        P("seq", None, "exp"),
        P("exp", "seq"),
        P("exp", "seq", None),
        P("exp", None, "seq"),
    )
    return jax.shard_map(local, mesh=mesh, in_specs=in_specs, out_specs=out_specs, check_vma=False)
```

```python
import functools
import math

import jax
import jax.numpy as jnp
import numpy as np
from jax import lax
from jax.experimental import pallas as pl
from jax.experimental.pallas import tpu as pltpu
from jax.sharding import PartitionSpec as P

NOPE = 128
ROPE = 64
VDIM = 128
LAT = 512
F = 1408
EXPERTS = 8
EPSILON = 1e-06

VM = pltpu.VMEM
f32 = jnp.float32
bf16 = jnp.bfloat16


class Sems:
    def __init__(self, send, recv):
        self.send, self.recv, self.used, self.sent = send, recv, 0, []

    def start(self, src, dst, peer):
        copy = pltpu.make_async_remote_copy(
            src_ref=src,
            dst_ref=dst,
            send_sem=self.send.at[self.used],
            recv_sem=self.recv.at[self.used],
            device_id=peer,
            device_id_type=pl.DeviceIdType.MESH,
        )
        copy.start()
        self.used += 1
        self.sent.append(copy)
        return copy

    def finish(self):
        for copy in self.sent:
            copy.wait_send()


class Place:
    def __init__(self):
        me, spot = lax.axis_index("exp"), lax.axis_index("seq")
        self.me = me
        self.chip, self.core = me // 2, me % 2
        self.z, self.y = spot // 4, spot % 4
        self.sibling = {"exp": self.chip * 2 + 1 - self.core}
        self.across = [lambda i: {"exp": i * 2 + self.core}, lambda i: {"seq": self.z * 4 + i}, lambda i: {"seq": i * 4 + self.y}]
        self.along = [self.chip, self.y, self.z]

    def hop(self, axis, distance):
        return self.across[axis](lax.rem(self.along[axis] + distance, 4))


def announce(peers):
    barrier = pltpu.get_barrier_semaphore()
    for peer in peers:
        pl.semaphore_signal(barrier, inc=1, device_id=peer, device_id_type=pl.DeviceIdType.MESH)
    return len(peers)


def meet(count):
    pl.semaphore_wait(pltpu.get_barrier_semaphore(), count)


def greet(peers):
    meet(announce(peers))


def together(*streams):
    streams = list(streams)
    while streams:
        for stream in list(streams):
            try:
                next(stream)
            except StopIteration:
                streams.remove(stream)


def gather_stream(sems, at, src, out, rows, local, arrived=None, stride=None, offset=0):
    half = rows // 2
    stride = stride or rows
    right, left = at.hop(0, 1), at.hop(0, 3)
    me = at.me
    near_right = lax.rem(at.chip + 1, 4) * 2 + at.core
    near_left = lax.rem(at.chip + 3, 4) * 2 + at.core
    far = lax.rem(at.chip + 2, 4) * 2 + at.core

    def part(owner, h):
        return out.at[pl.ds(pl.multiple_of(owner * stride + offset + h * half, half), half)]

    def own(h):
        return src.at[pl.ds(h * half, half)]

    ra = sems.start(own(0), part(me, 0), right)
    lb = sems.start(own(1), part(me, 1), left)
    rb = sems.start(own(1), part(me, 1), right)
    la = sems.start(own(0), part(me, 0), left)
    sib = [sems.start(src, out.at[pl.ds(pl.multiple_of(me * stride + offset, rows), rows)], at.sibling)]
    mine = pltpu.make_async_copy(src, out.at[pl.ds(pl.multiple_of(me * stride + offset, rows), rows)], local)
    mine.start()
    if arrived is None:
        yield
    else:
        mine.wait()
        sib[0].wait_recv()
        arrived(0)
    ra.wait_recv()
    far_a = sems.start(part(near_left, 0), part(near_left, 0), right)
    sib.append(sems.start(part(near_left, 0), part(near_left, 0), at.sibling))
    lb.wait_recv()
    far_b = sems.start(part(near_right, 1), part(near_right, 1), left)
    sib.append(sems.start(part(near_right, 1), part(near_right, 1), at.sibling))
    if arrived is None:
        yield
    rb.wait_recv()
    sib.append(sems.start(part(near_left, 1), part(near_left, 1), at.sibling))
    la.wait_recv()
    sib.append(sems.start(part(near_right, 0), part(near_right, 0), at.sibling))
    yield
    if arrived is not None:
        sib[1].wait_recv()
        sib[3].wait_recv()
        arrived(3)
    far_a.wait_recv()
    sib.append(sems.start(part(far, 0), part(far, 0), at.sibling))
    far_b.wait_recv()
    sib.append(sems.start(part(far, 1), part(far, 1), at.sibling))
    yield
    if arrived is None:
        mine.wait()
        for copy in sib:
            copy.wait_recv()
    else:
        sib[2].wait_recv()
        sib[4].wait_recv()
        arrived(1)
        yield
        sib[5].wait_recv()
        sib[6].wait_recv()
        arrived(2)


def scatter_stream(sems, at, src, pair, hop, last, rows, done, ready=None, stride=None, offset=0):
    half = rows // 2
    stride = stride or rows
    right, left = at.hop(0, 1), at.hop(0, 3)
    order = (2, 1, 3, 0)
    sib = []

    def offer(dist):
        if ready is not None:
            ready(dist)
        owner = lax.rem(at.chip + dist, 4) * 2 + 1 - at.core
        sib.append(sems.start(src.at[pl.ds(pl.multiple_of(owner * stride + offset, rows), rows)], pair.at[dist], at.sibling))

    def fold(i):
        sib[i].wait_recv()
        owner = lax.rem(at.chip + order[i], 4) * 2 + at.core
        mine = src[pl.ds(pl.multiple_of(owner * stride + offset, rows), rows)]
        pair[order[i]] = (pair[order[i]].astype(f32) + mine.astype(f32)).astype(bf16)

    def add(ref, other):
        ref[...] = (ref[...].astype(f32) + other[...].astype(f32)).astype(bf16)

    first, second = pl.ds(0, half), pl.ds(half, half)
    offer(2)
    if ready is not None:
        yield
    offer(1)
    if ready is None:
        offer(3)
        offer(0)
        yield
    fold(0)
    far_a = sems.start(pair.at[2, first], hop.at[0], right)
    far_b = sems.start(pair.at[2, second], hop.at[1], left)
    yield
    if ready is not None:
        offer(3)
    fold(1)
    dir_b = sems.start(pair.at[1, second], last.at[0], right)
    fold(2)
    dir_a = sems.start(pair.at[3, first], last.at[1], left)
    yield
    far_a.wait_recv()
    add(pair.at[1, first], hop.at[0])
    acc_a = sems.start(pair.at[1, first], last.at[2], right)
    far_b.wait_recv()
    add(pair.at[3, second], hop.at[1])
    acc_b = sems.start(pair.at[3, second], last.at[3], left)
    if ready is not None:
        offer(0)
    yield
    sib[3].wait_recv()
    dir_b.wait_recv()
    dir_a.wait_recv()
    acc_a.wait_recv()
    acc_b.wait_recv()
    for h, ends in ((0, (1, 2)), (1, (0, 3))):
        mine = src[pl.ds(pl.multiple_of(at.me * stride + offset + h * half, half), half)].astype(f32)
        total = mine + pair[0, pl.ds(h * half, half)].astype(f32)
        done(h, total + last[ends[0]].astype(f32) + last[ends[1]].astype(f32))


def scatter_scratch(rows, cols):
    return [
        pltpu.VMEM((4, rows, cols), bf16),
        pltpu.VMEM((2, rows // 2, cols), bf16),
        pltpu.VMEM((4, rows // 2, cols), bf16),
    ]


def ring_sum(sems, at, axis, block, hop, last):
    right, left = at.hop(axis, 1), at.hop(axis, 3)
    to = [lax.rem(at.along[axis] + d, 4) for d in range(4)]

    def add(ref, other):
        ref[...] = (ref[...].astype(f32) + other[...].astype(f32)).astype(bf16)

    far_a = sems.start(block(to[2], 0), hop.at[0], right)
    far_b = sems.start(block(to[2], 1), hop.at[1], left)
    dir_b = sems.start(block(to[1], 1), last.at[0], right)
    dir_a = sems.start(block(to[3], 0), last.at[1], left)
    yield
    far_a.wait_recv()
    add(block(to[1], 0), hop.at[0])
    acc_a = sems.start(block(to[1], 0), last.at[2], right)
    far_b.wait_recv()
    add(block(to[3], 1), hop.at[1])
    acc_b = sems.start(block(to[3], 1), last.at[3], left)
    yield
    dir_b.wait_recv()
    dir_a.wait_recv()
    acc_a.wait_recv()
    acc_b.wait_recv()
    for part, (one, two) in ((0, (1, 2)), (1, (0, 3))):
        ref = block(to[0], part)
        ref[...] = (ref[...].astype(f32) + last[one].astype(f32) + last[two].astype(f32)).astype(bf16)


def ring_gather(sems, at, axis, block):
    right, left = at.hop(axis, 1), at.hop(axis, 3)
    to = [lax.rem(at.along[axis] + d, 4) for d in range(4)]
    ra = sems.start(block(to[0], 0), block(to[0], 0), right)
    lb = sems.start(block(to[0], 1), block(to[0], 1), left)
    rb = sems.start(block(to[0], 1), block(to[0], 1), right)
    la = sems.start(block(to[0], 0), block(to[0], 0), left)
    yield
    ra.wait_recv()
    fa = sems.start(block(to[3], 0), block(to[3], 0), right)
    lb.wait_recv()
    fb = sems.start(block(to[1], 1), block(to[1], 1), left)
    yield
    for copy in (rb, la, fa, fb):
        copy.wait_recv()


def seq_stream(sems, at, work, out, scratch, axes):
    hop, last, narrow_in = scratch
    one, two = at.along[axes[0]], at.along[axes[1]]
    own = one * 4 + two

    def wide(ref):
        return lambda i, h: ref.at[pl.ds(i * 4 + 2 * h, 2)]

    yield from ring_sum(sems, at, axes[0], wide(work), hop, last)
    copies = [sems.start(work.at[one * 4 + lax.rem(two + d, 4)], narrow_in.at[d - 1], at.hop(axes[1], d)) for d in (1, 2, 3)]
    yield
    for copy in copies:
        copy.wait_recv()
    total = work[own].astype(f32) + narrow_in[0].astype(f32)
    out[own] = (total + (narrow_in[1].astype(f32) + narrow_in[2].astype(f32))).astype(bf16)
    copies = [sems.start(out.at[own], out.at[own], at.hop(axes[1], d)) for d in (1, 2, 3)]
    yield
    for copy in copies:
        copy.wait_recv()
    yield from ring_gather(sems, at, axes[0], wide(out))


def seq_scatter(sems, at, work, out, scratch, axes):
    hop, last, narrow_in = scratch
    one, two = at.along[axes[0]], at.along[axes[1]]
    yield from ring_sum(sems, at, axes[0], lambda i, h: work.at[pl.ds(i * 4 + 2 * h, 2)], hop, last)
    copies = [sems.start(work.at[one * 4 + lax.rem(two + d, 4)], narrow_in.at[d - 1], at.hop(axes[1], d)) for d in (1, 2, 3)]
    yield
    for copy in copies:
        copy.wait_recv()
    total = work[one * 4 + two].astype(f32) + narrow_in[0].astype(f32)
    out[...] = (total + (narrow_in[1].astype(f32) + narrow_in[2].astype(f32))).astype(bf16)


def seq_scratch(rows, cols):
    return [
        pltpu.VMEM((2, 2, rows, cols), bf16),
        pltpu.VMEM((4, 2, rows, cols), bf16),
        pltpu.VMEM((3, rows, cols), bf16),
    ]


def seq_direct(sems, at, work, out, wide_in, narrow_in):
    y, z = at.y, at.z
    copies = [sems.start(work.at[pl.ds(lax.rem(y + d, 4) * 4, 4)], wide_in.at[d - 1], at.hop(1, d)) for d in (1, 2, 3)]
    yield
    for copy in copies:
        copy.wait_recv()
    mine = pl.ds(y * 4, 4)
    work[mine] = (
        work[mine].astype(f32) + wide_in[0].astype(f32) + (wide_in[1].astype(f32) + wide_in[2].astype(f32))
    ).astype(bf16)
    copies = [sems.start(work.at[y * 4 + lax.rem(z + d, 4)], narrow_in.at[d - 1], at.hop(2, d)) for d in (1, 2, 3)]
    yield
    for copy in copies:
        copy.wait_recv()
    own = y * 4 + z
    out[own] = (
        work[own].astype(f32) + narrow_in[0].astype(f32) + (narrow_in[1].astype(f32) + narrow_in[2].astype(f32))
    ).astype(bf16)
    copies = [sems.start(out.at[own], out.at[own], at.hop(2, d)) for d in (1, 2, 3)]
    yield
    for copy in copies:
        copy.wait_recv()
    copies = [sems.start(out.at[mine], out.at[mine], at.hop(1, d)) for d in (1, 2, 3)]
    yield
    for copy in copies:
        copy.wait_recv()


def small_stream(sems, at, slots, out):
    stages = [(at.core, 2, lambda d: at.sibling)] + [
        (at.along[axis], 4, functools.partial(at.hop, axis)) for axis in range(3)
    ]
    for stage, (place, count, name) in enumerate(stages):
        slots[stage, place] = out[...].astype(bf16)
        copies = [sems.start(slots.at[stage, place], slots.at[stage, place], name(d)) for d in range(1, count)]
        yield
        for copy in copies:
            copy.wait_recv()
        total = slots[stage, 0].astype(f32)
        for i in range(1, count):
            total = total + slots[stage, i].astype(f32)
        out[...] = total


def swapped(tensor):
    lane = lax.broadcasted_iota(jnp.int32, tensor.shape, 1)
    return jnp.where(lane % 64 < 32, pltpu.roll(tensor, 96, 1), pltpu.roll(tensor, 32, 1))


PAD = 384
EARLY = 768
ROW_STEP = 256


def dot_nn(a, b):
    return lax.dot_general(a, b, (((1,), (0,)), ((), ())), preferred_element_type=f32)


def dot_nt(a, b):
    return lax.dot_general(a, b, (((1,), (1,)), ((), ())), preferred_element_type=f32)


def dot_tn(a, b):
    return lax.dot_general(a, b, (((0,), (0,)), ((), ())), preferred_element_type=f32)


def row_block(index):
    return pl.ds(pl.multiple_of(index * ROW_STEP, ROW_STEP), ROW_STEP)


def router_pieces(router):
    high = router.astype(bf16).astype(f32)
    middle_part = (router - high).astype(bf16).astype(f32)
    low = router - high - middle_part
    fill = jnp.zeros((128 - 3 * EXPERTS, router.shape[1]), f32)
    return jnp.concatenate([high, middle_part, low, fill], axis=0).astype(bf16)


def mlp_kernel(
    own_mid, own_grad, pair_s_h, pair_e_h, down_s_h, down_e_h, grad_h, router, hot,
    terms_h, act_h, dpre_h, logit, router_out, early,
    mid, grad, pair_s, pair_e, down_s, down_e, act, dpre, pieces, stage, work0, work1, r0, r1, r2, s0, s1, s2, load, store, keep, send, recv, local,
):
    at = Place()
    sems = Sems(send, recv)
    rows, width = mid.shape
    shared = down_s.shape[0]
    expert = lax.axis_index("exp")
    sources = [(pair_e_h, pair_e), (pair_s_h, pair_s), (down_s_h, down_s), (down_e_h, down_e)]
    loads = [pltpu.make_async_copy(src, dst, load.at[i]) for i, (src, dst) in enumerate(sources)]
    sent = own_grad.shape[0] // 2
    for owner in range(8):
        here = (grad_h.at[pl.ds(owner * sent, sent)], grad.at[pl.ds(owner * 2 * sent, sent)])
        loads.append(pltpu.make_async_copy(*here, load.at[len(loads)]))
    for c in loads:
        c.start()
    count = announce(
        [at.hop(0, 1), at.hop(0, 3), at.sibling] + [at.hop(axis, d) for axis in (1, 2) for d in (1, 2, 3)]
    )
    pieces[...] = router_pieces(router[...])
    meet(count)
    lane = lax.broadcasted_iota(jnp.int32, (ROW_STEP, 128), 1)
    own_lane = lane == expert

    def gates(r):
        raw = dot_nt(mid[r], pieces[...])
        raw = raw + (pltpu.roll(raw, 128 - EXPERTS, 1) + pltpu.roll(raw, 128 - 2 * EXPERTS, 1))
        raw = jnp.where(lane < EXPERTS, raw, -1e30)
        raw = jnp.exp(raw - jnp.max(raw, axis=1, keepdims=True))
        probs = raw / jnp.sum(raw, axis=1, keepdims=True)
        own = jnp.sum(jnp.where(own_lane, probs * hot[r].astype(f32), 0.0), axis=1, keepdims=True)
        return own, probs

    tiles = [(pair_e, start, min(512, F - start)) for start in range(0, F, 512)]

    def before_activation(dist):
        r = row_block(lax.rem(at.chip + dist, 4))
        if dist == 0:
            loads[0].wait()
        for _, start, size in tiles:
            dpre[r, start : start + size] = dot_nn(mid[r], pair_e[:, start : start + size]).astype(bf16)
            up = dot_nn(mid[r], pair_e[:, F + start : F + start + size])
            dpre[r, F + start : F + start + size] = up.astype(bf16)
        if dist == 0:
            loads[1].wait()
        dpre[r, 2 * F : 2 * F + shared] = dot_nt(mid[r], pair_s[:shared]).astype(bf16)
        dpre[r, 2 * F + PAD : 2 * F + PAD + shared] = dot_nt(mid[r], pair_s[shared:]).astype(bf16)

    def piece(r, dact, act_at, gate_at, up_at, own):
        size = dact.shape[1]
        gate, up = dpre[r, gate_at : gate_at + size].astype(f32), dpre[r, up_at : up_at + size].astype(f32)
        logistic = 1.0 / (1.0 + jnp.exp(-gate))
        passed = gate * logistic
        out = passed * up
        total = None
        if own is not None:
            total = jnp.sum(out * dact, axis=1, keepdims=True)
            out = out * own
            dact = dact * own
        act[r, act_at : act_at + size] = out.astype(bf16)
        slope = logistic + passed * (1.0 - logistic)
        dpre[r, gate_at : gate_at + size] = (dact * up * slope).astype(bf16)
        dpre[r, up_at : up_at + size] = (dact * passed).astype(bf16)
        return total

    mids = gather_stream(sems, at, own_mid, mid, own_mid.shape[0], local.at[0], before_activation)
    grads = gather_stream(sems, at, own_grad.at[pl.ds(sent, sent)], grad, sent, local.at[1], None, 2 * sent, sent)
    next(mids)
    next(grads)
    next(mids)
    next(mids)
    next(grads)
    together(mids)
    together(grads)
    for c in loads[2:]:
        c.wait()

    @pl.loop(0, rows // ROW_STEP)
    def _(index):
        r = row_block(index)
        piece(r, dot_nt(grad[r], down_s[...]), F, 2 * F, 2 * F + PAD, None)
        own, probs = gates(r)
        total = 0.0
        for _, start, size in tiles:
            total = total + piece(r, dot_nt(grad[r], down_e[start : start + size]), start, start, F + start, own)
        logit[r] = ((own * total) * (jnp.where(own_lane, 1.0, 0.0) - probs)).astype(bf16)

    keeps = [pltpu.make_async_copy(act, act_h, keep.at[0]), pltpu.make_async_copy(dpre, dpre_h, keep.at[1])]
    for c in keeps:
        c.start()

    half = width // 2
    slots = half // 128
    early_rows = EARLY // 2
    for work, start, axis in ((work0, 0, 1), (work1, early_rows, 2)):
        for part in range(2):
            value = dot_tn(act[:, start : start + early_rows], grad[:, part * half : (part + 1) * half]).astype(bf16)
            for s in range(slots):
                z, y = divmod(part * slots + s, 4)
                work[y * 4 + z if axis == 1 else z * 4 + y] = value[:, s * 128 : (s + 1) * 128]
    sums = [
        seq_scatter(sems, at, work0, early.at[pl.ds(0, early_rows)], (r0, r1, r2), (1, 2)),
        seq_scatter(sems, at, work1, early.at[pl.ds(early_rows, early_rows)], (s0, s1, s2), (2, 1)),
    ]
    for stream in sums:
        next(stream)
    jobs = []
    for start in range(0, 2 * F, 512):
        size = min(512, 2 * F - start)
        jobs.append((mid, dpre, start, size, start, True))
    for start in range(EARLY, F, 512):
        size = min(512, F - start)
        jobs.append((grad, act, start, size, 2 * F + start - EARLY, False))
    for index, (left, right, start) in enumerate(((mid, dpre, 2 * F), (mid, dpre, 2 * F + PAD), (grad, act, F))):
        jobs.append((left, right, start, shared, 3 * F - EARLY + index * shared, False))

    def flush(part, spot, size):
        return pltpu.make_async_copy(
            stage.at[part, :, pl.ds(0, size)], terms_h.at[pl.ds(part * slots, slots), pl.ds(spot, size)], store.at[part]
        )

    before = None
    for number, (left, right, start, size, spot, by_column) in enumerate(jobs):
        for part in range(2):
            if before is not None:
                flush(part, *before).wait()
            wide = left[:, part * half : (part + 1) * half]
            if by_column:
                value = dot_tn(wide, right[:, start : start + size]).astype(bf16)
                for s in range(slots):
                    for c in range(size // 128):
                        stage[part, s, c * 128 : (c + 1) * 128] = value[s * 128 : (s + 1) * 128, c * 128 : (c + 1) * 128]
            else:
                value = dot_tn(right[:, start : start + size], wide).astype(bf16)
                for s in range(slots):
                    stage[part, s, :size] = value[:, s * 128 : (s + 1) * 128]
            flush(part, spot, size).start()
        before = (spot, size)
        if number in (3, 7):
            for stream in sums:
                next(stream)
    router_out[...] = dot_tn(logit[...], mid[...])[:EXPERTS]
    for part in range(2):
        flush(part, *before).wait()
    for c in keeps:
        c.wait()
    together(*sums)
    sems.finish()


def mlp(own_mid, own_grad, pair_s, pair_e, down_s, down_e, grad_half, router, hot):
    rows, width = 8 * own_mid.shape[0], own_mid.shape[1]
    shared = down_s.shape[0]
    whole = pl.BlockSpec(memory_space=VM)
    held = pl.BlockSpec(memory_space=pl.ANY)
    act_shape, dpre_shape = (rows, F + PAD), (rows, 2 * (F + PAD))
    return pl.pallas_call(
        mlp_kernel,
        out_shape=[
            jax.ShapeDtypeStruct((width // 128, 3 * (F + shared) - EARLY, 128), bf16),
            jax.ShapeDtypeStruct(act_shape, bf16),
            jax.ShapeDtypeStruct(dpre_shape, bf16),
            jax.ShapeDtypeStruct((rows, 128), bf16),
            jax.ShapeDtypeStruct((EXPERTS, width), f32),
            jax.ShapeDtypeStruct((EARLY, 128), bf16),
        ],
        in_specs=[whole] * 2 + [held] * 5 + [whole] * 2,
        out_specs=[held, held, held, whole, whole, whole],
        scratch_shapes=[
            pltpu.VMEM((rows, width), bf16), pltpu.VMEM((rows, width), bf16),
            pltpu.VMEM(pair_s.shape, bf16), pltpu.VMEM(pair_e.shape, bf16),
            pltpu.VMEM(down_s.shape, bf16), pltpu.VMEM(down_e.shape, bf16),
            pltpu.VMEM(act_shape, bf16), pltpu.VMEM(dpre_shape, bf16),
            pltpu.VMEM((128, width), bf16), pltpu.VMEM((2, width // 256, 512, 128), bf16),
            pltpu.VMEM((width // 128, EARLY // 2, 128), bf16), pltpu.VMEM((width // 128, EARLY // 2, 128), bf16),
            *seq_scratch(EARLY // 2, 128), *seq_scratch(EARLY // 2, 128),
            pltpu.SemaphoreType.DMA((12,)), pltpu.SemaphoreType.DMA((2,)), pltpu.SemaphoreType.DMA((2,)),
            pltpu.SemaphoreType.DMA((44,)), pltpu.SemaphoreType.DMA((44,)), pltpu.SemaphoreType.DMA((2,)),
        ],
        compiler_params=pltpu.CompilerParams(collective_id=5, has_side_effects=True, vmem_limit_bytes=62 << 20),
        cost_estimate=pl.CostEstimate(flops=12 * rows * width * (F + shared), bytes_accessed=60 << 20, transcendentals=rows * F),
        name="mlp",
    )(own_mid, own_grad, pair_s, pair_e, down_s, down_e, grad_half, router, hot)


def turn_kernel(
    dpre_h, act_h, pair_s_h, pair_e_h, down_s_h, down_e_h, logit, router, residual, gain, upstream,
    residual_grad, gain_term, grad_all, moe_h,
    moe_part, dpre, act, pair_s, pair_e, down_s, down_e, part, pieces, own_grad, p0, p1, p2, o0, o1, o2, load, send, recv, local,
):
    at = Place()
    sems = Sems(send, recv)
    rows = residual.shape[0]
    half = rows // 2
    shared = down_s.shape[0]
    sources = [
        (pair_e_h.at[:, pl.ds(0, F)], pair_e.at[:, pl.ds(0, F)]),
        (pair_e_h.at[:, pl.ds(F, F)], pair_e.at[:, pl.ds(F, F)]), (pair_s_h, pair_s),
        (act_h, act), (down_e_h, down_e), (down_s_h, down_s),
    ]
    blocks = [row_block(lax.rem(at.chip + dist, 4)) for dist in (2, 1, 3, 0)]
    sources = [(dpre_h.at[blocks[0]], dpre.at[blocks[0]])] + sources
    sources[4:4] = [(dpre_h.at[r], dpre.at[r]) for r in blocks[1:]]
    loads = [pltpu.make_async_copy(src, dst, load.at[i]) for i, (src, dst) in enumerate(sources)]
    for c in loads:
        c.start()
    count = announce([at.hop(0, 1), at.hop(0, 3), at.sibling])
    gain_term[...] = jnp.zeros_like(gain_term)
    pieces[...] = router_pieces(router[...])
    loads[0].wait()

    def ready(dist):
        r = row_block(lax.rem(at.chip + dist, 4))
        if dist == 2:
            loads[1].wait()
        else:
            loads[{1: 4, 3: 5, 0: 6}[dist]].wait()
        total = dot_nt(dpre[r, :F], pair_e[:, :F])
        if dist == 2:
            loads[2].wait()
        total = total + dot_nt(dpre[r, F : 2 * F], pair_e[:, F:])
        if dist == 2:
            loads[3].wait()
        total = total + dot_nn(dpre[r, 2 * F : 2 * F + shared], pair_s[:shared])
        total = total + dot_nn(dpre[r, 2 * F + PAD : 2 * F + PAD + shared], pair_s[shared:])
        part[r] = (total + dot_nn(logit[r], pieces[...])).astype(bf16)
        if dist == 2:
            meet(count)

    def done_from(first):
        def done(h, total):
            r = slice(first + h * (half // 2), first + (h + 1) * (half // 2))
            x = residual[r]
            inverse = lax.rsqrt(jnp.mean(x * x, axis=1, keepdims=True) + EPSILON)
            gain_term[...] += jnp.sum(total * x * inverse, axis=0, keepdims=True)
            s = total * gain[...]
            inner = jnp.mean(s * x, axis=1, keepdims=True)
            grad = upstream[r].astype(f32) + (inverse * s - x * (inverse * inverse * inverse) * inner)
            residual_grad[r] = grad
            own_grad[r] = grad.astype(bf16)

        return done

    def moe(index):
        r = pl.ds(index * ROW_STEP, ROW_STEP)
        moe_part[r] = (dot_nn(act[r, :F], down_e[...]) + dot_nn(act[r, F : F + shared], down_s[...])).astype(bf16)

    ones = scatter_stream(sems, at, part, p0, p1, p2, half, done_from(0), ready, rows, 0)
    twos = scatter_stream(sems, at, part, o0, o1, o2, half, done_from(half), lambda dist: None, rows, half)
    for _ in range(4):
        next(ones)
        next(twos)
    together(ones)
    first = gather_stream(sems, at, own_grad.at[pl.ds(0, half)], grad_all, half, local.at[0], None, rows, 0)
    next(first)
    together(twos)
    second = gather_stream(sems, at, own_grad.at[pl.ds(half, half)], grad_all, half, local.at[1], None, rows, half)
    next(second)
    for c in loads[7:]:
        c.wait()
    for index in range(4):
        moe(index)
        next(first, None)
        next(second, None)
    keep = pltpu.make_async_copy(moe_part, moe_h, load.at[0])
    keep.start()
    together(first, second)
    keep.wait()
    sems.finish()


def turn(dpre, act, pair_s, pair_e, down_s, down_e, logit, router, residual, gain, upstream):
    whole = pl.BlockSpec(memory_space=VM)
    held = pl.BlockSpec(memory_space=pl.ANY)
    rows, width = residual.shape
    return pl.pallas_call(
        turn_kernel,
        out_shape=[
            jax.ShapeDtypeStruct((rows, width), f32),
            jax.ShapeDtypeStruct((1, width), f32),
            jax.ShapeDtypeStruct((8 * rows, width), bf16),
            jax.ShapeDtypeStruct((8 * rows, width), bf16),
        ],
        in_specs=[held] * 6 + [whole] * 5,
        out_specs=[whole] * 3 + [held],
        scratch_shapes=[
            pltpu.VMEM((8 * rows, width), bf16),
            pltpu.VMEM(dpre.shape, bf16), pltpu.VMEM(act.shape, bf16),
            pltpu.VMEM(pair_s.shape, bf16), pltpu.VMEM(pair_e.shape, bf16),
            pltpu.VMEM(down_s.shape, bf16), pltpu.VMEM(down_e.shape, bf16),
            pltpu.VMEM((8 * rows, width), bf16),
            pltpu.VMEM((128, width), bf16),
            pltpu.VMEM((rows, width), bf16),
            *scatter_scratch(rows // 2, width),
            *scatter_scratch(rows // 2, width),
            pltpu.SemaphoreType.DMA((10,)),
            pltpu.SemaphoreType.DMA((46,)),
            pltpu.SemaphoreType.DMA((46,)),
            pltpu.SemaphoreType.DMA((2,)),
        ],
        compiler_params=pltpu.CompilerParams(collective_id=2, has_side_effects=True, vmem_limit_bytes=62 << 20),
        name="turn",
    )(dpre, act, pair_s, pair_e, down_s, down_e, logit, router, residual, gain, upstream)


SPAN = LAT + 2 * ROPE
ATT = 256
SCALE = (NOPE + ROPE) ** (-0.5)
LOG2E = 1.4426950408889634


def segments(segs, count):
    spot = lax.axis_index("seq")
    own = segs[:, pl.ds(pl.multiple_of(spot * count, count), count)].astype(f32)
    before = segs[:, pl.ds(pl.multiple_of(jnp.maximum(spot - 1, 0) * count, count), count)].astype(f32)
    before = jnp.where(lax.rem(spot, 2) == 1, before, -1.0)
    column = jnp.transpose(jnp.broadcast_to(own, (128, count)))[:, :1]
    return column, jnp.concatenate([before, own], axis=1)


def attend_back_kernel(
    segs, wo_h, grad_h, moe_h, packed_h, keys_h, q_h, heads_h, lse_h, residual_h, kv_proj_h, cosine_h, sine_h,
    dq, key_own, prev_out, kvo, layer_out,
    key_prev, head_grad, dkey, dvalue, drope, dpacked, dquery, cosine, sine,
    wo, grad, moe_part, packed, keys_all, q, heads, lse, residual, kv_proj,
    p0, p1, p2, k0, k1, k2, send, recv, load,
):
    at = Place()
    sems = Sems(send, recv)
    rows = q.shape[0]
    prev = packed.shape[0] - rows
    block = pl.ds(pl.multiple_of(lax.rem(at.y, 2) * rows, rows), rows)
    sources = (
        (wo_h, wo), (grad_h, grad), (moe_h, moe_part), (packed_h, packed), (keys_h, keys_all), (q_h, q),
        (heads_h, heads), (lse_h, lse), (residual_h, residual), (kv_proj_h, kv_proj),
        (cosine_h.at[block], cosine), (sine_h.at[block], sine),
    )
    loads = [pltpu.make_async_copy(src, dst, load.at[i]) for i, (src, dst) in enumerate(sources)]
    for c in loads:
        c.start()
    count = announce([at.hop(0, 1), at.hop(0, 3), at.sibling])
    own_rows = residual.shape[0]

    def done(h, total):
        r = slice(h * (own_rows // 2), (h + 1) * (own_rows // 2))
        layer_out[r] = (residual[r] + total).astype(bf16)

    def keep_prev(h, total):
        prev_out[h * (own_rows // 2) : (h + 1) * (own_rows // 2)] = total.astype(bf16)

    step = 256
    loads[0].wait()
    loads[1].wait()
    for i in range(rows // step):
        r = pl.ds(i * step, step)
        head_grad[r] = dot_nt(grad[r], wo[...]).astype(bf16)
    meet(count)
    loads[2].wait()
    moe = scatter_stream(sems, at, moe_part, p0, p1, p2, own_rows, done)
    next(moe)
    for c in loads[3:]:
        c.wait()
    qseg, kseg = segments(segs, rows)

    def block_back(head, start, size, lo, hi, diagonal):
        r = slice(start, start + size)
        lane = lax.broadcasted_iota(jnp.int32, (size, 2 * ROPE), 1)
        rope = jnp.where(lane // ROPE == head, q[r, 2 * NOPE :], jnp.zeros((), bf16))
        query = jnp.concatenate([q[r, head * NOPE : (head + 1) * NOPE], rope], axis=1)
        keys = jnp.concatenate([packed[lo:hi, head * 2 * NOPE : head * 2 * NOPE + NOPE], keys_all[lo:hi, LAT:]], axis=1)
        scores = dot_nt(query, keys)
        allowed = qseg[r] == kseg[:, lo:hi]
        if diagonal:
            ahead = lax.broadcasted_iota(jnp.int32, scores.shape, 1) - lax.broadcasted_iota(jnp.int32, scores.shape, 0)
            allowed = allowed & (ahead <= start)
        p = jnp.exp2(jnp.where(allowed, scores * (SCALE * LOG2E) - lse[head, r], -1e30))
        upstream = head_grad[r, head * VDIM : (head + 1) * VDIM]
        out = heads[r, head * VDIM : (head + 1) * VDIM]
        inner = jnp.sum(upstream.astype(f32) * out.astype(f32), axis=1, keepdims=True)
        d = dot_nt(upstream, packed[lo:hi, head * 2 * NOPE + NOPE : (head + 1) * 2 * NOPE])
        ds = (p * (d - inner)).astype(bf16)
        dkey[lo:hi] += dot_tn(ds, query)
        dvalue[lo:hi] += dot_tn(p.astype(bf16), upstream)
        return dot_nn(ds, keys)

    def keys_back(head, lo, hi):
        dpacked[lo:hi, head * 2 * NOPE : head * 2 * NOPE + NOPE] = (dkey[lo:hi, :NOPE] * SCALE).astype(bf16)
        dpacked[lo:hi, head * 2 * NOPE + NOPE : (head + 1) * 2 * NOPE] = dvalue[lo:hi].astype(bf16)
        if head == 0:
            drope[lo:hi] = dkey[lo:hi, NOPE:]
        else:
            drope[lo:hi] += dkey[lo:hi, NOPE:]

    def latent_back(ref, lo):
        for start in range(0, rows, 512):
            r, to = slice(lo + start, lo + start + 512), slice(start, start + 512)
            ref[to, :LAT] = dot_nt(dpacked[r], kv_proj[...]).astype(bf16)
            rope = drope[r]
            ref[to, LAT:] = ((rope + pltpu.roll(rope, ROPE, 1)) * SCALE).astype(bf16)

    wide_step = 512
    for head in range(2):
        dkey[...] = jnp.zeros_like(dkey)
        dvalue[...] = jnp.zeros_like(dvalue)
        for start in range(0, rows, wide_step):
            dquery[head, start : start + wide_step] = block_back(head, start, wide_step, 0, prev, False)
            if (head, start) != (1, wide_step):
                next(moe, None)
        keys_back(head, 0, prev)
    latent_back(key_prev, 0)
    prevs = scatter_stream(sems, at, key_prev, k0, k1, k2, own_rows, keep_prev)
    next(prevs)
    for head in range(2):
        dkey[prev:] = jnp.zeros_like(dkey[prev:])
        dvalue[prev:] = jnp.zeros_like(dvalue[prev:])
        for i in range(rows // ATT):
            r = slice(ATT * i, ATT * (i + 1))
            total = dquery[head, r] + block_back(head, ATT * i, ATT, prev, prev + ATT * (i + 1), True)
            dquery[head, r] = total * SCALE
            if head == 1:
                lane = lax.broadcasted_iota(jnp.int32, (ATT, 2 * ROPE), 1)
                rope = jnp.where(lane < ROPE, dquery[0, r, NOPE:], dquery[1, r, NOPE:])
                rope = rope * cosine[r] - swapped(rope) * sine[r]
                turned = pltpu.roll(dquery[1, r, :NOPE], ROPE, 1)
                dq[r, :NOPE] = dquery[0, r, :NOPE].astype(bf16)
                dq[r, NOPE : 2 * NOPE] = jnp.where(lane < ROPE, rope, turned).astype(bf16)
                dq[r, 2 * NOPE :] = jnp.where(lane < ROPE, turned, rope).astype(bf16)
            if (head, i) in ((0, 2), (1, 0), (1, 2)):
                next(prevs, None)
            if (head, i) == (1, 1):
                together(moe)
        keys_back(head, prev, prev + rows)
    latent_back(key_own, prev)
    spots, wide = kvo.shape[0], kvo.shape[2]
    kv = dot_tn(keys_all[:, :LAT], dpacked[...]).astype(bf16)
    kv_rows = kv.shape[0] // spots
    kvo[:, :kv_rows] = kv.reshape(spots, kv_rows, wide)
    out_rows = wo.shape[0] // spots
    for j in range(grad.shape[1] // wide):
        term = dot_tn(heads[...], grad[:, j * wide : (j + 1) * wide]).astype(bf16)
        kvo[:, kv_rows + j * out_rows : kv_rows + (j + 1) * out_rows] = term.reshape(spots, out_rows, wide)
    together(prevs)
    sems.finish()


def attend_back(grad, wo, heads, q, packed, keys_all, segs, lse, kv_proj, moe_part, residual, cosine, sine):
    whole = pl.BlockSpec(memory_space=VM)
    held = pl.BlockSpec(memory_space=pl.ANY)
    rows, keys = q.shape[0], packed.shape[0]
    own_rows, width = residual.shape
    spots = lax.axis_size("seq")
    kvo_rows = (kv_proj.shape[0] * kv_proj.shape[1] + wo.shape[0] * wo.shape[1]) // spots // LAT
    return pl.pallas_call(
        attend_back_kernel,
        out_shape=[
            jax.ShapeDtypeStruct(q.shape, bf16),
            jax.ShapeDtypeStruct((rows, SPAN), bf16),
            jax.ShapeDtypeStruct((own_rows, SPAN), bf16),
            jax.ShapeDtypeStruct((spots, kvo_rows, LAT), bf16),
            jax.ShapeDtypeStruct((own_rows, width), bf16),
        ],
        in_specs=[whole] + [held] * 12,
        out_specs=[whole] * 5,
        scratch_shapes=[
            pltpu.VMEM((rows, SPAN), bf16),
            pltpu.VMEM((rows, 2 * VDIM), bf16),
            pltpu.VMEM((keys, 2 * NOPE), f32),
            pltpu.VMEM((keys, VDIM), f32),
            pltpu.VMEM((keys, 2 * ROPE), f32),
            pltpu.VMEM(packed.shape, bf16),
            pltpu.VMEM((2, rows, 2 * NOPE), f32),
            pltpu.VMEM((rows, 2 * ROPE), f32),
            pltpu.VMEM((rows, 2 * ROPE), f32),
            *(
                pltpu.VMEM(x.shape, x.dtype)
                for x in (wo, grad, moe_part, packed, keys_all, q, heads, lse, residual, kv_proj)
            ),
            *scatter_scratch(own_rows, width),
            *scatter_scratch(own_rows, SPAN),
            pltpu.SemaphoreType.DMA((20,)),
            pltpu.SemaphoreType.DMA((20,)),
            pltpu.SemaphoreType.DMA((12,)),
        ],
        compiler_params=pltpu.CompilerParams(collective_id=4, has_side_effects=True, vmem_limit_bytes=60 << 20),
        name="attend_back",
    )(segs, wo, grad, moe_part, packed, keys_all, q, heads, lse, residual, kv_proj, cosine, sine)


SEQ_TURNS = (1, 2, 3, 4, 5, 6)


def tail_kernel(
    dq, key_own, prev_out, kvo, raw, latent_gain, gain, router_in, ffn_in,
    normed_h, wq_h, wl_h, upstream_h, rows_h, cosine_h, sine_h,
    query_out, kvo_out, latent_out, grad_out, small_out,
    work0, work1, own_sum, in_part, in_sum, in_own, lat_rows, lat_all, lat_work, lat_sum, prev_in, small,
    r0, r1, r2, s0, s1, s2, k0, k1, k2, n0, n1, n2, lw, ln,
    normed, wq, wl, upstream, rows_in, cosine, sine, send, recv, local,
):
    at = Place()
    sems = Sems(send, recv)
    rows = raw.shape[0]
    half = rows // 2
    own = pl.ds(pl.multiple_of(at.me * rows, rows), rows)
    spot = pl.ds(pl.multiple_of(lax.rem(at.y, 2) * 8 * rows + at.me * rows, rows), rows)
    sources = (
        (normed_h, normed), (wq_h, wq), (wl_h, wl), (cosine_h.at[spot], cosine), (sine_h.at[spot], sine),
        (upstream_h, upstream), (rows_h, rows_in),
    )
    loads = [pltpu.make_async_copy(src, dst, local.at[2 + i]) for i, (src, dst) in enumerate(sources)]
    for c in loads:
        c.start()
    greet([at.sibling] + [at.hop(axis, d) for axis in range(3) for d in (1, 2, 3)])

    def keep_own(h, total):
        own_sum[h * half : (h + 1) * half] = total

    def keep_in(h, total):
        in_sum[h * half : (h + 1) * half] = total

    swap = sems.start(prev_out, prev_in, at.across[1](at.y + 1 - 2 * lax.rem(at.y, 2)))
    owns = scatter_stream(sems, at, key_own, k0, k1, k2, rows, keep_own)
    next(owns)
    work1[...] = kvo[...]
    second = seq_stream(sems, at, work1, kvo_out, (s0, s1, s2), (2, 1))
    next(second)
    next(owns)
    next(owns)
    loads[0].wait()
    work0[...] = dot_tn(normed[...], dq[...]).astype(bf16).reshape(work0.shape)
    first = seq_stream(sems, at, work0, query_out, (r0, r1, r2), (1, 2))
    next(first)
    next(owns)
    loads[1].wait()
    gain_part = jnp.zeros((1, normed.shape[1]), f32)
    step = 256
    for i in range(dq.shape[0] // step):
        r = pl.ds(i * step, step)
        part = dot_nt(dq[r], wq[...])
        gain_part = gain_part + jnp.sum(part * normed[r].astype(f32), axis=0, keepdims=True)
        in_part[r] = part.astype(bf16)
    in_rows = scatter_stream(sems, at, in_part, n0, n1, n2, rows, keep_in)
    running = []

    def latents():
        together(owns)
        swap.wait_recv()
        own_grad = own_sum[...] + jnp.where(lax.rem(at.y, 2) == 0, prev_in[...].astype(f32), 0.0)
        x = raw[...]
        inverse = lax.rsqrt(jnp.mean(x * x, axis=1, keepdims=True) + EPSILON)
        u = own_grad[:, :LAT]
        lat_gain_part = jnp.sum(u * x * inverse, axis=0, keepdims=True)
        s = u * latent_gain[...]
        inner = jnp.mean(s * x, axis=1, keepdims=True)
        lat_rows[:, :LAT] = (inverse * s - x * (inverse * inverse * inverse) * inner).astype(bf16)
        rope = own_grad[:, LAT:]
        loads[3].wait()
        loads[4].wait()
        rope = rope * cosine[...] - swapped(rope) * sine[...]
        lane = lax.broadcasted_iota(jnp.int32, rope.shape, 1)
        lat_rows[:, LAT:] = jnp.where(lane < ROPE, rope, 0.0).astype(bf16)
        gathered = gather_stream(sems, at, lat_rows, lat_all, rows, local.at[0])
        next(gathered)
        running.append(in_rows)
        loads[2].wait()
        in_own[...] = dot_nn(lat_rows[:, : LAT + ROPE], wl[...])
        attn_gain = gain_part + jnp.sum(in_own[...] * normed[own].astype(f32), axis=0, keepdims=True)
        small_out[:EXPERTS] = router_in[...]
        small_out[EXPERTS:] = jnp.zeros_like(router_in)
        small_out[EXPERTS : EXPERTS + 1] = attn_gain / gain[...]
        small_out[EXPERTS + 1 : EXPERTS + 2] = ffn_in[...]
        small_out[EXPERTS + 2 : EXPERTS + 3, :LAT] = lat_gain_part
        running.append(small_stream(sems, at, small, small_out))
        yield from gathered
        width = lat_work.shape[0] * lat_work.shape[1]
        mine = normed[:, pl.ds(pl.multiple_of(at.me * width, width), width)]
        lat_work[...] = dot_tn(mine, lat_all[...]).astype(bf16).reshape(lat_work.shape)
        yield from seq_direct(sems, at, lat_work, lat_sum, lw, ln)
        yield from gather_stream(sems, at, lat_sum, latent_out, lat_sum.shape[0], local.at[1])

    chain = latents()
    running.append(chain)
    count = 0
    while running:
        for stream in list(running):
            try:
                next(stream)
            except StopIteration:
                running.remove(stream)
        count += 1
        if count in SEQ_TURNS:
            next(first, None)
            next(second, None)
    together(first, second)
    loads[5].wait()
    loads[6].wait()
    u = in_sum[...] + in_own[...]
    x = rows_in[...].astype(f32)
    inverse = lax.rsqrt(jnp.mean(x * x, axis=1, keepdims=True) + EPSILON)
    s = u * gain[...]
    inner = jnp.mean(s * x, axis=1, keepdims=True)
    grad_out[...] = (upstream[...] + (inverse * s - x * (inverse * inverse * inverse) * inner)).astype(bf16)
    sems.finish()


def tail(dq, key_own, prev_out, kvo, normed, wq, wl, raw, latent_gain, gain, upstream, rows_in, router_in, ffn_in, cosine, sine):
    whole = pl.BlockSpec(memory_space=VM)
    rows, width = rows_in.shape
    spots = kvo.shape[0]
    query_shape = (spots, width // spots, dq.shape[1])
    slice_rows = width // lax.axis_size("exp") // spots
    lat_shape = (spots, slice_rows, SPAN)
    return pl.pallas_call(
        tail_kernel,
        out_shape=[
            jax.ShapeDtypeStruct(query_shape, bf16),
            jax.ShapeDtypeStruct(kvo.shape, bf16),
            jax.ShapeDtypeStruct((8 * spots, slice_rows, SPAN), bf16),
            jax.ShapeDtypeStruct((rows, width), bf16),
            jax.ShapeDtypeStruct((2 * EXPERTS, width), f32),
        ],
        in_specs=[whole] * 9 + [pl.BlockSpec(memory_space=pl.ANY)] * 7,
        out_specs=[whole] * 5,
        scratch_shapes=[
            pltpu.VMEM(query_shape, bf16),
            pltpu.VMEM(kvo.shape, bf16),
            pltpu.VMEM((rows, SPAN), f32),
            pltpu.VMEM((8 * rows, width), bf16),
            pltpu.VMEM((rows, width), f32),
            pltpu.VMEM((rows, width), f32),
            pltpu.VMEM((rows, SPAN), bf16),
            pltpu.VMEM((8 * rows, SPAN), bf16),
            pltpu.VMEM(lat_shape, bf16),
            pltpu.VMEM(lat_shape, bf16),
            pltpu.VMEM((rows, SPAN), bf16),
            pltpu.VMEM((4, 4, 2 * EXPERTS, width), bf16),
            *seq_scratch(*query_shape[1:]),
            *seq_scratch(*kvo.shape[1:]),
            *scatter_scratch(rows, SPAN),
            *scatter_scratch(rows, width),
            pltpu.VMEM((3, 4, slice_rows, SPAN), bf16),
            pltpu.VMEM((3, slice_rows, SPAN), bf16),
            pltpu.VMEM(normed.shape, bf16),
            pltpu.VMEM(wq.shape, bf16),
            pltpu.VMEM(wl.shape, bf16),
            pltpu.VMEM(upstream.shape, f32),
            pltpu.VMEM(rows_in.shape, bf16),
            pltpu.VMEM((rows, 2 * ROPE), f32),
            pltpu.VMEM((rows, 2 * ROPE), f32),
            pltpu.SemaphoreType.DMA((130,)),
            pltpu.SemaphoreType.DMA((130,)),
            pltpu.SemaphoreType.DMA((9,)),
        ],
        compiler_params=pltpu.CompilerParams(collective_id=3, has_side_effects=True, vmem_limit_bytes=60 << 20),
        name="tail",
    )(dq, key_own, prev_out, kvo, raw, latent_gain, gain, router_in, ffn_in, normed, wq, wl, upstream, rows_in, cosine, sine)


def start_kernel(
    rows_in, gain, latent_gain, routes, segs, ffn_gain, own_grad, wl_h, wq_h, kv_proj_h, wo_h, cosine_h, sine_h,
    normed_h, q_h, packed_h, keys_h, grad_h, hot_all, raw, heads, lse, residual, own_mid,
    normed, q, packed, keys, grad_half, wl, wq, kv_proj, wo,
    own_normed, ext, ext_all, prev_out, cosine, sine, part, column, p0, p1, p2, send, recv, local, load, store,
):
    at = Place()
    sems = Sems(send, recv)
    rows = rows_in.shape[0]
    block = 8 * rows
    half_seq = pl.ds(pl.multiple_of(lax.rem(at.y, 2) * block, block), block)
    sources = (
        (wl_h, wl), (cosine_h.at[half_seq], cosine), (sine_h.at[half_seq], sine), (wq_h, wq), (kv_proj_h, kv_proj), (wo_h, wo),
    )
    loads = [pltpu.make_async_copy(src, dst, load.at[i]) for i, (src, dst) in enumerate(sources)]
    for c in loads:
        c.start()
    partner = at.across[1](at.y + 1 - 2 * lax.rem(at.y, 2))
    count = announce([at.hop(0, 1), at.hop(0, 3), at.sibling, partner])
    x = rows_in[...].astype(f32)
    own_normed[...] = (x * lax.rsqrt(jnp.mean(x * x, axis=1, keepdims=True) + EPSILON) * gain[...]).astype(bf16)
    meet(count)
    big = gather_stream(sems, at, own_normed, normed, rows, local.at[0])
    next(big)
    loads[0].wait()
    lat = dot_nt(own_normed[...], wl[...])
    raw[...] = lat[:, :LAT]
    x = lat[:, :LAT]
    x = x * lax.rsqrt(jnp.mean(x * x, axis=1, keepdims=True) + EPSILON) * latent_gain[...]
    rope = jnp.concatenate([lat[:, LAT:], lat[:, LAT:]], axis=1)
    loads[1].wait()
    loads[2].wait()
    own = pl.ds(pl.multiple_of(at.me * rows, rows), rows)
    rope = rope * cosine[own] + swapped(rope) * sine[own]
    number = lax.broadcasted_iota(jnp.int32, (128, rows), 0)
    hot = jnp.zeros((128, rows), f32)
    for k in range(routes.shape[0]):
        hot = hot + jnp.where(number == routes[k : k + 1], 1.0, 0.0)
    hot = pltpu.roll(jnp.transpose(hot), ROPE, 1)
    lane = lax.broadcasted_iota(jnp.int32, rope.shape, 1)
    prev_out[:, :LAT] = x.astype(bf16)
    prev_out[:, LAT:] = jnp.where(lane < ROPE, rope, hot).astype(bf16)
    swap = sems.start(prev_out, ext.at[:, pl.ds(SPAN, SPAN)], partner)
    ext[:, :SPAN] = prev_out[...]
    next(big)
    swap.wait_recv()
    little = gather_stream(sems, at, ext, ext_all, rows, local.at[1])
    next(little)
    together(big)
    stores = [pltpu.make_async_copy(normed, normed_h, store.at[0])]
    stores[0].start()
    loads[3].wait()
    loads[4].wait()
    step = 256
    lane = lax.broadcasted_iota(jnp.int32, (step, 2 * ROPE), 1)
    for i in range(block // step):
        r = pl.ds(i * step, step)
        query = dot_nn(normed[r], wq[...])
        q[r, :NOPE] = query[:, :NOPE].astype(bf16)
        one, two = query[:, NOPE : 2 * NOPE], query[:, 2 * NOPE :]
        q[r, NOPE : 2 * NOPE] = jnp.where(lane < ROPE, pltpu.roll(one, ROPE, 1), pltpu.roll(two, ROPE, 1)).astype(bf16)
        rope = jnp.where(lane < ROPE, one, two)
        q[r, 2 * NOPE :] = (rope * cosine[r] + swapped(rope) * sine[r]).astype(bf16)
        if i % 2:
            next(little, None)
    stores.append(pltpu.make_async_copy(q, q_h, store.at[1]))
    stores[1].start()
    together(little)
    early = gather_stream(sems, at, own_grad.at[pl.ds(0, rows // 2)], grad_half, rows // 2, local.at[2])
    next(early)
    for side in range(2):
        r = pl.ds((1 - side) * block, block)
        keys[r, :LAT] = ext_all[:, side * SPAN : side * SPAN + LAT]
        rope = ext_all[:, side * SPAN + LAT : (side + 1) * SPAN].astype(f32)
        turned = pltpu.roll(rope, ROPE, 1)
        if side == 0:
            hot_all[...] = turned.astype(bf16)
        wide_lane = lax.broadcasted_iota(jnp.int32, rope.shape, 1)
        keys[r, LAT:] = jnp.where(wide_lane < ROPE, rope, turned).astype(bf16)
        packed[r] = dot_nn(ext_all[:, side * SPAN : side * SPAN + LAT], kv_proj[...]).astype(bf16)
        for ref, dst in ((keys, keys_h), (packed, packed_h)):
            stores.append(pltpu.make_async_copy(ref.at[r], dst.at[r], store.at[len(stores)]))
            stores[-1].start()
    qseg, kseg = segments(segs, block)
    column[...] = qseg
    shape = (ATT, 2 * block)
    ahead = lax.broadcasted_iota(jnp.int32, shape, 1) - lax.broadcasted_iota(jnp.int32, shape, 0)
    loads[5].wait()

    def ready(dist):
        index = lax.rem(at.chip + dist, 4)
        r = row_block(index)
        allowed = (column[r] == kseg) & (ahead <= index * ATT + block)
        for head in range(2):
            rope = jnp.where(lane // ROPE == head, q[r, 2 * NOPE :], jnp.zeros((), bf16))
            query = jnp.concatenate([q[r, head * NOPE : (head + 1) * NOPE], rope], axis=1)
            head_keys = jnp.concatenate([packed[:, head * 2 * NOPE : head * 2 * NOPE + NOPE], keys[:, LAT:]], axis=1)
            scores = jnp.where(allowed, dot_nt(query, head_keys), -1e30)
            top = jnp.max(scores, axis=1, keepdims=True)
            weights = jnp.exp2((scores - top) * (SCALE * LOG2E))
            total = jnp.sum(weights, axis=1, keepdims=True)
            out = dot_nn(weights.astype(bf16), packed[:, head * 2 * NOPE + NOPE : (head + 1) * 2 * NOPE])
            heads[r, head * VDIM : (head + 1) * VDIM] = (out / total).astype(bf16)
            lse[head, r] = top * (SCALE * LOG2E) + jnp.log2(total)
        part[r] = dot_nn(heads[r], wo[...]).astype(bf16)

    def done(h, total):
        r = slice(h * (rows // 2), (h + 1) * (rows // 2))
        x = rows_in[r].astype(f32) + total
        residual[r] = x
        own_mid[r] = (x * lax.rsqrt(jnp.mean(x * x, axis=1, keepdims=True) + EPSILON) * ffn_gain[...]).astype(bf16)

    out_rows = scatter_stream(sems, at, part, p0, p1, p2, rows, done, ready)
    next(out_rows)
    next(early)
    next(out_rows)
    next(early)
    next(out_rows)
    together(early)
    stores.append(pltpu.make_async_copy(grad_half, grad_h, store.at[len(stores)]))
    stores[-1].start()
    together(out_rows)
    for c in stores:
        c.wait()
    sems.finish()


def start(rows_in, gain, wl, latent_gain, wq, kv_proj, routes, cosine, sine, segs, wo, ffn_gain, own_grad):
    whole = pl.BlockSpec(memory_space=VM)
    held = pl.BlockSpec(memory_space=pl.ANY)
    rows, width = rows_in.shape
    block = 8 * rows
    shapes = [
        (block, width), (block, wq.shape[1]), (2 * block, kv_proj.shape[1]), (2 * block, SPAN), (block // 2, width),
    ]
    return pl.pallas_call(
        start_kernel,
        out_shape=[jax.ShapeDtypeStruct(shape, bf16) for shape in shapes]
        + [
            jax.ShapeDtypeStruct((block, 2 * ROPE), bf16),
            jax.ShapeDtypeStruct((rows, LAT), f32),
            jax.ShapeDtypeStruct((block, 2 * VDIM), bf16),
            jax.ShapeDtypeStruct((2, block, 1), f32),
            jax.ShapeDtypeStruct((rows, width), f32),
            jax.ShapeDtypeStruct((rows, width), bf16),
        ],
        in_specs=[whole] * 7 + [held] * 6,
        out_specs=[held] * 5 + [whole] * 6,
        scratch_shapes=[pltpu.VMEM(shape, bf16) for shape in shapes]
        + [pltpu.VMEM(x.shape, bf16) for x in (wl, wq, kv_proj, wo)]
        + [
            pltpu.VMEM((rows, width), bf16),
            pltpu.VMEM((rows, 2 * SPAN), bf16),
            pltpu.VMEM((block, 2 * SPAN), bf16),
            pltpu.VMEM((rows, SPAN), bf16),
            pltpu.VMEM((block, 2 * ROPE), f32),
            pltpu.VMEM((block, 2 * ROPE), f32),
            pltpu.VMEM((block, width), bf16),
            pltpu.VMEM((block, 1), f32),
            *scatter_scratch(rows, width),
            pltpu.SemaphoreType.DMA((50,)),
            pltpu.SemaphoreType.DMA((50,)),
            pltpu.SemaphoreType.DMA((3,)),
            pltpu.SemaphoreType.DMA((6,)),
            pltpu.SemaphoreType.DMA((7,)),
        ],
        compiler_params=pltpu.CompilerParams(collective_id=0, has_side_effects=True, vmem_limit_bytes=60 << 20),
        name="start",
    )(rows_in, gain, latent_gain, routes, segs, ffn_gain, own_grad, wl, wq, kv_proj, wo, cosine, sine)


def finish_kernel(
    weights_h, query_h, kvo_h, latent_h, small, early,
    expert_gate_h, expert_down_h, shared_gate_h, shared_down_h, query_out_h, kv_out_h, out_out_h, latent_out_h,
    router_out, attn_out, ffn_out, lat_gain_out,
    weights, query, kvo, latent, expert_gate, expert_down, shared_gate, shared_down, query_out, kv_out, out_out, latent_out,
    load, store,
):
    pairs = ((latent_h, latent), (query_h, query), (kvo_h, kvo), (weights_h, weights))
    loads = [pltpu.make_async_copy(src, dst, load.at[i]) for i, (src, dst) in enumerate(pairs)]
    for c in loads:
        c.start()
    stores = []

    def put(src, dst):
        c = pltpu.make_async_copy(src, dst, store.at[len(stores)])
        c.start()
        stores.append(c)

    router_out[...] = small[:EXPERTS]
    attn_out[...] = small[EXPERTS : EXPERTS + 1]
    ffn_out[...] = small[EXPERTS + 1 : EXPERTS + 2]
    lat_gain_out[...] = small[EXPERTS + 2 : EXPERTS + 3, :LAT]
    loads[0].wait()
    step = 512
    for i in range(latent_out.shape[1] // step):
        spot = step // latent.shape[1]
        rows = latent[i * spot : (i + 1) * spot].reshape(step, latent.shape[2]).astype(f32)
        latent_out[:, i * step : (i + 1) * step] = jnp.transpose(rows)[: latent_out.shape[0]]
    put(latent_out, latent_out_h)
    loads[1].wait()
    query_out[...] = query[...].reshape(query_out.shape).astype(f32)
    put(query_out, query_out_h)
    loads[2].wait()
    spots, _, wide = kvo.shape
    kv_rows = kv_out.shape[0] // spots
    kv_out[...] = kvo[:, :kv_rows].reshape(kv_out.shape).astype(f32)
    put(kv_out, kv_out_h)
    out_rows = out_out.shape[0] // spots
    for j in range(out_out.shape[1] // wide):
        piece = kvo[:, kv_rows + j * out_rows : kv_rows + (j + 1) * out_rows]
        out_out[:, j * wide : (j + 1) * wide] = piece.reshape(out_out.shape[0], wide).astype(f32)
    put(out_out, out_out_h)
    loads[3].wait()
    for c in range(expert_gate.shape[1] // 128):
        expert_gate[:, c * 128 : (c + 1) * 128] = weights[c * 128 : (c + 1) * 128].astype(f32)
    put(expert_gate, expert_gate_h)
    spot = expert_gate.shape[1]
    for ref, dst in ((expert_down, expert_down_h), (shared_gate, shared_gate_h), (shared_down, shared_down_h)):
        skip = 0
        if ref is expert_down:
            skip = early.shape[0]
            ref[:skip] = early[...].astype(f32)
        ref[skip:] = weights[spot : spot + ref.shape[0] - skip].astype(f32)
        put(ref, dst)
        spot += ref.shape[0] - skip
    for c in stores:
        c.wait()


def finish(weights, query, kvo, latent, small, early, shared, model_width, kv_shape, out_shape):
    whole = pl.BlockSpec(memory_space=VM)
    held = pl.BlockSpec(memory_space=pl.ANY)
    shapes = [
        (128, 2 * F), (F, 128), (2 * shared, 128), (shared, 128),
        (model_width, query.shape[2]), kv_shape, out_shape, (LAT + ROPE, model_width),
    ]
    little = [(EXPERTS, model_width), (1, model_width), (1, model_width), (1, LAT)]
    return pl.pallas_call(
        finish_kernel,
        out_shape=[jax.ShapeDtypeStruct(shape, f32) for shape in shapes + little],
        in_specs=[held] * 4 + [whole] * 2,
        out_specs=[held] * 8 + [whole] * 4,
        scratch_shapes=[pltpu.VMEM(x.shape, bf16) for x in (weights, query, kvo, latent)]
        + [pltpu.VMEM(shape, f32) for shape in shapes]
        + [pltpu.SemaphoreType.DMA((4,)), pltpu.SemaphoreType.DMA((8,))],
        compiler_params=pltpu.CompilerParams(vmem_limit_bytes=56 << 20),
        name="finish",
    )(weights, query, kvo, latent, small, early)


def tables(seq_rows):
    lane = np.arange(2 * ROPE)
    half = ROPE // 2
    frequency = np.exp((lane % half) * (-math.log(10000.0) / half))
    angles = np.arange(seq_rows)[:, None] * frequency[None, :]
    sign = np.where(lane % ROPE < half, -1.0, 1.0)
    return np.cos(angles).astype(np.float32), (np.sin(angles) * sign[None, :]).astype(np.float32)


def local(
    layer_input, attn_gain, query_proj, latent_proj, latent_gain, kv_proj, output_proj, ffn_gain, router_proj,
    shared_gate_up, shared_down, expert_gate_up, expert_down, segment_ids, expert_routes, out_grad,
):
    own_rows, model_width = layer_input.shape
    cosine, sine = tables(2 * own_rows * lax.axis_size("exp"))
    wl = latent_proj.T
    router = router_proj.T
    shared = shared_down.shape[0]
    pair_s = shared_gate_up.transpose(1, 2, 0).reshape(2 * shared, model_width)
    pair_e, down_e = expert_gate_up[0], expert_down[0]
    segs = segment_ids[None]
    attn_row, latent_row, ffn_row = attn_gain[None], latent_gain[None], ffn_gain[None]
    normed_all, q, packed, keys, grad_half, hot, latent_raw, heads, lse, residual, own_mid = start(
        layer_input, attn_row, wl, latent_row, query_proj, kv_proj, expert_routes.T, cosine, sine,
        segs, output_proj, ffn_row, out_grad,
    )
    terms, act, dpre, logit, router_term, early = mlp(
        own_mid, out_grad, pair_s, pair_e, shared_down, down_e, grad_half, router, hot
    )
    weight_sum = lax.psum_scatter(terms.reshape(-1, 128), "seq", scatter_dimension=0, tiled=True)
    residual_grad, ffn_term, attn_grad_all, moe_part = turn(
        dpre, act, pair_s, pair_e, shared_down, down_e, logit, router, residual, ffn_row, out_grad
    )
    dq, key_own, prev_sum, kvo, layer_output = attend_back(
        attn_grad_all, output_proj, heads, q, packed, keys, segs, lse, kv_proj, moe_part, residual, cosine, sine
    )
    query_sum, kvo_sum, latent_sum, input_grad, small = tail(
        dq, key_own, prev_sum, kvo, normed_all, query_proj, wl, latent_raw, latent_row, attn_row,
        residual_grad, layer_input, router_term, ffn_term, cosine, sine,
    )
    (
        expert_gate, expert_down_sum, shared_gate, shared_down_sum, query_sum, kv_sum, output_sum, latent_sum,
        router_sum, attn_gain_sum, ffn_gain_sum, latent_gain_sum,
    ) = finish(
        weight_sum, query_sum, kvo_sum, latent_sum, small, early, shared, model_width, kv_proj.shape, output_proj.shape
    )
    return (
        layer_output,
        input_grad,
        attn_gain_sum[0],
        query_sum,
        latent_sum.T,
        latent_gain_sum[0],
        kv_sum,
        output_sum,
        ffn_gain_sum[0],
        router_sum.T,
        shared_gate.reshape(2, shared, 128).transpose(2, 0, 1),
        shared_down_sum,
        expert_gate[None],
        expert_down_sum[None],
    )


def solution(mesh):
    in_specs = (
        P(("seq", "exp"), None),
        P(),
        P(None, "exp"),
        P(),
        P(),
        P(None, "exp"),
        P("exp", None),
        P(),
        P(),
        P(None, None, "exp"),
        P("exp", None),
        P("exp", None, None),
        P("exp", None, None),
        P(),
        P(("seq", "exp"), None),
        P(("seq", "exp"), None),
    )
    out_specs = (
        P(("seq", "exp"), None),
        P(("seq", "exp"), None),
        P(),
        P(None, "exp"),
        P(),
        P(),
        P(None, "exp"),
        P("exp", None),
        P(),
        P(),
        P("seq", None, "exp"),
        P("exp", "seq"),
        P("exp", "seq", None),
        P("exp", None, "seq"),
    )
    return jax.shard_map(local, mesh=mesh, in_specs=in_specs, out_specs=out_specs, check_vma=False)
```

```python
import functools
import math

import jax
import jax.numpy as jnp
import numpy as np
from jax import lax
from jax.experimental import pallas as pl
from jax.experimental.pallas import tpu as pltpu
from jax.sharding import PartitionSpec as P

NOPE = 128
ROPE = 64
VDIM = 128
LAT = 512
F = 1408
EXPERTS = 8
EPSILON = 1e-06

VM = pltpu.VMEM
f32 = jnp.float32
bf16 = jnp.bfloat16


class Sems:
    def __init__(self, send, recv):
        self.send, self.recv, self.used, self.sent = send, recv, 0, []

    def start(self, src, dst, peer):
        copy = pltpu.make_async_remote_copy(
            src_ref=src,
            dst_ref=dst,
            send_sem=self.send.at[self.used],
            recv_sem=self.recv.at[self.used],
            device_id=peer,
            device_id_type=pl.DeviceIdType.MESH,
        )
        copy.start()
        self.used += 1
        self.sent.append(copy)
        return copy

    def finish(self):
        for copy in self.sent:
            copy.wait_send()


class Place:
    def __init__(self):
        me, spot = lax.axis_index("exp"), lax.axis_index("seq")
        self.me = me
        self.chip, self.core = me // 2, me % 2
        self.z, self.y = spot // 4, spot % 4
        self.sibling = {"exp": self.chip * 2 + 1 - self.core}
        self.across = [lambda i: {"exp": i * 2 + self.core}, lambda i: {"seq": self.z * 4 + i}, lambda i: {"seq": i * 4 + self.y}]
        self.along = [self.chip, self.y, self.z]

    def hop(self, axis, distance):
        return self.across[axis](lax.rem(self.along[axis] + distance, 4))


def announce(peers):
    barrier = pltpu.get_barrier_semaphore()
    for peer in peers:
        pl.semaphore_signal(barrier, inc=1, device_id=peer, device_id_type=pl.DeviceIdType.MESH)
    return len(peers)


def meet(count):
    pl.semaphore_wait(pltpu.get_barrier_semaphore(), count)


def greet(peers):
    meet(announce(peers))


def together(*streams):
    streams = list(streams)
    while streams:
        for stream in list(streams):
            try:
                next(stream)
            except StopIteration:
                streams.remove(stream)


def gather_stream(sems, at, src, out, rows, local, arrived=None, stride=None, offset=0):
    half = rows // 2
    stride = stride or rows
    right, left = at.hop(0, 1), at.hop(0, 3)
    me = at.me
    near_right = lax.rem(at.chip + 1, 4) * 2 + at.core
    near_left = lax.rem(at.chip + 3, 4) * 2 + at.core
    far = lax.rem(at.chip + 2, 4) * 2 + at.core

    def part(owner, h):
        return out.at[pl.ds(pl.multiple_of(owner * stride + offset + h * half, half), half)]

    def own(h):
        return src.at[pl.ds(h * half, half)]

    ra = sems.start(own(0), part(me, 0), right)
    lb = sems.start(own(1), part(me, 1), left)
    rb = sems.start(own(1), part(me, 1), right)
    la = sems.start(own(0), part(me, 0), left)
    sib = [sems.start(src, out.at[pl.ds(pl.multiple_of(me * stride + offset, rows), rows)], at.sibling)]
    mine = pltpu.make_async_copy(src, out.at[pl.ds(pl.multiple_of(me * stride + offset, rows), rows)], local)
    mine.start()
    if arrived is None:
        yield
    else:
        mine.wait()
        sib[0].wait_recv()
        arrived(0)
    ra.wait_recv()
    far_a = sems.start(part(near_left, 0), part(near_left, 0), right)
    sib.append(sems.start(part(near_left, 0), part(near_left, 0), at.sibling))
    lb.wait_recv()
    far_b = sems.start(part(near_right, 1), part(near_right, 1), left)
    sib.append(sems.start(part(near_right, 1), part(near_right, 1), at.sibling))
    if arrived is None:
        yield
    rb.wait_recv()
    sib.append(sems.start(part(near_left, 1), part(near_left, 1), at.sibling))
    la.wait_recv()
    sib.append(sems.start(part(near_right, 0), part(near_right, 0), at.sibling))
    yield
    if arrived is not None:
        sib[1].wait_recv()
        sib[3].wait_recv()
        arrived(3)
    far_a.wait_recv()
    sib.append(sems.start(part(far, 0), part(far, 0), at.sibling))
    far_b.wait_recv()
    sib.append(sems.start(part(far, 1), part(far, 1), at.sibling))
    yield
    if arrived is None:
        mine.wait()
        for copy in sib:
            copy.wait_recv()
    else:
        sib[2].wait_recv()
        sib[4].wait_recv()
        arrived(1)
        yield
        sib[5].wait_recv()
        sib[6].wait_recv()
        arrived(2)


def scatter_stream(sems, at, src, pair, hop, last, rows, done, ready=None, stride=None, offset=0):
    half = rows // 2
    stride = stride or rows
    right, left = at.hop(0, 1), at.hop(0, 3)
    order = (2, 1, 3, 0)
    sib = []

    def offer(dist):
        if ready is not None:
            ready(dist)
        owner = lax.rem(at.chip + dist, 4) * 2 + 1 - at.core
        sib.append(sems.start(src.at[pl.ds(pl.multiple_of(owner * stride + offset, rows), rows)], pair.at[dist], at.sibling))

    def fold(i):
        sib[i].wait_recv()
        owner = lax.rem(at.chip + order[i], 4) * 2 + at.core
        mine = src[pl.ds(pl.multiple_of(owner * stride + offset, rows), rows)]
        pair[order[i]] = (pair[order[i]].astype(f32) + mine.astype(f32)).astype(bf16)

    def add(ref, other):
        ref[...] = (ref[...].astype(f32) + other[...].astype(f32)).astype(bf16)

    first, second = pl.ds(0, half), pl.ds(half, half)
    offer(2)
    if ready is not None:
        yield
    offer(1)
    if ready is None:
        offer(3)
        offer(0)
        yield
    fold(0)
    far_a = sems.start(pair.at[2, first], hop.at[0], right)
    far_b = sems.start(pair.at[2, second], hop.at[1], left)
    yield
    if ready is not None:
        offer(3)
    fold(1)
    dir_b = sems.start(pair.at[1, second], last.at[0], right)
    fold(2)
    dir_a = sems.start(pair.at[3, first], last.at[1], left)
    yield
    far_a.wait_recv()
    add(pair.at[1, first], hop.at[0])
    acc_a = sems.start(pair.at[1, first], last.at[2], right)
    far_b.wait_recv()
    add(pair.at[3, second], hop.at[1])
    acc_b = sems.start(pair.at[3, second], last.at[3], left)
    if ready is not None:
        offer(0)
    yield
    sib[3].wait_recv()
    dir_b.wait_recv()
    dir_a.wait_recv()
    acc_a.wait_recv()
    acc_b.wait_recv()
    for h, ends in ((0, (1, 2)), (1, (0, 3))):
        mine = src[pl.ds(pl.multiple_of(at.me * stride + offset + h * half, half), half)].astype(f32)
        total = mine + pair[0, pl.ds(h * half, half)].astype(f32)
        done(h, total + last[ends[0]].astype(f32) + last[ends[1]].astype(f32))


def scatter_scratch(rows, cols):
    return [
        pltpu.VMEM((4, rows, cols), bf16),
        pltpu.VMEM((2, rows // 2, cols), bf16),
        pltpu.VMEM((4, rows // 2, cols), bf16),
    ]


def ring_sum(sems, at, axis, block, hop, last):
    right, left = at.hop(axis, 1), at.hop(axis, 3)
    to = [lax.rem(at.along[axis] + d, 4) for d in range(4)]

    def add(ref, other):
        ref[...] = (ref[...].astype(f32) + other[...].astype(f32)).astype(bf16)

    far_a = sems.start(block(to[2], 0), hop.at[0], right)
    far_b = sems.start(block(to[2], 1), hop.at[1], left)
    dir_b = sems.start(block(to[1], 1), last.at[0], right)
    dir_a = sems.start(block(to[3], 0), last.at[1], left)
    yield
    far_a.wait_recv()
    add(block(to[1], 0), hop.at[0])
    acc_a = sems.start(block(to[1], 0), last.at[2], right)
    far_b.wait_recv()
    add(block(to[3], 1), hop.at[1])
    acc_b = sems.start(block(to[3], 1), last.at[3], left)
    yield
    dir_b.wait_recv()
    dir_a.wait_recv()
    acc_a.wait_recv()
    acc_b.wait_recv()
    for part, (one, two) in ((0, (1, 2)), (1, (0, 3))):
        ref = block(to[0], part)
        ref[...] = (ref[...].astype(f32) + last[one].astype(f32) + last[two].astype(f32)).astype(bf16)


def ring_gather(sems, at, axis, block):
    right, left = at.hop(axis, 1), at.hop(axis, 3)
    to = [lax.rem(at.along[axis] + d, 4) for d in range(4)]
    ra = sems.start(block(to[0], 0), block(to[0], 0), right)
    lb = sems.start(block(to[0], 1), block(to[0], 1), left)
    rb = sems.start(block(to[0], 1), block(to[0], 1), right)
    la = sems.start(block(to[0], 0), block(to[0], 0), left)
    yield
    ra.wait_recv()
    fa = sems.start(block(to[3], 0), block(to[3], 0), right)
    lb.wait_recv()
    fb = sems.start(block(to[1], 1), block(to[1], 1), left)
    yield
    for copy in (rb, la, fa, fb):
        copy.wait_recv()


def seq_stream(sems, at, work, out, scratch, axes):
    hop, last, narrow_in = scratch
    one, two = at.along[axes[0]], at.along[axes[1]]
    own = one * 4 + two

    def wide(ref):
        return lambda i, h: ref.at[pl.ds(i * 4 + 2 * h, 2)]

    yield from ring_sum(sems, at, axes[0], wide(work), hop, last)
    copies = [sems.start(work.at[one * 4 + lax.rem(two + d, 4)], narrow_in.at[d - 1], at.hop(axes[1], d)) for d in (1, 2, 3)]
    yield
    for copy in copies:
        copy.wait_recv()
    total = work[own].astype(f32) + narrow_in[0].astype(f32)
    out[own] = (total + (narrow_in[1].astype(f32) + narrow_in[2].astype(f32))).astype(bf16)
    copies = [sems.start(out.at[own], out.at[own], at.hop(axes[1], d)) for d in (1, 2, 3)]
    yield
    for copy in copies:
        copy.wait_recv()
    yield from ring_gather(sems, at, axes[0], wide(out))


def seq_scatter(sems, at, work, out, scratch, axes):
    hop, last, narrow_in = scratch
    one, two = at.along[axes[0]], at.along[axes[1]]
    yield from ring_sum(sems, at, axes[0], lambda i, h: work.at[pl.ds(i * 4 + 2 * h, 2)], hop, last)
    copies = [sems.start(work.at[one * 4 + lax.rem(two + d, 4)], narrow_in.at[d - 1], at.hop(axes[1], d)) for d in (1, 2, 3)]
    yield
    for copy in copies:
        copy.wait_recv()
    total = work[one * 4 + two].astype(f32) + narrow_in[0].astype(f32)
    out[...] = (total + (narrow_in[1].astype(f32) + narrow_in[2].astype(f32))).astype(bf16)


def seq_scratch(rows, cols):
    return [
        pltpu.VMEM((2, 2, rows, cols), bf16),
        pltpu.VMEM((4, 2, rows, cols), bf16),
        pltpu.VMEM((3, rows, cols), bf16),
    ]


def seq_direct(sems, at, work, out, wide_in, narrow_in):
    y, z = at.y, at.z
    copies = [sems.start(work.at[pl.ds(lax.rem(y + d, 4) * 4, 4)], wide_in.at[d - 1], at.hop(1, d)) for d in (1, 2, 3)]
    yield
    for copy in copies:
        copy.wait_recv()
    mine = pl.ds(y * 4, 4)
    work[mine] = (
        work[mine].astype(f32) + wide_in[0].astype(f32) + (wide_in[1].astype(f32) + wide_in[2].astype(f32))
    ).astype(bf16)
    copies = [sems.start(work.at[y * 4 + lax.rem(z + d, 4)], narrow_in.at[d - 1], at.hop(2, d)) for d in (1, 2, 3)]
    yield
    for copy in copies:
        copy.wait_recv()
    own = y * 4 + z
    out[own] = (
        work[own].astype(f32) + narrow_in[0].astype(f32) + (narrow_in[1].astype(f32) + narrow_in[2].astype(f32))
    ).astype(bf16)
    copies = [sems.start(out.at[own], out.at[own], at.hop(2, d)) for d in (1, 2, 3)]
    yield
    for copy in copies:
        copy.wait_recv()
    copies = [sems.start(out.at[mine], out.at[mine], at.hop(1, d)) for d in (1, 2, 3)]
    yield
    for copy in copies:
        copy.wait_recv()


def small_stream(sems, at, slots, out):
    stages = [(at.core, 2, lambda d: at.sibling)] + [
        (at.along[axis], 4, functools.partial(at.hop, axis)) for axis in range(3)
    ]
    for stage, (place, count, name) in enumerate(stages):
        slots[stage, place] = out[...].astype(bf16)
        copies = [sems.start(slots.at[stage, place], slots.at[stage, place], name(d)) for d in range(1, count)]
        yield
        for copy in copies:
            copy.wait_recv()
        total = slots[stage, 0].astype(f32)
        for i in range(1, count):
            total = total + slots[stage, i].astype(f32)
        out[...] = total


def swapped(tensor):
    lane = lax.broadcasted_iota(jnp.int32, tensor.shape, 1)
    return jnp.where(lane % 64 < 32, pltpu.roll(tensor, 96, 1), pltpu.roll(tensor, 32, 1))


PAD = 384
EARLY = 768
ROW_STEP = 256


def dot_nn(a, b):
    return lax.dot_general(a, b, (((1,), (0,)), ((), ())), preferred_element_type=f32)


def dot_nt(a, b):
    return lax.dot_general(a, b, (((1,), (1,)), ((), ())), preferred_element_type=f32)


def dot_tn(a, b):
    return lax.dot_general(a, b, (((0,), (0,)), ((), ())), preferred_element_type=f32)


def row_block(index):
    return pl.ds(pl.multiple_of(index * ROW_STEP, ROW_STEP), ROW_STEP)


def router_pieces(router):
    high = router.astype(bf16).astype(f32)
    middle_part = (router - high).astype(bf16).astype(f32)
    low = router - high - middle_part
    fill = jnp.zeros((128 - 3 * EXPERTS, router.shape[1]), f32)
    return jnp.concatenate([high, middle_part, low, fill], axis=0).astype(bf16)


def mlp_kernel(
    own_mid, own_grad, pair_s_h, pair_e_h, down_s_h, down_e_h, grad_h, router, hot,
    terms_h, act_h, dpre_h, logit, router_out, early,
    mid, grad, pair_s, pair_e, down_s, down_e, act, dpre, pieces, stage, work0, work1, r0, r1, r2, s0, s1, s2, load, store, keep, send, recv, local,
):
    at = Place()
    sems = Sems(send, recv)
    rows, width = mid.shape
    shared = down_s.shape[0]
    expert = lax.axis_index("exp")
    sources = [(pair_e_h, pair_e), (pair_s_h, pair_s), (down_s_h, down_s), (down_e_h, down_e)]
    loads = [pltpu.make_async_copy(src, dst, load.at[i]) for i, (src, dst) in enumerate(sources)]
    sent = own_grad.shape[0] // 2
    for owner in range(8):
        here = (grad_h.at[pl.ds(owner * sent, sent)], grad.at[pl.ds(owner * 2 * sent, sent)])
        loads.append(pltpu.make_async_copy(*here, load.at[len(loads)]))
    for c in loads:
        c.start()
    count = announce(
        [at.hop(0, 1), at.hop(0, 3), at.sibling] + [at.hop(axis, d) for axis in (1, 2) for d in (1, 2, 3)]
    )
    pieces[...] = router_pieces(router[...])
    meet(count)
    lane = lax.broadcasted_iota(jnp.int32, (ROW_STEP, 128), 1)
    own_lane = lane == expert

    def gates(r):
        raw = dot_nt(mid[r], pieces[...])
        raw = raw + (pltpu.roll(raw, 128 - EXPERTS, 1) + pltpu.roll(raw, 128 - 2 * EXPERTS, 1))
        raw = jnp.where(lane < EXPERTS, raw, -1e30)
        raw = jnp.exp(raw - jnp.max(raw, axis=1, keepdims=True))
        probs = raw / jnp.sum(raw, axis=1, keepdims=True)
        own = jnp.sum(jnp.where(own_lane, probs * hot[r].astype(f32), 0.0), axis=1, keepdims=True)
        return own, probs

    tiles = [(pair_e, start, min(512, F - start)) for start in range(0, F, 512)]

    def before_activation(dist):
        r = row_block(lax.rem(at.chip + dist, 4))
        if dist == 0:
            loads[0].wait()
        for _, start, size in tiles:
            dpre[r, start : start + size] = dot_nn(mid[r], pair_e[:, start : start + size]).astype(bf16)
            up = dot_nn(mid[r], pair_e[:, F + start : F + start + size])
            dpre[r, F + start : F + start + size] = up.astype(bf16)
        if dist == 0:
            loads[1].wait()
        dpre[r, 2 * F : 2 * F + shared] = dot_nt(mid[r], pair_s[:shared]).astype(bf16)
        dpre[r, 2 * F + PAD : 2 * F + PAD + shared] = dot_nt(mid[r], pair_s[shared:]).astype(bf16)

    def piece(r, dact, act_at, gate_at, up_at, own):
        size = dact.shape[1]
        gate, up = dpre[r, gate_at : gate_at + size].astype(f32), dpre[r, up_at : up_at + size].astype(f32)
        logistic = 1.0 / (1.0 + jnp.exp(-gate))
        passed = gate * logistic
        out = passed * up
        total = None
        if own is not None:
            total = jnp.sum(out * dact, axis=1, keepdims=True)
            out = out * own
            dact = dact * own
        act[r, act_at : act_at + size] = out.astype(bf16)
        slope = logistic + passed * (1.0 - logistic)
        dpre[r, gate_at : gate_at + size] = (dact * up * slope).astype(bf16)
        dpre[r, up_at : up_at + size] = (dact * passed).astype(bf16)
        return total

    mids = gather_stream(sems, at, own_mid, mid, own_mid.shape[0], local.at[0], before_activation)
    grads = gather_stream(sems, at, own_grad.at[pl.ds(sent, sent)], grad, sent, local.at[1], None, 2 * sent, sent)
    next(mids)
    next(grads)
    next(mids)
    next(mids)
    next(grads)
    together(mids)
    together(grads)
    for c in loads[2:]:
        c.wait()

    @pl.loop(0, rows // ROW_STEP)
    def _(index):
        r = row_block(index)
        piece(r, dot_nt(grad[r], down_s[...]), F, 2 * F, 2 * F + PAD, None)
        own, probs = gates(r)
        total = 0.0
        for _, start, size in tiles:
            total = total + piece(r, dot_nt(grad[r], down_e[start : start + size]), start, start, F + start, own)
        logit[r] = ((own * total) * (jnp.where(own_lane, 1.0, 0.0) - probs)).astype(bf16)

    keeps = [pltpu.make_async_copy(act, act_h, keep.at[0]), pltpu.make_async_copy(dpre, dpre_h, keep.at[1])]
    for c in keeps:
        c.start()

    half = width // 2
    slots = half // 128
    early_rows = EARLY // 2
    for work, start, axis in ((work0, 0, 1), (work1, early_rows, 2)):
        for part in range(2):
            value = dot_tn(act[:, start : start + early_rows], grad[:, part * half : (part + 1) * half]).astype(bf16)
            for s in range(slots):
                z, y = divmod(part * slots + s, 4)
                work[y * 4 + z if axis == 1 else z * 4 + y] = value[:, s * 128 : (s + 1) * 128]
    sums = [
        seq_scatter(sems, at, work0, early.at[pl.ds(0, early_rows)], (r0, r1, r2), (1, 2)),
        seq_scatter(sems, at, work1, early.at[pl.ds(early_rows, early_rows)], (s0, s1, s2), (2, 1)),
    ]
    for stream in sums:
        next(stream)
    jobs = []
    for start in range(0, 2 * F, 512):
        size = min(512, 2 * F - start)
        jobs.append((mid, dpre, start, size, start, True))
    for start in range(EARLY, F, 512):
        size = min(512, F - start)
        jobs.append((grad, act, start, size, 2 * F + start - EARLY, False))
    for index, (left, right, start) in enumerate(((mid, dpre, 2 * F), (mid, dpre, 2 * F + PAD), (grad, act, F))):
        jobs.append((left, right, start, shared, 3 * F - EARLY + index * shared, False))

    def flush(part, spot, size):
        return pltpu.make_async_copy(
            stage.at[part, :, pl.ds(0, size)], terms_h.at[pl.ds(part * slots, slots), pl.ds(spot, size)], store.at[part]
        )

    before = None
    for number, (left, right, start, size, spot, by_column) in enumerate(jobs):
        for part in range(2):
            if before is not None:
                flush(part, *before).wait()
            wide = left[:, part * half : (part + 1) * half]
            if by_column:
                value = dot_tn(wide, right[:, start : start + size]).astype(bf16)
                for s in range(slots):
                    for c in range(size // 128):
                        stage[part, s, c * 128 : (c + 1) * 128] = value[s * 128 : (s + 1) * 128, c * 128 : (c + 1) * 128]
            else:
                value = dot_tn(right[:, start : start + size], wide).astype(bf16)
                for s in range(slots):
                    stage[part, s, :size] = value[:, s * 128 : (s + 1) * 128]
            flush(part, spot, size).start()
        before = (spot, size)
        if number in (3, 7):
            for stream in sums:
                next(stream)
    router_out[...] = dot_tn(logit[...], mid[...])[:EXPERTS]
    for part in range(2):
        flush(part, *before).wait()
    for c in keeps:
        c.wait()
    together(*sums)
    sems.finish()


def mlp(own_mid, own_grad, pair_s, pair_e, down_s, down_e, grad_half, router, hot):
    rows, width = 8 * own_mid.shape[0], own_mid.shape[1]
    shared = down_s.shape[0]
    whole = pl.BlockSpec(memory_space=VM)
    held = pl.BlockSpec(memory_space=pl.ANY)
    act_shape, dpre_shape = (rows, F + PAD), (rows, 2 * (F + PAD))
    return pl.pallas_call(
        mlp_kernel,
        out_shape=[
            jax.ShapeDtypeStruct((width // 128, 3 * (F + shared) - EARLY, 128), bf16),
            jax.ShapeDtypeStruct(act_shape, bf16),
            jax.ShapeDtypeStruct(dpre_shape, bf16),
            jax.ShapeDtypeStruct((rows, 128), bf16),
            jax.ShapeDtypeStruct((EXPERTS, width), f32),
            jax.ShapeDtypeStruct((EARLY, 128), bf16),
        ],
        in_specs=[whole] * 2 + [held] * 5 + [whole] * 2,
        out_specs=[held, held, held, whole, whole, whole],
        scratch_shapes=[
            pltpu.VMEM((rows, width), bf16), pltpu.VMEM((rows, width), bf16),
            pltpu.VMEM(pair_s.shape, bf16), pltpu.VMEM(pair_e.shape, bf16),
            pltpu.VMEM(down_s.shape, bf16), pltpu.VMEM(down_e.shape, bf16),
            pltpu.VMEM(act_shape, bf16), pltpu.VMEM(dpre_shape, bf16),
            pltpu.VMEM((128, width), bf16), pltpu.VMEM((2, width // 256, 512, 128), bf16),
            pltpu.VMEM((width // 128, EARLY // 2, 128), bf16), pltpu.VMEM((width // 128, EARLY // 2, 128), bf16),
            *seq_scratch(EARLY // 2, 128), *seq_scratch(EARLY // 2, 128),
            pltpu.SemaphoreType.DMA((12,)), pltpu.SemaphoreType.DMA((2,)), pltpu.SemaphoreType.DMA((2,)),
            pltpu.SemaphoreType.DMA((44,)), pltpu.SemaphoreType.DMA((44,)), pltpu.SemaphoreType.DMA((2,)),
        ],
        compiler_params=pltpu.CompilerParams(collective_id=5, has_side_effects=True, vmem_limit_bytes=62 << 20),
        cost_estimate=pl.CostEstimate(flops=12 * rows * width * (F + shared), bytes_accessed=60 << 20, transcendentals=rows * F),
        name="mlp",
    )(own_mid, own_grad, pair_s, pair_e, down_s, down_e, grad_half, router, hot)


def turn_kernel(
    dpre_h, act_h, pair_s_h, pair_e_h, down_s_h, down_e_h, logit, router, residual, gain, upstream,
    residual_grad, gain_term, grad_all, moe_h,
    moe_part, dpre, act, pair_s, pair_e, down_s, down_e, part, pieces, own_grad, p0, p1, p2, o0, o1, o2, load, send, recv, local,
):
    at = Place()
    sems = Sems(send, recv)
    rows = residual.shape[0]
    half = rows // 2
    shared = down_s.shape[0]
    sources = [
        (pair_e_h.at[:, pl.ds(0, F)], pair_e.at[:, pl.ds(0, F)]),
        (pair_e_h.at[:, pl.ds(F, F)], pair_e.at[:, pl.ds(F, F)]), (pair_s_h, pair_s),
        (act_h, act), (down_e_h, down_e), (down_s_h, down_s),
    ]
    blocks = [row_block(lax.rem(at.chip + dist, 4)) for dist in (2, 1, 3, 0)]
    sources = [(dpre_h.at[blocks[0]], dpre.at[blocks[0]])] + sources
    sources[4:4] = [(dpre_h.at[r], dpre.at[r]) for r in blocks[1:]]
    loads = [pltpu.make_async_copy(src, dst, load.at[i]) for i, (src, dst) in enumerate(sources)]
    for c in loads:
        c.start()
    count = announce([at.hop(0, 1), at.hop(0, 3), at.sibling])
    gain_term[...] = jnp.zeros_like(gain_term)
    pieces[...] = router_pieces(router[...])
    loads[0].wait()

    def ready(dist):
        r = row_block(lax.rem(at.chip + dist, 4))
        if dist == 2:
            loads[1].wait()
        else:
            loads[{1: 4, 3: 5, 0: 6}[dist]].wait()
        total = dot_nt(dpre[r, :F], pair_e[:, :F])
        if dist == 2:
            loads[2].wait()
        total = total + dot_nt(dpre[r, F : 2 * F], pair_e[:, F:])
        if dist == 2:
            loads[3].wait()
        total = total + dot_nn(dpre[r, 2 * F : 2 * F + shared], pair_s[:shared])
        total = total + dot_nn(dpre[r, 2 * F + PAD : 2 * F + PAD + shared], pair_s[shared:])
        part[r] = (total + dot_nn(logit[r], pieces[...])).astype(bf16)
        if dist == 2:
            meet(count)

    def done_from(first):
        def done(h, total):
            r = slice(first + h * (half // 2), first + (h + 1) * (half // 2))
            x = residual[r]
            inverse = lax.rsqrt(jnp.mean(x * x, axis=1, keepdims=True) + EPSILON)
            gain_term[...] += jnp.sum(total * x * inverse, axis=0, keepdims=True)
            s = total * gain[...]
            inner = jnp.mean(s * x, axis=1, keepdims=True)
            grad = upstream[r].astype(f32) + (inverse * s - x * (inverse * inverse * inverse) * inner)
            residual_grad[r] = grad
            own_grad[r] = grad.astype(bf16)

        return done

    def moe(index):
        r = pl.ds(index * ROW_STEP, ROW_STEP)
        moe_part[r] = (dot_nn(act[r, :F], down_e[...]) + dot_nn(act[r, F : F + shared], down_s[...])).astype(bf16)

    ones = scatter_stream(sems, at, part, p0, p1, p2, half, done_from(0), ready, rows, 0)
    twos = scatter_stream(sems, at, part, o0, o1, o2, half, done_from(half), lambda dist: None, rows, half)
    for _ in range(4):
        next(ones)
        next(twos)
    together(ones)
    first = gather_stream(sems, at, own_grad.at[pl.ds(0, half)], grad_all, half, local.at[0], None, rows, 0)
    next(first)
    together(twos)
    second = gather_stream(sems, at, own_grad.at[pl.ds(half, half)], grad_all, half, local.at[1], None, rows, half)
    next(second)
    for c in loads[7:]:
        c.wait()
    for index in range(4):
        moe(index)
        next(first, None)
        next(second, None)
    keep = pltpu.make_async_copy(moe_part, moe_h, load.at[0])
    keep.start()
    together(first, second)
    keep.wait()
    sems.finish()


def turn(dpre, act, pair_s, pair_e, down_s, down_e, logit, router, residual, gain, upstream):
    whole = pl.BlockSpec(memory_space=VM)
    held = pl.BlockSpec(memory_space=pl.ANY)
    rows, width = residual.shape
    return pl.pallas_call(
        turn_kernel,
        out_shape=[
            jax.ShapeDtypeStruct((rows, width), f32),
            jax.ShapeDtypeStruct((1, width), f32),
            jax.ShapeDtypeStruct((8 * rows, width), bf16),
            jax.ShapeDtypeStruct((8 * rows, width), bf16),
        ],
        in_specs=[held] * 6 + [whole] * 5,
        out_specs=[whole] * 3 + [held],
        scratch_shapes=[
            pltpu.VMEM((8 * rows, width), bf16),
            pltpu.VMEM(dpre.shape, bf16), pltpu.VMEM(act.shape, bf16),
            pltpu.VMEM(pair_s.shape, bf16), pltpu.VMEM(pair_e.shape, bf16),
            pltpu.VMEM(down_s.shape, bf16), pltpu.VMEM(down_e.shape, bf16),
            pltpu.VMEM((8 * rows, width), bf16),
            pltpu.VMEM((128, width), bf16),
            pltpu.VMEM((rows, width), bf16),
            *scatter_scratch(rows // 2, width),
            *scatter_scratch(rows // 2, width),
            pltpu.SemaphoreType.DMA((10,)),
            pltpu.SemaphoreType.DMA((46,)),
            pltpu.SemaphoreType.DMA((46,)),
            pltpu.SemaphoreType.DMA((2,)),
        ],
        compiler_params=pltpu.CompilerParams(collective_id=2, has_side_effects=True, vmem_limit_bytes=62 << 20),
        name="turn",
    )(dpre, act, pair_s, pair_e, down_s, down_e, logit, router, residual, gain, upstream)


SPAN = LAT + 2 * ROPE
ATT = 256
SCALE = (NOPE + ROPE) ** (-0.5)
LOG2E = 1.4426950408889634


def segments(segs, count):
    spot = lax.axis_index("seq")
    own = segs[:, pl.ds(pl.multiple_of(spot * count, count), count)].astype(f32)
    before = segs[:, pl.ds(pl.multiple_of(jnp.maximum(spot - 1, 0) * count, count), count)].astype(f32)
    before = jnp.where(lax.rem(spot, 2) == 1, before, -1.0)
    column = jnp.transpose(jnp.broadcast_to(own, (128, count)))[:, :1]
    return column, jnp.concatenate([before, own], axis=1)


def attend_back_kernel(
    segs, wo_h, grad_h, moe_h, packed_h, keys_h, q_h, heads_h, lse_h, residual_h, kv_proj_h, cosine_h, sine_h,
    dq, key_own, prev_out, kvo, layer_out,
    key_prev, head_grad, dkey, dvalue, drope, dpacked, dquery, cosine, sine,
    wo, grad, moe_part, packed, keys_all, q, heads, lse, residual, kv_proj,
    p0, p1, p2, k0, k1, k2, send, recv, load,
):
    at = Place()
    sems = Sems(send, recv)
    rows = q.shape[0]
    prev = packed.shape[0] - rows
    block = pl.ds(pl.multiple_of(lax.rem(at.y, 2) * rows, rows), rows)
    sources = (
        (wo_h, wo), (grad_h, grad), (moe_h, moe_part), (packed_h, packed), (keys_h, keys_all), (q_h, q),
        (heads_h, heads), (lse_h, lse), (residual_h, residual), (kv_proj_h, kv_proj),
        (cosine_h.at[block], cosine), (sine_h.at[block], sine),
    )
    loads = [pltpu.make_async_copy(src, dst, load.at[i]) for i, (src, dst) in enumerate(sources)]
    for c in loads:
        c.start()
    count = announce([at.hop(0, 1), at.hop(0, 3), at.sibling])
    own_rows = residual.shape[0]

    def done(h, total):
        r = slice(h * (own_rows // 2), (h + 1) * (own_rows // 2))
        layer_out[r] = (residual[r] + total).astype(bf16)

    def keep_prev(h, total):
        prev_out[h * (own_rows // 2) : (h + 1) * (own_rows // 2)] = total.astype(bf16)

    step = 256
    loads[0].wait()
    loads[1].wait()
    for i in range(rows // step):
        r = pl.ds(i * step, step)
        head_grad[r] = dot_nt(grad[r], wo[...]).astype(bf16)
    meet(count)
    loads[2].wait()
    moe = scatter_stream(sems, at, moe_part, p0, p1, p2, own_rows, done)
    next(moe)
    for c in loads[3:]:
        c.wait()
    qseg, kseg = segments(segs, rows)

    def block_back(head, start, size, lo, hi, diagonal):
        r = slice(start, start + size)
        lane = lax.broadcasted_iota(jnp.int32, (size, 2 * ROPE), 1)
        rope = jnp.where(lane // ROPE == head, q[r, 2 * NOPE :], jnp.zeros((), bf16))
        query = jnp.concatenate([q[r, head * NOPE : (head + 1) * NOPE], rope], axis=1)
        keys = jnp.concatenate([packed[lo:hi, head * 2 * NOPE : head * 2 * NOPE + NOPE], keys_all[lo:hi, LAT:]], axis=1)
        scores = dot_nt(query, keys)
        allowed = qseg[r] == kseg[:, lo:hi]
        if diagonal:
            ahead = lax.broadcasted_iota(jnp.int32, scores.shape, 1) - lax.broadcasted_iota(jnp.int32, scores.shape, 0)
            allowed = allowed & (ahead <= start)
        p = jnp.exp2(jnp.where(allowed, scores * (SCALE * LOG2E) - lse[head, r], -1e30))
        upstream = head_grad[r, head * VDIM : (head + 1) * VDIM]
        out = heads[r, head * VDIM : (head + 1) * VDIM]
        inner = jnp.sum(upstream.astype(f32) * out.astype(f32), axis=1, keepdims=True)
        d = dot_nt(upstream, packed[lo:hi, head * 2 * NOPE + NOPE : (head + 1) * 2 * NOPE])
        ds = (p * (d - inner)).astype(bf16)
        dkey[lo:hi] += dot_tn(ds, query)
        dvalue[lo:hi] += dot_tn(p.astype(bf16), upstream)
        return dot_nn(ds, keys)

    def keys_back(head, lo, hi):
        dpacked[lo:hi, head * 2 * NOPE : head * 2 * NOPE + NOPE] = (dkey[lo:hi, :NOPE] * SCALE).astype(bf16)
        dpacked[lo:hi, head * 2 * NOPE + NOPE : (head + 1) * 2 * NOPE] = dvalue[lo:hi].astype(bf16)
        if head == 0:
            drope[lo:hi] = dkey[lo:hi, NOPE:]
        else:
            drope[lo:hi] += dkey[lo:hi, NOPE:]

    def latent_back(ref, lo):
        for start in range(0, rows, 512):
            r, to = slice(lo + start, lo + start + 512), slice(start, start + 512)
            ref[to, :LAT] = dot_nt(dpacked[r], kv_proj[...]).astype(bf16)
            rope = drope[r]
            ref[to, LAT:] = ((rope + pltpu.roll(rope, ROPE, 1)) * SCALE).astype(bf16)

    wide_step = 512
    for head in range(2):
        dkey[...] = jnp.zeros_like(dkey)
        dvalue[...] = jnp.zeros_like(dvalue)
        for start in range(0, rows, wide_step):
            dquery[head, start : start + wide_step] = block_back(head, start, wide_step, 0, prev, False)
            if (head, start) != (1, wide_step):
                next(moe, None)
        keys_back(head, 0, prev)
    latent_back(key_prev, 0)
    prevs = scatter_stream(sems, at, key_prev, k0, k1, k2, own_rows, keep_prev)
    next(prevs)
    for head in range(2):
        dkey[prev:] = jnp.zeros_like(dkey[prev:])
        dvalue[prev:] = jnp.zeros_like(dvalue[prev:])
        for i in range(rows // ATT):
            r = slice(ATT * i, ATT * (i + 1))
            total = dquery[head, r] + block_back(head, ATT * i, ATT, prev, prev + ATT * (i + 1), True)
            dquery[head, r] = total * SCALE
            if head == 1:
                lane = lax.broadcasted_iota(jnp.int32, (ATT, 2 * ROPE), 1)
                rope = jnp.where(lane < ROPE, dquery[0, r, NOPE:], dquery[1, r, NOPE:])
                rope = rope * cosine[r] - swapped(rope) * sine[r]
                turned = pltpu.roll(dquery[1, r, :NOPE], ROPE, 1)
                dq[r, :NOPE] = dquery[0, r, :NOPE].astype(bf16)
                dq[r, NOPE : 2 * NOPE] = jnp.where(lane < ROPE, rope, turned).astype(bf16)
                dq[r, 2 * NOPE :] = jnp.where(lane < ROPE, turned, rope).astype(bf16)
            if (head, i) in ((0, 2), (1, 0), (1, 2)):
                next(prevs, None)
            if (head, i) == (1, 1):
                together(moe)
        keys_back(head, prev, prev + rows)
    latent_back(key_own, prev)
    spots, wide = kvo.shape[0], kvo.shape[2]
    kv = dot_tn(keys_all[:, :LAT], dpacked[...]).astype(bf16)
    kv_rows = kv.shape[0] // spots
    kvo[:, :kv_rows] = kv.reshape(spots, kv_rows, wide)
    out_rows = wo.shape[0] // spots
    for j in range(grad.shape[1] // wide):
        term = dot_tn(heads[...], grad[:, j * wide : (j + 1) * wide]).astype(bf16)
        kvo[:, kv_rows + j * out_rows : kv_rows + (j + 1) * out_rows] = term.reshape(spots, out_rows, wide)
    together(prevs)
    sems.finish()


def attend_back(grad, wo, heads, q, packed, keys_all, segs, lse, kv_proj, moe_part, residual, cosine, sine):
    whole = pl.BlockSpec(memory_space=VM)
    held = pl.BlockSpec(memory_space=pl.ANY)
    rows, keys = q.shape[0], packed.shape[0]
    own_rows, width = residual.shape
    spots = lax.axis_size("seq")
    kvo_rows = (kv_proj.shape[0] * kv_proj.shape[1] + wo.shape[0] * wo.shape[1]) // spots // LAT
    return pl.pallas_call(
        attend_back_kernel,
        out_shape=[
            jax.ShapeDtypeStruct(q.shape, bf16),
            jax.ShapeDtypeStruct((rows, SPAN), bf16),
            jax.ShapeDtypeStruct((own_rows, SPAN), bf16),
            jax.ShapeDtypeStruct((spots, kvo_rows, LAT), bf16),
            jax.ShapeDtypeStruct((own_rows, width), bf16),
        ],
        in_specs=[whole] + [held] * 12,
        out_specs=[whole] * 5,
        scratch_shapes=[
            pltpu.VMEM((rows, SPAN), bf16),
            pltpu.VMEM((rows, 2 * VDIM), bf16),
            pltpu.VMEM((keys, 2 * NOPE), f32),
            pltpu.VMEM((keys, VDIM), f32),
            pltpu.VMEM((keys, 2 * ROPE), f32),
            pltpu.VMEM(packed.shape, bf16),
            pltpu.VMEM((2, rows, 2 * NOPE), f32),
            pltpu.VMEM((rows, 2 * ROPE), f32),
            pltpu.VMEM((rows, 2 * ROPE), f32),
            *(
                pltpu.VMEM(x.shape, x.dtype)
                for x in (wo, grad, moe_part, packed, keys_all, q, heads, lse, residual, kv_proj)
            ),
            *scatter_scratch(own_rows, width),
            *scatter_scratch(own_rows, SPAN),
            pltpu.SemaphoreType.DMA((20,)),
            pltpu.SemaphoreType.DMA((20,)),
            pltpu.SemaphoreType.DMA((12,)),
        ],
        compiler_params=pltpu.CompilerParams(collective_id=4, has_side_effects=True, vmem_limit_bytes=60 << 20),
        name="attend_back",
    )(segs, wo, grad, moe_part, packed, keys_all, q, heads, lse, residual, kv_proj, cosine, sine)


SEQ_TURNS = (1, 2, 3, 4, 5, 6)


def tail_kernel(
    key_own, prev_out, raw, latent_gain, gain, router_in, ffn_in,
    kvo_h, dq_h, normed_h, wq_h, wl_h, upstream_h, rows_h, cosine_h, sine_h,
    query_h, kvo_out_h, latent_out, grad_out, small_out,
    query_out, kvo_out, dq,
    work0, work1, own_sum, in_part, in_sum, in_own, lat_rows, lat_all, lat_work, lat_sum, prev_in, small,
    r0, r1, r2, s0, s1, s2, k0, k1, k2, n0, n1, n2, lw, ln,
    normed, wq, wl, upstream, rows_in, cosine, sine, send, recv, local,
):
    at = Place()
    sems = Sems(send, recv)
    rows = raw.shape[0]
    half = rows // 2
    own = pl.ds(pl.multiple_of(at.me * rows, rows), rows)
    spot = pl.ds(pl.multiple_of(lax.rem(at.y, 2) * 8 * rows + at.me * rows, rows), rows)
    sources = (
        (normed_h, normed), (wq_h, wq), (wl_h, wl), (cosine_h.at[spot], cosine), (sine_h.at[spot], sine),
        (upstream_h, upstream), (rows_h, rows_in), (kvo_h, work1), (dq_h, dq),
    )
    loads = [pltpu.make_async_copy(src, dst, local.at[4 + i]) for i, (src, dst) in enumerate(sources)]
    for i in (7, 8, 0, 1, 2, 3, 4, 5, 6):
        loads[i].start()
    greet([at.sibling] + [at.hop(axis, d) for axis in range(3) for d in (1, 2, 3)])

    def keep_own(h, total):
        own_sum[h * half : (h + 1) * half] = total

    def keep_in(h, total):
        in_sum[h * half : (h + 1) * half] = total

    swap = sems.start(prev_out, prev_in, at.across[1](at.y + 1 - 2 * lax.rem(at.y, 2)))
    owns = scatter_stream(sems, at, key_own, k0, k1, k2, rows, keep_own)
    next(owns)
    keeps = [pltpu.make_async_copy(query_out, query_h, local.at[2]), pltpu.make_async_copy(kvo_out, kvo_out_h, local.at[3])]

    def kept(stream, copy):
        yield from stream
        copy.start()

    loads[7].wait()
    second = kept(seq_stream(sems, at, work1, kvo_out, (s0, s1, s2), (2, 1)), keeps[1])
    next(second)
    next(owns)
    next(owns)
    loads[0].wait()
    loads[8].wait()
    work0[...] = dot_tn(normed[...], dq[...]).astype(bf16).reshape(work0.shape)
    first = kept(seq_stream(sems, at, work0, query_out, (r0, r1, r2), (1, 2)), keeps[0])
    next(first)
    next(owns)
    loads[1].wait()
    gain_part = jnp.zeros((1, normed.shape[1]), f32)
    step = 256
    for i in range(dq.shape[0] // step):
        r = pl.ds(i * step, step)
        part = dot_nt(dq[r], wq[...])
        gain_part = gain_part + jnp.sum(part * normed[r].astype(f32), axis=0, keepdims=True)
        in_part[r] = part.astype(bf16)
    in_rows = scatter_stream(sems, at, in_part, n0, n1, n2, rows, keep_in)
    running = []

    def latents():
        together(owns)
        swap.wait_recv()
        own_grad = own_sum[...] + jnp.where(lax.rem(at.y, 2) == 0, prev_in[...].astype(f32), 0.0)
        x = raw[...]
        inverse = lax.rsqrt(jnp.mean(x * x, axis=1, keepdims=True) + EPSILON)
        u = own_grad[:, :LAT]
        lat_gain_part = jnp.sum(u * x * inverse, axis=0, keepdims=True)
        s = u * latent_gain[...]
        inner = jnp.mean(s * x, axis=1, keepdims=True)
        lat_rows[:, :LAT] = (inverse * s - x * (inverse * inverse * inverse) * inner).astype(bf16)
        rope = own_grad[:, LAT:]
        loads[3].wait()
        loads[4].wait()
        rope = rope * cosine[...] - swapped(rope) * sine[...]
        lane = lax.broadcasted_iota(jnp.int32, rope.shape, 1)
        lat_rows[:, LAT:] = jnp.where(lane < ROPE, rope, 0.0).astype(bf16)
        gathered = gather_stream(sems, at, lat_rows, lat_all, rows, local.at[0])
        next(gathered)
        running.append(in_rows)
        loads[2].wait()
        in_own[...] = dot_nn(lat_rows[:, : LAT + ROPE], wl[...])
        attn_gain = gain_part + jnp.sum(in_own[...] * normed[own].astype(f32), axis=0, keepdims=True)
        small_out[:EXPERTS] = router_in[...]
        small_out[EXPERTS:] = jnp.zeros_like(router_in)
        small_out[EXPERTS : EXPERTS + 1] = attn_gain / gain[...]
        small_out[EXPERTS + 1 : EXPERTS + 2] = ffn_in[...]
        small_out[EXPERTS + 2 : EXPERTS + 3, :LAT] = lat_gain_part
        running.append(small_stream(sems, at, small, small_out))
        yield from gathered
        width = lat_work.shape[0] * lat_work.shape[1]
        mine = normed[:, pl.ds(pl.multiple_of(at.me * width, width), width)]
        lat_work[...] = dot_tn(mine, lat_all[...]).astype(bf16).reshape(lat_work.shape)
        yield from seq_direct(sems, at, lat_work, lat_sum, lw, ln)
        yield from gather_stream(sems, at, lat_sum, latent_out, lat_sum.shape[0], local.at[1])

    chain = latents()
    running.append(chain)
    count = 0
    while running:
        for stream in list(running):
            try:
                next(stream)
            except StopIteration:
                running.remove(stream)
        count += 1
        if count in SEQ_TURNS:
            next(first, None)
            next(second, None)
    together(first, second)
    loads[5].wait()
    loads[6].wait()
    u = in_sum[...] + in_own[...]
    x = rows_in[...].astype(f32)
    inverse = lax.rsqrt(jnp.mean(x * x, axis=1, keepdims=True) + EPSILON)
    s = u * gain[...]
    inner = jnp.mean(s * x, axis=1, keepdims=True)
    grad_out[...] = (upstream[...] + (inverse * s - x * (inverse * inverse * inverse) * inner)).astype(bf16)
    for c in keeps:
        c.wait()
    sems.finish()


def tail(dq, key_own, prev_out, kvo, normed, wq, wl, raw, latent_gain, gain, upstream, rows_in, router_in, ffn_in, cosine, sine):
    whole = pl.BlockSpec(memory_space=VM)
    held = pl.BlockSpec(memory_space=pl.ANY)
    rows, width = rows_in.shape
    spots = kvo.shape[0]
    query_shape = (spots, width // spots, dq.shape[1])
    slice_rows = width // lax.axis_size("exp") // spots
    lat_shape = (spots, slice_rows, SPAN)
    return pl.pallas_call(
        tail_kernel,
        out_shape=[
            jax.ShapeDtypeStruct(query_shape, bf16),
            jax.ShapeDtypeStruct(kvo.shape, bf16),
            jax.ShapeDtypeStruct((8 * spots, slice_rows, SPAN), bf16),
            jax.ShapeDtypeStruct((rows, width), bf16),
            jax.ShapeDtypeStruct((2 * EXPERTS, width), f32),
        ],
        in_specs=[whole] * 7 + [held] * 9,
        out_specs=[held] * 2 + [whole] * 3,
        scratch_shapes=[
            pltpu.VMEM(query_shape, bf16),
            pltpu.VMEM(kvo.shape, bf16),
            pltpu.VMEM(dq.shape, bf16),
            pltpu.VMEM(query_shape, bf16),
            pltpu.VMEM(kvo.shape, bf16),
            pltpu.VMEM((rows, SPAN), f32),
            pltpu.VMEM((8 * rows, width), bf16),
            pltpu.VMEM((rows, width), f32),
            pltpu.VMEM((rows, width), f32),
            pltpu.VMEM((rows, SPAN), bf16),
            pltpu.VMEM((8 * rows, SPAN), bf16),
            pltpu.VMEM(lat_shape, bf16),
            pltpu.VMEM(lat_shape, bf16),
            pltpu.VMEM((rows, SPAN), bf16),
            pltpu.VMEM((4, 4, 2 * EXPERTS, width), bf16),
            *seq_scratch(*query_shape[1:]),
            *seq_scratch(*kvo.shape[1:]),
            *scatter_scratch(rows, SPAN),
            *scatter_scratch(rows, width),
            pltpu.VMEM((3, 4, slice_rows, SPAN), bf16),
            pltpu.VMEM((3, slice_rows, SPAN), bf16),
            pltpu.VMEM(normed.shape, bf16),
            pltpu.VMEM(wq.shape, bf16),
            pltpu.VMEM(wl.shape, bf16),
            pltpu.VMEM(upstream.shape, f32),
            pltpu.VMEM(rows_in.shape, bf16),
            pltpu.VMEM((rows, 2 * ROPE), f32),
            pltpu.VMEM((rows, 2 * ROPE), f32),
            pltpu.SemaphoreType.DMA((130,)),
            pltpu.SemaphoreType.DMA((130,)),
            pltpu.SemaphoreType.DMA((13,)),
        ],
        compiler_params=pltpu.CompilerParams(collective_id=3, has_side_effects=True, vmem_limit_bytes=60 << 20),
        name="tail",
    )(key_own, prev_out, raw, latent_gain, gain, router_in, ffn_in, kvo, dq, normed, wq, wl, upstream, rows_in, cosine, sine)


def start_kernel(
    rows_in, gain, latent_gain, routes, segs, ffn_gain, own_grad, wl_h, wq_h, kv_proj_h, wo_h, cosine_h, sine_h,
    normed_h, q_h, packed_h, keys_h, grad_h, hot_all, raw, heads, lse, residual, own_mid,
    normed, q, packed, keys, grad_half, wl, wq, kv_proj, wo,
    own_normed, ext, ext_all, prev_out, cosine, sine, part, column, p0, p1, p2, send, recv, local, load, store,
):
    at = Place()
    sems = Sems(send, recv)
    rows = rows_in.shape[0]
    block = 8 * rows
    half_seq = pl.ds(pl.multiple_of(lax.rem(at.y, 2) * block, block), block)
    sources = (
        (wl_h, wl), (cosine_h.at[half_seq], cosine), (sine_h.at[half_seq], sine), (wq_h, wq), (kv_proj_h, kv_proj), (wo_h, wo),
    )
    loads = [pltpu.make_async_copy(src, dst, load.at[i]) for i, (src, dst) in enumerate(sources)]
    for c in loads:
        c.start()
    partner = at.across[1](at.y + 1 - 2 * lax.rem(at.y, 2))
    count = announce([at.hop(0, 1), at.hop(0, 3), at.sibling, partner])
    x = rows_in[...].astype(f32)
    own_normed[...] = (x * lax.rsqrt(jnp.mean(x * x, axis=1, keepdims=True) + EPSILON) * gain[...]).astype(bf16)
    meet(count)
    big = gather_stream(sems, at, own_normed, normed, rows, local.at[0])
    next(big)
    loads[0].wait()
    lat = dot_nt(own_normed[...], wl[...])
    raw[...] = lat[:, :LAT]
    x = lat[:, :LAT]
    x = x * lax.rsqrt(jnp.mean(x * x, axis=1, keepdims=True) + EPSILON) * latent_gain[...]
    rope = jnp.concatenate([lat[:, LAT:], lat[:, LAT:]], axis=1)
    loads[1].wait()
    loads[2].wait()
    own = pl.ds(pl.multiple_of(at.me * rows, rows), rows)
    rope = rope * cosine[own] + swapped(rope) * sine[own]
    number = lax.broadcasted_iota(jnp.int32, (128, rows), 0)
    hot = jnp.zeros((128, rows), f32)
    for k in range(routes.shape[0]):
        hot = hot + jnp.where(number == routes[k : k + 1], 1.0, 0.0)
    hot = pltpu.roll(jnp.transpose(hot), ROPE, 1)
    lane = lax.broadcasted_iota(jnp.int32, rope.shape, 1)
    prev_out[:, :LAT] = x.astype(bf16)
    prev_out[:, LAT:] = jnp.where(lane < ROPE, rope, hot).astype(bf16)
    swap = sems.start(prev_out, ext.at[:, pl.ds(SPAN, SPAN)], partner)
    ext[:, :SPAN] = prev_out[...]
    next(big)
    swap.wait_recv()
    little = gather_stream(sems, at, ext, ext_all, rows, local.at[1])
    next(little)
    together(big)
    stores = [pltpu.make_async_copy(normed, normed_h, store.at[0])]
    stores[0].start()
    loads[3].wait()
    loads[4].wait()
    step = 256
    lane = lax.broadcasted_iota(jnp.int32, (step, 2 * ROPE), 1)
    for i in range(block // step):
        r = pl.ds(i * step, step)
        query = dot_nn(normed[r], wq[...])
        q[r, :NOPE] = query[:, :NOPE].astype(bf16)
        one, two = query[:, NOPE : 2 * NOPE], query[:, 2 * NOPE :]
        q[r, NOPE : 2 * NOPE] = jnp.where(lane < ROPE, pltpu.roll(one, ROPE, 1), pltpu.roll(two, ROPE, 1)).astype(bf16)
        rope = jnp.where(lane < ROPE, one, two)
        q[r, 2 * NOPE :] = (rope * cosine[r] + swapped(rope) * sine[r]).astype(bf16)
        if i % 2:
            next(little, None)
    stores.append(pltpu.make_async_copy(q, q_h, store.at[1]))
    stores[1].start()
    together(little)
    early = gather_stream(sems, at, own_grad.at[pl.ds(0, rows // 2)], grad_half, rows // 2, local.at[2])
    next(early)
    for side in range(2):
        r = pl.ds((1 - side) * block, block)
        keys[r, :LAT] = ext_all[:, side * SPAN : side * SPAN + LAT]
        rope = ext_all[:, side * SPAN + LAT : (side + 1) * SPAN].astype(f32)
        turned = pltpu.roll(rope, ROPE, 1)
        if side == 0:
            hot_all[...] = turned.astype(bf16)
        wide_lane = lax.broadcasted_iota(jnp.int32, rope.shape, 1)
        keys[r, LAT:] = jnp.where(wide_lane < ROPE, rope, turned).astype(bf16)
        packed[r] = dot_nn(ext_all[:, side * SPAN : side * SPAN + LAT], kv_proj[...]).astype(bf16)
        for ref, dst in ((keys, keys_h), (packed, packed_h)):
            stores.append(pltpu.make_async_copy(ref.at[r], dst.at[r], store.at[len(stores)]))
            stores[-1].start()
    qseg, kseg = segments(segs, block)
    column[...] = qseg
    shape = (ATT, 2 * block)
    ahead = lax.broadcasted_iota(jnp.int32, shape, 1) - lax.broadcasted_iota(jnp.int32, shape, 0)
    loads[5].wait()

    def ready(dist):
        index = lax.rem(at.chip + dist, 4)
        r = row_block(index)
        allowed = (column[r] == kseg) & (ahead <= index * ATT + block)
        for head in range(2):
            rope = jnp.where(lane // ROPE == head, q[r, 2 * NOPE :], jnp.zeros((), bf16))
            query = jnp.concatenate([q[r, head * NOPE : (head + 1) * NOPE], rope], axis=1)
            head_keys = jnp.concatenate([packed[:, head * 2 * NOPE : head * 2 * NOPE + NOPE], keys[:, LAT:]], axis=1)
            scores = jnp.where(allowed, dot_nt(query, head_keys), -1e30)
            top = jnp.max(scores, axis=1, keepdims=True)
            weights = jnp.exp2((scores - top) * (SCALE * LOG2E))
            total = jnp.sum(weights, axis=1, keepdims=True)
            out = dot_nn(weights.astype(bf16), packed[:, head * 2 * NOPE + NOPE : (head + 1) * 2 * NOPE])
            heads[r, head * VDIM : (head + 1) * VDIM] = (out / total).astype(bf16)
            lse[head, r] = top * (SCALE * LOG2E) + jnp.log2(total)
        part[r] = dot_nn(heads[r], wo[...]).astype(bf16)

    def done(h, total):
        r = slice(h * (rows // 2), (h + 1) * (rows // 2))
        x = rows_in[r].astype(f32) + total
        residual[r] = x
        own_mid[r] = (x * lax.rsqrt(jnp.mean(x * x, axis=1, keepdims=True) + EPSILON) * ffn_gain[...]).astype(bf16)

    out_rows = scatter_stream(sems, at, part, p0, p1, p2, rows, done, ready)
    next(out_rows)
    next(early)
    next(out_rows)
    next(early)
    next(out_rows)
    together(early)
    stores.append(pltpu.make_async_copy(grad_half, grad_h, store.at[len(stores)]))
    stores[-1].start()
    together(out_rows)
    for c in stores:
        c.wait()
    sems.finish()


def start(rows_in, gain, wl, latent_gain, wq, kv_proj, routes, cosine, sine, segs, wo, ffn_gain, own_grad):
    whole = pl.BlockSpec(memory_space=VM)
    held = pl.BlockSpec(memory_space=pl.ANY)
    rows, width = rows_in.shape
    block = 8 * rows
    shapes = [
        (block, width), (block, wq.shape[1]), (2 * block, kv_proj.shape[1]), (2 * block, SPAN), (block // 2, width),
    ]
    return pl.pallas_call(
        start_kernel,
        out_shape=[jax.ShapeDtypeStruct(shape, bf16) for shape in shapes]
        + [
            jax.ShapeDtypeStruct((block, 2 * ROPE), bf16),
            jax.ShapeDtypeStruct((rows, LAT), f32),
            jax.ShapeDtypeStruct((block, 2 * VDIM), bf16),
            jax.ShapeDtypeStruct((2, block, 1), f32),
            jax.ShapeDtypeStruct((rows, width), f32),
            jax.ShapeDtypeStruct((rows, width), bf16),
        ],
        in_specs=[whole] * 7 + [held] * 6,
        out_specs=[held] * 5 + [whole] * 6,
        scratch_shapes=[pltpu.VMEM(shape, bf16) for shape in shapes]
        + [pltpu.VMEM(x.shape, bf16) for x in (wl, wq, kv_proj, wo)]
        + [
            pltpu.VMEM((rows, width), bf16),
            pltpu.VMEM((rows, 2 * SPAN), bf16),
            pltpu.VMEM((block, 2 * SPAN), bf16),
            pltpu.VMEM((rows, SPAN), bf16),
            pltpu.VMEM((block, 2 * ROPE), f32),
            pltpu.VMEM((block, 2 * ROPE), f32),
            pltpu.VMEM((block, width), bf16),
            pltpu.VMEM((block, 1), f32),
            *scatter_scratch(rows, width),
            pltpu.SemaphoreType.DMA((50,)),
            pltpu.SemaphoreType.DMA((50,)),
            pltpu.SemaphoreType.DMA((3,)),
            pltpu.SemaphoreType.DMA((6,)),
            pltpu.SemaphoreType.DMA((7,)),
        ],
        compiler_params=pltpu.CompilerParams(collective_id=0, has_side_effects=True, vmem_limit_bytes=60 << 20),
        name="start",
    )(rows_in, gain, latent_gain, routes, segs, ffn_gain, own_grad, wl, wq, kv_proj, wo, cosine, sine)


def finish_kernel(
    weights_h, query_h, kvo_h, latent_h, layer_h, grad_h, small, early,
    expert_gate_h, expert_down_h, shared_gate_h, shared_down_h, query_out_h, kv_out_h, out_out_h, latent_out_h,
    layer_out_h, grad_out_h, router_out, attn_out, ffn_out, lat_gain_out,
    weights, query, kvo, latent, expert_gate, expert_down, shared_gate, shared_down, query_out, kv_out, out_out, latent_out,
    load, store,
):
    pairs = ((query_h, query), (latent_h, latent), (kvo_h, kvo), (weights_h, weights))
    loads = [pltpu.make_async_copy(src, dst, load.at[i]) for i, (src, dst) in enumerate(pairs)]
    for c in loads:
        c.start()
    stores = []

    def put(src, dst):
        c = pltpu.make_async_copy(src, dst, store.at[len(stores)])
        c.start()
        stores.append(c)

    put(layer_h, layer_out_h)
    put(grad_h, grad_out_h)
    router_out[...] = small[:EXPERTS]
    attn_out[...] = small[EXPERTS : EXPERTS + 1]
    ffn_out[...] = small[EXPERTS + 1 : EXPERTS + 2]
    lat_gain_out[...] = small[EXPERTS + 2 : EXPERTS + 3, :LAT]
    loads[0].wait()
    query_out[...] = query[...].reshape(query_out.shape).astype(f32)
    put(query_out, query_out_h)
    loads[1].wait()
    step = 512
    for i in range(latent_out.shape[1] // step):
        spot = step // latent.shape[1]
        rows = latent[i * spot : (i + 1) * spot].reshape(step, latent.shape[2]).astype(f32)
        latent_out[:, i * step : (i + 1) * step] = jnp.transpose(rows)[: latent_out.shape[0]]
        put(latent_out.at[:, pl.ds(i * step, step)], latent_out_h.at[:, pl.ds(i * step, step)])
    loads[2].wait()
    spots, _, wide = kvo.shape
    kv_rows = kv_out.shape[0] // spots
    kv_out[...] = kvo[:, :kv_rows].reshape(kv_out.shape).astype(f32)
    put(kv_out, kv_out_h)
    out_rows = out_out.shape[0] // spots
    for j in range(out_out.shape[1] // wide):
        piece = kvo[:, kv_rows + j * out_rows : kv_rows + (j + 1) * out_rows]
        out_out[:, j * wide : (j + 1) * wide] = piece.reshape(out_out.shape[0], wide).astype(f32)
    put(out_out, out_out_h)
    loads[3].wait()
    for c in range(expert_gate.shape[1] // 128):
        expert_gate[:, c * 128 : (c + 1) * 128] = weights[c * 128 : (c + 1) * 128].astype(f32)
    put(expert_gate, expert_gate_h)
    spot = expert_gate.shape[1]
    for ref, dst in ((expert_down, expert_down_h), (shared_gate, shared_gate_h), (shared_down, shared_down_h)):
        skip = 0
        if ref is expert_down:
            skip = early.shape[0]
            ref[:skip] = early[...].astype(f32)
        ref[skip:] = weights[spot : spot + ref.shape[0] - skip].astype(f32)
        put(ref, dst)
        spot += ref.shape[0] - skip
    for c in stores:
        c.wait()


def finish(weights, query, kvo, latent, layer_output, input_grad, small, early, shared, model_width, kv_shape, out_shape):
    whole = pl.BlockSpec(memory_space=VM)
    held = pl.BlockSpec(memory_space=pl.ANY)
    shapes = [
        (128, 2 * F), (F, 128), (2 * shared, 128), (shared, 128),
        (model_width, query.shape[2]), kv_shape, out_shape, (LAT + ROPE, model_width),
    ]
    little = [(EXPERTS, model_width), (1, model_width), (1, model_width), (1, LAT)]
    return pl.pallas_call(
        finish_kernel,
        out_shape=[jax.ShapeDtypeStruct(shape, f32) for shape in shapes]
        + [jax.ShapeDtypeStruct(x.shape, bf16) for x in (layer_output, input_grad)]
        + [jax.ShapeDtypeStruct(shape, f32) for shape in little],
        in_specs=[held] * 6 + [whole] * 2,
        out_specs=[held] * 10 + [whole] * 4,
        scratch_shapes=[pltpu.VMEM(x.shape, bf16) for x in (weights, query, kvo, latent)]
        + [pltpu.VMEM(shape, f32) for shape in shapes]
        + [pltpu.SemaphoreType.DMA((4,)), pltpu.SemaphoreType.DMA((16,))],
        compiler_params=pltpu.CompilerParams(vmem_limit_bytes=56 << 20),
        name="finish",
    )(weights, query, kvo, latent, layer_output, input_grad, small, early)


def tables(seq_rows):
    lane = np.arange(2 * ROPE)
    half = ROPE // 2
    frequency = np.exp((lane % half) * (-math.log(10000.0) / half))
    angles = np.arange(seq_rows)[:, None] * frequency[None, :]
    sign = np.where(lane % ROPE < half, -1.0, 1.0)
    return np.cos(angles).astype(np.float32), (np.sin(angles) * sign[None, :]).astype(np.float32)


def local(
    layer_input, attn_gain, query_proj, latent_proj, latent_gain, kv_proj, output_proj, ffn_gain, router_proj,
    shared_gate_up, shared_down, expert_gate_up, expert_down, segment_ids, expert_routes, out_grad,
):
    own_rows, model_width = layer_input.shape
    cosine, sine = tables(2 * own_rows * lax.axis_size("exp"))
    wl = latent_proj.T
    router = router_proj.T
    shared = shared_down.shape[0]
    pair_s = shared_gate_up.transpose(1, 2, 0).reshape(2 * shared, model_width)
    pair_e, down_e = expert_gate_up[0], expert_down[0]
    segs = segment_ids[None]
    attn_row, latent_row, ffn_row = attn_gain[None], latent_gain[None], ffn_gain[None]
    normed_all, q, packed, keys, grad_half, hot, latent_raw, heads, lse, residual, own_mid = start(
        layer_input, attn_row, wl, latent_row, query_proj, kv_proj, expert_routes.T, cosine, sine,
        segs, output_proj, ffn_row, out_grad,
    )
    terms, act, dpre, logit, router_term, early = mlp(
        own_mid, out_grad, pair_s, pair_e, shared_down, down_e, grad_half, router, hot
    )
    weight_sum = lax.psum_scatter(terms.reshape(-1, 128), "seq", scatter_dimension=0, tiled=True)
    residual_grad, ffn_term, attn_grad_all, moe_part = turn(
        dpre, act, pair_s, pair_e, shared_down, down_e, logit, router, residual, ffn_row, out_grad
    )
    dq, key_own, prev_sum, kvo, layer_output = attend_back(
        attn_grad_all, output_proj, heads, q, packed, keys, segs, lse, kv_proj, moe_part, residual, cosine, sine
    )
    query_sum, kvo_sum, latent_sum, input_grad, small = tail(
        dq, key_own, prev_sum, kvo, normed_all, query_proj, wl, latent_raw, latent_row, attn_row,
        residual_grad, layer_input, router_term, ffn_term, cosine, sine,
    )
    (
        expert_gate, expert_down_sum, shared_gate, shared_down_sum, query_sum, kv_sum, output_sum, latent_sum,
        layer_output, input_grad, router_sum, attn_gain_sum, ffn_gain_sum, latent_gain_sum,
    ) = finish(
        weight_sum, query_sum, kvo_sum, latent_sum, layer_output, input_grad, small, early, shared, model_width, kv_proj.shape, output_proj.shape
    )
    return (
        layer_output,
        input_grad,
        attn_gain_sum[0],
        query_sum,
        latent_sum.T,
        latent_gain_sum[0],
        kv_sum,
        output_sum,
        ffn_gain_sum[0],
        router_sum.T,
        shared_gate.reshape(2, shared, 128).transpose(2, 0, 1),
        shared_down_sum,
        expert_gate[None],
        expert_down_sum[None],
    )


def solution(mesh):
    in_specs = (
        P(("seq", "exp"), None),
        P(),
        P(None, "exp"),
        P(),
        P(),
        P(None, "exp"),
        P("exp", None),
        P(),
        P(),
        P(None, None, "exp"),
        P("exp", None),
        P("exp", None, None),
        P("exp", None, None),
        P(),
        P(("seq", "exp"), None),
        P(("seq", "exp"), None),
    )
    out_specs = (
        P(("seq", "exp"), None),
        P(("seq", "exp"), None),
        P(),
        P(None, "exp"),
        P(),
        P(),
        P(None, "exp"),
        P("exp", None),
        P(),
        P(),
        P("seq", None, "exp"),
        P("exp", "seq"),
        P("exp", "seq", None),
        P("exp", None, "seq"),
    )
    return jax.shard_map(local, mesh=mesh, in_specs=in_specs, out_specs=out_specs, check_vma=False)
```
